32 devices in a mesh: gx: 4 (over z), gy: 2 (over x), gz: 4 (over y, core).
Axes of the slice: x: 2, y: 2, z: 4, core: 2. Of those that a mesh axis runs over, the one named last changes fastest.
Arguments:
- populations: float32 [19, 16, 16, 512], P(None, 'gx', 'gy', 'gz'), may hold values from 0.02 to 0.09
- solid_cells: int32 [16, 16, 512], P('gx', 'gy', 'gz'), may hold values 0 or 1
- slot_cells: int32 [4, 2, 4, 64, 8, 128], P('gx', 'gy', 'gz'), may hold values from 0 to 4095
- slot_weights: float32 [4, 2, 4, 64, 8, 128], P('gx', 'gy', 'gz'), may hold values from 0 to 0.0625
- slot_owner: int32 [4, 2, 4, 64, 1], P('gx', 'gy', 'gz'), may hold values from 0 to 7; in each aligned block of 64 rows (0 to 63, 64 to 127, ..., all dimensions but the last counted through in order) at most 16 rows name the same one
- slot_block: int32 [4, 2, 4, 64], P('gx', 'gy', 'gz'), may hold values from 0 to 31
- train_of_block: int32 [4, 2, 4, 32], P('gx', 'gy', 'gz'), may hold values from 0 to 3
- marker_area: float32 [4, 2, 4, 32, 128], P('gx', 'gy', 'gz'), may hold values from 0.5 to 2
- train_velocity: float32 [4, 3], replicated, may hold values from -0.1 to 0.1
Outputs:
- populations_next: float32 [19, 16, 16, 512], P(None, 'gx', 'gy', 'gz')
- marker_force: float32 [4, 2, 4, 32, 3, 128], P('gx', 'gy', 'gz')
The draws below stay inside these ranges and needn't reach their ends.
Inputs may be any that keep to these rules, and one draw needn't show every extreme that they name: `slot_owner`: among the 64 slots of one device no owner is named more than 16 times, a bound that some block reaches.
All inputs are finite; a program needn't handle non-finite values. No bound on the sum of `solid_cells` on one device may be relied on, other than what follows from the above.
Results may differ from the reference program's by a relative error of at most 0.000065.
Values sent between devices are 32-bit elements; how exact they have to be, the bound alone decides.
No kernel may reach another device: no remote copies, remote signals or barrier semaphores. Data moves between devices by JAX's collectives and lax.ppermute only.
A program may use at most 128 MiB of HBM per device.

```python
import math
import jax
import jax.numpy as jnp
import numpy as np
from jax import lax

CX = 4
CY = 8
CZ = 128
SLOTS = 64
OWN = 32
MARK = 128
KERN = 8
TRAINS = 4
CAP = 16
NX = 16
NY = 16
NZ = 512
N_GX = 4
N_GY = 2
N_GZ = 4


def set_ends(entries, rng, least, top_value):
    shape = entries.shape
    index_at = [jax.random.randint(jax.random.fold_in(rng, axis), (), 0, shape[axis]) for axis in range(len(shape))]
    entries = entries.at[tuple(index_at)].set(least)
    longest = shape.index(max(shape))
    index_at[longest] = (index_at[longest] + 1) % shape[longest]
    return entries.at[tuple(index_at)].set(top_value)


def level_of(stream_key, dims, pieces, least, largest):
    loudness = 1.0
    for dim, shards_of in pieces:
        heights = jax.random.uniform(jax.random.fold_in(jax.random.fold_in(stream_key, 6), dim), (shards_of,), jnp.float32, least / len(pieces), largest / len(pieces))
        loudness = loudness * jnp.repeat(jnp.exp(heights), dims[dim] // shards_of).reshape((-1,) + (1,) * (len(dims) - 1 - dim))
    return loudness


def deal_out(rng, own, number, rows, amount, top, most, slope):
    ranking = jax.random.permutation(rng, amount)
    heavy_load, usual = portions_of(amount, rows * top, most, slope, True), portions_of(amount, rows * top, most, slope, False)
    places = jnp.arange(amount)

    def named(tallies, rotation):
        used = int((tallies > 0).sum())
        fixed = max(1, used // 4)
        shifted = fixed + (places - fixed + rotation * (used - fixed)) % max(1, amount - fixed)
        return jnp.zeros((amount,), jnp.int32).at[ranking[jnp.where(places < fixed, places, shifted)]].set(jnp.asarray(tallies, jnp.int32))

    tallies = jnp.where(number % 4 == 0, named(heavy_load, number // 4), named(usual, number - number // 4 - 1))
    mixed = jax.random.permutation(jax.random.fold_in(own, 3), amount)
    source_of, taker = mixed[0:amount // 2 * 2:2], mixed[1:amount // 2 * 2:2]
    slack = jnp.minimum(tallies[source_of] - 1, most - tallies[taker]) // 2
    slack = jnp.where((source_of == ranking[0]) | (taker == ranking[0]) | (tallies[taker] == 0), 0, jnp.maximum(slack, 0))
    shifted = jax.random.randint(jax.random.fold_in(own, 4), (amount // 2,), 0, 1 << 20) % (slack + 1)
    tallies = tallies.at[source_of].add(-shifted).at[taker].add(shifted)
    items = jnp.searchsorted(jnp.cumsum(tallies), jnp.arange(rows * top), side="right").astype(jnp.int32)
    listing = items.reshape(top, rows).T
    listing = listing[jax.random.permutation(jax.random.fold_in(own, 1), rows)]
    rotation = jax.random.randint(jax.random.fold_in(own, 2), (rows, 1), 0, top)
    return jnp.take_along_axis(listing, (jnp.arange(top)[None, :] + rotation) % top, axis=1)


def portions_of(amount, total, most, skew, full):
    portions = [(1 << 20) // math.isqrt(grade ** skew) + 1 for grade in range(1, amount + 1)]
    largest = most if full else min(most, max(-(-total // amount), total * portions[0] // sum(portions)))
    least = 1 if total - largest >= amount - 1 else 0
    holding, spare = [largest] + [least] * (amount - 1), total - largest - least * (amount - 1)
    while spare > 0:
        movable = [i for i in range(1, amount) if holding[i] < largest] or [i for i in range(1, amount) if holding[i] < most]
        mass, left = sum([portions[i] for i in movable]), spare
        for i in movable:
            more = min(most - holding[i], max(1, left * portions[i] // mass), spare)
            holding[i] = holding[i] + more
            spare = spare - more
    return np.array(holding)


def setup_inputs(seed: int = 0) -> dict:
    seeds = jax.random.split(jax.random.key(seed), 10)
    populations = jnp.clip(0.02 + 0.07000000402331352 * jax.random.uniform(seeds[0], (19, NX, NY, NZ), jnp.float32) ** level_of(seeds[0], (19, NX, NY, NZ), ((1, 4), (2, 2), (3, 4)), -0.2, 0.2), 0.02, 0.09)
    solid_cells = set_ends((jax.random.randint(seeds[1], (NX, NY, NZ), 0, 8) < 1).astype(jnp.int32), jax.random.fold_in(seeds[1], 1), 0, 1)
    slot_cells = set_ends(jax.random.randint(seeds[2], (N_GX, N_GY, N_GZ, SLOTS, KERN, MARK), 0, min(CX * CY * CZ, 16369)), jax.random.fold_in(seeds[2], 1), 0, (min(CX * CY * CZ, 16369)) - 1).astype(jnp.int32)
    slot_weights = jnp.clip(0.0625 * jax.random.uniform(seeds[3], (N_GX, N_GY, N_GZ, SLOTS, KERN, MARK), jnp.float32) ** level_of(seeds[3], (N_GX, N_GY, N_GZ, SLOTS, KERN, MARK), ((0, 4), (1, 2), (2, 4)), -0.2, 0.2), 0.0, 0.0625)
    slot_owner_keys = jax.random.split(jax.random.fold_in(seeds[4], 1), N_GX * N_GY * N_GZ * SLOTS // SLOTS)
    slot_owner_turns = jax.random.permutation(jax.random.fold_in(seeds[4], 3), N_GX * N_GY * N_GZ * SLOTS // SLOTS)
    slot_owner = jax.vmap(lambda own, number: deal_out(jax.random.fold_in(seeds[4], 2), own, number, SLOTS, N_GX * N_GY, 1, CAP, 2))(slot_owner_keys, slot_owner_turns).reshape((N_GX, N_GY, N_GZ, SLOTS, 1))
    slot_block = set_ends(jax.random.randint(seeds[5], (N_GX, N_GY, N_GZ, SLOTS), 0, OWN), jax.random.fold_in(seeds[5], 1), 0, OWN - 1).astype(jnp.int32)
    train_of_block = set_ends(jax.random.randint(seeds[6], (N_GX, N_GY, N_GZ, OWN), 0, TRAINS), jax.random.fold_in(seeds[6], 1), 0, TRAINS - 1).astype(jnp.int32)
    marker_area = jnp.clip(jnp.exp(math.log(2.0) - 1.3862944 * jax.random.uniform(seeds[7], (N_GX, N_GY, N_GZ, OWN, MARK), jnp.float32) ** level_of(seeds[7], (N_GX, N_GY, N_GZ, OWN, MARK), ((0, 4), (1, 2), (2, 4)), -0.2, 0.2)), 0.5, 2.0)
    train_velocity = jnp.clip(jax.random.uniform(seeds[8], (TRAINS, 3), jnp.float32, -0.1, 0.1), -0.1, 0.1)
    return dict(populations=populations, solid_cells=solid_cells, slot_cells=slot_cells, slot_weights=slot_weights, slot_owner=slot_owner, slot_block=slot_block, train_of_block=train_of_block, marker_area=marker_area, train_velocity=train_velocity)


velocity_table = np.array([[0, 0, 0], [1, 0, 0], [-1, 0, 0], [0, 1, 0], [0, -1, 0], [0, 0, 1], [0, 0, -1], [1, 1, 0], [-1, -1, 0], [1, -1, 0], [-1, 1, 0], [1, 0, 1], [-1, 0, -1], [1, 0, -1], [-1, 0, 1], [0, 1, 1], [0, -1, -1], [0, 1, -1], [0, -1, 1]])
weight_table = [1.0 / 3.0] + [1.0 / 18.0] * 6 + [1.0 / 36.0] * 12
opposite_table = [0, 2, 1, 4, 3, 6, 5, 8, 7, 10, 9, 12, 11, 14, 13, 16, 15, 18, 17]
stress_pairs = [(0, 0), (1, 1), (2, 2), (0, 1), (0, 2), (1, 2)]
tau_base = 0.55
smag_term = 18.0 * 1.4142135623730951 * 0.17 * 0.17
regular_eps = 0.0001
stiffness = 2.0
far_velocity = (0.02, 0.06, 0.0)

def project(direction, vector):
    projection = 0.0 * vector[0]
    for component in range(3):
        lattice_step = int(velocity_table[direction][component])
        if lattice_step != 0:
            projection = projection + lattice_step * vector[component]
    return projection

def moments(populations):
    density = populations[0]
    momentum = [jnp.zeros_like(density) for component in range(3)]
    for direction in range(1, 19):
        density = density + populations[direction]
        for component in range(3):
            lattice_step = int(velocity_table[direction][component])
            if lattice_step == 1:
                momentum[component] = momentum[component] + populations[direction]
            elif lattice_step == -1:
                momentum[component] = momentum[component] - populations[direction]
    return (density, momentum)

def equilibrium(density, velocity):
    speed_sq = velocity[0] * velocity[0] + velocity[1] * velocity[1] + velocity[2] * velocity[2]
    result = []
    for direction in range(19):
        projected = project(direction, velocity)
        result.append(weight_table[direction] * density * (1.0 + 3.0 * projected + 4.5 * projected * projected - 1.5 * speed_sq))
    return result

def collide(populations, cell_force, solid_cells):
    density, momentum = moments(populations)
    velocity = [(momentum[component] + 0.5 * cell_force[component]) / density for component in range(3)]
    balance = equilibrium(density, velocity)
    stress = [jnp.zeros_like(density) for pair_pos in range(6)]
    for direction in range(19):
        non_eq = populations[direction] - balance[direction]
        for pair_pos in range(6):
            row_axis, col_axis = stress_pairs[pair_pos]
            factor = int(velocity_table[direction][row_axis] * velocity_table[direction][col_axis])
            if factor != 0:
                stress[pair_pos] = stress[pair_pos] + factor * non_eq
    shear_sq = stress[0] * stress[0] + stress[1] * stress[1] + stress[2] * stress[2]
    shear_sq = shear_sq + 2.0 * (stress[3] * stress[3] + stress[4] * stress[4] + stress[5] * stress[5])
    magnitude = jnp.sqrt(shear_sq + regular_eps)
    relax_time = 0.5 * (tau_base + jnp.sqrt(tau_base * tau_base + smag_term * magnitude / density))
    guo_factor = 1.0 - 0.5 / relax_time
    speed_force = velocity[0] * cell_force[0] + velocity[1] * cell_force[1] + velocity[2] * cell_force[2]
    result = []
    for direction in range(19):
        along_force = project(direction, cell_force)
        along_speed = project(direction, velocity)
        source = guo_factor * weight_table[direction] * (3.0 * (along_force - speed_force) + 9.0 * along_speed * along_force)
        relaxed = populations[direction] - (populations[direction] - balance[direction]) / relax_time + source
        result.append(jnp.where(solid_cells == 1, populations[opposite_table[direction]], relaxed))
    return jnp.stack(result)

def reference(populations, solid_cells, slot_cells, slot_weights, slot_owner, slot_block, train_of_block, marker_area, train_velocity):
    density, momentum = moments(populations)
    rest_velocity = jnp.stack([momentum[component] / density for component in range(3)])
    cell_count = CX * CY * CZ
    tile_velocity = rest_velocity.reshape(3, N_GX, CX, N_GY, CY, N_GZ, CZ).transpose(1, 3, 5, 0, 2, 4, 6)
    tile_velocity = tile_velocity.reshape(N_GX, N_GY, N_GZ, 3, cell_count)

    def sample_tile(velocity_tile, cells_tile, weight_tile):
        return lax.optimization_barrier(jnp.sum(velocity_tile[:, cells_tile] * weight_tile[None], axis=2))

    def sample_plane(inputs):
        return jax.vmap(jax.vmap(sample_tile))(inputs[0], inputs[1], inputs[2])
    partial_value = lax.map(sample_plane, (tile_velocity, slot_cells, slot_weights))
    slot_rows = partial_value.transpose(0, 1, 2, 4, 3, 5).reshape(-1, 3 * MARK)
    layer = jnp.arange(N_GZ, dtype=jnp.int32)[None, None, :, None]
    block_id = ((slot_owner[..., 0] * N_GZ + layer) * OWN + slot_block).reshape(-1).astype(jnp.int32)
    marker_velocity = jax.ops.segment_sum(slot_rows, block_id, num_segments=N_GX * N_GY * N_GZ * OWN)
    marker_velocity = marker_velocity.reshape(N_GX, N_GY, N_GZ, OWN, 3, MARK)
    target = train_velocity[train_of_block]
    marker_force = stiffness * marker_area[..., None, :] * (target[..., None] - marker_velocity)
    slot_force = marker_force.reshape(-1, 3 * MARK)[block_id].reshape(N_GX, N_GY, N_GZ, SLOTS, 3, MARK)

    def spread_tile(force_tile, cells_tile, weight_tile):
        contrib = weight_tile[None] * force_tile.transpose(1, 0, 2)[:, :, None, :]
        return jnp.zeros((3, cell_count), jnp.float32).at[:, cells_tile.reshape(-1)].add(contrib.reshape(3, -1))

    def spread_plane(inputs):
        return jax.vmap(jax.vmap(spread_tile))(inputs[0], inputs[1], inputs[2])
    force_tiles = lax.map(spread_plane, (slot_force, slot_cells, slot_weights))
    cell_force = force_tiles.reshape(N_GX, N_GY, N_GZ, 3, CX, CY, CZ).transpose(3, 0, 4, 1, 5, 2, 6).reshape(3, NX, NY, NZ)
    relaxed = collide(populations, cell_force, solid_cells)
    read = jnp.stack([jnp.roll(relaxed[direction], tuple((int(lattice_step) for lattice_step in velocity_table[direction])), axis=(0, 1, 2)) for direction in range(19)])
    global_y = jnp.arange(NY, dtype=jnp.int32)
    global_z = jnp.arange(NZ, dtype=jnp.int32)
    on_side = ((global_y == 0) | (global_y == NY - 1))[:, None] | ((global_z == 0) | (global_z == NZ - 1))[None, :]
    far_field = jnp.array(equilibrium(1.0, list(far_velocity)), dtype=jnp.float32)
    populations_next = jnp.where(on_side[None, None], far_field[:, None, None, None], read)
    return (populations_next, marker_force)
```

```python
import functools
import jax
import jax.numpy as jnp
import numpy as np
from jax import lax
from jax.experimental import pallas as pl
from jax.experimental.pallas import tpu as pltpu
from jax.sharding import PartitionSpec as P

velocity_table = np.array(
    [
        [0, 0, 0],
        [1, 0, 0],
        [-1, 0, 0],
        [0, 1, 0],
        [0, -1, 0],
        [0, 0, 1],
        [0, 0, -1],
        [1, 1, 0],
        [-1, -1, 0],
        [1, -1, 0],
        [-1, 1, 0],
        [1, 0, 1],
        [-1, 0, -1],
        [1, 0, -1],
        [-1, 0, 1],
        [0, 1, 1],
        [0, -1, -1],
        [0, 1, -1],
        [0, -1, 1],
    ]
)
weight_table = [1.0 / 3.0] + [1.0 / 18.0] * 6 + [1.0 / 36.0] * 12
opposite_table = [0, 2, 1, 4, 3, 6, 5, 8, 7, 10, 9, 12, 11, 14, 13, 16, 15, 18, 17]
stress_pairs = [(0, 0), (1, 1), (2, 2), (0, 1), (0, 2), (1, 2)]
tau_base = 0.55
smag_term = 18.0 * 1.4142135623730951 * 0.17 * 0.17
regular_eps = 0.0001
stiffness = 2.0
far_velocity = (0.02, 0.06, 0.0)
vmem_bytes = 40 << 20
group = 8


def going(axis, step):
    return [q for q in range(19) if int(velocity_table[q][axis]) == step]


def project(direction, vector):
    projection = 0.0 * vector[0]
    for component in range(3):
        lattice_step = int(velocity_table[direction][component])
        if lattice_step != 0:
            projection = projection + lattice_step * vector[component]
    return projection


def moments(populations):
    density = populations[0]
    momentum = [jnp.zeros_like(density) for component in range(3)]
    for direction in range(1, 19):
        density = density + populations[direction]
        for component in range(3):
            lattice_step = int(velocity_table[direction][component])
            if lattice_step == 1:
                momentum[component] = momentum[component] + populations[direction]
            elif lattice_step == -1:
                momentum[component] = momentum[component] - populations[direction]
    return (density, momentum)


def equilibrium(density, velocity):
    speed_sq = velocity[0] * velocity[0] + velocity[1] * velocity[1] + velocity[2] * velocity[2]
    result = []
    for direction in range(19):
        projected = project(direction, velocity)
        result.append(
            weight_table[direction]
            * density
            * (1.0 + 3.0 * projected + 4.5 * projected * projected - 1.5 * speed_sq)
        )
    return result


far_field = [float(np.float32(value)) for value in equilibrium(1.0, list(far_velocity))]


def collide(populations, cell_force, solid_cells):
    density, momentum = moments(populations)
    velocity = [
        (momentum[component] + 0.5 * cell_force[component]) / density for component in range(3)
    ]
    balance = equilibrium(density, velocity)
    stress = [jnp.zeros_like(density) for pair_pos in range(6)]
    for direction in range(19):
        non_eq = populations[direction] - balance[direction]
        for pair_pos in range(6):
            row_axis, col_axis = stress_pairs[pair_pos]
            factor = int(velocity_table[direction][row_axis] * velocity_table[direction][col_axis])
            if factor != 0:
                stress[pair_pos] = stress[pair_pos] + factor * non_eq
    shear_sq = stress[0] * stress[0] + stress[1] * stress[1] + stress[2] * stress[2]
    shear_sq = shear_sq + 2.0 * (
        stress[3] * stress[3] + stress[4] * stress[4] + stress[5] * stress[5]
    )
    magnitude = jnp.sqrt(shear_sq + regular_eps)
    relax_time = 0.5 * (tau_base + jnp.sqrt(tau_base * tau_base + smag_term * magnitude / density))
    relax_rate = 1.0 / relax_time
    guo_factor = 1.0 - 0.5 * relax_rate
    speed_force = (
        velocity[0] * cell_force[0] + velocity[1] * cell_force[1] + velocity[2] * cell_force[2]
    )
    result = []
    for direction in range(19):
        along_force = project(direction, cell_force)
        along_speed = project(direction, velocity)
        source = (
            guo_factor
            * weight_table[direction]
            * (3.0 * (along_force - speed_force) + 9.0 * along_speed * along_force)
        )
        relaxed = (
            populations[direction]
            - (populations[direction] - balance[direction]) * relax_rate
            + source
        )
        result.append(jnp.where(solid_cells == 1, populations[opposite_table[direction]], relaxed))
    return result


def full(shape):
    return jax.ShapeDtypeStruct(shape, jnp.float32)


def sample_kernel(pop_ref, cells_ref, weights_ref, ids_ref, trains_ref, areas_ref, out_ref, table):
    rows, lanes = (pop_ref.shape[1], pop_ref.shape[2])
    mark = cells_ref.shape[1]
    slots = ids_ref.shape[1]
    kernel = cells_ref.shape[0] // slots
    owned = areas_ref.shape[0]
    density, momentum = moments([pop_ref[q] for q in range(19)])
    for c in range(3):
        table[c] = momentum[c] / density
    out_ref[3 * slots : 3 * slots + owned, :] = areas_ref[...]
    out_ref[3 * slots + owned : 3 * slots + owned + 8, :] = jnp.zeros((8, mark), jnp.float32)
    out_ref[3 * slots + owned : 3 * slots + owned + 1, 0:slots] = ids_ref[...].astype(jnp.float32)
    out_ref[3 * slots + owned + 1 : 3 * slots + owned + 2, 0:owned] = trains_ref[...].astype(
        jnp.float32
    )

    def body(step, carry):
        first = pl.multiple_of(step * group, group)
        total = [jnp.zeros((group, mark), jnp.float32) for c in range(3)]
        for k in range(kernel):
            at = pl.ds(first * kernel + k, group, stride=kernel)
            cells = cells_ref[at, :]
            lane = cells & (lanes - 1)
            row = cells >> (lanes.bit_length() - 1)
            picked = [jnp.zeros((group, mark), jnp.float32) for c in range(3)]
            for r in range(rows):
                here = row == r
                for c in range(3):
                    line = jnp.broadcast_to(table[c, r : r + 1, :], (group, lanes))
                    got = jnp.take_along_axis(line, lane, axis=1, mode="promise_in_bounds")
                    picked[c] = jnp.where(here, got, picked[c])
            weight = weights_ref[at, :]
            total = [total[c] + weight * picked[c] for c in range(3)]
        for c in range(3):
            out_ref[pl.ds(pl.multiple_of(c * slots + first, group), group), :] = total[c]
        return carry

    lax.fori_loop(0, slots // group, body, 0)


def sample(populations, cells, weights, ids, trains, areas):
    slots = ids.shape[1]
    rows = 3 * slots + areas.shape[0] + 8
    return pl.pallas_call(
        sample_kernel,
        out_shape=full((rows, cells.shape[1])),
        scratch_shapes=[pltpu.VMEM((3,) + populations.shape[1:], jnp.float32)],
        compiler_params=pltpu.CompilerParams(vmem_limit_bytes=vmem_bytes),
        name="sample",
    )(populations, cells, weights, ids, trains, areas)


def split_dot(match, values):
    match = match.astype(jnp.bfloat16)
    total = None
    for part in range(3):
        piece = values.astype(jnp.bfloat16)
        values = values - piece.astype(jnp.float32)
        product = jnp.dot(match, piece, preferred_element_type=jnp.float32)
        total = product if total is None else total + product
    return total


def train_target(trains, speeds_ref, component):
    target = jnp.zeros(trains.shape, jnp.float32)
    for train in range(speeds_ref.shape[0]):
        target = jnp.where(trains == float(train), speeds_ref[train, component], target)
    return target


def spread_kernel(
    place_ref,
    speeds_ref,
    rows_ref,
    ids_ref,
    trains_ref,
    areas_ref,
    cells_ref,
    weights_ref,
    pop_ref,
    solid_ref,
    relaxed_ref,
    side_ref,
    up_ref,
    down_ref,
    marker_ref,
    force_ref,
    acc,
):
    rows, lanes = (pop_ref.shape[1], pop_ref.shape[2])
    mark = cells_ref.shape[1]
    slots = ids_ref.shape[0]
    kernel = cells_ref.shape[0] // slots
    owned = areas_ref.shape[0]
    peers = rows_ref.shape[0]
    bf = jnp.bfloat16

    ids = ids_ref[...].astype(jnp.float32)
    mine = place_ref[0] * owned + lax.broadcasted_iota(jnp.int32, (owned, 1), 0)
    wanted = jnp.concatenate([ids, mine.astype(jnp.float32)], axis=0)
    summed = [None] * 3
    area = None
    train = None
    for peer in range(peers):
        meta = 3 * slots + owned
        labels = rows_ref[peer, meta : meta + 1, 0:slots]
        match = (wanted == labels).astype(jnp.float32)
        for c in range(3):
            got = split_dot(match, rows_ref[peer, c * slots : (c + 1) * slots, :])
            summed[c] = got if summed[c] is None else summed[c] + got
        blocks = peer * owned + lax.broadcasted_iota(jnp.int32, (1, owned), 1)
        held = (ids == blocks.astype(jnp.float32)).astype(jnp.float32)
        got = split_dot(held, rows_ref[peer, 3 * slots : 3 * slots + owned, :])
        area = got if area is None else area + got
        got = jnp.sum(
            held * rows_ref[peer, meta + 1 : meta + 2, 0:owned], axis=1, keepdims=True
        )
        train = got if train is None else train + got
    for c in range(3):
        speed = train_target(train, speeds_ref, c)
        force_ref[:, c * mark : (c + 1) * mark] = stiffness * area * (speed - summed[c][0:slots])
        speed = train_target(trains_ref[...].astype(jnp.float32), speeds_ref, c)
        marker_ref[c] = stiffness * areas_ref[...] * (speed - summed[c][slots : slots + owned])

    acc[...] = jnp.zeros_like(acc)
    iota = lax.broadcasted_iota(jnp.int32, (16, mark), 0).astype(jnp.float32)
    steps = [(iota + 16.0 * j).astype(bf) for j in range(max(rows, lanes) // 16)]
    one, zero = (jnp.ones((16, mark), bf), jnp.zeros((16, mark), bf))

    def wide(entries, i):
        return jnp.broadcast_to(entries[i : i + 1, :], (16, mark)).astype(bf)

    def body(step, carry):
        first = pl.multiple_of(step * group, group)
        force = [force_ref[pl.ds(first, group), c * mark : (c + 1) * mark] for c in range(3)]
        for k in range(kernel):
            at = pl.ds(first * kernel + k, group, stride=kernel)
            cells = cells_ref[at, :]
            weight = weights_ref[at, :]
            lane = (cells & (lanes - 1)).astype(jnp.float32)
            row = (cells >> (lanes.bit_length() - 1)).astype(jnp.float32)
            parts = []
            for c in range(3):
                value = weight * force[c]
                high = value.astype(bf).astype(jnp.float32)
                parts += [high, value - high]
            left, right = ([], [])
            for i in range(group):
                lane_i, row_i = (wide(lane, i), wide(row, i))
                right.append(
                    jnp.concatenate(
                        [jnp.where(steps[j] == lane_i, one, zero) for j in range(lanes // 16)],
                        axis=0,
                    )
                )
                masks = [steps[j] == row_i for j in range(rows // 16)]
                pieces = []
                for part in parts:
                    part_i = wide(part, i)
                    pieces += [jnp.where(mask, part_i, zero) for mask in masks]
                left.append(jnp.concatenate(pieces, axis=0))
            acc[...] += lax.dot_general(
                jnp.concatenate(left, axis=1),
                jnp.concatenate(right, axis=1),
                (((1,), (1,)), ((), ())),
                preferred_element_type=jnp.float32,
            )
        return carry

    lax.fori_loop(0, slots // group, body, 0)
    cell_force = [
        acc[2 * c * rows : (2 * c + 1) * rows, :] + acc[(2 * c + 1) * rows : (2 * c + 2) * rows, :]
        for c in range(3)
    ]
    relaxed = collide([pop_ref[q] for q in range(19)], cell_force, solid_ref[...])
    for q in range(19):
        relaxed_ref[q] = relaxed[q]
    lane_at = lax.broadcasted_iota(jnp.int32, (rows, lanes), 1)
    for ref, step in ((up_ref, 1), (down_ref, -1)):
        packed = jnp.zeros((rows, lanes), jnp.float32)
        for i, q in enumerate(going(2, step)):
            edge = lanes - 1 if step == 1 else 0
            packed = jnp.where(
                lane_at == i, pltpu.roll(relaxed[q], (i - edge) % lanes, 1), packed
            )
        ref[...] = packed
    lower = place_ref[1] == 0
    for i in range(5):
        for x in range(rows // 8):
            side_ref[i, x : x + 1, :] = jnp.where(
                lower,
                relaxed[going(1, 1)[i]][8 * x + 7 : 8 * x + 8, :],
                relaxed[going(1, -1)[i]][8 * x : 8 * x + 1, :],
            )


def spread(place, speeds, rows, ids, trains, areas, cells, weights, populations, solid):
    mark = cells.shape[1]
    slots, owned = (ids.shape[0], areas.shape[0])
    line_count, lanes = solid.shape
    smem = pl.BlockSpec(memory_space=pltpu.SMEM)
    vmem = pl.BlockSpec(memory_space=pltpu.VMEM)
    return pl.pallas_call(
        spread_kernel,
        out_shape=(
            full(populations.shape),
            full((5, line_count // 8, lanes)),
            full((line_count, lanes)),
            full((line_count, lanes)),
            full((3, owned, mark)),
        ),
        in_specs=[smem, smem] + [vmem] * 8,
        scratch_shapes=[
            pltpu.VMEM((slots, 3 * mark), jnp.float32),
            pltpu.VMEM((6 * line_count, lanes), jnp.float32),
        ],
        compiler_params=pltpu.CompilerParams(vmem_limit_bytes=vmem_bytes),
        name="spread",
    )(place, speeds, rows, ids, trains, areas, cells, weights, populations, solid)


def stream_kernel(
    total_z, place_ref, relaxed_ref, side_ref, up_ref, down_ref, side_up_ref, side_down_ref,
    out_ref, ahead_ref, behind_ref,
):
    size_x, size_y, lanes = out_ref.shape[1:]
    shape = (size_y, lanes)
    y_at = lax.broadcasted_iota(jnp.int32, shape, 0)
    z_at = lax.broadcasted_iota(jnp.int32, shape, 1)
    lower = place_ref[1] == 0
    global_z = z_at + place_ref[2] * lanes
    on_side = (z_at < 0) | (y_at == jnp.where(lower, 0, size_y - 1))
    on_side = on_side | (global_z == 0) | (global_z == total_z - 1)
    for q in range(19):
        step_x, step_y, step_z = (int(step) for step in velocity_table[q])
        for x in range(size_x):
            here = slice(x * size_y, (x + 1) * size_y)
            cells = relaxed_ref[q, here, :]
            if step_y != 0:
                edge = 0 if step_y == 1 else size_y - 1
                halo = side_ref[going(1, step_y).index(q), x : x + 1, :]
                cells = jnp.where(y_at == edge, halo, pltpu.roll(cells, step_y % size_y, 0))
            if step_z != 0:
                pick = going(2, step_z).index(q)
                near = (up_ref if step_z == 1 else down_ref)[here, :]
                if step_y != 0:
                    far = (side_up_ref if step_z == 1 else side_down_ref)[here, :]
                    near = jnp.where(
                        y_at == edge,
                        pltpu.roll(far, step_y % size_y, 0),
                        pltpu.roll(near, step_y % size_y, 0),
                    )
                end = 0 if step_z == 1 else lanes - 1
                cells = jnp.where(
                    z_at == end,
                    pltpu.roll(near, (end - pick) % lanes, 1),
                    pltpu.roll(cells, step_z % lanes, 1),
                )
            cells = jnp.where(on_side, far_field[q], cells)
            target = x + step_x
            if target == size_x:
                ahead_ref[going(0, 1).index(q)] = cells
            elif target == -1:
                behind_ref[going(0, -1).index(q)] = cells
            else:
                out_ref[q, target] = cells
    for q in going(0, 1):
        out_ref[q, 0] = jnp.zeros(shape, jnp.float32)
    for q in going(0, -1):
        out_ref[q, size_x - 1] = jnp.zeros(shape, jnp.float32)


def stream(total_z, size_y, place, relaxed, side, up, down, side_up, side_down):
    rows, lanes = relaxed.shape[1:]
    smem = pl.BlockSpec(memory_space=pltpu.SMEM)
    vmem = pl.BlockSpec(memory_space=pltpu.VMEM)
    face = full((5, size_y, lanes))
    return pl.pallas_call(
        functools.partial(stream_kernel, total_z),
        out_shape=(full((19, rows // size_y, size_y, lanes)), face, face),
        in_specs=[smem] + [vmem] * 6,
        compiler_params=pltpu.CompilerParams(vmem_limit_bytes=vmem_bytes),
        name="stream",
    )(place, relaxed, side, up, down, side_up, side_down)


def place_kernel(next_ref, ahead_ref, behind_ref, out_ref, sems):
    size_x = out_ref.shape[1]
    copies = []
    for i in range(5):
        for which, ref, q, x in (
            (0, ahead_ref, going(0, 1)[i], 0),
            (1, behind_ref, going(0, -1)[i], size_x - 1),
        ):
            copies.append(
                pltpu.make_async_copy(ref.at[i], out_ref.at[q, x], sems.at[2 * i + which])
            )
    for copy in copies:
        copy.start()
    for copy in copies:
        copy.wait()


def place_faces(inner, ahead, behind):
    anywhere = pl.BlockSpec(memory_space=pl.ANY)
    vmem = pl.BlockSpec(memory_space=pltpu.VMEM)
    return pl.pallas_call(
        place_kernel,
        out_shape=full(inner.shape),
        in_specs=[anywhere, vmem, vmem],
        out_specs=anywhere,
        scratch_shapes=[pltpu.SemaphoreType.DMA((10,))],
        input_output_aliases={0: 0},
        name="place_faces",
    )(inner, ahead, behind)


def with_halo(cells, sides, width):
    for axis, dim in sides:
        count = lax.axis_size(axis)
        head = lax.slice_in_dim(cells, 0, width, axis=dim)
        tail = lax.slice_in_dim(cells, cells.shape[dim] - width, cells.shape[dim], axis=dim)
        cells = jnp.concatenate(
            [
                lax.ppermute(tail, axis, [(i, (i + 1) % count) for i in range(count)]),
                cells,
                lax.ppermute(head, axis, [((i + 1) % count, i) for i in range(count)]),
            ],
            axis=dim,
        )
    return cells


def settle(received, labels, owned, train_of_block, marker_area, train_velocity, mark):
    rows_in = received.reshape(-1, 3 * mark)
    label_rows = labels.reshape(-1)
    owner_match = (label_rows[None, :] == jnp.arange(owned, dtype=jnp.int32)[:, None]).astype(
        jnp.float32
    )
    marker_velocity = jnp.dot(owner_match, rows_in, precision=lax.Precision.HIGHEST).reshape(
        owned, 3, mark
    )
    trains = train_velocity.shape[0]
    train_rows = train_of_block.reshape(owned)
    train_match = (train_rows[:, None] == jnp.arange(trains, dtype=jnp.int32)[None, :]).astype(
        jnp.float32
    )
    target = jnp.dot(train_match, train_velocity, precision=lax.Precision.HIGHEST)
    areas = marker_area.reshape(owned, mark)
    marker_force = stiffness * areas[:, None, :] * (target[:, :, None] - marker_velocity)
    back_rows = jnp.dot(
        owner_match.T, marker_force.reshape(owned, 3 * mark), precision=lax.Precision.HIGHEST
    )
    return (marker_force, back_rows)


def per_device_general(
    populations,
    solid_cells,
    slot_cells,
    slot_weights,
    slot_owner,
    slot_block,
    train_of_block,
    marker_area,
    train_velocity,
):
    size_x, size_y, size_z = (populations.shape[1], populations.shape[2], populations.shape[3])
    cell_count = size_x * size_y * size_z
    slots, kernel, mark = (slot_cells.shape[3], slot_cells.shape[4], slot_cells.shape[5])
    owned = train_of_block.shape[3]
    peers_x = lax.axis_size("gx")
    peers_y = lax.axis_size("gy")
    peers = peers_x * peers_y
    capacity = max(2, 2 * slots // peers)
    density, momentum = moments(populations)
    rest_velocity = jnp.stack([momentum[component] / density for component in range(3)]).reshape(
        3, cell_count
    )
    cells = slot_cells.reshape(slots, kernel, mark)
    weights = slot_weights.reshape(slots, kernel, mark)
    partial_value = jnp.sum(rest_velocity[:, cells] * weights[None], axis=2)
    slot_rows = partial_value.transpose(1, 0, 2).reshape(slots, 3 * mark)
    slot_dest = slot_owner.reshape(slots)
    blocks = slot_block.reshape(slots)
    order = jnp.arange(slots, dtype=jnp.int32)
    earlier = (slot_dest[None, :] == slot_dest[:, None]) & (order[None, :] < order[:, None])
    slot_rank = jnp.sum(earlier.astype(jnp.int32), axis=1)
    target_row = slot_dest * capacity + slot_rank
    buffer_rows = jnp.arange(peers * capacity, dtype=jnp.int32)
    matches = buffer_rows[:, None] == target_row[None, :]
    placement = matches.astype(jnp.float32)
    outgoing = jnp.dot(placement, slot_rows, precision=lax.Precision.HIGHEST)
    labels = jnp.sum(jnp.where(matches, blocks[None, :] + 1, 0), axis=1) - 1
    received, got_labels = (
        lax.all_to_all(
            outgoing.reshape(peers, capacity, 3 * mark),
            ("gx", "gy"),
            split_axis=0,
            concat_axis=0,
            tiled=True,
        ),
        lax.all_to_all(
            labels.reshape(peers, capacity), ("gx", "gy"), split_axis=0, concat_axis=0, tiled=True
        ),
    )
    marker_force, back_rows = settle(
        received, got_labels, owned, train_of_block, marker_area, train_velocity, mark
    )
    returned = lax.all_to_all(
        back_rows.reshape(peers, capacity, 3 * mark),
        ("gx", "gy"),
        split_axis=0,
        concat_axis=0,
        tiled=True,
    )
    slot_force = jnp.dot(
        placement.T, returned.reshape(peers * capacity, 3 * mark), precision=lax.Precision.HIGHEST
    )
    slot_force = slot_force.reshape(slots, 3, mark).transpose(1, 0, 2)
    contrib = weights[None] * slot_force[:, :, None, :]
    cell_force = (
        jnp.zeros((3, cell_count), jnp.float32).at[:, cells.reshape(-1)].add(contrib.reshape(3, -1))
    )
    cell_force = cell_force.reshape(3, size_x, size_y, size_z)
    relaxed = collide(populations, cell_force, solid_cells)
    padded = with_halo(jnp.stack(relaxed), (("gx", 1), ("gy", 2), ("gz", 3)), 1)
    parts = []
    for direction in range(19):
        shift_x = 1 - int(velocity_table[direction][0])
        shift_y = 1 - int(velocity_table[direction][1])
        shift_z = 1 - int(velocity_table[direction][2])
        parts.append(
            padded[
                direction,
                shift_x : shift_x + size_x,
                shift_y : shift_y + size_y,
                shift_z : shift_z + size_z,
            ]
        )
    read = jnp.stack(parts)
    total_y = size_y * lax.axis_size("gy")
    total_z = size_z * lax.axis_size("gz")
    global_y = lax.axis_index("gy") * size_y + jnp.arange(size_y, dtype=jnp.int32)
    global_z = lax.axis_index("gz") * size_z + jnp.arange(size_z, dtype=jnp.int32)
    on_side = ((global_y == 0) | (global_y == total_y - 1))[:, None] | (
        (global_z == 0) | (global_z == total_z - 1)
    )[None, :]
    far_field = jnp.array(equilibrium(1.0, list(far_velocity)), dtype=jnp.float32)
    populations_next = jnp.where(on_side[None, None], far_field[:, None, None, None], read)
    return (populations_next, marker_force.reshape(1, 1, 1, owned, 3, mark))


def per_device(
    populations,
    solid_cells,
    slot_cells,
    slot_weights,
    slot_owner,
    slot_block,
    train_of_block,
    marker_area,
    train_velocity,
):
    size_x, size_y, size_z = (populations.shape[1], populations.shape[2], populations.shape[3])
    lines = size_x * size_y
    slots, kernel, mark = (slot_cells.shape[3], slot_cells.shape[4], slot_cells.shape[5])
    owned = train_of_block.shape[3]
    count_x, count_y, count_z = (lax.axis_size(axis) for axis in ("gx", "gy", "gz"))
    place = jnp.stack(
        [
            lax.axis_index("gx") * count_y + lax.axis_index("gy"),
            lax.axis_index("gy"),
            lax.axis_index("gz"),
        ]
    ).astype(jnp.int32)
    pops = populations.reshape(19, lines, size_z)
    cells = slot_cells.reshape(slots * kernel, mark)
    weights = slot_weights.reshape(slots * kernel, mark)
    areas = marker_area.reshape(owned, mark)
    ids = slot_owner.reshape(slots) * owned + slot_block.reshape(slots)
    trains = train_of_block.reshape(owned)
    rows = sample(
        pops, cells, weights, ids.reshape(1, slots), trains.reshape(1, owned), areas
    )
    rows = lax.all_gather(rows, ("gx", "gy"), axis=0)
    relaxed, side, up, down, marker_force = spread(
        place,
        train_velocity,
        rows,
        ids.reshape(slots, 1),
        trains.reshape(owned, 1),
        areas,
        cells,
        weights,
        pops,
        solid_cells.reshape(lines, size_z),
    )
    marker_force = marker_force.transpose(1, 0, 2).reshape(1, 1, 1, owned, 3, mark)
    swap = [(0, 1), (1, 0)]
    rise = [(i, i + 1) for i in range(count_z - 1)]
    fall = [(i + 1, i) for i in range(count_z - 1)]
    cross = lambda pairs: [
        (a * count_z + i, b * count_z + j) for a, b in swap for i, j in pairs
    ]
    got_side = lax.ppermute(side, "gy", swap)
    got_up = lax.ppermute(up, "gz", rise)
    got_down = lax.ppermute(down, "gz", fall)
    side_up = lax.ppermute(up, ("gy", "gz"), cross(rise))
    side_down = lax.ppermute(down, ("gy", "gz"), cross(fall))
    inner, ahead, behind = stream(
        size_z * count_z, size_y, place, relaxed, got_side, got_up, got_down, side_up, side_down
    )
    ahead = lax.ppermute(ahead, "gx", [(i, (i + 1) % count_x) for i in range(count_x)])
    behind = lax.ppermute(behind, "gx", [((i + 1) % count_x, i) for i in range(count_x)])
    return (place_faces(inner, ahead, behind), marker_force)


def solution(mesh):
    placed = (
        P(None, "gx", "gy", "gz"),
        P("gx", "gy", "gz"),
        P("gx", "gy", "gz", None, None, None),
        P("gx", "gy", "gz", None, None, None),
        P("gx", "gy", "gz", None, None),
        P("gx", "gy", "gz", None),
        P("gx", "gy", "gz", None),
        P("gx", "gy", "gz", None, None),
        P(),
    )
    small = mesh.shape["gy"] == 2 and mesh.shape["gx"] * mesh.shape["gy"] <= 16
    return jax.shard_map(
        per_device if small else per_device_general,
        mesh=mesh,
        in_specs=placed,
        out_specs=(P(None, "gx", "gy", "gz"), P("gx", "gy", "gz", None, None, None)),
        check_vma=False,
    )
```

```python
import functools
import jax
import jax.numpy as jnp
import numpy as np
from jax import lax
from jax.experimental import pallas as pl
from jax.experimental.pallas import tpu as pltpu
from jax.sharding import PartitionSpec as P

velocity_table = np.array(
    [
        [0, 0, 0],
        [1, 0, 0],
        [-1, 0, 0],
        [0, 1, 0],
        [0, -1, 0],
        [0, 0, 1],
        [0, 0, -1],
        [1, 1, 0],
        [-1, -1, 0],
        [1, -1, 0],
        [-1, 1, 0],
        [1, 0, 1],
        [-1, 0, -1],
        [1, 0, -1],
        [-1, 0, 1],
        [0, 1, 1],
        [0, -1, -1],
        [0, 1, -1],
        [0, -1, 1],
    ]
)
weight_table = [1.0 / 3.0] + [1.0 / 18.0] * 6 + [1.0 / 36.0] * 12
opposite_table = [0, 2, 1, 4, 3, 6, 5, 8, 7, 10, 9, 12, 11, 14, 13, 16, 15, 18, 17]
stress_pairs = [(0, 0), (1, 1), (2, 2), (0, 1), (0, 2), (1, 2)]
tau_base = 0.55
smag_term = 18.0 * 1.4142135623730951 * 0.17 * 0.17
regular_eps = 0.0001
stiffness = 2.0
far_velocity = (0.02, 0.06, 0.0)
vmem_bytes = 40 << 20
group = 8


def going(axis, step):
    return [q for q in range(19) if int(velocity_table[q][axis]) == step]


def project(direction, vector):
    projection = 0.0 * vector[0]
    for component in range(3):
        lattice_step = int(velocity_table[direction][component])
        if lattice_step != 0:
            projection = projection + lattice_step * vector[component]
    return projection


def moments(populations):
    density = populations[0]
    momentum = [jnp.zeros_like(density) for component in range(3)]
    for direction in range(1, 19):
        density = density + populations[direction]
        for component in range(3):
            lattice_step = int(velocity_table[direction][component])
            if lattice_step == 1:
                momentum[component] = momentum[component] + populations[direction]
            elif lattice_step == -1:
                momentum[component] = momentum[component] - populations[direction]
    return (density, momentum)


def equilibrium(density, velocity):
    speed_sq = velocity[0] * velocity[0] + velocity[1] * velocity[1] + velocity[2] * velocity[2]
    result = []
    for direction in range(19):
        projected = project(direction, velocity)
        result.append(
            weight_table[direction]
            * density
            * (1.0 + 3.0 * projected + 4.5 * projected * projected - 1.5 * speed_sq)
        )
    return result


far_field = [float(np.float32(value)) for value in equilibrium(1.0, list(far_velocity))]


def collide(populations, cell_force, solid_cells):
    density, momentum = moments(populations)
    velocity = [
        (momentum[component] + 0.5 * cell_force[component]) / density for component in range(3)
    ]
    balance = equilibrium(density, velocity)
    stress = [jnp.zeros_like(density) for pair_pos in range(6)]
    for direction in range(19):
        non_eq = populations[direction] - balance[direction]
        for pair_pos in range(6):
            row_axis, col_axis = stress_pairs[pair_pos]
            factor = int(velocity_table[direction][row_axis] * velocity_table[direction][col_axis])
            if factor != 0:
                stress[pair_pos] = stress[pair_pos] + factor * non_eq
    shear_sq = stress[0] * stress[0] + stress[1] * stress[1] + stress[2] * stress[2]
    shear_sq = shear_sq + 2.0 * (
        stress[3] * stress[3] + stress[4] * stress[4] + stress[5] * stress[5]
    )
    magnitude = jnp.sqrt(shear_sq + regular_eps)
    relax_time = 0.5 * (tau_base + jnp.sqrt(tau_base * tau_base + smag_term * magnitude / density))
    relax_rate = 1.0 / relax_time
    guo_factor = 1.0 - 0.5 * relax_rate
    speed_force = (
        velocity[0] * cell_force[0] + velocity[1] * cell_force[1] + velocity[2] * cell_force[2]
    )
    result = []
    for direction in range(19):
        along_force = project(direction, cell_force)
        along_speed = project(direction, velocity)
        source = (
            guo_factor
            * weight_table[direction]
            * (3.0 * (along_force - speed_force) + 9.0 * along_speed * along_force)
        )
        relaxed = (
            populations[direction]
            - (populations[direction] - balance[direction]) * relax_rate
            + source
        )
        result.append(jnp.where(solid_cells == 1, populations[opposite_table[direction]], relaxed))
    return result


def with_halo(cells, sides, width):
    for axis, dim in sides:
        count = lax.axis_size(axis)
        head = lax.slice_in_dim(cells, 0, width, axis=dim)
        tail = lax.slice_in_dim(cells, cells.shape[dim] - width, cells.shape[dim], axis=dim)
        cells = jnp.concatenate(
            [
                lax.ppermute(tail, axis, [(i, (i + 1) % count) for i in range(count)]),
                cells,
                lax.ppermute(head, axis, [((i + 1) % count, i) for i in range(count)]),
            ],
            axis=dim,
        )
    return cells


def settle(received, labels, owned, train_of_block, marker_area, train_velocity, mark):
    rows_in = received.reshape(-1, 3 * mark)
    label_rows = labels.reshape(-1)
    owner_match = (label_rows[None, :] == jnp.arange(owned, dtype=jnp.int32)[:, None]).astype(
        jnp.float32
    )
    marker_velocity = jnp.dot(owner_match, rows_in, precision=lax.Precision.HIGHEST).reshape(
        owned, 3, mark
    )
    trains = train_velocity.shape[0]
    train_rows = train_of_block.reshape(owned)
    train_match = (train_rows[:, None] == jnp.arange(trains, dtype=jnp.int32)[None, :]).astype(
        jnp.float32
    )
    target = jnp.dot(train_match, train_velocity, precision=lax.Precision.HIGHEST)
    areas = marker_area.reshape(owned, mark)
    marker_force = stiffness * areas[:, None, :] * (target[:, :, None] - marker_velocity)
    back_rows = jnp.dot(
        owner_match.T, marker_force.reshape(owned, 3 * mark), precision=lax.Precision.HIGHEST
    )
    return (marker_force, back_rows)


def per_device_general(
    populations,
    solid_cells,
    slot_cells,
    slot_weights,
    slot_owner,
    slot_block,
    train_of_block,
    marker_area,
    train_velocity,
):
    size_x, size_y, size_z = (populations.shape[1], populations.shape[2], populations.shape[3])
    cell_count = size_x * size_y * size_z
    slots, kernel, mark = (slot_cells.shape[3], slot_cells.shape[4], slot_cells.shape[5])
    owned = train_of_block.shape[3]
    peers_x = lax.axis_size("gx")
    peers_y = lax.axis_size("gy")
    peers = peers_x * peers_y
    capacity = max(2, 2 * slots // peers)
    density, momentum = moments(populations)
    rest_velocity = jnp.stack([momentum[component] / density for component in range(3)]).reshape(
        3, cell_count
    )
    cells = slot_cells.reshape(slots, kernel, mark)
    weights = slot_weights.reshape(slots, kernel, mark)
    partial_value = jnp.sum(rest_velocity[:, cells] * weights[None], axis=2)
    slot_rows = partial_value.transpose(1, 0, 2).reshape(slots, 3 * mark)
    slot_dest = slot_owner.reshape(slots)
    blocks = slot_block.reshape(slots)
    order = jnp.arange(slots, dtype=jnp.int32)
    earlier = (slot_dest[None, :] == slot_dest[:, None]) & (order[None, :] < order[:, None])
    slot_rank = jnp.sum(earlier.astype(jnp.int32), axis=1)
    target_row = slot_dest * capacity + slot_rank
    buffer_rows = jnp.arange(peers * capacity, dtype=jnp.int32)
    matches = buffer_rows[:, None] == target_row[None, :]
    placement = matches.astype(jnp.float32)
    outgoing = jnp.dot(placement, slot_rows, precision=lax.Precision.HIGHEST)
    labels = jnp.sum(jnp.where(matches, blocks[None, :] + 1, 0), axis=1) - 1
    received, got_labels = (
        lax.all_to_all(
            outgoing.reshape(peers, capacity, 3 * mark),
            ("gx", "gy"),
            split_axis=0,
            concat_axis=0,
            tiled=True,
        ),
        lax.all_to_all(
            labels.reshape(peers, capacity), ("gx", "gy"), split_axis=0, concat_axis=0, tiled=True
        ),
    )
    marker_force, back_rows = settle(
        received, got_labels, owned, train_of_block, marker_area, train_velocity, mark
    )
    returned = lax.all_to_all(
        back_rows.reshape(peers, capacity, 3 * mark),
        ("gx", "gy"),
        split_axis=0,
        concat_axis=0,
        tiled=True,
    )
    slot_force = jnp.dot(
        placement.T, returned.reshape(peers * capacity, 3 * mark), precision=lax.Precision.HIGHEST
    )
    slot_force = slot_force.reshape(slots, 3, mark).transpose(1, 0, 2)
    contrib = weights[None] * slot_force[:, :, None, :]
    cell_force = (
        jnp.zeros((3, cell_count), jnp.float32).at[:, cells.reshape(-1)].add(contrib.reshape(3, -1))
    )
    cell_force = cell_force.reshape(3, size_x, size_y, size_z)
    relaxed = collide(populations, cell_force, solid_cells)
    padded = with_halo(jnp.stack(relaxed), (("gx", 1), ("gy", 2), ("gz", 3)), 1)
    parts = []
    for direction in range(19):
        shift_x = 1 - int(velocity_table[direction][0])
        shift_y = 1 - int(velocity_table[direction][1])
        shift_z = 1 - int(velocity_table[direction][2])
        parts.append(
            padded[
                direction,
                shift_x : shift_x + size_x,
                shift_y : shift_y + size_y,
                shift_z : shift_z + size_z,
            ]
        )
    read = jnp.stack(parts)
    total_y = size_y * lax.axis_size("gy")
    total_z = size_z * lax.axis_size("gz")
    global_y = lax.axis_index("gy") * size_y + jnp.arange(size_y, dtype=jnp.int32)
    global_z = lax.axis_index("gz") * size_z + jnp.arange(size_z, dtype=jnp.int32)
    on_side = ((global_y == 0) | (global_y == total_y - 1))[:, None] | (
        (global_z == 0) | (global_z == total_z - 1)
    )[None, :]
    far_field = jnp.array(equilibrium(1.0, list(far_velocity)), dtype=jnp.float32)
    populations_next = jnp.where(on_side[None, None], far_field[:, None, None, None], read)
    return (populations_next, marker_force.reshape(1, 1, 1, owned, 3, mark))


def full(shape):
    return jax.ShapeDtypeStruct(shape, jnp.float32)


def kernel_params():
    return pltpu.CompilerParams(vmem_limit_bytes=vmem_bytes)


def low_half(shape):
    return lax.broadcasted_iota(jnp.int32, shape, 1) < shape[1] // 2


def join(left, right):
    return jnp.where(low_half(left.shape), left, pltpu.roll(right, right.shape[1] // 2, 1))


def join_high(left, right):
    return jnp.where(low_half(left.shape), pltpu.roll(left, left.shape[1] // 2, 1), right)


def sample_kernel(
    pop_any, cells_any, weights_any, areas_ref, meta_ref, out_ref,
    pop_ref, cells_ref, weights_ref, table, partial, sems,
):
    rows, lanes = (pop_ref.shape[1], pop_ref.shape[2])
    mark = cells_ref.shape[1]
    slots = partial.shape[1]
    kernel = cells_ref.shape[0] // slots
    peers = out_ref.shape[0]
    owned = areas_ref.shape[0]
    copies = [
        pltpu.make_async_copy(source, target, sems.at[i])
        for i, (source, target) in enumerate(
            ((pop_any, pop_ref), (cells_any, cells_ref), (weights_any, weights_ref))
        )
    ]
    for copy in copies:
        copy.start()
    copies[0].wait()
    density, momentum = moments([pop_ref[q] for q in range(19)])
    for c in range(3):
        table[c] = momentum[c] / density
    copies[1].wait()
    copies[2].wait()

    def body(step, carry):
        first = pl.multiple_of(step * group, group)
        total = [jnp.zeros((group, mark), jnp.float32) for c in range(3)]
        for k in range(kernel):
            at = pl.ds(first * kernel + k, group, stride=kernel)
            cells = cells_ref[at, :]
            lane = cells & (lanes - 1)
            row = cells >> (lanes.bit_length() - 1)
            picked = [jnp.zeros((group, mark), jnp.float32) for c in range(3)]
            for r in range(rows):
                here = row == r
                for c in range(3):
                    line = jnp.broadcast_to(table[c, r : r + 1, :], (group, lanes))
                    got = jnp.take_along_axis(line, lane, axis=1, mode="promise_in_bounds")
                    picked[c] = jnp.where(here, got, picked[c])
            weight = weights_ref[at, :]
            total = [total[c] + weight * picked[c] for c in range(3)]
        for c in range(3):
            partial[c, pl.ds(first, group), :] = total[c]
        return carry

    lax.fori_loop(0, slots // group, body, 0)
    areas = areas_ref[...]
    area_rows = jnp.concatenate([pltpu.roll(areas, mark // 2, 1), areas], axis=0)
    first, second, third = (partial[c] for c in range(3))
    empty = jnp.zeros_like(third)
    turned = (
        jnp.concatenate([join(first, second), join_high(first, second)], axis=0).T,
        jnp.concatenate(
            [
                jnp.where(low_half(third.shape), third, area_rows),
                join_high(third, empty),
            ],
            axis=0,
        ).T,
    )
    half = mark // 2
    for peer in range(peers):
        here = peer * 8
        out_ref[peer, 0:8, :] = turned[0][here : here + 8]
        out_ref[peer, 8:16, :] = turned[0][half + here : half + here + 8]
        out_ref[peer, 16:24, :] = turned[1][here : here + 8]
        out_ref[peer, 24:32, :] = turned[1][half + here : half + here + 8] + meta_ref[...]


def sample(peers, slots, populations, cells, weights, areas, meta):
    hbm = pl.BlockSpec(memory_space=pltpu.HBM)
    vmem = pl.BlockSpec(memory_space=pltpu.VMEM)
    return pl.pallas_call(
        sample_kernel,
        out_shape=full((peers, 32, cells.shape[1])),
        in_specs=[hbm, hbm, hbm, vmem, vmem],
        scratch_shapes=[
            pltpu.VMEM(populations.shape, jnp.float32),
            pltpu.VMEM(cells.shape, jnp.int32),
            pltpu.VMEM(weights.shape, jnp.float32),
            pltpu.VMEM((3,) + populations.shape[1:], jnp.float32),
            pltpu.VMEM((3, slots, cells.shape[1]), jnp.float32),
            pltpu.SemaphoreType.DMA((3,)),
        ],
        compiler_params=kernel_params(),
        name="sample",
    )(populations, cells, weights, areas, meta)


def split_dot(values, match, dims):
    total = None
    for part in range(3):
        piece = values.astype(jnp.bfloat16)
        values = values - piece.astype(jnp.float32)
        product = lax.dot_general(piece, match, (dims, ((), ())), preferred_element_type=jnp.float32)
        total = product if total is None else total + product
    return total


def settle_kernel(owned, speeds_ref, in_ref, out_ref):
    peers, _, mark = in_ref.shape
    blocks = peers * owned
    pairs = peers // 2
    per_tile = mark // owned
    tiles = blocks // mark
    lane = lax.broadcasted_iota(jnp.int32, (8, mark), 1)
    metas = [in_ref[peer, 24:32, :] for peer in range(peers)]
    labels = [join_high(metas[2 * p], metas[2 * p + 1])[0:1] for p in range(pairs)]
    labels = jnp.concatenate(labels, axis=1).astype(jnp.int32)
    match = lax.broadcasted_iota(jnp.int32, (blocks, peers * mark // 2), 0) == labels
    match = jnp.where(match, 1.0, 0.0).astype(jnp.bfloat16)
    found = [
        jnp.concatenate(
            [way(in_ref[2 * p, 0:24, :], in_ref[2 * p + 1, 0:24, :]) for p in range(pairs)], axis=1
        )
        for way in (join, join_high)
    ]
    sums = split_dot(jnp.concatenate(found, axis=0), match, ((1,), (1,)))

    def by_block(offset):
        result = []
        for tile in range(tiles):
            total = jnp.zeros((8, mark), jnp.float32)
            for i in range(per_tile):
                moved = pltpu.roll(metas[tile * per_tile + i], (owned * i - offset) % mark, 1)
                total = jnp.where(lane // owned == i, moved, total)
            result.append(total)
        return jnp.concatenate(result, axis=1)

    areas = [by_block(0), by_block(owned)]
    trains = by_block(mark // 2)[1:2]
    forces = []
    for half in range(2):
        for c in range(3):
            target = jnp.zeros((1, blocks), jnp.float32)
            for train in range(speeds_ref.shape[0]):
                target = jnp.where(trains == float(train), speeds_ref[train, c], target)
            here = 24 * half + 8 * c
            forces.append(stiffness * areas[half] * (target - sums[here : here + 8]))
    forces = jnp.concatenate(forces, axis=0)
    back = split_dot(forces, match, ((1,), (0,)))
    for p in range(pairs):
        lower = back[0:24, p * mark : (p + 1) * mark]
        upper = back[24:48, p * mark : (p + 1) * mark]
        out_ref[2 * p, 0:24, :] = join(lower, upper)
        out_ref[2 * p + 1, 0:24, :] = join_high(lower, upper)
    for peer in range(peers):
        tile, i = divmod(peer, per_tile)
        kept = [jnp.zeros((8, mark), jnp.float32) for _ in range(2)]
        for c in range(3):
            for half in range(2):
                here = 24 * half + 8 * c
                place = 2 * (c % 2) + half
                moved = pltpu.roll(
                    forces[here : here + 8, tile * mark : (tile + 1) * mark],
                    (owned * (place - i)) % mark,
                    1,
                )
                kept[c // 2] = jnp.where(lane // owned == place, moved, kept[c // 2])
        out_ref[peer, 24:32, :] = kept[0]
        out_ref[peer, 32:40, :] = kept[1]


def settle_columns(owned, speeds, received):
    peers, _, mark = received.shape
    return pl.pallas_call(
        functools.partial(settle_kernel, owned),
        out_shape=full((peers, 40, mark)),
        in_specs=[pl.BlockSpec(memory_space=pltpu.SMEM), pl.BlockSpec(memory_space=pltpu.VMEM)],
        compiler_params=kernel_params(),
        name="settle",
    )(speeds, received)


def spread_kernel(
    place_ref,
    rows_ref,
    cells_ref,
    weights_ref,
    pop_ref,
    solid_ref,
    relaxed_ref,
    send_ref,
    marker_ref,
    force_ref,
    acc,
):
    rows, lanes = (pop_ref.shape[1], pop_ref.shape[2])
    size_y = 8
    mark = cells_ref.shape[1]
    slots = mark // 2
    owned = marker_ref.shape[0]
    kernel = cells_ref.shape[0] // slots
    peers = rows_ref.shape[0]
    bf = jnp.bfloat16

    def turn(*starts):
        return jnp.concatenate(
            [rows_ref[peer, at : at + 8, :] for at in starts for peer in range(peers)], axis=0
        ).T

    both = turn(0, 8)
    force_ref[0] = join(both[0:slots], both[slots:])
    force_ref[1] = join_high(both[0:slots], both[slots:])
    both = turn(16, 24)
    force_ref[2] = join(both[0:slots], both[slots:])
    marker_ref[:, 0, :] = join_high(both[0:owned], both[owned : 2 * owned])
    marker_ref[:, 1, :] = join_high(both[2 * owned : 3 * owned], both[3 * owned : 4 * owned])
    both = turn(32, 32)
    marker_ref[:, 2, :] = join(both[0:owned], both[owned : 2 * owned])

    acc[...] = jnp.zeros_like(acc)
    iota = lax.broadcasted_iota(jnp.int32, (16, mark), 0).astype(jnp.float32)
    steps = [(iota + 16.0 * j).astype(bf) for j in range(max(rows, lanes) // 16)]
    one, zero = (jnp.ones((16, mark), bf), jnp.zeros((16, mark), bf))

    def wide(entries, i):
        return jnp.broadcast_to(entries[i : i + 1, :], (16, mark)).astype(bf)

    def body(step, carry):
        first = pl.multiple_of(step * group, group)
        force = [force_ref[c, pl.ds(first, group), :] for c in range(3)]
        for k in range(kernel):
            at = pl.ds(first * kernel + k, group, stride=kernel)
            cells = cells_ref[at, :]
            weight = weights_ref[at, :]
            lane = (cells & (lanes - 1)).astype(jnp.float32)
            row = (cells >> (lanes.bit_length() - 1)).astype(jnp.float32)
            parts = []
            for c in range(3):
                value = weight * force[c]
                high = value.astype(bf).astype(jnp.float32)
                parts += [high, value - high]
            left, right = ([], [])
            for i in range(group):
                lane_i, row_i = (wide(lane, i), wide(row, i))
                right.append(
                    jnp.concatenate(
                        [jnp.where(steps[j] == lane_i, one, zero) for j in range(lanes // 16)],
                        axis=0,
                    )
                )
                masks = [steps[j] == row_i for j in range(rows // 16)]
                pieces = []
                for part in parts:
                    part_i = wide(part, i)
                    pieces += [jnp.where(mask, part_i, zero) for mask in masks]
                left.append(jnp.concatenate(pieces, axis=0))
            acc[...] += lax.dot_general(
                jnp.concatenate(left, axis=1),
                jnp.concatenate(right, axis=1),
                (((1,), (1,)), ((), ())),
                preferred_element_type=jnp.float32,
            )
        return carry

    lax.fori_loop(0, slots // group, body, 0)
    cell_force = [
        acc[2 * c * rows : (2 * c + 1) * rows, :] + acc[(2 * c + 1) * rows : (2 * c + 2) * rows, :]
        for c in range(3)
    ]
    relaxed = collide([pop_ref[q] for q in range(19)], cell_force, solid_ref[...])
    for q in range(19):
        relaxed_ref[q] = relaxed[q]
    lane_at = lax.broadcasted_iota(jnp.int32, (size_y, lanes), 1)
    packs = []
    for step in (1, -1):
        packed = jnp.zeros((size_y, lanes), jnp.float32)
        for i, q in enumerate(going(2, step)):
            edge = lanes - 1 if step == 1 else 0
            for x in range(rows // size_y):
                moved = pltpu.roll(
                    relaxed[q][x * size_y : (x + 1) * size_y], (8 * x + i - edge) % lanes, 1
                )
                packed = jnp.where(lane_at == 8 * x + i, moved, packed)
        packs.append(packed)
    y_index, z_index = (place_ref[0], place_ref[1])
    count_z = peers_z(send_ref)
    side = 1 - y_index
    for peer in range(send_ref.shape[0]):
        peer_y, peer_z = divmod(peer, count_z)
        send_ref[peer, 0:8, :] = jnp.where(z_index < peer_z, packs[0], packs[1])
    face = side * count_z + z_index
    for i in range(5):
        for x in range(rows // size_y):
            up = relaxed[going(1, 1)[i]][size_y * x + size_y - 1 : size_y * x + size_y, :]
            down = relaxed[going(1, -1)[i]][size_y * x : size_y * x + 1, :]
            send_ref[face, 4 * i + x : 4 * i + x + 1, :] = jnp.where(y_index == 0, up, down)


def peers_z(ref):
    return ref.shape[0] // 2


def spread(count_z, owned, place, rows, cells, weights, populations, solid):
    mark = cells.shape[1]
    line_count, lanes = solid.shape
    smem = pl.BlockSpec(memory_space=pltpu.SMEM)
    vmem = pl.BlockSpec(memory_space=pltpu.VMEM)
    return pl.pallas_call(
        spread_kernel,
        out_shape=(
            full(populations.shape),
            full((2 * count_z, 24, lanes)),
            full((owned, 3, mark)),
        ),
        in_specs=[smem] + [vmem] * 5,
        scratch_shapes=[
            pltpu.VMEM((3, mark // 2, mark), jnp.float32),
            pltpu.VMEM((6 * line_count, lanes), jnp.float32),
        ],
        compiler_params=kernel_params(),
        name="spread",
    )(place, rows, cells, weights, populations, solid)


def stream_kernel(place_ref, relaxed_ref, got_ref, out_ref, ahead_ref, behind_ref):
    size_x, size_y, lanes = out_ref.shape[1:]
    shape = (size_y, lanes)
    y_at = lax.broadcasted_iota(jnp.int32, shape, 0)
    z_at = lax.broadcasted_iota(jnp.int32, shape, 1)
    y_index, z_index = (place_ref[0], place_ref[1])
    count_z = peers_z(got_ref)
    side = (1 - y_index) * count_z
    here = y_index * count_z
    z_from = {1: jnp.maximum(z_index - 1, 0), -1: jnp.minimum(z_index + 1, count_z - 1)}
    near = {step: got_ref[here + z_from[step], 0:8, :] for step in (1, -1)}
    far = {step: got_ref[side + z_from[step], 0:8, :] for step in (1, -1)}
    near[0] = None
    on_side = y_at == jnp.where(y_index == 0, 0, size_y - 1)
    on_side = on_side | ((z_at == 0) & (z_index == 0))
    on_side = on_side | ((z_at == lanes - 1) & (z_index == count_z - 1))
    for q in range(19):
        step_x, step_y, step_z = (int(step) for step in velocity_table[q])
        y_edge = 0 if step_y == 1 else size_y - 1
        z_edge = 0 if step_z == 1 else lanes - 1
        column = near[step_z]
        if step_z != 0 and step_y != 0:
            column = jnp.where(
                y_at == y_edge,
                pltpu.roll(far[step_z], step_y % size_y, 0),
                pltpu.roll(column, step_y % size_y, 0),
            )
        for x in range(size_x):
            cells = relaxed_ref[q, x * size_y : (x + 1) * size_y, :]
            if step_y != 0:
                at = 4 * going(1, step_y).index(q) + x
                halo = got_ref[side + z_index, at : at + 1, :]
                cells = jnp.where(y_at == y_edge, halo, pltpu.roll(cells, step_y % size_y, 0))
            if step_z != 0:
                at = 8 * x + going(2, step_z).index(q)
                cells = jnp.where(
                    z_at == z_edge,
                    pltpu.roll(column, (z_edge - at) % lanes, 1),
                    pltpu.roll(cells, step_z % lanes, 1),
                )
            cells = jnp.where(on_side, far_field[q], cells)
            target = x + step_x
            if target == size_x:
                ahead_ref[going(0, 1).index(q)] = cells
            elif target == -1:
                behind_ref[going(0, -1).index(q)] = cells
            else:
                out_ref[q, target] = cells
    for q in going(0, 1):
        out_ref[q, 0] = jnp.zeros(shape, jnp.float32)
    for q in going(0, -1):
        out_ref[q, size_x - 1] = jnp.zeros(shape, jnp.float32)


def stream(size_y, place, relaxed, got):
    rows, lanes = relaxed.shape[1:]
    smem = pl.BlockSpec(memory_space=pltpu.SMEM)
    vmem = pl.BlockSpec(memory_space=pltpu.VMEM)
    face = full((5, size_y, lanes))
    return pl.pallas_call(
        stream_kernel,
        out_shape=(full((19, rows // size_y, size_y, lanes)), face, face),
        in_specs=[smem, vmem, vmem],
        compiler_params=kernel_params(),
        name="stream",
    )(place, relaxed, got)


def place_kernel(next_ref, ahead_ref, behind_ref, out_ref, sems):
    size_x = out_ref.shape[1]
    copies = []
    for i in range(5):
        for which, ref, q, x in (
            (0, ahead_ref, going(0, 1)[i], 0),
            (1, behind_ref, going(0, -1)[i], size_x - 1),
        ):
            copies.append(
                pltpu.make_async_copy(ref.at[i], out_ref.at[q, x], sems.at[2 * i + which])
            )
    for copy in copies:
        copy.start()
    for copy in copies:
        copy.wait()


def place_faces(inner, ahead, behind):
    anywhere = pl.BlockSpec(memory_space=pl.ANY)
    vmem = pl.BlockSpec(memory_space=pltpu.VMEM)
    return pl.pallas_call(
        place_kernel,
        out_shape=full(inner.shape),
        in_specs=[anywhere, vmem, vmem],
        out_specs=anywhere,
        scratch_shapes=[pltpu.SemaphoreType.DMA((10,))],
        input_output_aliases={0: 0},
        name="place_faces",
    )(inner, ahead, behind)


def per_device(
    populations,
    solid_cells,
    slot_cells,
    slot_weights,
    slot_owner,
    slot_block,
    train_of_block,
    marker_area,
    train_velocity,
):
    size_x, size_y, size_z = (populations.shape[1], populations.shape[2], populations.shape[3])
    lines = size_x * size_y
    slots, kernel, mark = (slot_cells.shape[3], slot_cells.shape[4], slot_cells.shape[5])
    owned = train_of_block.shape[3]
    count_x, count_y, count_z = (lax.axis_size(axis) for axis in ("gx", "gy", "gz"))
    peers = count_x * count_y
    place = jnp.stack([lax.axis_index("gy"), lax.axis_index("gz")]).astype(jnp.int32)
    pops = populations.reshape(19, lines, size_z)
    cells = slot_cells.reshape(slots * kernel, mark)
    weights = slot_weights.reshape(slots * kernel, mark)
    ids = slot_owner.reshape(1, slots) * owned + slot_block.reshape(1, slots)
    trains = train_of_block.reshape(1, owned)
    meta = jnp.concatenate(
        [
            jnp.pad(ids, ((0, 0), (mark - slots, 0))),
            jnp.pad(trains, ((0, 0), (mark - slots, slots - owned))),
        ],
        axis=0,
    )
    meta = jnp.pad(meta, ((0, 6), (0, 0))).astype(jnp.float32)
    columns = sample(peers, slots, pops, cells, weights, marker_area.reshape(owned, mark), meta)
    layer = dict(axis_name=("gx", "gy"), split_axis=0, concat_axis=0, tiled=True)
    columns = lax.all_to_all(columns, **layer)
    columns = settle_columns(owned, train_velocity, columns)
    columns = lax.all_to_all(columns, **layer)
    relaxed, sides, marker_force = spread(
        count_z, owned, place, columns, cells, weights, pops, solid_cells.reshape(lines, size_z)
    )
    sides = lax.all_to_all(sides, ("gy", "gz"), split_axis=0, concat_axis=0, tiled=True)
    inner, ahead, behind = stream(size_y, place, relaxed, sides)
    ahead = lax.ppermute(ahead, "gx", [(i, (i + 1) % count_x) for i in range(count_x)])
    behind = lax.ppermute(behind, "gx", [((i + 1) % count_x, i) for i in range(count_x)])
    return (
        place_faces(inner, ahead, behind),
        marker_force.reshape(1, 1, 1, owned, 3, mark),
    )


def solution(mesh):
    placed = (
        P(None, "gx", "gy", "gz"),
        P("gx", "gy", "gz"),
        P("gx", "gy", "gz", None, None, None),
        P("gx", "gy", "gz", None, None, None),
        P("gx", "gy", "gz", None, None),
        P("gx", "gy", "gz", None),
        P("gx", "gy", "gz", None),
        P("gx", "gy", "gz", None, None),
        P(),
    )
    small = mesh.shape["gy"] == 2 and mesh.shape["gx"] == 4 and mesh.shape["gz"] > 1
    return jax.shard_map(
        per_device if small else per_device_general,
        mesh=mesh,
        in_specs=placed,
        out_specs=(P(None, "gx", "gy", "gz"), P("gx", "gy", "gz", None, None, None)),
        check_vma=False,
    )
```

```python
import functools
import jax
import jax.numpy as jnp
import numpy as np
from jax import lax
from jax.experimental import pallas as pl
from jax.experimental.pallas import tpu as pltpu
from jax.sharding import PartitionSpec as P

velocity_table = np.array(
    [
        [0, 0, 0],
        [1, 0, 0],
        [-1, 0, 0],
        [0, 1, 0],
        [0, -1, 0],
        [0, 0, 1],
        [0, 0, -1],
        [1, 1, 0],
        [-1, -1, 0],
        [1, -1, 0],
        [-1, 1, 0],
        [1, 0, 1],
        [-1, 0, -1],
        [1, 0, -1],
        [-1, 0, 1],
        [0, 1, 1],
        [0, -1, -1],
        [0, 1, -1],
        [0, -1, 1],
    ]
)
weight_table = [1.0 / 3.0] + [1.0 / 18.0] * 6 + [1.0 / 36.0] * 12
opposite_table = [0, 2, 1, 4, 3, 6, 5, 8, 7, 10, 9, 12, 11, 14, 13, 16, 15, 18, 17]
stress_pairs = [(0, 0), (1, 1), (2, 2), (0, 1), (0, 2), (1, 2)]
tau_base = 0.55
smag_term = 18.0 * 1.4142135623730951 * 0.17 * 0.17
regular_eps = 0.0001
stiffness = 2.0
far_velocity = (0.02, 0.06, 0.0)
vmem_bytes = 40 << 20
group = 8


def going(axis, step):
    return [q for q in range(19) if int(velocity_table[q][axis]) == step]


def project(direction, vector):
    projection = 0.0 * vector[0]
    for component in range(3):
        lattice_step = int(velocity_table[direction][component])
        if lattice_step != 0:
            projection = projection + lattice_step * vector[component]
    return projection


def moments(populations):
    density = populations[0]
    momentum = [jnp.zeros_like(density) for component in range(3)]
    for direction in range(1, 19):
        density = density + populations[direction]
        for component in range(3):
            lattice_step = int(velocity_table[direction][component])
            if lattice_step == 1:
                momentum[component] = momentum[component] + populations[direction]
            elif lattice_step == -1:
                momentum[component] = momentum[component] - populations[direction]
    return (density, momentum)


def equilibrium(density, velocity):
    speed_sq = velocity[0] * velocity[0] + velocity[1] * velocity[1] + velocity[2] * velocity[2]
    result = []
    for direction in range(19):
        projected = project(direction, velocity)
        result.append(
            weight_table[direction]
            * density
            * (1.0 + 3.0 * projected + 4.5 * projected * projected - 1.5 * speed_sq)
        )
    return result


far_field = [float(np.float32(value)) for value in equilibrium(1.0, list(far_velocity))]


def collide(populations, cell_force, solid_cells):
    density, momentum = moments(populations)
    velocity = [
        (momentum[component] + 0.5 * cell_force[component]) / density for component in range(3)
    ]
    balance = equilibrium(density, velocity)
    stress = [jnp.zeros_like(density) for pair_pos in range(6)]
    for direction in range(19):
        non_eq = populations[direction] - balance[direction]
        for pair_pos in range(6):
            row_axis, col_axis = stress_pairs[pair_pos]
            factor = int(velocity_table[direction][row_axis] * velocity_table[direction][col_axis])
            if factor != 0:
                stress[pair_pos] = stress[pair_pos] + factor * non_eq
    shear_sq = stress[0] * stress[0] + stress[1] * stress[1] + stress[2] * stress[2]
    shear_sq = shear_sq + 2.0 * (
        stress[3] * stress[3] + stress[4] * stress[4] + stress[5] * stress[5]
    )
    magnitude = jnp.sqrt(shear_sq + regular_eps)
    relax_time = 0.5 * (tau_base + jnp.sqrt(tau_base * tau_base + smag_term * magnitude / density))
    relax_rate = 1.0 / relax_time
    guo_factor = 1.0 - 0.5 * relax_rate
    speed_force = (
        velocity[0] * cell_force[0] + velocity[1] * cell_force[1] + velocity[2] * cell_force[2]
    )
    result = []
    for direction in range(19):
        along_force = project(direction, cell_force)
        along_speed = project(direction, velocity)
        source = (
            guo_factor
            * weight_table[direction]
            * (3.0 * (along_force - speed_force) + 9.0 * along_speed * along_force)
        )
        relaxed = (
            populations[direction]
            - (populations[direction] - balance[direction]) * relax_rate
            + source
        )
        result.append(jnp.where(solid_cells == 1, populations[opposite_table[direction]], relaxed))
    return result


def with_halo(cells, sides, width):
    for axis, dim in sides:
        count = lax.axis_size(axis)
        head = lax.slice_in_dim(cells, 0, width, axis=dim)
        tail = lax.slice_in_dim(cells, cells.shape[dim] - width, cells.shape[dim], axis=dim)
        cells = jnp.concatenate(
            [
                lax.ppermute(tail, axis, [(i, (i + 1) % count) for i in range(count)]),
                cells,
                lax.ppermute(head, axis, [((i + 1) % count, i) for i in range(count)]),
            ],
            axis=dim,
        )
    return cells


def settle(received, labels, owned, train_of_block, marker_area, train_velocity, mark):
    rows_in = received.reshape(-1, 3 * mark)
    label_rows = labels.reshape(-1)
    owner_match = (label_rows[None, :] == jnp.arange(owned, dtype=jnp.int32)[:, None]).astype(
        jnp.float32
    )
    marker_velocity = jnp.dot(owner_match, rows_in, precision=lax.Precision.HIGHEST).reshape(
        owned, 3, mark
    )
    trains = train_velocity.shape[0]
    train_rows = train_of_block.reshape(owned)
    train_match = (train_rows[:, None] == jnp.arange(trains, dtype=jnp.int32)[None, :]).astype(
        jnp.float32
    )
    target = jnp.dot(train_match, train_velocity, precision=lax.Precision.HIGHEST)
    areas = marker_area.reshape(owned, mark)
    marker_force = stiffness * areas[:, None, :] * (target[:, :, None] - marker_velocity)
    back_rows = jnp.dot(
        owner_match.T, marker_force.reshape(owned, 3 * mark), precision=lax.Precision.HIGHEST
    )
    return (marker_force, back_rows)


def per_device_general(
    populations,
    solid_cells,
    slot_cells,
    slot_weights,
    slot_owner,
    slot_block,
    train_of_block,
    marker_area,
    train_velocity,
):
    size_x, size_y, size_z = (populations.shape[1], populations.shape[2], populations.shape[3])
    cell_count = size_x * size_y * size_z
    slots, kernel, mark = (slot_cells.shape[3], slot_cells.shape[4], slot_cells.shape[5])
    owned = train_of_block.shape[3]
    peers_x = lax.axis_size("gx")
    peers_y = lax.axis_size("gy")
    peers = peers_x * peers_y
    capacity = max(2, 2 * slots // peers)
    density, momentum = moments(populations)
    rest_velocity = jnp.stack([momentum[component] / density for component in range(3)]).reshape(
        3, cell_count
    )
    cells = slot_cells.reshape(slots, kernel, mark)
    weights = slot_weights.reshape(slots, kernel, mark)
    partial_value = jnp.sum(rest_velocity[:, cells] * weights[None], axis=2)
    slot_rows = partial_value.transpose(1, 0, 2).reshape(slots, 3 * mark)
    slot_dest = slot_owner.reshape(slots)
    blocks = slot_block.reshape(slots)
    order = jnp.arange(slots, dtype=jnp.int32)
    earlier = (slot_dest[None, :] == slot_dest[:, None]) & (order[None, :] < order[:, None])
    slot_rank = jnp.sum(earlier.astype(jnp.int32), axis=1)
    target_row = slot_dest * capacity + slot_rank
    buffer_rows = jnp.arange(peers * capacity, dtype=jnp.int32)
    matches = buffer_rows[:, None] == target_row[None, :]
    placement = matches.astype(jnp.float32)
    outgoing = jnp.dot(placement, slot_rows, precision=lax.Precision.HIGHEST)
    labels = jnp.sum(jnp.where(matches, blocks[None, :] + 1, 0), axis=1) - 1
    received, got_labels = (
        lax.all_to_all(
            outgoing.reshape(peers, capacity, 3 * mark),
            ("gx", "gy"),
            split_axis=0,
            concat_axis=0,
            tiled=True,
        ),
        lax.all_to_all(
            labels.reshape(peers, capacity), ("gx", "gy"), split_axis=0, concat_axis=0, tiled=True
        ),
    )
    marker_force, back_rows = settle(
        received, got_labels, owned, train_of_block, marker_area, train_velocity, mark
    )
    returned = lax.all_to_all(
        back_rows.reshape(peers, capacity, 3 * mark),
        ("gx", "gy"),
        split_axis=0,
        concat_axis=0,
        tiled=True,
    )
    slot_force = jnp.dot(
        placement.T, returned.reshape(peers * capacity, 3 * mark), precision=lax.Precision.HIGHEST
    )
    slot_force = slot_force.reshape(slots, 3, mark).transpose(1, 0, 2)
    contrib = weights[None] * slot_force[:, :, None, :]
    cell_force = (
        jnp.zeros((3, cell_count), jnp.float32).at[:, cells.reshape(-1)].add(contrib.reshape(3, -1))
    )
    cell_force = cell_force.reshape(3, size_x, size_y, size_z)
    relaxed = collide(populations, cell_force, solid_cells)
    padded = with_halo(jnp.stack(relaxed), (("gx", 1), ("gy", 2), ("gz", 3)), 1)
    parts = []
    for direction in range(19):
        shift_x = 1 - int(velocity_table[direction][0])
        shift_y = 1 - int(velocity_table[direction][1])
        shift_z = 1 - int(velocity_table[direction][2])
        parts.append(
            padded[
                direction,
                shift_x : shift_x + size_x,
                shift_y : shift_y + size_y,
                shift_z : shift_z + size_z,
            ]
        )
    read = jnp.stack(parts)
    total_y = size_y * lax.axis_size("gy")
    total_z = size_z * lax.axis_size("gz")
    global_y = lax.axis_index("gy") * size_y + jnp.arange(size_y, dtype=jnp.int32)
    global_z = lax.axis_index("gz") * size_z + jnp.arange(size_z, dtype=jnp.int32)
    on_side = ((global_y == 0) | (global_y == total_y - 1))[:, None] | (
        (global_z == 0) | (global_z == total_z - 1)
    )[None, :]
    far_field = jnp.array(equilibrium(1.0, list(far_velocity)), dtype=jnp.float32)
    populations_next = jnp.where(on_side[None, None], far_field[:, None, None, None], read)
    return (populations_next, marker_force.reshape(1, 1, 1, owned, 3, mark))


def full(shape):
    return jax.ShapeDtypeStruct(shape, jnp.float32)


def kernel_params():
    return pltpu.CompilerParams(vmem_limit_bytes=vmem_bytes)


def low_half(shape):
    return lax.broadcasted_iota(jnp.int32, shape, 1) < shape[1] // 2


def fetch(pairs, sems):
    copies = [
        pltpu.make_async_copy(source, target, sems.at[i])
        for i, (source, target) in enumerate(pairs)
    ]
    for copy in copies:
        copy.start()
    return copies


def shard_rows(slots, owned):
    return 3 * slots + owned + 8


def sample_kernel(
    place_ref, pop_any, cells_any, weights_any, areas_ref, owner_ref, block_ref, trains_ref,
    out_ref, pop_ref, cells_ref, weights_ref, table, sems,
):
    rows, lanes = (pop_ref.shape[1], pop_ref.shape[2])
    mark = cells_ref.shape[1]
    owned = areas_ref.shape[0]
    slots = owner_ref.shape[1]
    kernel = cells_ref.shape[0] // slots
    copies = fetch(
        ((pop_any, pop_ref), (cells_any, cells_ref), (weights_any, weights_ref)), sems
    )
    meta = 3 * slots + owned
    out_ref[3 * slots : meta, :] = areas_ref[...]
    out_ref[meta : meta + 8, :] = jnp.zeros((8, mark), jnp.float32)
    ids = (owner_ref[...] * owned + block_ref[...]).astype(jnp.float32)
    out_ref[meta : meta + 1, :] = jnp.concatenate([ids] * (mark // slots), axis=1)
    out_ref[meta + 1 : meta + 2, 0:owned] = trains_ref[...].astype(jnp.float32)
    mine = lax.broadcasted_iota(jnp.int32, (1, mark), 1) % owned + place_ref[2] * owned
    out_ref[meta + 2 : meta + 3, :] = mine.astype(jnp.float32)
    copies[0].wait()
    density, momentum = moments([pop_ref[q] for q in range(19)])
    fixed = [
        ((momentum[c] / density) * float(2**bits) + (2.0 ** (bits - 1) + 0.5)).astype(jnp.int32)
        for c, bits in enumerate((21, 21, 22))
    ]
    table[0] = (fixed[0] << 11) | (fixed[2] >> 11)
    table[1] = (fixed[1] << 11) | (fixed[2] & 2047)
    copies[1].wait()
    copies[2].wait()

    def body(step, carry):
        first = pl.multiple_of(step * group, group)
        total = [jnp.zeros((group, mark), jnp.float32) for c in range(3)]
        for k in range(kernel):
            at = pl.ds(first * kernel + k, group, stride=kernel)
            cells = cells_ref[at, :]
            lane = cells & (lanes - 1)
            row = cells >> (lanes.bit_length() - 1)
            words = [jnp.zeros((group, mark), jnp.int32) for c in range(2)]
            for r in range(rows):
                here = row == r
                for c in range(2):
                    line = jnp.broadcast_to(table[c, r : r + 1, :], (group, lanes))
                    got = jnp.take_along_axis(line, lane, axis=1, mode="promise_in_bounds")
                    words[c] = jnp.where(here, got, words[c])
            last = ((words[0] & 2047) << 11) | (words[1] & 2047)
            picked = [
                lax.shift_right_logical(words[0], 11),
                lax.shift_right_logical(words[1], 11),
                last,
            ]
            weight = weights_ref[at, :]
            for c, bits in enumerate((21, 21, 22)):
                value = (picked[c].astype(jnp.float32) - 2.0 ** (bits - 1)) * 2.0**-bits
                total[c] = total[c] + weight * value
        for c in range(3):
            out_ref[pl.ds(pl.multiple_of(c * slots + first, group), group), :] = total[c]
        return carry

    lax.fori_loop(0, slots // group, body, 0)


def sample(place, populations, cells, weights, areas, owner, block, trains):
    smem = pl.BlockSpec(memory_space=pltpu.SMEM)
    hbm = pl.BlockSpec(memory_space=pltpu.HBM)
    vmem = pl.BlockSpec(memory_space=pltpu.VMEM)
    return pl.pallas_call(
        sample_kernel,
        out_shape=full((shard_rows(owner.shape[1], areas.shape[0]), cells.shape[1])),
        in_specs=[smem] + [hbm] * 3 + [vmem] * 4,
        scratch_shapes=[
            pltpu.VMEM(populations.shape, jnp.float32),
            pltpu.VMEM(cells.shape, jnp.int32),
            pltpu.VMEM(weights.shape, jnp.float32),
            pltpu.VMEM((2,) + populations.shape[1:], jnp.int32),
            pltpu.SemaphoreType.DMA((3,)),
        ],
        compiler_params=kernel_params(),
        name="sample",
    )(place, populations, cells, weights, areas, owner, block, trains)


def three_parts(values):
    parts = []
    for _ in range(3):
        parts.append(values.astype(jnp.bfloat16))
        values = values - parts[-1].astype(jnp.float32)
    return parts


def one_hot(mask):
    return jnp.where(mask, 1.0, 0.0).astype(jnp.bfloat16)


def settle_rows(speeds_ref, shards, slots, owned):
    mark = shards[0].shape[1]
    meta = 3 * slots + owned
    own = shards[0][meta : meta + 8, :]
    ids = jnp.broadcast_to(own[0:1], (mark, mark)).T[0:slots]
    mine = jnp.broadcast_to(own[2:3], (mark, mark)).T[0:owned]
    wanted = jnp.concatenate([ids, mine], axis=0)
    sums = area = trains = None
    for shard in shards:
        labels = shard[meta : meta + 1, :]
        match = one_hot(wanted == labels)
        match = jnp.concatenate([match, match[:, 0:slots]], axis=1)
        values = jnp.concatenate([shard[c * slots : (c + 1) * slots, :] for c in range(3)], axis=1)
        got = jnp.dot(
            match, jnp.concatenate(three_parts(values), axis=0), preferred_element_type=jnp.float32
        )
        sums = got if sums is None else sums + got
        held = ids == shard[meta + 2 : meta + 3, :]
        parts = three_parts(shard[3 * slots : meta, :])
        parts.append(jnp.zeros_like(parts[0]))
        got = jnp.dot(
            one_hot(held), jnp.concatenate(parts, axis=0), preferred_element_type=jnp.float32
        )
        area = got if area is None else area + got
        got = jnp.where(held, shard[meta + 1 : meta + 2, :], 0.0)
        trains = got if trains is None else trains + got
    trains = jnp.sum(trains, axis=1, keepdims=True)
    own_trains = jnp.broadcast_to(own[1:2], (mark, mark)).T[0:owned]
    forces = []
    own_forces = []
    for c in range(3):
        target = jnp.zeros(trains.shape, jnp.float32)
        own_target = jnp.zeros(own_trains.shape, jnp.float32)
        for train in range(speeds_ref.shape[0]):
            speed = speeds_ref[train, c]
            target = jnp.where(trains == float(train), speed, target)
            own_target = jnp.where(own_trains == float(train), speed, own_target)
        got = sums[:, c * mark : (c + 1) * mark]
        forces.append(stiffness * area * (target - got[0:slots]))
        own_area = shards[0][3 * slots : meta, :]
        own_forces.append(stiffness * own_area * (own_target - got[slots:]))
    return (forces, own_forces)


def spread_kernel(shard_count, slots, owned, place_ref, speeds_ref, *refs):
    shards, refs = (refs[:shard_count], refs[shard_count:])
    cells_any, weights_any, pop_any, solid_ref, relaxed_ref, send_ref, marker_ref = refs[:7]
    cells_ref, weights_ref, pop_ref, force_ref, acc, sems = refs[7:]
    rows, lanes = (pop_ref.shape[1], pop_ref.shape[2])
    size_y = 8
    mark = cells_ref.shape[1]
    kernel = cells_ref.shape[0] // slots
    bf = jnp.bfloat16
    copies = fetch(
        ((cells_any, cells_ref), (weights_any, weights_ref), (pop_any, pop_ref)), sems
    )
    forces, own_forces = settle_rows(speeds_ref, shards, slots, owned)
    for c in range(3):
        force_ref[c] = forces[c]
        marker_ref[:, c, :] = own_forces[c]

    acc[...] = jnp.zeros_like(acc)
    iota = lax.broadcasted_iota(jnp.int32, (16, mark), 0).astype(jnp.float32)
    steps = [(iota + 16.0 * j).astype(bf) for j in range(max(rows, lanes) // 16)]
    one, zero = (jnp.ones((16, mark), bf), jnp.zeros((16, mark), bf))
    copies[0].wait()
    copies[1].wait()

    def wide(entries, i):
        return jnp.broadcast_to(entries[i : i + 1, :], (16, mark)).astype(bf)

    def body(step, carry):
        first = pl.multiple_of(step * group, group)
        force = [force_ref[c, pl.ds(first, group), :] for c in range(3)]
        for k in range(kernel):
            at = pl.ds(first * kernel + k, group, stride=kernel)
            cells = cells_ref[at, :]
            weight = weights_ref[at, :]
            lane = (cells & (lanes - 1)).astype(jnp.float32)
            row = (cells >> (lanes.bit_length() - 1)).astype(jnp.float32)
            parts = []
            for c in range(3):
                value = weight * force[c]
                high = value.astype(bf).astype(jnp.float32)
                parts += [high, value - high]
            left, right = ([], [])
            for i in range(group):
                lane_i, row_i = (wide(lane, i), wide(row, i))
                left.append(
                    jnp.concatenate(
                        [jnp.where(steps[j] == lane_i, one, zero) for j in range(lanes // 16)],
                        axis=0,
                    )
                )
                masks = [steps[j] == row_i for j in range(rows // 16)]
                pieces = []
                for part in parts:
                    part_i = wide(part, i)
                    pieces += [jnp.where(mask, part_i, zero) for mask in masks]
                right.append(jnp.concatenate(pieces, axis=0))
            acc[...] += lax.dot_general(
                jnp.concatenate(left, axis=1),
                jnp.concatenate(right, axis=1),
                (((1,), (1,)), ((), ())),
                preferred_element_type=jnp.float32,
            )
        return carry

    lax.fori_loop(0, slots // group, body, 0)
    copies[2].wait()
    spare = jnp.zeros((lanes, -acc.shape[1] % 128), jnp.float32)
    turned = jnp.concatenate([acc[...], spare], axis=1)
    turned = jnp.concatenate([turned[:, 0:128].T, turned[:, 128:256].T], axis=0)
    cell_force = [
        turned[2 * c * rows : (2 * c + 1) * rows] + turned[(2 * c + 1) * rows : (2 * c + 2) * rows]
        for c in range(3)
    ]
    relaxed = collide([pop_ref[q] for q in range(19)], cell_force, solid_ref[...])
    for q in range(19):
        relaxed_ref[q] = relaxed[q]
    lane_at = lax.broadcasted_iota(jnp.int32, (size_y, lanes), 1)
    packs = []
    for step in (1, -1):
        packed = jnp.zeros((size_y, lanes), jnp.float32)
        for i, q in enumerate(going(2, step)):
            edge = lanes - 1 if step == 1 else 0
            for x in range(rows // size_y):
                moved = pltpu.roll(
                    relaxed[q][x * size_y : (x + 1) * size_y], (8 * x + i - edge) % lanes, 1
                )
                packed = jnp.where(lane_at == 8 * x + i, moved, packed)
        packs.append(packed)
    y_index, z_index = (place_ref[0], place_ref[1])
    count_z = peers_z(send_ref)
    side = 1 - y_index
    for peer in range(send_ref.shape[0]):
        peer_y, peer_z = divmod(peer, count_z)
        send_ref[peer, 0:8, :] = jnp.where(z_index < peer_z, packs[0], packs[1])
    face = side * count_z + z_index
    for i in range(5):
        for x in range(rows // size_y):
            up = relaxed[going(1, 1)[i]][size_y * x + size_y - 1 : size_y * x + size_y, :]
            down = relaxed[going(1, -1)[i]][size_y * x : size_y * x + 1, :]
            send_ref[face, 4 * i + x : 4 * i + x + 1, :] = jnp.where(y_index == 0, up, down)


def peers_z(ref):
    return ref.shape[0] // 2


def spread(count_z, slots, owned, place, speeds, shards, cells, weights, populations, solid):
    mark = cells.shape[1]
    line_count, lanes = solid.shape
    smem = pl.BlockSpec(memory_space=pltpu.SMEM)
    hbm = pl.BlockSpec(memory_space=pltpu.HBM)
    vmem = pl.BlockSpec(memory_space=pltpu.VMEM)
    return pl.pallas_call(
        functools.partial(spread_kernel, len(shards), slots, owned),
        out_shape=(
            full(populations.shape),
            full((2 * count_z, 24, lanes)),
            full((owned, 3, mark)),
        ),
        in_specs=[smem] * 2 + [vmem] * len(shards) + [hbm] * 3 + [vmem],
        scratch_shapes=[
            pltpu.VMEM(cells.shape, jnp.int32),
            pltpu.VMEM(weights.shape, jnp.float32),
            pltpu.VMEM(populations.shape, jnp.float32),
            pltpu.VMEM((3, slots, mark), jnp.float32),
            pltpu.VMEM((lanes, 6 * line_count), jnp.float32),
            pltpu.SemaphoreType.DMA((3,)),
        ],
        compiler_params=kernel_params(),
        name="spread",
    )(place, speeds, *shards, cells, weights, populations, solid)


def stream_kernel(place_ref, relaxed_ref, got_ref, out_any, far_ref, near_ref, out_ref, sem):
    size_x, size_y, lanes = out_ref.shape[1:]
    shape = (size_y, lanes)
    y_at = lax.broadcasted_iota(jnp.int32, shape, 0)
    z_at = lax.broadcasted_iota(jnp.int32, shape, 1)
    y_index, z_index = (place_ref[0], place_ref[1])
    count_z = peers_z(got_ref)
    side = (1 - y_index) * count_z
    here = y_index * count_z
    z_from = {1: jnp.maximum(z_index - 1, 0), -1: jnp.minimum(z_index + 1, count_z - 1)}
    near = {step: got_ref[here + z_from[step], 0:8, :] for step in (1, -1)}
    far = {step: got_ref[side + z_from[step], 0:8, :] for step in (1, -1)}
    near[0] = None
    on_side = y_at == jnp.where(y_index == 0, 0, size_y - 1)
    on_side = on_side | ((z_at == 0) & (z_index == 0))
    on_side = on_side | ((z_at == lanes - 1) & (z_index == count_z - 1))
    leaving = {}
    for q in range(19):
        step_x, step_y, step_z = (int(step) for step in velocity_table[q])
        y_edge = 0 if step_y == 1 else size_y - 1
        z_edge = 0 if step_z == 1 else lanes - 1
        column = near[step_z]
        if step_z != 0 and step_y != 0:
            column = jnp.where(
                y_at == y_edge,
                pltpu.roll(far[step_z], step_y % size_y, 0),
                pltpu.roll(column, step_y % size_y, 0),
            )
        for x in range(size_x):
            cells = relaxed_ref[q, x * size_y : (x + 1) * size_y, :]
            if step_y != 0:
                at = 4 * going(1, step_y).index(q) + x
                halo = got_ref[side + z_index, at : at + 1, :]
                cells = jnp.where(y_at == y_edge, halo, pltpu.roll(cells, step_y % size_y, 0))
            if step_z != 0:
                at = 8 * x + going(2, step_z).index(q)
                cells = jnp.where(
                    z_at == z_edge,
                    pltpu.roll(column, (z_edge - at) % lanes, 1),
                    pltpu.roll(cells, step_z % lanes, 1),
                )
            cells = jnp.where(on_side, far_field[q], cells)
            target = x + step_x
            if 0 <= target < size_x:
                out_ref[q, target] = cells
            else:
                leaving[q] = cells
    for q in going(0, 1):
        out_ref[q, 0] = jnp.zeros(shape, jnp.float32)
    for q in going(0, -1):
        out_ref[q, size_x - 1] = jnp.zeros(shape, jnp.float32)
    copy = pltpu.make_async_copy(out_ref, out_any, sem)
    copy.start()
    even = place_ref[3] == 0
    for i in range(5):
        ahead, behind = (leaving[going(0, 1)[i]], leaving[going(0, -1)[i]])
        far_ref[i] = jnp.where(even, behind, ahead)
        near_ref[i] = jnp.where(even, ahead, behind)
    copy.wait()


def stream(size_y, place, relaxed, got):
    rows, lanes = relaxed.shape[1:]
    smem = pl.BlockSpec(memory_space=pltpu.SMEM)
    hbm = pl.BlockSpec(memory_space=pltpu.HBM)
    vmem = pl.BlockSpec(memory_space=pltpu.VMEM)
    face = full((5, size_y, lanes))
    shape = (19, rows // size_y, size_y, lanes)
    return pl.pallas_call(
        stream_kernel,
        out_shape=(full(shape), face, face),
        in_specs=[smem, vmem, vmem],
        out_specs=[hbm, vmem, vmem],
        scratch_shapes=[pltpu.VMEM(shape, jnp.float32), pltpu.SemaphoreType.DMA],
        compiler_params=kernel_params(),
        name="stream",
    )(place, relaxed, got)


def place_kernel(place_ref, next_any, far_any, near_any, out_any, sems):
    size_x = out_any.shape[1]
    odd = place_ref[3]
    copies = []
    for i in range(5):
        ahead, behind = (going(0, 1)[i], going(0, -1)[i])
        for which, source in enumerate((far_any, near_any)):
            from_behind = odd == which
            q = jnp.where(from_behind, ahead, behind)
            x = jnp.where(from_behind, 0, size_x - 1)
            copies.append((source.at[i], out_any.at[q, x]))
    for copy in fetch(copies, sems):
        copy.wait()


def place_faces(place, inner, far, near):
    smem = pl.BlockSpec(memory_space=pltpu.SMEM)
    anywhere = pl.BlockSpec(memory_space=pl.ANY)
    hbm = pl.BlockSpec(memory_space=pltpu.HBM)
    return pl.pallas_call(
        place_kernel,
        out_shape=full(inner.shape),
        in_specs=[smem, hbm, anywhere, anywhere],
        out_specs=hbm,
        scratch_shapes=[pltpu.SemaphoreType.DMA((10,))],
        input_output_aliases={1: 0},
        name="place_faces",
    )(place, inner, far, near)


def per_device(
    populations,
    solid_cells,
    slot_cells,
    slot_weights,
    slot_owner,
    slot_block,
    train_of_block,
    marker_area,
    train_velocity,
):
    size_x, size_y, size_z = (populations.shape[1], populations.shape[2], populations.shape[3])
    lines = size_x * size_y
    slots, kernel, mark = (slot_cells.shape[3], slot_cells.shape[4], slot_cells.shape[5])
    owned = train_of_block.shape[3]
    count_x, count_y, count_z = (lax.axis_size(axis) for axis in ("gx", "gy", "gz"))
    x_index, y_index, z_index = (lax.axis_index(axis) for axis in ("gx", "gy", "gz"))
    place = jnp.stack([y_index, z_index, x_index * count_y + y_index, x_index % 2])
    place = place.astype(jnp.int32)
    pops = populations.reshape(19, lines, size_z)
    cells = slot_cells.reshape(slots * kernel, mark)
    weights = slot_weights.reshape(slots * kernel, mark)
    own = sample(
        place,
        pops,
        cells,
        weights,
        marker_area.reshape(owned, mark),
        slot_owner.reshape(1, slots),
        slot_block.reshape(1, slots),
        train_of_block.reshape(1, owned),
    )
    swap = [(0, 1), (1, 0)]
    column = [own]
    for distance in reversed(range(1, count_x)):
        column.append(lax.ppermute(own, "gx", [(i, i ^ distance) for i in range(count_x)]))
    shards = column + [lax.ppermute(shard, "gy", swap) for shard in column]
    relaxed, sides, marker_force = spread(
        count_z,
        slots,
        owned,
        place,
        train_velocity,
        shards,
        cells,
        weights,
        pops,
        solid_cells.reshape(lines, size_z),
    )
    sides = lax.all_to_all(sides, ("gy", "gz"), split_axis=0, concat_axis=0, tiled=True)
    inner, far, near = stream(size_y, place, relaxed, sides)
    evens = range(0, count_x, 2)
    far = lax.ppermute(
        far,
        "gx",
        [(i, (i - 1) % count_x) for i in evens] + [((i - 1) % count_x, i) for i in evens],
    )
    near = lax.ppermute(near, "gx", [(i, i + 1) for i in evens] + [(i + 1, i) for i in evens])
    return (place_faces(place, inner, far, near), marker_force.reshape(1, 1, 1, owned, 3, mark))


def solution(mesh):
    placed = (
        P(None, "gx", "gy", "gz"),
        P("gx", "gy", "gz"),
        P("gx", "gy", "gz", None, None, None),
        P("gx", "gy", "gz", None, None, None),
        P("gx", "gy", "gz", None, None),
        P("gx", "gy", "gz", None),
        P("gx", "gy", "gz", None),
        P("gx", "gy", "gz", None, None),
        P(),
    )
    small = mesh.shape["gy"] == 2 and mesh.shape["gx"] == 4 and mesh.shape["gz"] > 1
    return jax.shard_map(
        per_device if small else per_device_general,
        mesh=mesh,
        in_specs=placed,
        out_specs=(P(None, "gx", "gy", "gz"), P("gx", "gy", "gz", None, None, None)),
        check_vma=False,
    )
```

```python
import functools
import jax
import jax.numpy as jnp
import numpy as np
from jax import lax
from jax.experimental import pallas as pl
from jax.experimental.pallas import tpu as pltpu
from jax.sharding import PartitionSpec as P

velocity_table = np.array(
    [
        [0, 0, 0],
        [1, 0, 0],
        [-1, 0, 0],
        [0, 1, 0],
        [0, -1, 0],
        [0, 0, 1],
        [0, 0, -1],
        [1, 1, 0],
        [-1, -1, 0],
        [1, -1, 0],
        [-1, 1, 0],
        [1, 0, 1],
        [-1, 0, -1],
        [1, 0, -1],
        [-1, 0, 1],
        [0, 1, 1],
        [0, -1, -1],
        [0, 1, -1],
        [0, -1, 1],
    ]
)
weight_table = [1.0 / 3.0] + [1.0 / 18.0] * 6 + [1.0 / 36.0] * 12
opposite_table = [0, 2, 1, 4, 3, 6, 5, 8, 7, 10, 9, 12, 11, 14, 13, 16, 15, 18, 17]
stress_pairs = [(0, 0), (1, 1), (2, 2), (0, 1), (0, 2), (1, 2)]
tau_base = 0.55
smag_term = 18.0 * 1.4142135623730951 * 0.17 * 0.17
regular_eps = 0.0001
stiffness = 2.0
far_velocity = (0.02, 0.06, 0.0)
vmem_bytes = 40 << 20
group = 8


def going(axis, step):
    return [q for q in range(19) if int(velocity_table[q][axis]) == step]


def project(direction, vector):
    projection = 0.0 * vector[0]
    for component in range(3):
        lattice_step = int(velocity_table[direction][component])
        if lattice_step != 0:
            projection = projection + lattice_step * vector[component]
    return projection


def moments(populations):
    density = populations[0]
    momentum = [jnp.zeros_like(density) for component in range(3)]
    for direction in range(1, 19):
        density = density + populations[direction]
        for component in range(3):
            lattice_step = int(velocity_table[direction][component])
            if lattice_step == 1:
                momentum[component] = momentum[component] + populations[direction]
            elif lattice_step == -1:
                momentum[component] = momentum[component] - populations[direction]
    return (density, momentum)


def equilibrium(density, velocity):
    speed_sq = velocity[0] * velocity[0] + velocity[1] * velocity[1] + velocity[2] * velocity[2]
    result = []
    for direction in range(19):
        projected = project(direction, velocity)
        result.append(
            weight_table[direction]
            * density
            * (1.0 + 3.0 * projected + 4.5 * projected * projected - 1.5 * speed_sq)
        )
    return result


far_field = [float(np.float32(value)) for value in equilibrium(1.0, list(far_velocity))]


def collide(populations, cell_force, solid_cells):
    density, momentum = moments(populations)
    velocity = [
        (momentum[component] + 0.5 * cell_force[component]) / density for component in range(3)
    ]
    balance = equilibrium(density, velocity)
    stress = [jnp.zeros_like(density) for pair_pos in range(6)]
    for direction in range(19):
        non_eq = populations[direction] - balance[direction]
        for pair_pos in range(6):
            row_axis, col_axis = stress_pairs[pair_pos]
            factor = int(velocity_table[direction][row_axis] * velocity_table[direction][col_axis])
            if factor != 0:
                stress[pair_pos] = stress[pair_pos] + factor * non_eq
    shear_sq = stress[0] * stress[0] + stress[1] * stress[1] + stress[2] * stress[2]
    shear_sq = shear_sq + 2.0 * (
        stress[3] * stress[3] + stress[4] * stress[4] + stress[5] * stress[5]
    )
    magnitude = jnp.sqrt(shear_sq + regular_eps)
    relax_time = 0.5 * (tau_base + jnp.sqrt(tau_base * tau_base + smag_term * magnitude / density))
    relax_rate = 1.0 / relax_time
    guo_factor = 1.0 - 0.5 * relax_rate
    speed_force = (
        velocity[0] * cell_force[0] + velocity[1] * cell_force[1] + velocity[2] * cell_force[2]
    )
    result = []
    for direction in range(19):
        along_force = project(direction, cell_force)
        along_speed = project(direction, velocity)
        source = (
            guo_factor
            * weight_table[direction]
            * (3.0 * (along_force - speed_force) + 9.0 * along_speed * along_force)
        )
        relaxed = (
            populations[direction]
            - (populations[direction] - balance[direction]) * relax_rate
            + source
        )
        result.append(jnp.where(solid_cells == 1, populations[opposite_table[direction]], relaxed))
    return result


def with_halo(cells, sides, width):
    for axis, dim in sides:
        count = lax.axis_size(axis)
        head = lax.slice_in_dim(cells, 0, width, axis=dim)
        tail = lax.slice_in_dim(cells, cells.shape[dim] - width, cells.shape[dim], axis=dim)
        cells = jnp.concatenate(
            [
                lax.ppermute(tail, axis, [(i, (i + 1) % count) for i in range(count)]),
                cells,
                lax.ppermute(head, axis, [((i + 1) % count, i) for i in range(count)]),
            ],
            axis=dim,
        )
    return cells


def settle(received, labels, owned, train_of_block, marker_area, train_velocity, mark):
    rows_in = received.reshape(-1, 3 * mark)
    label_rows = labels.reshape(-1)
    owner_match = (label_rows[None, :] == jnp.arange(owned, dtype=jnp.int32)[:, None]).astype(
        jnp.float32
    )
    marker_velocity = jnp.dot(owner_match, rows_in, precision=lax.Precision.HIGHEST).reshape(
        owned, 3, mark
    )
    trains = train_velocity.shape[0]
    train_rows = train_of_block.reshape(owned)
    train_match = (train_rows[:, None] == jnp.arange(trains, dtype=jnp.int32)[None, :]).astype(
        jnp.float32
    )
    target = jnp.dot(train_match, train_velocity, precision=lax.Precision.HIGHEST)
    areas = marker_area.reshape(owned, mark)
    marker_force = stiffness * areas[:, None, :] * (target[:, :, None] - marker_velocity)
    back_rows = jnp.dot(
        owner_match.T, marker_force.reshape(owned, 3 * mark), precision=lax.Precision.HIGHEST
    )
    return (marker_force, back_rows)


def per_device_general(
    populations,
    solid_cells,
    slot_cells,
    slot_weights,
    slot_owner,
    slot_block,
    train_of_block,
    marker_area,
    train_velocity,
):
    size_x, size_y, size_z = (populations.shape[1], populations.shape[2], populations.shape[3])
    cell_count = size_x * size_y * size_z
    slots, kernel, mark = (slot_cells.shape[3], slot_cells.shape[4], slot_cells.shape[5])
    owned = train_of_block.shape[3]
    peers_x = lax.axis_size("gx")
    peers_y = lax.axis_size("gy")
    peers = peers_x * peers_y
    capacity = max(2, 2 * slots // peers)
    density, momentum = moments(populations)
    rest_velocity = jnp.stack([momentum[component] / density for component in range(3)]).reshape(
        3, cell_count
    )
    cells = slot_cells.reshape(slots, kernel, mark)
    weights = slot_weights.reshape(slots, kernel, mark)
    partial_value = jnp.sum(rest_velocity[:, cells] * weights[None], axis=2)
    slot_rows = partial_value.transpose(1, 0, 2).reshape(slots, 3 * mark)
    slot_dest = slot_owner.reshape(slots)
    blocks = slot_block.reshape(slots)
    order = jnp.arange(slots, dtype=jnp.int32)
    earlier = (slot_dest[None, :] == slot_dest[:, None]) & (order[None, :] < order[:, None])
    slot_rank = jnp.sum(earlier.astype(jnp.int32), axis=1)
    target_row = slot_dest * capacity + slot_rank
    buffer_rows = jnp.arange(peers * capacity, dtype=jnp.int32)
    matches = buffer_rows[:, None] == target_row[None, :]
    placement = matches.astype(jnp.float32)
    outgoing = jnp.dot(placement, slot_rows, precision=lax.Precision.HIGHEST)
    labels = jnp.sum(jnp.where(matches, blocks[None, :] + 1, 0), axis=1) - 1
    received, got_labels = (
        lax.all_to_all(
            outgoing.reshape(peers, capacity, 3 * mark),
            ("gx", "gy"),
            split_axis=0,
            concat_axis=0,
            tiled=True,
        ),
        lax.all_to_all(
            labels.reshape(peers, capacity), ("gx", "gy"), split_axis=0, concat_axis=0, tiled=True
        ),
    )
    marker_force, back_rows = settle(
        received, got_labels, owned, train_of_block, marker_area, train_velocity, mark
    )
    returned = lax.all_to_all(
        back_rows.reshape(peers, capacity, 3 * mark),
        ("gx", "gy"),
        split_axis=0,
        concat_axis=0,
        tiled=True,
    )
    slot_force = jnp.dot(
        placement.T, returned.reshape(peers * capacity, 3 * mark), precision=lax.Precision.HIGHEST
    )
    slot_force = slot_force.reshape(slots, 3, mark).transpose(1, 0, 2)
    contrib = weights[None] * slot_force[:, :, None, :]
    cell_force = (
        jnp.zeros((3, cell_count), jnp.float32).at[:, cells.reshape(-1)].add(contrib.reshape(3, -1))
    )
    cell_force = cell_force.reshape(3, size_x, size_y, size_z)
    relaxed = collide(populations, cell_force, solid_cells)
    padded = with_halo(jnp.stack(relaxed), (("gx", 1), ("gy", 2), ("gz", 3)), 1)
    parts = []
    for direction in range(19):
        shift_x = 1 - int(velocity_table[direction][0])
        shift_y = 1 - int(velocity_table[direction][1])
        shift_z = 1 - int(velocity_table[direction][2])
        parts.append(
            padded[
                direction,
                shift_x : shift_x + size_x,
                shift_y : shift_y + size_y,
                shift_z : shift_z + size_z,
            ]
        )
    read = jnp.stack(parts)
    total_y = size_y * lax.axis_size("gy")
    total_z = size_z * lax.axis_size("gz")
    global_y = lax.axis_index("gy") * size_y + jnp.arange(size_y, dtype=jnp.int32)
    global_z = lax.axis_index("gz") * size_z + jnp.arange(size_z, dtype=jnp.int32)
    on_side = ((global_y == 0) | (global_y == total_y - 1))[:, None] | (
        (global_z == 0) | (global_z == total_z - 1)
    )[None, :]
    far_field = jnp.array(equilibrium(1.0, list(far_velocity)), dtype=jnp.float32)
    populations_next = jnp.where(on_side[None, None], far_field[:, None, None, None], read)
    return (populations_next, marker_force.reshape(1, 1, 1, owned, 3, mark))


def full(shape):
    return jax.ShapeDtypeStruct(shape, jnp.float32)


def kernel_params():
    return pltpu.CompilerParams(vmem_limit_bytes=vmem_bytes)


def low_half(shape):
    return lax.broadcasted_iota(jnp.int32, shape, 1) < shape[1] // 2


def fetch(pairs, sems):
    copies = [
        pltpu.make_async_copy(source, target, sems.at[i])
        for i, (source, target) in enumerate(pairs)
    ]
    for copy in copies:
        copy.start()
    return copies


def shard_rows(slots, owned):
    return 3 * slots + owned + 8


def sample_kernel(
    place_ref, pop_any, cells_any, weights_any, areas_any, owner_any, block_any, trains_any,
    out_ref, pop_ref, cells_ref, weights_ref, areas_ref, owner_ref, block_ref, trains_ref,
    table, sems,
):
    rows, lanes = (pop_ref.shape[1], pop_ref.shape[2])
    mark = cells_ref.shape[1]
    owned = areas_ref.shape[0]
    slots = owner_ref.shape[1]
    kernel = cells_ref.shape[0] // slots
    copies = fetch(
        (
            (pop_any, pop_ref),
            (cells_any, cells_ref),
            (weights_any, weights_ref),
            (areas_any, areas_ref),
            (owner_any, owner_ref),
            (block_any, block_ref),
            (trains_any, trains_ref),
        ),
        sems,
    )
    copies[0].wait()
    density, momentum = moments([pop_ref[q] for q in range(19)])
    fixed = [
        ((momentum[c] / density) * float(2**bits) + (2.0 ** (bits - 1) + 0.5)).astype(jnp.int32)
        for c, bits in enumerate((21, 21, 22))
    ]
    table[0] = (fixed[0] << 11) | (fixed[2] >> 11)
    table[1] = (fixed[1] << 11) | (fixed[2] & 2047)
    for copy in copies[1:]:
        copy.wait()
    meta = 3 * slots + owned
    out_ref[3 * slots : meta, :] = areas_ref[...]
    out_ref[meta : meta + 8, :] = jnp.zeros((8, mark), jnp.float32)
    ids = (owner_ref[...] * owned + block_ref[...]).astype(jnp.float32)
    out_ref[meta : meta + 1, :] = jnp.concatenate([ids] * (mark // slots), axis=1)
    out_ref[meta + 1 : meta + 2, 0:owned] = trains_ref[...].astype(jnp.float32)
    mine = lax.broadcasted_iota(jnp.int32, (1, mark), 1) % owned + place_ref[2] * owned
    out_ref[meta + 2 : meta + 3, :] = mine.astype(jnp.float32)

    def body(step, carry):
        first = pl.multiple_of(step * group, group)
        total = [jnp.zeros((group, mark), jnp.float32) for c in range(3)]
        for k in range(kernel):
            at = pl.ds(first * kernel + k, group, stride=kernel)
            cells = cells_ref[at, :]
            lane = cells & (lanes - 1)
            row = cells >> (lanes.bit_length() - 1)
            words = [jnp.zeros((group, mark), jnp.int32) for c in range(2)]
            for r in range(rows):
                here = row == r
                for c in range(2):
                    line = jnp.broadcast_to(table[c, r : r + 1, :], (group, lanes))
                    got = jnp.take_along_axis(line, lane, axis=1, mode="promise_in_bounds")
                    words[c] = jnp.where(here, got, words[c])
            last = ((words[0] & 2047) << 11) | (words[1] & 2047)
            picked = [
                lax.shift_right_logical(words[0], 11),
                lax.shift_right_logical(words[1], 11),
                last,
            ]
            weight = weights_ref[at, :]
            for c, bits in enumerate((21, 21, 22)):
                value = (picked[c].astype(jnp.float32) - 2.0 ** (bits - 1)) * 2.0**-bits
                total[c] = total[c] + weight * value
        for c in range(3):
            out_ref[pl.ds(pl.multiple_of(c * slots + first, group), group), :] = total[c]
        return carry

    lax.fori_loop(0, slots // group, body, 0)


def sample(place, populations, cells, weights, areas, owner, block, trains):
    smem = pl.BlockSpec(memory_space=pltpu.SMEM)
    hbm = pl.BlockSpec(memory_space=pltpu.HBM)
    vmem = pl.BlockSpec(memory_space=pltpu.VMEM)
    return pl.pallas_call(
        sample_kernel,
        out_shape=full((shard_rows(owner.shape[1], areas.shape[0]), cells.shape[1])),
        in_specs=[smem] + [hbm] * 7,
        scratch_shapes=[
            pltpu.VMEM(entries.shape, entries.dtype)
            for entries in (populations, cells, weights, areas, owner, block, trains)
        ]
        + [
            pltpu.VMEM((2,) + populations.shape[1:], jnp.int32),
            pltpu.SemaphoreType.DMA((7,)),
        ],
        compiler_params=kernel_params(),
        name="sample",
    )(place, populations, cells, weights, areas, owner, block, trains)


def three_parts(values):
    parts = []
    for _ in range(3):
        parts.append(values.astype(jnp.bfloat16))
        values = values - parts[-1].astype(jnp.float32)
    return parts


def one_hot(mask):
    return jnp.where(mask, 1.0, 0.0).astype(jnp.bfloat16)


def settle_rows(speeds_ref, shards, slots, owned):
    mark = shards[0].shape[1]
    meta = 3 * slots + owned
    own = shards[0][meta : meta + 8, :]
    ids = jnp.broadcast_to(own[0:1], (mark, mark)).T[0:slots]
    mine = jnp.broadcast_to(own[2:3], (mark, mark)).T[0:owned]
    wanted = jnp.concatenate([ids, mine], axis=0)
    sums = area = trains = None
    for shard in shards:
        labels = shard[meta : meta + 1, :]
        match = one_hot(wanted == labels)
        match = jnp.concatenate([match, match[:, 0:slots]], axis=1)
        values = jnp.concatenate([shard[c * slots : (c + 1) * slots, :] for c in range(3)], axis=1)
        got = jnp.dot(
            match, jnp.concatenate(three_parts(values), axis=0), preferred_element_type=jnp.float32
        )
        sums = got if sums is None else sums + got
        held = ids == shard[meta + 2 : meta + 3, :]
        parts = three_parts(shard[3 * slots : meta, :])
        parts.append(jnp.zeros_like(parts[0]))
        got = jnp.dot(
            one_hot(held), jnp.concatenate(parts, axis=0), preferred_element_type=jnp.float32
        )
        area = got if area is None else area + got
        got = jnp.where(held, shard[meta + 1 : meta + 2, :], 0.0)
        trains = got if trains is None else trains + got
    trains = jnp.sum(trains, axis=1, keepdims=True)
    own_trains = jnp.broadcast_to(own[1:2], (mark, mark)).T[0:owned]
    forces = []
    own_forces = []
    for c in range(3):
        target = jnp.zeros(trains.shape, jnp.float32)
        own_target = jnp.zeros(own_trains.shape, jnp.float32)
        for train in range(speeds_ref.shape[0]):
            speed = speeds_ref[train, c]
            target = jnp.where(trains == float(train), speed, target)
            own_target = jnp.where(own_trains == float(train), speed, own_target)
        got = sums[:, c * mark : (c + 1) * mark]
        forces.append(stiffness * area * (target - got[0:slots]))
        own_area = shards[0][3 * slots : meta, :]
        own_forces.append(stiffness * own_area * (own_target - got[slots:]))
    return (forces, own_forces)


def spread_kernel(shard_count, slots, owned, place_ref, speeds_ref, *refs):
    shards, refs = (refs[:shard_count], refs[shard_count:])
    cells_any, weights_any, pop_any, solid_ref = refs[:4]
    relaxed_ref, far_ref, near_ref, marker_ref = refs[4:8]
    cells_ref, weights_ref, pop_ref, force_ref, lines_ref, acc, sems = refs[8:]
    rows, lanes = (pop_ref.shape[1], pop_ref.shape[2])
    size_y = 8
    mark = cells_ref.shape[1]
    kernel = cells_ref.shape[0] // slots
    bf = jnp.bfloat16
    copies = fetch(
        ((cells_any, cells_ref), (weights_any, weights_ref), (pop_any, pop_ref)), sems
    )
    forces, own_forces = settle_rows(speeds_ref, shards, slots, owned)
    for c in range(3):
        force_ref[c] = forces[c]
        marker_ref[c] = own_forces[c]

    acc[...] = jnp.zeros_like(acc)
    iota = lax.broadcasted_iota(jnp.int32, (16, mark), 0).astype(jnp.float32)
    steps = [(iota + 16.0 * j).astype(bf) for j in range(max(rows, lanes) // 16)]
    one, zero = (jnp.ones((16, mark), bf), jnp.zeros((16, mark), bf))
    copies[0].wait()
    copies[1].wait()

    def body(step, carry):
        first = pl.multiple_of(step * group, group)
        force = [force_ref[c, pl.ds(first, group), :] for c in range(3)]
        for k in range(kernel):
            at = pl.ds(first * kernel + k, group, stride=kernel)
            cells = cells_ref[at, :]
            weight = weights_ref[at, :]
            lane = (cells & (lanes - 1)).astype(jnp.float32)
            row = (cells >> (lanes.bit_length() - 1)).astype(jnp.float32)
            parts = []
            for c in range(3):
                value = weight * force[c]
                high = value.astype(bf).astype(jnp.float32)
                parts += [high, value - high]
            for which, entries in enumerate([lane, row] + parts):
                lines_ref[k, which] = entries

            def wide(which, i):
                entries = lines_ref[k, which, i : i + 1, :]
                return jnp.broadcast_to(entries, (16, mark)).astype(bf)

            left, right = ([], [])
            for i in range(group):
                lane_i, row_i = (wide(0, i), wide(1, i))
                left.append(
                    jnp.concatenate(
                        [jnp.where(steps[j] == lane_i, one, zero) for j in range(lanes // 16)],
                        axis=0,
                    )
                )
                masks = [steps[j] == row_i for j in range(rows // 16)]
                pieces = []
                for which in range(len(parts)):
                    part_i = wide(2 + which, i)
                    pieces += [jnp.where(mask, part_i, zero) for mask in masks]
                right.append(jnp.concatenate(pieces, axis=0))
            acc[...] += lax.dot_general(
                jnp.concatenate(left, axis=1),
                jnp.concatenate(right, axis=1),
                (((1,), (1,)), ((), ())),
                preferred_element_type=jnp.float32,
            )
        return carry

    lax.fori_loop(0, slots // group, body, 0)
    copies[2].wait()
    spare = jnp.zeros((lanes, -acc.shape[1] % 128), jnp.float32)
    turned = jnp.concatenate([acc[...], spare], axis=1)
    turned = jnp.concatenate([turned[:, 0:128].T, turned[:, 128:256].T], axis=0)
    cell_force = [
        turned[2 * c * rows : (2 * c + 1) * rows] + turned[(2 * c + 1) * rows : (2 * c + 2) * rows]
        for c in range(3)
    ]
    relaxed = collide([pop_ref[q] for q in range(19)], cell_force, solid_ref[...])
    for q in range(19):
        relaxed_ref[q] = relaxed[q]
    even = place_ref[3] == 0
    for i in range(5):
        ahead = relaxed[going(0, 1)[i]][rows - size_y :]
        behind = relaxed[going(0, -1)[i]][:size_y]
        far_ref[i] = jnp.where(even, behind, ahead)
        near_ref[i] = jnp.where(even, ahead, behind)


def peers_z(ref):
    return ref.shape[0] // 2


def spread(slots, owned, place, speeds, shards, cells, weights, populations, solid):
    mark = cells.shape[1]
    line_count, lanes = solid.shape
    smem = pl.BlockSpec(memory_space=pltpu.SMEM)
    hbm = pl.BlockSpec(memory_space=pltpu.HBM)
    vmem = pl.BlockSpec(memory_space=pltpu.VMEM)
    return pl.pallas_call(
        functools.partial(spread_kernel, len(shards), slots, owned),
        out_shape=(
            full(populations.shape),
            full((5, 8, lanes)),
            full((5, 8, lanes)),
            full((3, owned, mark)),
        ),
        in_specs=[smem] * 2 + [vmem] * len(shards) + [hbm] * 3 + [vmem],
        scratch_shapes=[
            pltpu.VMEM(cells.shape, jnp.int32),
            pltpu.VMEM(weights.shape, jnp.float32),
            pltpu.VMEM(populations.shape, jnp.float32),
            pltpu.VMEM((3, slots, mark), jnp.float32),
            pltpu.VMEM((cells.shape[0] // slots, 8, group, mark), jnp.float32),
            pltpu.VMEM((lanes, 6 * line_count), jnp.float32),
            pltpu.SemaphoreType.DMA((3,)),
        ],
        compiler_params=kernel_params(),
        name="spread",
    )(place, speeds, *shards, cells, weights, populations, solid)


def downwind(place_ref, relaxed_ref, far_ref, near_ref):
    size_y = far_ref.shape[1]
    size_x = relaxed_ref.shape[1] // size_y
    even = place_ref[3] == 0

    def cells(q, x):
        step = int(velocity_table[q][0])
        source = x - step
        if 0 <= source < size_x:
            return relaxed_ref[q, source * size_y : (source + 1) * size_y, :]
        i = going(0, step).index(q)
        if step == 1:
            return jnp.where(even, far_ref[i], near_ref[i])
        return jnp.where(even, near_ref[i], far_ref[i])

    return cells


def pack_kernel(place_ref, relaxed_ref, far_ref, near_ref, send_ref):
    size_y, lanes = far_ref.shape[1:]
    size_x = relaxed_ref.shape[1] // size_y
    cells = downwind(place_ref, relaxed_ref, far_ref, near_ref)
    lane_at = lax.broadcasted_iota(jnp.int32, (size_y, lanes), 1)
    packs = []
    for step in (1, -1):
        packed = jnp.zeros((size_y, lanes), jnp.float32)
        for i, q in enumerate(going(2, step)):
            edge = lanes - 1 if step == 1 else 0
            for x in range(size_x):
                at = 8 * x + i
                moved = pltpu.roll(cells(q, x), (at - edge) % lanes, 1)
                packed = jnp.where(lane_at == at, moved, packed)
        packs.append(packed)
    y_index, z_index = (place_ref[0], place_ref[1])
    count_z = peers_z(send_ref)
    for peer in range(send_ref.shape[0]):
        send_ref[peer, 0:8, :] = jnp.where(z_index < peer % count_z, packs[0], packs[1])
    face = (1 - y_index) * count_z + z_index
    for i in range(5):
        for x in range(size_x):
            up = cells(going(1, 1)[i], x)[size_y - 1 : size_y, :]
            down = cells(going(1, -1)[i], x)[0:1, :]
            at = size_x * i + x
            send_ref[face, at : at + 1, :] = jnp.where(y_index == 0, up, down)


def pack(count_z, place, relaxed, far, near):
    lanes = relaxed.shape[2]
    smem = pl.BlockSpec(memory_space=pltpu.SMEM)
    vmem = pl.BlockSpec(memory_space=pltpu.VMEM)
    return pl.pallas_call(
        pack_kernel,
        out_shape=full((2 * count_z, 24, lanes)),
        in_specs=[smem] + [vmem] * 3,
        compiler_params=kernel_params(),
        name="pack",
    )(place, relaxed, far, near)


def stream_kernel(
    place_ref, relaxed_ref, far_ref, near_ref, got_ref, out_any, out_ref, sems
):
    size_x, size_y, lanes = out_ref.shape[1:]
    shape = (size_y, lanes)
    streamed = downwind(place_ref, relaxed_ref, far_ref, near_ref)
    y_at = lax.broadcasted_iota(jnp.int32, shape, 0)
    z_at = lax.broadcasted_iota(jnp.int32, shape, 1)
    y_index, z_index = (place_ref[0], place_ref[1])
    count_z = peers_z(got_ref)
    side = (1 - y_index) * count_z
    here = y_index * count_z
    z_from = {1: jnp.maximum(z_index - 1, 0), -1: jnp.minimum(z_index + 1, count_z - 1)}
    level = {step: got_ref[here + z_from[step], 0:8, :] for step in (1, -1)}
    across = {step: got_ref[side + z_from[step], 0:8, :] for step in (1, -1)}
    on_side = y_at == jnp.where(y_index == 0, 0, size_y - 1)
    on_side = on_side | ((z_at == 0) & (z_index == 0))
    on_side = on_side | ((z_at == lanes - 1) & (z_index == count_z - 1))
    copies = []
    for q in range(19):
        _, step_y, step_z = (int(step) for step in velocity_table[q])
        y_edge = 0 if step_y == 1 else size_y - 1
        z_edge = 0 if step_z == 1 else lanes - 1
        column = level.get(step_z)
        if step_z != 0 and step_y != 0:
            column = jnp.where(
                y_at == y_edge,
                pltpu.roll(across[step_z], step_y % size_y, 0),
                pltpu.roll(column, step_y % size_y, 0),
            )
        for x in range(size_x):
            cells = streamed(q, x)
            if step_y != 0:
                at = size_x * going(1, step_y).index(q) + x
                halo = got_ref[side + z_index, at : at + 1, :]
                cells = jnp.where(y_at == y_edge, halo, pltpu.roll(cells, step_y % size_y, 0))
            if step_z != 0:
                at = 8 * x + going(2, step_z).index(q)
                cells = jnp.where(
                    z_at == z_edge,
                    pltpu.roll(column, (z_edge - at) % lanes, 1),
                    pltpu.roll(cells, step_z % lanes, 1),
                )
            out_ref[q, x] = jnp.where(on_side, far_field[q], cells)
        copies.append(pltpu.make_async_copy(out_ref.at[q], out_any.at[q], sems.at[q]))
        copies[-1].start()
    for copy in copies:
        copy.wait()


def stream(place, relaxed, far, near, got):
    rows, lanes = relaxed.shape[1:]
    size_y = far.shape[1]
    smem = pl.BlockSpec(memory_space=pltpu.SMEM)
    vmem = pl.BlockSpec(memory_space=pltpu.VMEM)
    shape = (19, rows // size_y, size_y, lanes)
    return pl.pallas_call(
        stream_kernel,
        out_shape=full(shape),
        in_specs=[smem] + [vmem] * 4,
        out_specs=pl.BlockSpec(memory_space=pltpu.HBM),
        scratch_shapes=[pltpu.VMEM(shape, jnp.float32), pltpu.SemaphoreType.DMA((19,))],
        compiler_params=kernel_params(),
        name="stream",
    )(place, relaxed, far, near, got)


def per_device(
    populations,
    solid_cells,
    slot_cells,
    slot_weights,
    slot_owner,
    slot_block,
    train_of_block,
    marker_area,
    train_velocity,
):
    size_x, size_y, size_z = (populations.shape[1], populations.shape[2], populations.shape[3])
    lines = size_x * size_y
    slots, kernel, mark = (slot_cells.shape[3], slot_cells.shape[4], slot_cells.shape[5])
    owned = train_of_block.shape[3]
    count_x, count_y, count_z = (lax.axis_size(axis) for axis in ("gx", "gy", "gz"))
    x_index, y_index, z_index = (lax.axis_index(axis) for axis in ("gx", "gy", "gz"))
    place = jnp.stack([y_index, z_index, x_index * count_y + y_index, x_index % 2])
    place = place.astype(jnp.int32)
    inputs = [
        pltpu.with_memory_space_constraint(entries, pltpu.HBM)
        for entries in (
            populations.reshape(19, lines, size_z),
            slot_cells.reshape(slots * kernel, mark),
            slot_weights.reshape(slots * kernel, mark),
            marker_area.reshape(owned, mark),
            slot_owner.reshape(1, slots),
            slot_block.reshape(1, slots),
            train_of_block.reshape(1, owned),
        )
    ]
    pops, cells, weights = inputs[:3]
    own = sample(place, *inputs)
    swap = [(0, 1), (1, 0)]
    column = [own]
    for distance in reversed(range(1, count_x)):
        column.append(lax.ppermute(own, "gx", [(i, i ^ distance) for i in range(count_x)]))
    shards = column + [lax.ppermute(shard, "gy", swap) for shard in column]
    relaxed, far, near, marker_force = spread(
        slots,
        owned,
        place,
        train_velocity,
        shards,
        cells,
        weights,
        pops,
        solid_cells.reshape(lines, size_z),
    )
    evens = range(0, count_x, 2)
    far = lax.ppermute(
        far,
        "gx",
        [(i, (i - 1) % count_x) for i in evens] + [((i - 1) % count_x, i) for i in evens],
    )
    near = lax.ppermute(near, "gx", [(i, i + 1) for i in evens] + [(i + 1, i) for i in evens])
    sides = pack(count_z, place, relaxed, far, near)
    sides = lax.all_to_all(sides, ("gy", "gz"), split_axis=0, concat_axis=0, tiled=True)
    populations_next = stream(place, relaxed, far, near, sides)
    marker_force = marker_force.transpose(1, 0, 2).reshape(1, 1, 1, owned, 3, mark)
    return (populations_next, marker_force)


def solution(mesh):
    placed = (
        P(None, "gx", "gy", "gz"),
        P("gx", "gy", "gz"),
        P("gx", "gy", "gz", None, None, None),
        P("gx", "gy", "gz", None, None, None),
        P("gx", "gy", "gz", None, None),
        P("gx", "gy", "gz", None),
        P("gx", "gy", "gz", None),
        P("gx", "gy", "gz", None, None),
        P(),
    )
    small = mesh.shape["gy"] == 2 and mesh.shape["gx"] == 4 and mesh.shape["gz"] > 1
    return jax.shard_map(
        per_device if small else per_device_general,
        mesh=mesh,
        in_specs=placed,
        out_specs=(P(None, "gx", "gy", "gz"), P("gx", "gy", "gz", None, None, None)),
        check_vma=False,
    )
```

```python
import functools
import jax
import jax.numpy as jnp
import numpy as np
from jax import lax
from jax.experimental import pallas as pl
from jax.experimental.pallas import tpu as pltpu
from jax.sharding import PartitionSpec as P

velocity_table = np.array(
    [
        [0, 0, 0],
        [1, 0, 0],
        [-1, 0, 0],
        [0, 1, 0],
        [0, -1, 0],
        [0, 0, 1],
        [0, 0, -1],
        [1, 1, 0],
        [-1, -1, 0],
        [1, -1, 0],
        [-1, 1, 0],
        [1, 0, 1],
        [-1, 0, -1],
        [1, 0, -1],
        [-1, 0, 1],
        [0, 1, 1],
        [0, -1, -1],
        [0, 1, -1],
        [0, -1, 1],
    ]
)
weight_table = [1.0 / 3.0] + [1.0 / 18.0] * 6 + [1.0 / 36.0] * 12
opposite_table = [0, 2, 1, 4, 3, 6, 5, 8, 7, 10, 9, 12, 11, 14, 13, 16, 15, 18, 17]
stress_pairs = [(0, 0), (1, 1), (2, 2), (0, 1), (0, 2), (1, 2)]
tau_base = 0.55
smag_term = 18.0 * 1.4142135623730951 * 0.17 * 0.17
regular_eps = 0.0001
stiffness = 2.0
far_velocity = (0.02, 0.06, 0.0)
vmem_bytes = 40 << 20
group = 8


def going(axis, step):
    return [q for q in range(19) if int(velocity_table[q][axis]) == step]


def project(direction, vector):
    projection = 0.0 * vector[0]
    for component in range(3):
        lattice_step = int(velocity_table[direction][component])
        if lattice_step != 0:
            projection = projection + lattice_step * vector[component]
    return projection


def moments(populations):
    density = populations[0]
    momentum = [jnp.zeros_like(density) for component in range(3)]
    for direction in range(1, 19):
        density = density + populations[direction]
        for component in range(3):
            lattice_step = int(velocity_table[direction][component])
            if lattice_step == 1:
                momentum[component] = momentum[component] + populations[direction]
            elif lattice_step == -1:
                momentum[component] = momentum[component] - populations[direction]
    return (density, momentum)


def equilibrium(density, velocity):
    speed_sq = velocity[0] * velocity[0] + velocity[1] * velocity[1] + velocity[2] * velocity[2]
    result = []
    for direction in range(19):
        projected = project(direction, velocity)
        result.append(
            weight_table[direction]
            * density
            * (1.0 + 3.0 * projected + 4.5 * projected * projected - 1.5 * speed_sq)
        )
    return result


far_field = [float(np.float32(value)) for value in equilibrium(1.0, list(far_velocity))]


def collide(populations, cell_force, solid_cells):
    density, momentum = moments(populations)
    velocity = [
        (momentum[component] + 0.5 * cell_force[component]) / density for component in range(3)
    ]
    balance = equilibrium(density, velocity)
    stress = [jnp.zeros_like(density) for pair_pos in range(6)]
    for direction in range(19):
        non_eq = populations[direction] - balance[direction]
        for pair_pos in range(6):
            row_axis, col_axis = stress_pairs[pair_pos]
            factor = int(velocity_table[direction][row_axis] * velocity_table[direction][col_axis])
            if factor != 0:
                stress[pair_pos] = stress[pair_pos] + factor * non_eq
    shear_sq = stress[0] * stress[0] + stress[1] * stress[1] + stress[2] * stress[2]
    shear_sq = shear_sq + 2.0 * (
        stress[3] * stress[3] + stress[4] * stress[4] + stress[5] * stress[5]
    )
    magnitude = jnp.sqrt(shear_sq + regular_eps)
    relax_time = 0.5 * (tau_base + jnp.sqrt(tau_base * tau_base + smag_term * magnitude / density))
    relax_rate = 1.0 / relax_time
    guo_factor = 1.0 - 0.5 * relax_rate
    speed_force = (
        velocity[0] * cell_force[0] + velocity[1] * cell_force[1] + velocity[2] * cell_force[2]
    )
    result = []
    for direction in range(19):
        along_force = project(direction, cell_force)
        along_speed = project(direction, velocity)
        source = (
            guo_factor
            * weight_table[direction]
            * (3.0 * (along_force - speed_force) + 9.0 * along_speed * along_force)
        )
        relaxed = (
            populations[direction]
            - (populations[direction] - balance[direction]) * relax_rate
            + source
        )
        result.append(jnp.where(solid_cells == 1, populations[opposite_table[direction]], relaxed))
    return result


def with_halo(cells, sides, width):
    for axis, dim in sides:
        count = lax.axis_size(axis)
        head = lax.slice_in_dim(cells, 0, width, axis=dim)
        tail = lax.slice_in_dim(cells, cells.shape[dim] - width, cells.shape[dim], axis=dim)
        cells = jnp.concatenate(
            [
                lax.ppermute(tail, axis, [(i, (i + 1) % count) for i in range(count)]),
                cells,
                lax.ppermute(head, axis, [((i + 1) % count, i) for i in range(count)]),
            ],
            axis=dim,
        )
    return cells


def settle(received, labels, owned, train_of_block, marker_area, train_velocity, mark):
    rows_in = received.reshape(-1, 3 * mark)
    label_rows = labels.reshape(-1)
    owner_match = (label_rows[None, :] == jnp.arange(owned, dtype=jnp.int32)[:, None]).astype(
        jnp.float32
    )
    marker_velocity = jnp.dot(owner_match, rows_in, precision=lax.Precision.HIGHEST).reshape(
        owned, 3, mark
    )
    trains = train_velocity.shape[0]
    train_rows = train_of_block.reshape(owned)
    train_match = (train_rows[:, None] == jnp.arange(trains, dtype=jnp.int32)[None, :]).astype(
        jnp.float32
    )
    target = jnp.dot(train_match, train_velocity, precision=lax.Precision.HIGHEST)
    areas = marker_area.reshape(owned, mark)
    marker_force = stiffness * areas[:, None, :] * (target[:, :, None] - marker_velocity)
    back_rows = jnp.dot(
        owner_match.T, marker_force.reshape(owned, 3 * mark), precision=lax.Precision.HIGHEST
    )
    return (marker_force, back_rows)


def per_device_general(
    populations,
    solid_cells,
    slot_cells,
    slot_weights,
    slot_owner,
    slot_block,
    train_of_block,
    marker_area,
    train_velocity,
):
    size_x, size_y, size_z = (populations.shape[1], populations.shape[2], populations.shape[3])
    cell_count = size_x * size_y * size_z
    slots, kernel, mark = (slot_cells.shape[3], slot_cells.shape[4], slot_cells.shape[5])
    owned = train_of_block.shape[3]
    peers_x = lax.axis_size("gx")
    peers_y = lax.axis_size("gy")
    peers = peers_x * peers_y
    capacity = max(2, 2 * slots // peers)
    density, momentum = moments(populations)
    rest_velocity = jnp.stack([momentum[component] / density for component in range(3)]).reshape(
        3, cell_count
    )
    cells = slot_cells.reshape(slots, kernel, mark)
    weights = slot_weights.reshape(slots, kernel, mark)
    partial_value = jnp.sum(rest_velocity[:, cells] * weights[None], axis=2)
    slot_rows = partial_value.transpose(1, 0, 2).reshape(slots, 3 * mark)
    slot_dest = slot_owner.reshape(slots)
    blocks = slot_block.reshape(slots)
    order = jnp.arange(slots, dtype=jnp.int32)
    earlier = (slot_dest[None, :] == slot_dest[:, None]) & (order[None, :] < order[:, None])
    slot_rank = jnp.sum(earlier.astype(jnp.int32), axis=1)
    target_row = slot_dest * capacity + slot_rank
    buffer_rows = jnp.arange(peers * capacity, dtype=jnp.int32)
    matches = buffer_rows[:, None] == target_row[None, :]
    placement = matches.astype(jnp.float32)
    outgoing = jnp.dot(placement, slot_rows, precision=lax.Precision.HIGHEST)
    labels = jnp.sum(jnp.where(matches, blocks[None, :] + 1, 0), axis=1) - 1
    received, got_labels = (
        lax.all_to_all(
            outgoing.reshape(peers, capacity, 3 * mark),
            ("gx", "gy"),
            split_axis=0,
            concat_axis=0,
            tiled=True,
        ),
        lax.all_to_all(
            labels.reshape(peers, capacity), ("gx", "gy"), split_axis=0, concat_axis=0, tiled=True
        ),
    )
    marker_force, back_rows = settle(
        received, got_labels, owned, train_of_block, marker_area, train_velocity, mark
    )
    returned = lax.all_to_all(
        back_rows.reshape(peers, capacity, 3 * mark),
        ("gx", "gy"),
        split_axis=0,
        concat_axis=0,
        tiled=True,
    )
    slot_force = jnp.dot(
        placement.T, returned.reshape(peers * capacity, 3 * mark), precision=lax.Precision.HIGHEST
    )
    slot_force = slot_force.reshape(slots, 3, mark).transpose(1, 0, 2)
    contrib = weights[None] * slot_force[:, :, None, :]
    cell_force = (
        jnp.zeros((3, cell_count), jnp.float32).at[:, cells.reshape(-1)].add(contrib.reshape(3, -1))
    )
    cell_force = cell_force.reshape(3, size_x, size_y, size_z)
    relaxed = collide(populations, cell_force, solid_cells)
    padded = with_halo(jnp.stack(relaxed), (("gx", 1), ("gy", 2), ("gz", 3)), 1)
    parts = []
    for direction in range(19):
        shift_x = 1 - int(velocity_table[direction][0])
        shift_y = 1 - int(velocity_table[direction][1])
        shift_z = 1 - int(velocity_table[direction][2])
        parts.append(
            padded[
                direction,
                shift_x : shift_x + size_x,
                shift_y : shift_y + size_y,
                shift_z : shift_z + size_z,
            ]
        )
    read = jnp.stack(parts)
    total_y = size_y * lax.axis_size("gy")
    total_z = size_z * lax.axis_size("gz")
    global_y = lax.axis_index("gy") * size_y + jnp.arange(size_y, dtype=jnp.int32)
    global_z = lax.axis_index("gz") * size_z + jnp.arange(size_z, dtype=jnp.int32)
    on_side = ((global_y == 0) | (global_y == total_y - 1))[:, None] | (
        (global_z == 0) | (global_z == total_z - 1)
    )[None, :]
    far_field = jnp.array(equilibrium(1.0, list(far_velocity)), dtype=jnp.float32)
    populations_next = jnp.where(on_side[None, None], far_field[:, None, None, None], read)
    return (populations_next, marker_force.reshape(1, 1, 1, owned, 3, mark))


def full(shape):
    return jax.ShapeDtypeStruct(shape, jnp.float32)


def kernel_params():
    return pltpu.CompilerParams(vmem_limit_bytes=vmem_bytes)


def low_half(shape):
    return lax.broadcasted_iota(jnp.int32, shape, 1) < shape[1] // 2


def fetch(pairs, sems):
    copies = [
        pltpu.make_async_copy(source, target, sems.at[i])
        for i, (source, target) in enumerate(pairs)
    ]
    for copy in copies:
        copy.start()
    return copies


def shard_rows(slots, owned):
    return 3 * slots + owned + 8


def sample_kernel(
    place_ref, pop_any, cells_any, weights_any, areas_any, owner_any, block_any, trains_any,
    out_ref, pop_ref, cells_ref, weights_ref, areas_ref, owner_ref, block_ref, trains_ref,
    table, sems,
):
    rows, lanes = (pop_ref.shape[1], pop_ref.shape[2])
    mark = cells_ref.shape[1]
    owned = areas_ref.shape[0]
    slots = owner_ref.shape[1]
    kernel = cells_ref.shape[0] // slots
    copies = fetch(
        (
            (pop_any, pop_ref),
            (cells_any, cells_ref),
            (weights_any, weights_ref),
            (areas_any, areas_ref),
            (owner_any, owner_ref),
            (block_any, block_ref),
            (trains_any, trains_ref),
        ),
        sems,
    )
    copies[0].wait()
    density, momentum = moments([pop_ref[q] for q in range(19)])
    fixed = [
        ((momentum[c] / density) * float(2**bits) + (2.0 ** (bits - 1) + 0.5)).astype(jnp.int32)
        for c, bits in enumerate((21, 21, 22))
    ]
    table[0] = (fixed[0] << 11) | (fixed[2] >> 11)
    table[1] = (fixed[1] << 11) | (fixed[2] & 2047)
    for copy in copies[1:]:
        copy.wait()
    meta = 3 * slots + owned
    out_ref[3 * slots : meta, :] = areas_ref[...]
    out_ref[meta : meta + 8, :] = jnp.zeros((8, mark), jnp.float32)
    ids = (owner_ref[...] * owned + block_ref[...]).astype(jnp.float32)
    out_ref[meta : meta + 1, :] = jnp.concatenate([ids] * (mark // slots), axis=1)
    out_ref[meta + 1 : meta + 2, 0:owned] = trains_ref[...].astype(jnp.float32)
    mine = lax.broadcasted_iota(jnp.int32, (1, mark), 1) % owned + place_ref[2] * owned
    out_ref[meta + 2 : meta + 3, :] = mine.astype(jnp.float32)

    def body(step, carry):
        first = pl.multiple_of(step * group, group)
        total = [jnp.zeros((group, mark), jnp.float32) for c in range(3)]
        for k in range(kernel):
            at = pl.ds(first * kernel + k, group, stride=kernel)
            cells = cells_ref[at, :]
            lane = cells & (lanes - 1)
            row = cells >> (lanes.bit_length() - 1)
            bits = [(row >> bit) & 1 == 1 for bit in range(rows.bit_length() - 1)]

            def choose(c, low, level):
                if level < 0:
                    line = jnp.broadcast_to(table[c, low : low + 1, :], (group, lanes))
                    return jnp.take_along_axis(line, lane, axis=1, mode="promise_in_bounds")
                lower = choose(c, low, level - 1)
                return jnp.where(bits[level], choose(c, low + (1 << level), level - 1), lower)

            words = [choose(c, 0, len(bits) - 1) for c in range(2)]
            last = ((words[0] & 2047) << 11) | (words[1] & 2047)
            picked = [
                lax.shift_right_logical(words[0], 11),
                lax.shift_right_logical(words[1], 11),
                last,
            ]
            weight = weights_ref[at, :]
            for c, width in enumerate((21, 21, 22)):
                value = (picked[c].astype(jnp.float32) - 2.0 ** (width - 1)) * 2.0**-width
                total[c] = total[c] + weight * value
        for c in range(3):
            out_ref[pl.ds(pl.multiple_of(c * slots + first, group), group), :] = total[c]
        return carry

    lax.fori_loop(0, slots // group, body, 0)


def sample(place, populations, cells, weights, areas, owner, block, trains):
    smem = pl.BlockSpec(memory_space=pltpu.SMEM)
    hbm = pl.BlockSpec(memory_space=pltpu.HBM)
    vmem = pl.BlockSpec(memory_space=pltpu.VMEM)
    return pl.pallas_call(
        sample_kernel,
        out_shape=full((shard_rows(owner.shape[1], areas.shape[0]), cells.shape[1])),
        in_specs=[smem] + [hbm] * 7,
        scratch_shapes=[
            pltpu.VMEM(entries.shape, entries.dtype)
            for entries in (populations, cells, weights, areas, owner, block, trains)
        ]
        + [
            pltpu.VMEM((2,) + populations.shape[1:], jnp.int32),
            pltpu.SemaphoreType.DMA((7,)),
        ],
        compiler_params=kernel_params(),
        name="sample",
    )(place, populations, cells, weights, areas, owner, block, trains)


def three_parts(values):
    parts = []
    for _ in range(3):
        parts.append(values.astype(jnp.bfloat16))
        values = values - parts[-1].astype(jnp.float32)
    return parts


def one_hot(mask):
    return jnp.where(mask, 1.0, 0.0).astype(jnp.bfloat16)


def settle_rows(speeds_ref, shards, slots, owned):
    mark = shards[0].shape[1]
    meta = 3 * slots + owned
    own = shards[0][meta : meta + 8, :]
    ids = jnp.broadcast_to(own[0:1], (mark, mark)).T[0:slots]
    mine = jnp.broadcast_to(own[2:3], (mark, mark)).T[0:owned]
    wanted = jnp.concatenate([ids, mine], axis=0)
    sums = area = trains = None
    for shard in shards:
        labels = shard[meta : meta + 1, :]
        match = one_hot(wanted == labels)
        match = jnp.concatenate([match, match[:, 0:slots]], axis=1)
        values = jnp.concatenate([shard[c * slots : (c + 1) * slots, :] for c in range(3)], axis=1)
        got = jnp.dot(
            match, jnp.concatenate(three_parts(values), axis=0), preferred_element_type=jnp.float32
        )
        sums = got if sums is None else sums + got
        held = ids == shard[meta + 2 : meta + 3, :]
        parts = three_parts(shard[3 * slots : meta, :])
        parts.append(jnp.zeros_like(parts[0]))
        got = jnp.dot(
            one_hot(held), jnp.concatenate(parts, axis=0), preferred_element_type=jnp.float32
        )
        area = got if area is None else area + got
        got = jnp.where(held, shard[meta + 1 : meta + 2, :], 0.0)
        trains = got if trains is None else trains + got
    trains = jnp.sum(trains, axis=1, keepdims=True)
    own_trains = jnp.broadcast_to(own[1:2], (mark, mark)).T[0:owned]
    forces = []
    own_forces = []
    for c in range(3):
        target = jnp.zeros(trains.shape, jnp.float32)
        own_target = jnp.zeros(own_trains.shape, jnp.float32)
        for train in range(speeds_ref.shape[0]):
            speed = speeds_ref[train, c]
            target = jnp.where(trains == float(train), speed, target)
            own_target = jnp.where(own_trains == float(train), speed, own_target)
        got = sums[:, c * mark : (c + 1) * mark]
        forces.append(stiffness * area * (target - got[0:slots]))
        own_area = shards[0][3 * slots : meta, :]
        own_forces.append(stiffness * own_area * (own_target - got[slots:]))
    return (forces, own_forces)


def spread_kernel(shard_count, slots, owned, place_ref, speeds_ref, *refs):
    shards, refs = (refs[:shard_count], refs[shard_count:])
    cells_any, weights_any, pop_any, solid_ref = refs[:4]
    relaxed_ref, far_ref, near_ref, marker_ref = refs[4:8]
    cells_ref, weights_ref, pop_ref, force_ref, lines_ref, acc, sems = refs[8:]
    rows, lanes = (pop_ref.shape[1], pop_ref.shape[2])
    size_y = 8
    mark = cells_ref.shape[1]
    kernel = cells_ref.shape[0] // slots
    bf = jnp.bfloat16
    copies = fetch(
        ((cells_any, cells_ref), (weights_any, weights_ref), (pop_any, pop_ref)), sems
    )
    forces, own_forces = settle_rows(speeds_ref, shards, slots, owned)
    for c in range(3):
        force_ref[c] = forces[c]
        marker_ref[c] = own_forces[c]

    acc[...] = jnp.zeros_like(acc)
    iota = lax.broadcasted_iota(jnp.int32, (16, mark), 0).astype(jnp.float32)
    steps = [(iota + 16.0 * j).astype(bf) for j in range(max(rows, lanes) // 16)]
    one, zero = (jnp.ones((16, mark), bf), jnp.zeros((16, mark), bf))
    copies[0].wait()
    copies[1].wait()

    def body(step, carry):
        first = pl.multiple_of(step * group, group)
        force = [force_ref[c, pl.ds(first, group), :] for c in range(3)]
        for k in range(kernel):
            at = pl.ds(first * kernel + k, group, stride=kernel)
            cells = cells_ref[at, :]
            weight = weights_ref[at, :]
            lane = (cells & (lanes - 1)).astype(jnp.float32)
            row = (cells >> (lanes.bit_length() - 1)).astype(jnp.float32)
            parts = []
            for c in range(3):
                value = weight * force[c]
                high = value.astype(bf).astype(jnp.float32)
                parts += [high, value - high]
            for which, entries in enumerate([lane, row] + parts):
                lines_ref[k, which] = entries

            def wide(which, i):
                entries = lines_ref[k, which, i : i + 1, :]
                return jnp.broadcast_to(entries, (16, mark)).astype(bf)

            left, right = ([], [])
            for i in range(group):
                lane_i, row_i = (wide(0, i), wide(1, i))
                right.append(
                    jnp.concatenate(
                        [jnp.where(steps[j] == lane_i, one, zero) for j in range(lanes // 16)],
                        axis=0,
                    )
                )
                masks = [steps[j] == row_i for j in range(rows // 16)]
                pieces = []
                for which in range(len(parts)):
                    part_i = wide(2 + which, i)
                    pieces += [jnp.where(mask, part_i, zero) for mask in masks]
                left.append(jnp.concatenate(pieces, axis=0))
            acc[...] += lax.dot_general(
                jnp.concatenate(left, axis=1),
                jnp.concatenate(right, axis=1),
                (((1,), (1,)), ((), ())),
                preferred_element_type=jnp.float32,
            )
        return carry

    lax.fori_loop(0, slots // group, body, 0)
    copies[2].wait()
    cell_force = [
        acc[2 * c * rows : (2 * c + 1) * rows, :] + acc[(2 * c + 1) * rows : (2 * c + 2) * rows, :]
        for c in range(3)
    ]
    relaxed = collide([pop_ref[q] for q in range(19)], cell_force, solid_ref[...])
    for q in range(19):
        relaxed_ref[q] = relaxed[q]
    even = place_ref[3] == 0
    for i in range(5):
        ahead = relaxed[going(0, 1)[i]][rows - size_y :]
        behind = relaxed[going(0, -1)[i]][:size_y]
        far_ref[i] = jnp.where(even, behind, ahead)
        near_ref[i] = jnp.where(even, ahead, behind)


def peers_z(ref):
    return ref.shape[0] // 2


def spread(slots, owned, place, speeds, shards, cells, weights, populations, solid):
    mark = cells.shape[1]
    line_count, lanes = solid.shape
    smem = pl.BlockSpec(memory_space=pltpu.SMEM)
    hbm = pl.BlockSpec(memory_space=pltpu.HBM)
    vmem = pl.BlockSpec(memory_space=pltpu.VMEM)
    return pl.pallas_call(
        functools.partial(spread_kernel, len(shards), slots, owned),
        out_shape=(
            full(populations.shape),
            full((5, 8, lanes)),
            full((5, 8, lanes)),
            full((3, owned, mark)),
        ),
        in_specs=[smem] * 2 + [vmem] * len(shards) + [hbm] * 3 + [vmem],
        scratch_shapes=[
            pltpu.VMEM(cells.shape, jnp.int32),
            pltpu.VMEM(weights.shape, jnp.float32),
            pltpu.VMEM(populations.shape, jnp.float32),
            pltpu.VMEM((3, slots, mark), jnp.float32),
            pltpu.VMEM((cells.shape[0] // slots, 8, group, mark), jnp.float32),
            pltpu.VMEM((6 * line_count, lanes), jnp.float32),
            pltpu.SemaphoreType.DMA((3,)),
        ],
        compiler_params=kernel_params(),
        name="spread",
    )(place, speeds, *shards, cells, weights, populations, solid)


def downwind(place_ref, relaxed_ref, far_ref, near_ref):
    size_y = far_ref.shape[1]
    size_x = relaxed_ref.shape[1] // size_y
    even = place_ref[3] == 0

    def cells(q, x):
        step = int(velocity_table[q][0])
        source = x - step
        if 0 <= source < size_x:
            return relaxed_ref[q, source * size_y : (source + 1) * size_y, :]
        i = going(0, step).index(q)
        if step == 1:
            return jnp.where(even, far_ref[i], near_ref[i])
        return jnp.where(even, near_ref[i], far_ref[i])

    return cells


def pack_kernel(place_ref, relaxed_ref, far_ref, near_ref, send_ref):
    size_y, lanes = far_ref.shape[1:]
    size_x = relaxed_ref.shape[1] // size_y
    cells = downwind(place_ref, relaxed_ref, far_ref, near_ref)
    lane_at = lax.broadcasted_iota(jnp.int32, (size_y, lanes), 1)
    packs = []
    for step in (1, -1):
        packed = jnp.zeros((size_y, lanes), jnp.float32)
        for i, q in enumerate(going(2, step)):
            edge = lanes - 1 if step == 1 else 0
            for x in range(size_x):
                at = 8 * x + i
                moved = pltpu.roll(cells(q, x), (at - edge) % lanes, 1)
                packed = jnp.where(lane_at == at, moved, packed)
        packs.append(packed)
    y_index, z_index = (place_ref[0], place_ref[1])
    count_z = peers_z(send_ref)
    for peer in range(send_ref.shape[0]):
        send_ref[peer, 0:8, :] = jnp.where(z_index < peer % count_z, packs[0], packs[1])
    face = (1 - y_index) * count_z + z_index
    for i in range(5):
        for x in range(size_x):
            up = cells(going(1, 1)[i], x)[size_y - 1 : size_y, :]
            down = cells(going(1, -1)[i], x)[0:1, :]
            at = size_x * i + x
            send_ref[face, at : at + 1, :] = jnp.where(y_index == 0, up, down)


def pack(count_z, place, relaxed, far, near):
    lanes = relaxed.shape[2]
    smem = pl.BlockSpec(memory_space=pltpu.SMEM)
    vmem = pl.BlockSpec(memory_space=pltpu.VMEM)
    return pl.pallas_call(
        pack_kernel,
        out_shape=full((2 * count_z, 24, lanes)),
        in_specs=[smem] + [vmem] * 3,
        compiler_params=kernel_params(),
        name="pack",
    )(place, relaxed, far, near)


def stream_kernel(
    place_ref, relaxed_ref, far_ref, near_ref, got_ref, out_any, out_ref, sems
):
    size_x, size_y, lanes = out_ref.shape[1:]
    shape = (size_y, lanes)
    streamed = downwind(place_ref, relaxed_ref, far_ref, near_ref)
    y_at = lax.broadcasted_iota(jnp.int32, shape, 0)
    z_at = lax.broadcasted_iota(jnp.int32, shape, 1)
    y_index, z_index = (place_ref[0], place_ref[1])
    count_z = peers_z(got_ref)
    side = (1 - y_index) * count_z
    here = y_index * count_z
    z_from = {1: jnp.maximum(z_index - 1, 0), -1: jnp.minimum(z_index + 1, count_z - 1)}
    level = {step: got_ref[here + z_from[step], 0:8, :] for step in (1, -1)}
    across = {step: got_ref[side + z_from[step], 0:8, :] for step in (1, -1)}
    on_side = y_at == jnp.where(y_index == 0, 0, size_y - 1)
    on_side = on_side | ((z_at == 0) & (z_index == 0))
    on_side = on_side | ((z_at == lanes - 1) & (z_index == count_z - 1))
    copies = []
    for q in range(19):
        _, step_y, step_z = (int(step) for step in velocity_table[q])
        y_edge = 0 if step_y == 1 else size_y - 1
        z_edge = 0 if step_z == 1 else lanes - 1
        column = level.get(step_z)
        if step_z != 0 and step_y != 0:
            column = jnp.where(
                y_at == y_edge,
                pltpu.roll(across[step_z], step_y % size_y, 0),
                pltpu.roll(column, step_y % size_y, 0),
            )
        for x in range(size_x):
            cells = streamed(q, x)
            if step_y != 0:
                at = size_x * going(1, step_y).index(q) + x
                halo = got_ref[side + z_index, at : at + 1, :]
                cells = jnp.where(y_at == y_edge, halo, pltpu.roll(cells, step_y % size_y, 0))
            if step_z != 0:
                at = 8 * x + going(2, step_z).index(q)
                cells = jnp.where(
                    z_at == z_edge,
                    pltpu.roll(column, (z_edge - at) % lanes, 1),
                    pltpu.roll(cells, step_z % lanes, 1),
                )
            out_ref[q, x] = jnp.where(on_side, far_field[q], cells)
        copies.append(pltpu.make_async_copy(out_ref.at[q], out_any.at[q], sems.at[q]))
        copies[-1].start()
    for copy in copies:
        copy.wait()


def stream(place, relaxed, far, near, got):
    rows, lanes = relaxed.shape[1:]
    size_y = far.shape[1]
    smem = pl.BlockSpec(memory_space=pltpu.SMEM)
    vmem = pl.BlockSpec(memory_space=pltpu.VMEM)
    shape = (19, rows // size_y, size_y, lanes)
    return pl.pallas_call(
        stream_kernel,
        out_shape=full(shape),
        in_specs=[smem] + [vmem] * 4,
        out_specs=pl.BlockSpec(memory_space=pltpu.HBM),
        scratch_shapes=[pltpu.VMEM(shape, jnp.float32), pltpu.SemaphoreType.DMA((19,))],
        compiler_params=kernel_params(),
        name="stream",
    )(place, relaxed, far, near, got)


def per_device(
    populations,
    solid_cells,
    slot_cells,
    slot_weights,
    slot_owner,
    slot_block,
    train_of_block,
    marker_area,
    train_velocity,
):
    size_x, size_y, size_z = (populations.shape[1], populations.shape[2], populations.shape[3])
    lines = size_x * size_y
    slots, kernel, mark = (slot_cells.shape[3], slot_cells.shape[4], slot_cells.shape[5])
    owned = train_of_block.shape[3]
    count_x, count_y, count_z = (lax.axis_size(axis) for axis in ("gx", "gy", "gz"))
    x_index, y_index, z_index = (lax.axis_index(axis) for axis in ("gx", "gy", "gz"))
    place = jnp.stack([y_index, z_index, x_index * count_y + y_index, x_index % 2])
    place = place.astype(jnp.int32)
    inputs = [
        pltpu.with_memory_space_constraint(entries, pltpu.HBM)
        for entries in (
            populations.reshape(19, lines, size_z),
            slot_cells.reshape(slots * kernel, mark),
            slot_weights.reshape(slots * kernel, mark),
            marker_area.reshape(owned, mark),
            slot_owner.reshape(1, slots),
            slot_block.reshape(1, slots),
            train_of_block.reshape(1, owned),
        )
    ]
    pops, cells, weights = inputs[:3]
    own = sample(place, *inputs)
    swap = [(0, 1), (1, 0)]
    column = {0: own}
    for distance in reversed(range(1, count_x)):
        column[distance] = lax.ppermute(own, "gx", [(i, i ^ distance) for i in range(count_x)])
    shards = []
    for distance in (0, 2, 3, 1):
        shards += [column[distance], lax.ppermute(column[distance], "gy", swap)]
    relaxed, far, near, marker_force = spread(
        slots,
        owned,
        place,
        train_velocity,
        shards,
        cells,
        weights,
        pops,
        solid_cells.reshape(lines, size_z),
    )
    evens = range(0, count_x, 2)
    far = lax.ppermute(
        far,
        "gx",
        [(i, (i - 1) % count_x) for i in evens] + [((i - 1) % count_x, i) for i in evens],
    )
    near = lax.ppermute(near, "gx", [(i, i + 1) for i in evens] + [(i + 1, i) for i in evens])
    sides = pack(count_z, place, relaxed, far, near)
    sides = lax.all_to_all(sides, ("gy", "gz"), split_axis=0, concat_axis=0, tiled=True)
    populations_next = stream(place, relaxed, far, near, sides)
    marker_force = marker_force.transpose(1, 0, 2).reshape(1, 1, 1, owned, 3, mark)
    return (populations_next, marker_force)


def solution(mesh):
    placed = (
        P(None, "gx", "gy", "gz"),
        P("gx", "gy", "gz"),
        P("gx", "gy", "gz", None, None, None),
        P("gx", "gy", "gz", None, None, None),
        P("gx", "gy", "gz", None, None),
        P("gx", "gy", "gz", None),
        P("gx", "gy", "gz", None),
        P("gx", "gy", "gz", None, None),
        P(),
    )
    small = mesh.shape["gy"] == 2 and mesh.shape["gx"] == 4 and mesh.shape["gz"] > 1
    return jax.shard_map(
        per_device if small else per_device_general,
        mesh=mesh,
        in_specs=placed,
        out_specs=(P(None, "gx", "gy", "gz"), P("gx", "gy", "gz", None, None, None)),
        check_vma=False,
    )
```

```python
import functools
import jax
import jax.numpy as jnp
import numpy as np
from jax import lax
from jax.experimental import pallas as pl
from jax.experimental.pallas import tpu as pltpu
from jax.sharding import PartitionSpec as P

velocity_table = np.array(
    [
        [0, 0, 0],
        [1, 0, 0],
        [-1, 0, 0],
        [0, 1, 0],
        [0, -1, 0],
        [0, 0, 1],
        [0, 0, -1],
        [1, 1, 0],
        [-1, -1, 0],
        [1, -1, 0],
        [-1, 1, 0],
        [1, 0, 1],
        [-1, 0, -1],
        [1, 0, -1],
        [-1, 0, 1],
        [0, 1, 1],
        [0, -1, -1],
        [0, 1, -1],
        [0, -1, 1],
    ]
)
weight_table = [1.0 / 3.0] + [1.0 / 18.0] * 6 + [1.0 / 36.0] * 12
opposite_table = [0, 2, 1, 4, 3, 6, 5, 8, 7, 10, 9, 12, 11, 14, 13, 16, 15, 18, 17]
stress_pairs = [(0, 0), (1, 1), (2, 2), (0, 1), (0, 2), (1, 2)]
tau_base = 0.55
smag_term = 18.0 * 1.4142135623730951 * 0.17 * 0.17
regular_eps = 0.0001
stiffness = 2.0
far_velocity = (0.02, 0.06, 0.0)
vmem_bytes = 40 << 20
group = 8


def going(axis, step):
    return [q for q in range(19) if int(velocity_table[q][axis]) == step]


def project(direction, vector):
    projection = 0.0 * vector[0]
    for component in range(3):
        lattice_step = int(velocity_table[direction][component])
        if lattice_step != 0:
            projection = projection + lattice_step * vector[component]
    return projection


def moments(populations):
    density = populations[0]
    momentum = [jnp.zeros_like(density) for component in range(3)]
    for direction in range(1, 19):
        density = density + populations[direction]
        for component in range(3):
            lattice_step = int(velocity_table[direction][component])
            if lattice_step == 1:
                momentum[component] = momentum[component] + populations[direction]
            elif lattice_step == -1:
                momentum[component] = momentum[component] - populations[direction]
    return (density, momentum)


def equilibrium(density, velocity):
    speed_sq = velocity[0] * velocity[0] + velocity[1] * velocity[1] + velocity[2] * velocity[2]
    result = []
    for direction in range(19):
        projected = project(direction, velocity)
        result.append(
            weight_table[direction]
            * density
            * (1.0 + 3.0 * projected + 4.5 * projected * projected - 1.5 * speed_sq)
        )
    return result


far_field = [float(np.float32(value)) for value in equilibrium(1.0, list(far_velocity))]


def collide(populations, cell_force, solid_cells):
    density, momentum = moments(populations)
    velocity = [
        (momentum[component] + 0.5 * cell_force[component]) / density for component in range(3)
    ]
    balance = equilibrium(density, velocity)
    stress = [jnp.zeros_like(density) for pair_pos in range(6)]
    for direction in range(19):
        non_eq = populations[direction] - balance[direction]
        for pair_pos in range(6):
            row_axis, col_axis = stress_pairs[pair_pos]
            factor = int(velocity_table[direction][row_axis] * velocity_table[direction][col_axis])
            if factor != 0:
                stress[pair_pos] = stress[pair_pos] + factor * non_eq
    shear_sq = stress[0] * stress[0] + stress[1] * stress[1] + stress[2] * stress[2]
    shear_sq = shear_sq + 2.0 * (
        stress[3] * stress[3] + stress[4] * stress[4] + stress[5] * stress[5]
    )
    magnitude = jnp.sqrt(shear_sq + regular_eps)
    relax_time = 0.5 * (tau_base + jnp.sqrt(tau_base * tau_base + smag_term * magnitude / density))
    relax_rate = 1.0 / relax_time
    guo_factor = 1.0 - 0.5 * relax_rate
    speed_force = (
        velocity[0] * cell_force[0] + velocity[1] * cell_force[1] + velocity[2] * cell_force[2]
    )
    result = []
    for direction in range(19):
        along_force = project(direction, cell_force)
        along_speed = project(direction, velocity)
        source = (
            guo_factor
            * weight_table[direction]
            * (3.0 * (along_force - speed_force) + 9.0 * along_speed * along_force)
        )
        relaxed = (
            populations[direction]
            - (populations[direction] - balance[direction]) * relax_rate
            + source
        )
        result.append(jnp.where(solid_cells == 1, populations[opposite_table[direction]], relaxed))
    return result


def with_halo(cells, sides, width):
    for axis, dim in sides:
        count = lax.axis_size(axis)
        head = lax.slice_in_dim(cells, 0, width, axis=dim)
        tail = lax.slice_in_dim(cells, cells.shape[dim] - width, cells.shape[dim], axis=dim)
        cells = jnp.concatenate(
            [
                lax.ppermute(tail, axis, [(i, (i + 1) % count) for i in range(count)]),
                cells,
                lax.ppermute(head, axis, [((i + 1) % count, i) for i in range(count)]),
            ],
            axis=dim,
        )
    return cells


def settle(received, labels, owned, train_of_block, marker_area, train_velocity, mark):
    rows_in = received.reshape(-1, 3 * mark)
    label_rows = labels.reshape(-1)
    owner_match = (label_rows[None, :] == jnp.arange(owned, dtype=jnp.int32)[:, None]).astype(
        jnp.float32
    )
    marker_velocity = jnp.dot(owner_match, rows_in, precision=lax.Precision.HIGHEST).reshape(
        owned, 3, mark
    )
    trains = train_velocity.shape[0]
    train_rows = train_of_block.reshape(owned)
    train_match = (train_rows[:, None] == jnp.arange(trains, dtype=jnp.int32)[None, :]).astype(
        jnp.float32
    )
    target = jnp.dot(train_match, train_velocity, precision=lax.Precision.HIGHEST)
    areas = marker_area.reshape(owned, mark)
    marker_force = stiffness * areas[:, None, :] * (target[:, :, None] - marker_velocity)
    back_rows = jnp.dot(
        owner_match.T, marker_force.reshape(owned, 3 * mark), precision=lax.Precision.HIGHEST
    )
    return (marker_force, back_rows)


def per_device_general(
    populations,
    solid_cells,
    slot_cells,
    slot_weights,
    slot_owner,
    slot_block,
    train_of_block,
    marker_area,
    train_velocity,
):
    size_x, size_y, size_z = (populations.shape[1], populations.shape[2], populations.shape[3])
    cell_count = size_x * size_y * size_z
    slots, kernel, mark = (slot_cells.shape[3], slot_cells.shape[4], slot_cells.shape[5])
    owned = train_of_block.shape[3]
    peers_x = lax.axis_size("gx")
    peers_y = lax.axis_size("gy")
    peers = peers_x * peers_y
    capacity = max(2, 2 * slots // peers)
    density, momentum = moments(populations)
    rest_velocity = jnp.stack([momentum[component] / density for component in range(3)]).reshape(
        3, cell_count
    )
    cells = slot_cells.reshape(slots, kernel, mark)
    weights = slot_weights.reshape(slots, kernel, mark)
    partial_value = jnp.sum(rest_velocity[:, cells] * weights[None], axis=2)
    slot_rows = partial_value.transpose(1, 0, 2).reshape(slots, 3 * mark)
    slot_dest = slot_owner.reshape(slots)
    blocks = slot_block.reshape(slots)
    order = jnp.arange(slots, dtype=jnp.int32)
    earlier = (slot_dest[None, :] == slot_dest[:, None]) & (order[None, :] < order[:, None])
    slot_rank = jnp.sum(earlier.astype(jnp.int32), axis=1)
    target_row = slot_dest * capacity + slot_rank
    buffer_rows = jnp.arange(peers * capacity, dtype=jnp.int32)
    matches = buffer_rows[:, None] == target_row[None, :]
    placement = matches.astype(jnp.float32)
    outgoing = jnp.dot(placement, slot_rows, precision=lax.Precision.HIGHEST)
    labels = jnp.sum(jnp.where(matches, blocks[None, :] + 1, 0), axis=1) - 1
    received, got_labels = (
        lax.all_to_all(
            outgoing.reshape(peers, capacity, 3 * mark),
            ("gx", "gy"),
            split_axis=0,
            concat_axis=0,
            tiled=True,
        ),
        lax.all_to_all(
            labels.reshape(peers, capacity), ("gx", "gy"), split_axis=0, concat_axis=0, tiled=True
        ),
    )
    marker_force, back_rows = settle(
        received, got_labels, owned, train_of_block, marker_area, train_velocity, mark
    )
    returned = lax.all_to_all(
        back_rows.reshape(peers, capacity, 3 * mark),
        ("gx", "gy"),
        split_axis=0,
        concat_axis=0,
        tiled=True,
    )
    slot_force = jnp.dot(
        placement.T, returned.reshape(peers * capacity, 3 * mark), precision=lax.Precision.HIGHEST
    )
    slot_force = slot_force.reshape(slots, 3, mark).transpose(1, 0, 2)
    contrib = weights[None] * slot_force[:, :, None, :]
    cell_force = (
        jnp.zeros((3, cell_count), jnp.float32).at[:, cells.reshape(-1)].add(contrib.reshape(3, -1))
    )
    cell_force = cell_force.reshape(3, size_x, size_y, size_z)
    relaxed = collide(populations, cell_force, solid_cells)
    padded = with_halo(jnp.stack(relaxed), (("gx", 1), ("gy", 2), ("gz", 3)), 1)
    parts = []
    for direction in range(19):
        shift_x = 1 - int(velocity_table[direction][0])
        shift_y = 1 - int(velocity_table[direction][1])
        shift_z = 1 - int(velocity_table[direction][2])
        parts.append(
            padded[
                direction,
                shift_x : shift_x + size_x,
                shift_y : shift_y + size_y,
                shift_z : shift_z + size_z,
            ]
        )
    read = jnp.stack(parts)
    total_y = size_y * lax.axis_size("gy")
    total_z = size_z * lax.axis_size("gz")
    global_y = lax.axis_index("gy") * size_y + jnp.arange(size_y, dtype=jnp.int32)
    global_z = lax.axis_index("gz") * size_z + jnp.arange(size_z, dtype=jnp.int32)
    on_side = ((global_y == 0) | (global_y == total_y - 1))[:, None] | (
        (global_z == 0) | (global_z == total_z - 1)
    )[None, :]
    far_field = jnp.array(equilibrium(1.0, list(far_velocity)), dtype=jnp.float32)
    populations_next = jnp.where(on_side[None, None], far_field[:, None, None, None], read)
    return (populations_next, marker_force.reshape(1, 1, 1, owned, 3, mark))


def full(shape):
    return jax.ShapeDtypeStruct(shape, jnp.float32)


def kernel_params():
    return pltpu.CompilerParams(vmem_limit_bytes=vmem_bytes)


def low_half(shape):
    return lax.broadcasted_iota(jnp.int32, shape, 1) < shape[1] // 2


def fetch(pairs, sems):
    copies = [
        pltpu.make_async_copy(source, target, sems.at[i])
        for i, (source, target) in enumerate(pairs)
    ]
    for copy in copies:
        copy.start()
    return copies


def shard_rows(slots, owned):
    return 3 * slots + owned + 8


def sample_kernel(
    place_ref, pop_any, cells_any, weights_any, areas_any, owner_any, block_any, trains_any,
    out_ref, pop_ref, cells_ref, weights_ref, areas_ref, owner_ref, block_ref, trains_ref,
    table, sems, group_sems,
):
    rows, lanes = (pop_ref.shape[1], pop_ref.shape[2])
    mark = cells_ref.shape[1]
    owned = areas_ref.shape[0]
    slots = owner_ref.shape[1]
    kernel = cells_ref.shape[0] // slots
    copies = fetch(
        (
            (pop_any, pop_ref),
            (areas_any, areas_ref),
            (owner_any, owner_ref),
            (block_any, block_ref),
            (trains_any, trains_ref),
        ),
        sems,
    )

    def group_copies(step):
        here = pl.ds(pl.multiple_of(step * group * kernel, group * kernel), group * kernel)
        return (
            pltpu.make_async_copy(cells_any.at[here], cells_ref.at[here], group_sems.at[0, step]),
            pltpu.make_async_copy(
                weights_any.at[here], weights_ref.at[here], group_sems.at[1, step]
            ),
        )

    for step in range(slots // group):
        for copy in group_copies(step):
            copy.start()
    copies[0].wait()
    density, momentum = moments([pop_ref[q] for q in range(19)])
    fixed = [
        ((momentum[c] / density) * float(2**bits) + (2.0 ** (bits - 1) + 0.5)).astype(jnp.int32)
        for c, bits in enumerate((21, 21, 22))
    ]
    table[0] = (fixed[0] << 11) | (fixed[2] >> 11)
    table[1] = (fixed[1] << 11) | (fixed[2] & 2047)
    for copy in copies[1:]:
        copy.wait()
    meta = 3 * slots + owned
    out_ref[3 * slots : meta, :] = areas_ref[...]
    out_ref[meta : meta + 8, :] = jnp.zeros((8, mark), jnp.float32)
    ids = (owner_ref[...] * owned + block_ref[...]).astype(jnp.float32)
    out_ref[meta : meta + 1, :] = jnp.concatenate([ids] * (mark // slots), axis=1)
    out_ref[meta + 1 : meta + 2, 0:owned] = trains_ref[...].astype(jnp.float32)
    mine = lax.broadcasted_iota(jnp.int32, (1, mark), 1) % owned + place_ref[2] * owned
    out_ref[meta + 2 : meta + 3, :] = mine.astype(jnp.float32)

    def body(step, carry):
        for copy in group_copies(step):
            copy.wait()
        first = pl.multiple_of(step * group, group)
        total = [jnp.zeros((group, mark), jnp.float32) for c in range(3)]
        for k in range(kernel):
            at = pl.ds(first * kernel + k, group, stride=kernel)
            cells = cells_ref[at, :]
            lane = cells & (lanes - 1)
            row = cells >> (lanes.bit_length() - 1)
            bits = [(row >> bit) & 1 == 1 for bit in range(rows.bit_length() - 1)]

            def choose(c, low, level):
                if level < 0:
                    line = jnp.broadcast_to(table[c, low : low + 1, :], (group, lanes))
                    return jnp.take_along_axis(line, lane, axis=1, mode="promise_in_bounds")
                lower = choose(c, low, level - 1)
                return jnp.where(bits[level], choose(c, low + (1 << level), level - 1), lower)

            words = [choose(c, 0, len(bits) - 1) for c in range(2)]
            last = ((words[0] & 2047) << 11) | (words[1] & 2047)
            picked = [
                lax.shift_right_logical(words[0], 11),
                lax.shift_right_logical(words[1], 11),
                last,
            ]
            weight = weights_ref[at, :]
            for c, width in enumerate((21, 21, 22)):
                value = (picked[c].astype(jnp.float32) - 2.0 ** (width - 1)) * 2.0**-width
                total[c] = total[c] + weight * value
        for c in range(3):
            out_ref[pl.ds(pl.multiple_of(c * slots + first, group), group), :] = total[c]
        return carry

    lax.fori_loop(0, slots // group, body, 0, unroll=2)


def sample(place, populations, cells, weights, areas, owner, block, trains):
    smem = pl.BlockSpec(memory_space=pltpu.SMEM)
    hbm = pl.BlockSpec(memory_space=pltpu.HBM)
    vmem = pl.BlockSpec(memory_space=pltpu.VMEM)
    return pl.pallas_call(
        sample_kernel,
        out_shape=full((shard_rows(owner.shape[1], areas.shape[0]), cells.shape[1])),
        in_specs=[smem] + [hbm] * 7,
        scratch_shapes=[
            pltpu.VMEM(entries.shape, entries.dtype)
            for entries in (populations, cells, weights, areas, owner, block, trains)
        ]
        + [
            pltpu.VMEM((2,) + populations.shape[1:], jnp.int32),
            pltpu.SemaphoreType.DMA((5,)),
            pltpu.SemaphoreType.DMA((2, owner.shape[1] // group)),
        ],
        compiler_params=kernel_params(),
        name="sample",
    )(place, populations, cells, weights, areas, owner, block, trains)


def three_parts(values):
    parts = []
    for _ in range(3):
        parts.append(values.astype(jnp.bfloat16))
        values = values - parts[-1].astype(jnp.float32)
    return parts


def one_hot(mask):
    return jnp.where(mask, 1.0, 0.0).astype(jnp.bfloat16)


def wanted_labels(own_ref, slots, owned):
    mark = own_ref.shape[1]
    own = own_ref[3 * slots + owned : 3 * slots + owned + 8, :]
    ids, trains, mine = (jnp.broadcast_to(own[i : i + 1], (mark, mark)).T for i in range(3))
    return (ids[0:slots], mine[0:owned], trains[0:owned])


def add_shards(totals, shards, ids, mine):
    slots, owned = (ids.shape[0], mine.shape[0])
    meta = 3 * slots + owned
    wanted = jnp.concatenate([ids, mine], axis=0)
    for shard in shards:
        match = one_hot(wanted == shard[meta : meta + 1, :])
        match = jnp.concatenate([match, match[:, 0:slots]], axis=1)
        values = jnp.concatenate([shard[c * slots : (c + 1) * slots, :] for c in range(3)], axis=1)
        sums = jnp.dot(
            match, jnp.concatenate(three_parts(values), axis=0), preferred_element_type=jnp.float32
        )
        held = ids == shard[meta + 2 : meta + 3, :]
        parts = three_parts(shard[3 * slots : meta, :])
        parts.append(jnp.zeros_like(parts[0]))
        area = jnp.dot(
            one_hot(held), jnp.concatenate(parts, axis=0), preferred_element_type=jnp.float32
        )
        trains = jnp.where(held, shard[meta + 1 : meta + 2, :], 0.0)
        got = (sums, area, trains)
        totals = got if totals is None else [total + new for total, new in zip(totals, got)]
    return totals


def settle_kernel(slots, owned, *refs):
    shards, (sums_ref, area_ref, trains_ref) = (refs[:-3], refs[-3:])
    ids, mine, _ = wanted_labels(shards[0], slots, owned)
    sums_ref[...], area_ref[...], trains_ref[...] = add_shards(None, shards, ids, mine)


def settle_early(slots, owned, shards):
    mark = shards[0].shape[1]
    vmem = pl.BlockSpec(memory_space=pltpu.VMEM)
    return pl.pallas_call(
        functools.partial(settle_kernel, slots, owned),
        out_shape=(full((slots + owned, 3 * mark)), full((slots, mark)), full((slots, mark))),
        in_specs=[vmem] * len(shards),
        compiler_params=kernel_params(),
        cost_estimate=pl.CostEstimate(
            flops=10**9, bytes_accessed=len(shards) * shards[0].size * 4, transcendentals=0
        ),
        name="settle",
    )(*shards)


def block_forces(speeds_ref, totals, own_ref, slots, owned):
    mark = own_ref.shape[1]
    ids, mine, own_trains = wanted_labels(own_ref, slots, owned)
    sums, area, trains = totals
    trains = jnp.sum(trains, axis=1, keepdims=True)
    own_area = own_ref[3 * slots : 3 * slots + owned, :]
    forces, own_forces = ([], [])
    for c in range(3):
        target = jnp.zeros(trains.shape, jnp.float32)
        own_target = jnp.zeros(own_trains.shape, jnp.float32)
        for train in range(speeds_ref.shape[0]):
            speed = speeds_ref[train, c]
            target = jnp.where(trains == float(train), speed, target)
            own_target = jnp.where(own_trains == float(train), speed, own_target)
        got = sums[:, c * mark : (c + 1) * mark]
        forces.append(stiffness * area * (target - got[0:slots]))
        own_forces.append(stiffness * own_area * (own_target - got[slots:]))
    return (forces, own_forces)


def spread_kernel(shard_count, slots, owned, place_ref, speeds_ref, *refs):
    shards, refs = (refs[:shard_count], refs[shard_count:])
    sums_ref, area_ref, trains_ref, cells_any, weights_any, pop_any, solid_ref = refs[:7]
    relaxed_ref, far_ref, near_ref, side_ref, marker_ref = refs[7:12]
    cells_ref, weights_ref, pop_ref, force_ref, lines_ref, acc, sems = refs[12:]
    rows, lanes = (pop_ref.shape[1], pop_ref.shape[2])
    size_y = 8
    mark = cells_ref.shape[1]
    kernel = cells_ref.shape[0] // slots
    bf = jnp.bfloat16
    copies = fetch(
        ((cells_any, cells_ref), (weights_any, weights_ref), (pop_any, pop_ref)), sems
    )
    own_ref = shards[0]
    ids, mine, _ = wanted_labels(own_ref, slots, owned)
    totals = (sums_ref[...], area_ref[...], trains_ref[...])
    totals = add_shards(totals, shards[1:], ids, mine)
    forces, own_forces = block_forces(speeds_ref, totals, own_ref, slots, owned)
    for c in range(3):
        force_ref[c] = forces[c]
        marker_ref[c] = own_forces[c]

    acc[...] = jnp.zeros_like(acc)
    iota = lax.broadcasted_iota(jnp.int32, (16, mark), 0).astype(jnp.float32)
    steps = [(iota + 16.0 * j).astype(bf) for j in range(max(rows, lanes) // 16)]
    one, zero = (jnp.ones((16, mark), bf), jnp.zeros((16, mark), bf))
    copies[0].wait()
    copies[1].wait()

    def body(step, carry):
        first = pl.multiple_of(step * group, group)
        force = [force_ref[c, pl.ds(first, group), :] for c in range(3)]
        for k in range(kernel):
            at = pl.ds(first * kernel + k, group, stride=kernel)
            cells = cells_ref[at, :]
            weight = weights_ref[at, :]
            lane = (cells & (lanes - 1)).astype(jnp.float32)
            row = (cells >> (lanes.bit_length() - 1)).astype(jnp.float32)
            parts = []
            for c in range(3):
                value = weight * force[c]
                high = value.astype(bf).astype(jnp.float32)
                parts += [high, value - high]
            for which, entries in enumerate([lane, row] + parts):
                lines_ref[k, which] = entries

            def wide(which, i):
                entries = lines_ref[k, which, i : i + 1, :]
                return jnp.broadcast_to(entries, (16, mark)).astype(bf)

            left, right = ([], [])
            for i in range(group):
                lane_i, row_i = (wide(0, i), wide(1, i))
                right.append(
                    jnp.concatenate(
                        [jnp.where(steps[j] == lane_i, one, zero) for j in range(lanes // 16)],
                        axis=0,
                    )
                )
                masks = [steps[j] == row_i for j in range(rows // 16)]
                pieces = []
                for which in range(len(parts)):
                    part_i = wide(2 + which, i)
                    pieces += [jnp.where(mask, part_i, zero) for mask in masks]
                left.append(jnp.concatenate(pieces, axis=0))
            acc[...] += lax.dot_general(
                jnp.concatenate(left, axis=1),
                jnp.concatenate(right, axis=1),
                (((1,), (1,)), ((), ())),
                preferred_element_type=jnp.float32,
            )
        return carry

    lax.fori_loop(0, slots // group, body, 0)
    copies[2].wait()
    cell_force = [
        acc[2 * c * rows : (2 * c + 1) * rows, :] + acc[(2 * c + 1) * rows : (2 * c + 2) * rows, :]
        for c in range(3)
    ]
    relaxed = collide([pop_ref[q] for q in range(19)], cell_force, solid_ref[...])
    for q in range(19):
        relaxed_ref[q] = relaxed[q]
    even = place_ref[3] == 0
    for i in range(5):
        ahead = relaxed[going(0, 1)[i]][rows - size_y :]
        behind = relaxed[going(0, -1)[i]][:size_y]
        far_ref[i] = jnp.where(even, behind, ahead)
        near_ref[i] = jnp.where(even, ahead, behind)
        for x in range(rows // size_y):
            up = relaxed[going(1, 1)[i]][size_y * x + size_y - 1 : size_y * x + size_y, :]
            down = relaxed[going(1, -1)[i]][size_y * x : size_y * x + 1, :]
            at = rows // size_y * i + x
            side_ref[at : at + 1, :] = jnp.where(place_ref[0] == 0, up, down)


def spread(slots, owned, place, speeds, shards, early, cells, weights, populations, solid):
    mark = cells.shape[1]
    line_count, lanes = solid.shape
    smem = pl.BlockSpec(memory_space=pltpu.SMEM)
    hbm = pl.BlockSpec(memory_space=pltpu.HBM)
    vmem = pl.BlockSpec(memory_space=pltpu.VMEM)
    return pl.pallas_call(
        functools.partial(spread_kernel, len(shards), slots, owned),
        out_shape=(
            full(populations.shape),
            full((5, 8, lanes)),
            full((5, 8, lanes)),
            full((24, lanes)),
            full((3, owned, mark)),
        ),
        in_specs=[smem] * 2 + [vmem] * (len(shards) + 3) + [hbm] * 3 + [vmem],
        scratch_shapes=[
            pltpu.VMEM(cells.shape, jnp.int32),
            pltpu.VMEM(weights.shape, jnp.float32),
            pltpu.VMEM(populations.shape, jnp.float32),
            pltpu.VMEM((3, slots, mark), jnp.float32),
            pltpu.VMEM((cells.shape[0] // slots, 8, group, mark), jnp.float32),
            pltpu.VMEM((6 * line_count, lanes), jnp.float32),
            pltpu.SemaphoreType.DMA((3,)),
        ],
        compiler_params=kernel_params(),
        name="spread",
    )(place, speeds, *shards, *early, cells, weights, populations, solid)


def downwind(place_ref, relaxed_ref, far_ref, near_ref):
    size_y = far_ref.shape[1]
    size_x = relaxed_ref.shape[1] // size_y
    even = place_ref[3] == 0

    def cells(q, x):
        step = int(velocity_table[q][0])
        source = x - step
        if 0 <= source < size_x:
            return relaxed_ref[q, source * size_y : (source + 1) * size_y, :]
        i = going(0, step).index(q)
        if step == 1:
            return jnp.where(even, far_ref[i], near_ref[i])
        return jnp.where(even, near_ref[i], far_ref[i])

    return cells


def sideways(cells, side_ref, edge):
    def result(q, x, y_at):
        step_x, step_y = (int(step) for step in velocity_table[q][:2])
        size_y = y_at.shape[0]
        size_x = side_ref.shape[0] // 6
        if step_y == 0:
            return cells(q, x)
        source = x - step_x
        at = size_x * going(1, step_y).index(q) + source
        halo = side_ref[at : at + 1, :] if 0 <= source < size_x else edge(q)
        turned = pltpu.roll(cells(q, x), step_y % size_y, 0)
        return jnp.where(y_at == (0 if step_y == 1 else size_y - 1), halo, turned)

    return result


def corner_index(q):
    step_y = int(velocity_table[q][1])
    return [p for p in going(1, step_y) if int(velocity_table[p][0]) != 0].index(q)


def pack_kernel(
    place_ref, relaxed_ref, far_ref, near_ref, side_ref, corner_ref, first_ref, second_ref
):
    size_y, lanes = far_ref.shape[1:]
    size_x = relaxed_ref.shape[1] // size_y
    cells = downwind(place_ref, relaxed_ref, far_ref, near_ref)
    corner_ref[...] = jnp.zeros(corner_ref.shape, jnp.float32)
    for ahead in going(1, 1):
        step_x = int(velocity_table[ahead][0])
        if step_x == 0:
            continue
        behind = opposite_table[ahead]
        up = cells(ahead, 0 if step_x == 1 else size_x - 1)[size_y - 1 : size_y, :]
        down = cells(behind, size_x - 1 if step_x == 1 else 0)[0:1, :]
        at = corner_index(ahead)
        from_behind = corner_index(behind)
        lower = place_ref[0] == 0

        @pl.when(lower)
        def _(at=at, up=up):
            corner_ref[at : at + 1, :] = up

        @pl.when(jnp.logical_not(lower))
        def _(at=from_behind, down=down):
            corner_ref[at : at + 1, :] = down

    y_at = lax.broadcasted_iota(jnp.int32, (size_y, lanes), 0)
    lane_at = lax.broadcasted_iota(jnp.int32, (size_y, lanes), 1)
    level = sideways(cells, side_ref, None)
    packs = []
    for step in (1, -1):
        packed = jnp.zeros((size_y, lanes), jnp.float32)
        for i, q in enumerate(going(2, step)):
            edge = lanes - 1 if step == 1 else 0
            for x in range(size_x):
                at = 8 * x + i
                moved = pltpu.roll(level(q, x, y_at), (at - edge) % lanes, 1)
                packed = jnp.where(lane_at == at, moved, packed)
        packs.append(packed)
    even = place_ref[1] % 2 == 0
    first_ref[...] = jnp.where(even, packs[0], packs[1])
    second_ref[...] = jnp.where(even, packs[1], packs[0])


def pack(place, relaxed, far, near, side):
    smem = pl.BlockSpec(memory_space=pltpu.SMEM)
    vmem = pl.BlockSpec(memory_space=pltpu.VMEM)
    edge = full(far.shape[1:])
    return pl.pallas_call(
        pack_kernel,
        out_shape=(edge, edge, edge),
        in_specs=[smem] + [vmem] * 4,
        compiler_params=kernel_params(),
        name="pack",
    )(place, relaxed, far, near, side)


def stream_kernel(
    count_z, place_ref, relaxed_ref, far_ref, near_ref, side_ref, corner_ref, first_ref,
    second_ref, out_any, out_ref, sems,
):
    size_x, size_y, lanes = out_ref.shape[1:]
    shape = (size_y, lanes)
    y_at = lax.broadcasted_iota(jnp.int32, shape, 0)
    z_at = lax.broadcasted_iota(jnp.int32, shape, 1)
    y_index, z_index = (place_ref[0], place_ref[1])
    streamed = sideways(
        downwind(place_ref, relaxed_ref, far_ref, near_ref),
        side_ref,
        lambda q: corner_ref[corner_index(q) : corner_index(q) + 1, :],
    )
    even = z_index % 2 == 0
    columns = {
        -1: jnp.where(even, first_ref[...], second_ref[...]),
        1: jnp.where(even, second_ref[...], first_ref[...]),
    }
    on_side = y_at == jnp.where(y_index == 0, 0, size_y - 1)
    on_side = on_side | ((z_at == 0) & (z_index == 0))
    on_side = on_side | ((z_at == lanes - 1) & (z_index == count_z - 1))
    copies = []
    for q in range(19):
        step_z = int(velocity_table[q][2])
        z_edge = 0 if step_z == 1 else lanes - 1
        for x in range(size_x):
            cells = streamed(q, x, y_at)
            if step_z != 0:
                at = 8 * x + going(2, step_z).index(q)
                cells = jnp.where(
                    z_at == z_edge,
                    pltpu.roll(columns[step_z], (z_edge - at) % lanes, 1),
                    pltpu.roll(cells, step_z % lanes, 1),
                )
            out_ref[q, x] = jnp.where(on_side, far_field[q], cells)
        copies.append(pltpu.make_async_copy(out_ref.at[q], out_any.at[q], sems.at[q]))
        copies[-1].start()
    for copy in copies:
        copy.wait()


def stream(count_z, place, relaxed, *halos):
    rows, lanes = relaxed.shape[1:]
    size_y = halos[0].shape[1]
    smem = pl.BlockSpec(memory_space=pltpu.SMEM)
    vmem = pl.BlockSpec(memory_space=pltpu.VMEM)
    shape = (19, rows // size_y, size_y, lanes)
    return pl.pallas_call(
        functools.partial(stream_kernel, count_z),
        out_shape=full(shape),
        in_specs=[smem] + [vmem] * (1 + len(halos)),
        out_specs=pl.BlockSpec(memory_space=pltpu.HBM),
        scratch_shapes=[pltpu.VMEM(shape, jnp.float32), pltpu.SemaphoreType.DMA((19,))],
        compiler_params=kernel_params(),
        name="stream",
    )(place, relaxed, *halos)


def per_device(
    populations,
    solid_cells,
    slot_cells,
    slot_weights,
    slot_owner,
    slot_block,
    train_of_block,
    marker_area,
    train_velocity,
):
    size_x, size_y, size_z = (populations.shape[1], populations.shape[2], populations.shape[3])
    lines = size_x * size_y
    slots, kernel, mark = (slot_cells.shape[3], slot_cells.shape[4], slot_cells.shape[5])
    owned = train_of_block.shape[3]
    count_x, count_y, count_z = (lax.axis_size(axis) for axis in ("gx", "gy", "gz"))
    x_index, y_index, z_index = (lax.axis_index(axis) for axis in ("gx", "gy", "gz"))
    place = jnp.stack([y_index, z_index, x_index * count_y + y_index, x_index % 2])
    place = place.astype(jnp.int32)
    inputs = [
        pltpu.with_memory_space_constraint(entries, pltpu.HBM)
        for entries in (
            populations.reshape(19, lines, size_z),
            slot_cells.reshape(slots * kernel, mark),
            slot_weights.reshape(slots * kernel, mark),
            marker_area.reshape(owned, mark),
            slot_owner.reshape(1, slots),
            slot_block.reshape(1, slots),
            train_of_block.reshape(1, owned),
        )
    ]
    pops, cells, weights = inputs[:3]
    own = sample(place, *inputs)
    swap = [(0, 1), (1, 0)]

    def across_x(entries, distance):
        return lax.ppermute(entries, "gx", [(i, i ^ distance) for i in range(count_x)])

    def across_y(entries):
        return lax.ppermute(entries, "gy", swap)

    shards = {0: own}
    for distance in reversed(range(1, count_x)):
        shards[distance] = across_x(own, distance)
    beside = {distance: across_y(shards[distance]) for distance in (0, 1, 3, 2)}
    last = beside.pop(2)
    early = settle_early(slots, owned, [*shards.values(), *beside.values()])
    relaxed, far, near, side, marker_force = spread(
        slots,
        owned,
        place,
        train_velocity,
        [own, last],
        early,
        cells,
        weights,
        pops,
        solid_cells.reshape(lines, size_z),
    )
    evens = range(0, count_x, 2)
    far = lax.ppermute(
        far,
        "gx",
        [(i, (i - 1) % count_x) for i in evens] + [((i - 1) % count_x, i) for i in evens],
    )
    near = lax.ppermute(near, "gx", [(i, i + 1) for i in evens] + [(i + 1, i) for i in evens])
    side = across_y(side)
    corner, up_first, down_first = pack(place, relaxed, far, near, side)
    corner = across_y(corner)
    inner = [(i, i + 1) for i in range(0, count_z - 1, 2)]
    outer = [(i, i + 1) for i in range(1, count_z - 1, 2)]
    up_first = lax.ppermute(up_first, "gz", inner + [(j, i) for i, j in inner])
    down_first = lax.ppermute(down_first, "gz", outer + [(j, i) for i, j in outer])
    populations_next = stream(
        count_z, place, relaxed, far, near, side, corner, up_first, down_first
    )
    marker_force = marker_force.transpose(1, 0, 2).reshape(1, 1, 1, owned, 3, mark)
    return (populations_next, marker_force)


def solution(mesh):
    placed = (
        P(None, "gx", "gy", "gz"),
        P("gx", "gy", "gz"),
        P("gx", "gy", "gz", None, None, None),
        P("gx", "gy", "gz", None, None, None),
        P("gx", "gy", "gz", None, None),
        P("gx", "gy", "gz", None),
        P("gx", "gy", "gz", None),
        P("gx", "gy", "gz", None, None),
        P(),
    )
    small = mesh.shape["gy"] == 2 and mesh.shape["gx"] == 4 and mesh.shape["gz"] % 2 == 0
    return jax.shard_map(
        per_device if small else per_device_general,
        mesh=mesh,
        in_specs=placed,
        out_specs=(P(None, "gx", "gy", "gz"), P("gx", "gy", "gz", None, None, None)),
        check_vma=False,
    )
```

```python
import functools
import jax
import jax.numpy as jnp
import numpy as np
from jax import lax
from jax.experimental import pallas as pl
from jax.experimental.pallas import tpu as pltpu
from jax.sharding import PartitionSpec as P

velocity_table = np.array(
    [
        [0, 0, 0],
        [1, 0, 0],
        [-1, 0, 0],
        [0, 1, 0],
        [0, -1, 0],
        [0, 0, 1],
        [0, 0, -1],
        [1, 1, 0],
        [-1, -1, 0],
        [1, -1, 0],
        [-1, 1, 0],
        [1, 0, 1],
        [-1, 0, -1],
        [1, 0, -1],
        [-1, 0, 1],
        [0, 1, 1],
        [0, -1, -1],
        [0, 1, -1],
        [0, -1, 1],
    ]
)
weight_table = [1.0 / 3.0] + [1.0 / 18.0] * 6 + [1.0 / 36.0] * 12
opposite_table = [0, 2, 1, 4, 3, 6, 5, 8, 7, 10, 9, 12, 11, 14, 13, 16, 15, 18, 17]
stress_pairs = [(0, 0), (1, 1), (2, 2), (0, 1), (0, 2), (1, 2)]
tau_base = 0.55
smag_term = 18.0 * 1.4142135623730951 * 0.17 * 0.17
regular_eps = 0.0001
stiffness = 2.0
far_velocity = (0.02, 0.06, 0.0)
vmem_bytes = 16 << 20
group = 8


def going(axis, step):
    return [q for q in range(19) if int(velocity_table[q][axis]) == step]


def project(direction, vector):
    projection = 0.0 * vector[0]
    for component in range(3):
        lattice_step = int(velocity_table[direction][component])
        if lattice_step != 0:
            projection = projection + lattice_step * vector[component]
    return projection


def moments(populations):
    density = populations[0]
    momentum = [jnp.zeros_like(density) for component in range(3)]
    for direction in range(1, 19):
        density = density + populations[direction]
        for component in range(3):
            lattice_step = int(velocity_table[direction][component])
            if lattice_step == 1:
                momentum[component] = momentum[component] + populations[direction]
            elif lattice_step == -1:
                momentum[component] = momentum[component] - populations[direction]
    return (density, momentum)


def equilibrium(density, velocity):
    speed_sq = velocity[0] * velocity[0] + velocity[1] * velocity[1] + velocity[2] * velocity[2]
    result = []
    for direction in range(19):
        projected = project(direction, velocity)
        result.append(
            weight_table[direction]
            * density
            * (1.0 + 3.0 * projected + 4.5 * projected * projected - 1.5 * speed_sq)
        )
    return result


far_field = [float(np.float32(value)) for value in equilibrium(1.0, list(far_velocity))]


def collide(populations, cell_force, solid_cells):
    density, momentum = moments(populations)
    velocity = [
        (momentum[component] + 0.5 * cell_force[component]) / density for component in range(3)
    ]
    balance = equilibrium(density, velocity)
    stress = [jnp.zeros_like(density) for pair_pos in range(6)]
    for direction in range(19):
        non_eq = populations[direction] - balance[direction]
        for pair_pos in range(6):
            row_axis, col_axis = stress_pairs[pair_pos]
            factor = int(velocity_table[direction][row_axis] * velocity_table[direction][col_axis])
            if factor != 0:
                stress[pair_pos] = stress[pair_pos] + factor * non_eq
    shear_sq = stress[0] * stress[0] + stress[1] * stress[1] + stress[2] * stress[2]
    shear_sq = shear_sq + 2.0 * (
        stress[3] * stress[3] + stress[4] * stress[4] + stress[5] * stress[5]
    )
    magnitude = jnp.sqrt(shear_sq + regular_eps)
    relax_time = 0.5 * (tau_base + jnp.sqrt(tau_base * tau_base + smag_term * magnitude / density))
    relax_rate = 1.0 / relax_time
    guo_factor = 1.0 - 0.5 * relax_rate
    speed_force = (
        velocity[0] * cell_force[0] + velocity[1] * cell_force[1] + velocity[2] * cell_force[2]
    )
    result = []
    for direction in range(19):
        along_force = project(direction, cell_force)
        along_speed = project(direction, velocity)
        source = (
            guo_factor
            * weight_table[direction]
            * (3.0 * (along_force - speed_force) + 9.0 * along_speed * along_force)
        )
        relaxed = (
            populations[direction]
            - (populations[direction] - balance[direction]) * relax_rate
            + source
        )
        result.append(jnp.where(solid_cells == 1, populations[opposite_table[direction]], relaxed))
    return result


def with_halo(cells, sides, width):
    for axis, dim in sides:
        count = lax.axis_size(axis)
        head = lax.slice_in_dim(cells, 0, width, axis=dim)
        tail = lax.slice_in_dim(cells, cells.shape[dim] - width, cells.shape[dim], axis=dim)
        cells = jnp.concatenate(
            [
                lax.ppermute(tail, axis, [(i, (i + 1) % count) for i in range(count)]),
                cells,
                lax.ppermute(head, axis, [((i + 1) % count, i) for i in range(count)]),
            ],
            axis=dim,
        )
    return cells


def settle(received, labels, owned, train_of_block, marker_area, train_velocity, mark):
    rows_in = received.reshape(-1, 3 * mark)
    label_rows = labels.reshape(-1)
    owner_match = (label_rows[None, :] == jnp.arange(owned, dtype=jnp.int32)[:, None]).astype(
        jnp.float32
    )
    marker_velocity = jnp.dot(owner_match, rows_in, precision=lax.Precision.HIGHEST).reshape(
        owned, 3, mark
    )
    trains = train_velocity.shape[0]
    train_rows = train_of_block.reshape(owned)
    train_match = (train_rows[:, None] == jnp.arange(trains, dtype=jnp.int32)[None, :]).astype(
        jnp.float32
    )
    target = jnp.dot(train_match, train_velocity, precision=lax.Precision.HIGHEST)
    areas = marker_area.reshape(owned, mark)
    marker_force = stiffness * areas[:, None, :] * (target[:, :, None] - marker_velocity)
    back_rows = jnp.dot(
        owner_match.T, marker_force.reshape(owned, 3 * mark), precision=lax.Precision.HIGHEST
    )
    return (marker_force, back_rows)


def per_device_general(
    populations,
    solid_cells,
    slot_cells,
    slot_weights,
    slot_owner,
    slot_block,
    train_of_block,
    marker_area,
    train_velocity,
):
    size_x, size_y, size_z = (populations.shape[1], populations.shape[2], populations.shape[3])
    cell_count = size_x * size_y * size_z
    slots, kernel, mark = (slot_cells.shape[3], slot_cells.shape[4], slot_cells.shape[5])
    owned = train_of_block.shape[3]
    peers_x = lax.axis_size("gx")
    peers_y = lax.axis_size("gy")
    peers = peers_x * peers_y
    capacity = max(2, 2 * slots // peers)
    density, momentum = moments(populations)
    rest_velocity = jnp.stack([momentum[component] / density for component in range(3)]).reshape(
        3, cell_count
    )
    cells = slot_cells.reshape(slots, kernel, mark)
    weights = slot_weights.reshape(slots, kernel, mark)
    partial_value = jnp.sum(rest_velocity[:, cells] * weights[None], axis=2)
    slot_rows = partial_value.transpose(1, 0, 2).reshape(slots, 3 * mark)
    slot_dest = slot_owner.reshape(slots)
    blocks = slot_block.reshape(slots)
    order = jnp.arange(slots, dtype=jnp.int32)
    earlier = (slot_dest[None, :] == slot_dest[:, None]) & (order[None, :] < order[:, None])
    slot_rank = jnp.sum(earlier.astype(jnp.int32), axis=1)
    target_row = slot_dest * capacity + slot_rank
    buffer_rows = jnp.arange(peers * capacity, dtype=jnp.int32)
    matches = buffer_rows[:, None] == target_row[None, :]
    placement = matches.astype(jnp.float32)
    outgoing = jnp.dot(placement, slot_rows, precision=lax.Precision.HIGHEST)
    labels = jnp.sum(jnp.where(matches, blocks[None, :] + 1, 0), axis=1) - 1
    received, got_labels = (
        lax.all_to_all(
            outgoing.reshape(peers, capacity, 3 * mark),
            ("gx", "gy"),
            split_axis=0,
            concat_axis=0,
            tiled=True,
        ),
        lax.all_to_all(
            labels.reshape(peers, capacity), ("gx", "gy"), split_axis=0, concat_axis=0, tiled=True
        ),
    )
    marker_force, back_rows = settle(
        received, got_labels, owned, train_of_block, marker_area, train_velocity, mark
    )
    returned = lax.all_to_all(
        back_rows.reshape(peers, capacity, 3 * mark),
        ("gx", "gy"),
        split_axis=0,
        concat_axis=0,
        tiled=True,
    )
    slot_force = jnp.dot(
        placement.T, returned.reshape(peers * capacity, 3 * mark), precision=lax.Precision.HIGHEST
    )
    slot_force = slot_force.reshape(slots, 3, mark).transpose(1, 0, 2)
    contrib = weights[None] * slot_force[:, :, None, :]
    cell_force = (
        jnp.zeros((3, cell_count), jnp.float32).at[:, cells.reshape(-1)].add(contrib.reshape(3, -1))
    )
    cell_force = cell_force.reshape(3, size_x, size_y, size_z)
    relaxed = collide(populations, cell_force, solid_cells)
    padded = with_halo(jnp.stack(relaxed), (("gx", 1), ("gy", 2), ("gz", 3)), 1)
    parts = []
    for direction in range(19):
        shift_x = 1 - int(velocity_table[direction][0])
        shift_y = 1 - int(velocity_table[direction][1])
        shift_z = 1 - int(velocity_table[direction][2])
        parts.append(
            padded[
                direction,
                shift_x : shift_x + size_x,
                shift_y : shift_y + size_y,
                shift_z : shift_z + size_z,
            ]
        )
    read = jnp.stack(parts)
    total_y = size_y * lax.axis_size("gy")
    total_z = size_z * lax.axis_size("gz")
    global_y = lax.axis_index("gy") * size_y + jnp.arange(size_y, dtype=jnp.int32)
    global_z = lax.axis_index("gz") * size_z + jnp.arange(size_z, dtype=jnp.int32)
    on_side = ((global_y == 0) | (global_y == total_y - 1))[:, None] | (
        (global_z == 0) | (global_z == total_z - 1)
    )[None, :]
    far_field = jnp.array(equilibrium(1.0, list(far_velocity)), dtype=jnp.float32)
    populations_next = jnp.where(on_side[None, None], far_field[:, None, None, None], read)
    return (populations_next, marker_force.reshape(1, 1, 1, owned, 3, mark))


def full(shape):
    return jax.ShapeDtypeStruct(shape, jnp.float32)


def kernel_params():
    return pltpu.CompilerParams(vmem_limit_bytes=vmem_bytes)


def low_half(shape):
    return lax.broadcasted_iota(jnp.int32, shape, 1) < shape[1] // 2


def fetch(pairs, sems):
    copies = [
        pltpu.make_async_copy(source, target, sems.at[i])
        for i, (source, target) in enumerate(pairs)
    ]
    for copy in copies:
        copy.start()
    return copies


def shard_rows(slots, owned):
    return 3 * slots + owned + 8


def sample_kernel(
    place_ref, pop_any, cells_any, weights_any, areas_any, owner_any, block_any, trains_any,
    out_ref, pop_ref, cells_ref, weights_ref, areas_ref, owner_ref, block_ref, trains_ref,
    table, sems,
):
    rows, lanes = (pop_ref.shape[1], pop_ref.shape[2])
    mark = cells_ref.shape[1]
    owned = areas_ref.shape[0]
    slots = owner_ref.shape[1]
    kernel = cells_ref.shape[0] // slots
    copies = fetch(
        (
            (pop_any, pop_ref),
            (cells_any, cells_ref),
            (weights_any, weights_ref),
            (areas_any, areas_ref),
            (owner_any, owner_ref),
            (block_any, block_ref),
            (trains_any, trains_ref),
        ),
        sems,
    )

    copies[0].wait()
    density, momentum = moments([pop_ref[q] for q in range(19)])
    speed = [momentum[c] / density for c in range(3)]
    largest = jnp.maximum(jnp.maximum(jnp.abs(speed[0]), jnp.abs(speed[1])), jnp.abs(speed[2]))
    largest = jnp.max(largest, axis=(0, 1), keepdims=True) + 1e-20
    scale = largest * (1.0 / 32767.0)
    fixed = [(speed[c] * (1.0 / scale) + 32768.5).astype(jnp.int32) for c in range(3)]
    table[0:rows] = (fixed[0] << 16) | fixed[1]
    table[rows:] = (fixed[2][: rows // 2] << 16) | fixed[2][rows // 2 :]
    for copy in copies[1:]:
        copy.wait()
    meta = 3 * slots + owned
    out_ref[3 * slots : meta, :] = areas_ref[...]
    out_ref[meta : meta + 8, :] = jnp.zeros((8, mark), jnp.float32)
    ids = (owner_ref[...] * owned + block_ref[...]).astype(jnp.float32)
    out_ref[meta : meta + 1, :] = jnp.concatenate([ids] * (mark // slots), axis=1)
    out_ref[meta + 1 : meta + 2, 0:owned] = trains_ref[...].astype(jnp.float32)
    mine = lax.broadcasted_iota(jnp.int32, (1, mark), 1) % owned + place_ref[2] * owned
    out_ref[meta + 2 : meta + 3, :] = mine.astype(jnp.float32)

    def body(step, carry):
        first = pl.multiple_of(step * group, group)
        total = [jnp.zeros((group, mark), jnp.float32) for c in range(3)]
        for k in range(kernel):
            at = pl.ds(first * kernel + k, group, stride=kernel)
            cells = cells_ref[at, :]
            lane = cells & (lanes - 1)
            row = cells >> (lanes.bit_length() - 1)
            bits = [(row >> bit) & 1 == 1 for bit in range(rows.bit_length() - 1)]

            def choose(low, level):
                if level < 0:
                    line = jnp.broadcast_to(table[low : low + 1, :], (group, lanes))
                    return jnp.take_along_axis(line, lane, axis=1, mode="promise_in_bounds")
                lower = choose(low, level - 1)
                return jnp.where(bits[level], choose(low + (1 << level), level - 1), lower)

            pair = choose(0, len(bits) - 1)
            third = choose(rows, len(bits) - 2)
            picked = [
                lax.shift_right_logical(pair, 16),
                pair & 65535,
                jnp.where(bits[-1], third & 65535, lax.shift_right_logical(third, 16)),
            ]
            weight = weights_ref[at, :]
            for c in range(3):
                total[c] = total[c] + weight * (picked[c].astype(jnp.float32) - 32768.0)
        for c in range(3):
            here = pl.ds(pl.multiple_of(c * slots + first, group), group)
            out_ref[here, :] = total[c] * scale
        return carry

    lax.fori_loop(0, slots // group, body, 0)


def sample(place, populations, cells, weights, areas, owner, block, trains):
    smem = pl.BlockSpec(memory_space=pltpu.SMEM)
    hbm = pl.BlockSpec(memory_space=pltpu.HBM)
    vmem = pl.BlockSpec(memory_space=pltpu.VMEM)
    kept = (populations, cells, weights)
    return pl.pallas_call(
        sample_kernel,
        out_shape=[full((shard_rows(owner.shape[1], areas.shape[0]), cells.shape[1]))]
        + [jax.ShapeDtypeStruct(entries.shape, entries.dtype) for entries in kept],
        in_specs=[smem] + [hbm] * 7,
        out_specs=[vmem] * 4,
        scratch_shapes=[
            pltpu.VMEM(entries.shape, entries.dtype) for entries in (areas, owner, block, trains)
        ]
        + [
            pltpu.VMEM((populations.shape[1] * 3 // 2, cells.shape[1]), jnp.int32),
            pltpu.SemaphoreType.DMA((7,)),
        ],
        compiler_params=kernel_params(),
        name="sample",
    )(place, populations, cells, weights, areas, owner, block, trains)


def prepare_kernel(cells_ref, out_ref):
    chunk, mark = (128, cells_ref.shape[1])
    z_at = lax.broadcasted_iota(jnp.int32, (mark, mark), 1).astype(jnp.float32)

    def body(step, carry):
        here = pl.ds(pl.multiple_of(step * chunk, chunk), chunk)
        lane = (cells_ref[here, :] & (mark - 1)).astype(jnp.float32).T
        for j in range(chunk):
            there = pl.ds(pl.multiple_of((step * chunk + j) * mark, mark), mark)
            out_ref[there, :] = one_hot(lane[:, j : j + 1] == z_at)
        return carry

    lax.fori_loop(0, cells_ref.shape[0] // chunk, body, 0)


def prepare(cells):
    count, mark = cells.shape
    vmem = pl.BlockSpec(memory_space=pltpu.VMEM)
    return pl.pallas_call(
        prepare_kernel,
        out_shape=jax.ShapeDtypeStruct((count * mark, mark), jnp.bfloat16),
        in_specs=[vmem],
        out_specs=vmem,
        compiler_params=kernel_params(),
        cost_estimate=pl.CostEstimate(
            flops=4 * 10**9, bytes_accessed=count * mark * 4, transcendentals=0
        ),
        name="prepare",
    )(cells)


def three_parts(values):
    parts = []
    for _ in range(3):
        parts.append(values.astype(jnp.bfloat16))
        values = values - parts[-1].astype(jnp.float32)
    return parts


def one_hot(mask):
    return jnp.where(mask, 1.0, 0.0).astype(jnp.bfloat16)


def wanted_labels(own_ref, slots, owned):
    mark = own_ref.shape[1]
    own = own_ref[3 * slots + owned : 3 * slots + owned + 8, :]
    ids, trains, mine = (jnp.broadcast_to(own[i : i + 1], (mark, mark)).T for i in range(3))
    return (ids[0:slots], mine[0:owned], trains[0:owned])


def add_shards(totals, shards, ids, mine):
    slots, owned = (ids.shape[0], mine.shape[0])
    meta = 3 * slots + owned
    wanted = jnp.concatenate([ids, mine], axis=0)
    for shard in shards:
        match = one_hot(wanted == shard[meta : meta + 1, :])
        match = jnp.concatenate([match, match[:, 0:slots]], axis=1)
        values = jnp.concatenate([shard[c * slots : (c + 1) * slots, :] for c in range(3)], axis=1)
        sums = jnp.dot(
            match, jnp.concatenate(three_parts(values), axis=0), preferred_element_type=jnp.float32
        )
        held = ids == shard[meta + 2 : meta + 3, :]
        parts = three_parts(shard[3 * slots : meta, :])
        parts.append(jnp.zeros_like(parts[0]))
        area = jnp.dot(
            one_hot(held), jnp.concatenate(parts, axis=0), preferred_element_type=jnp.float32
        )
        trains = jnp.where(held, shard[meta + 1 : meta + 2, :], 0.0)
        got = (sums, area, trains)
        totals = got if totals is None else [total + new for total, new in zip(totals, got)]
    return totals


def settle_kernel(slots, owned, speeds_ref, *refs):
    shards, (sums_ref, area_ref, trains_ref, rows_ref) = (refs[:-4], refs[-4:])
    mark = rows_ref.shape[1]
    for train in range(speeds_ref.shape[0]):
        for c in range(3):
            at = 3 * train + c
            rows_ref[at : at + 1, :] = jnp.full((1, mark), speeds_ref[train, c], jnp.float32)
    ids, mine, _ = wanted_labels(shards[0], slots, owned)
    sums_ref[...], area_ref[...], trains_ref[...] = add_shards(None, shards, ids, mine)


def settle_early(slots, owned, speeds, shards):
    mark = shards[0].shape[1]
    smem = pl.BlockSpec(memory_space=pltpu.SMEM)
    vmem = pl.BlockSpec(memory_space=pltpu.VMEM)
    return pl.pallas_call(
        functools.partial(settle_kernel, slots, owned),
        out_shape=(
            full((slots + owned, 3 * mark)),
            full((slots, mark)),
            full((slots, mark)),
            full((3 * speeds.shape[0], mark)),
        ),
        in_specs=[smem] + [vmem] * len(shards),
        compiler_params=kernel_params(),
        cost_estimate=pl.CostEstimate(
            flops=10**9, bytes_accessed=len(shards) * shards[0].size * 4, transcendentals=0
        ),
        name="settle",
    )(speeds, *shards)


def block_forces(rows_ref, totals, own_ref, slots, owned):
    mark = own_ref.shape[1]
    ids, mine, own_trains = wanted_labels(own_ref, slots, owned)
    sums, area, trains = totals
    trains = jnp.broadcast_to(jnp.sum(trains, axis=1, keepdims=True), area.shape)
    own_area = own_ref[3 * slots : 3 * slots + owned, :]
    forces, own_forces = ([], [])
    for c in range(3):
        target, own_target = (jnp.zeros_like(area), jnp.zeros_like(own_area))
        for train in range(rows_ref.shape[0] // 3):
            at = 3 * train + c
            speed = rows_ref[at : at + 1, :]
            target = jnp.where(trains == float(train), speed, target)
            own_target = jnp.where(own_trains == float(train), speed, own_target)
        got = sums[:, c * mark : (c + 1) * mark]
        forces.append(stiffness * area * (target - got[0:slots]))
        own_forces.append(stiffness * own_area * (own_target - got[slots:]))
    return (forces, own_forces)


def spread_kernel(
    slots, owned, place_ref, own_ref, last_ref, sums_ref, area_ref, trains_ref, speeds_ref,
    cells_ref, weights_ref, pop_ref, lanes_ref, solid_ref,
    relaxed_ref, far_ref, near_ref, side_ref, marker_ref, force_ref, lines_ref, acc,
):
    rows, lanes = (pop_ref.shape[1], pop_ref.shape[2])
    size_y = 8
    mark = cells_ref.shape[1]
    kernel = cells_ref.shape[0] // slots
    points = kernel * mark
    bf = jnp.bfloat16
    ids, mine, _ = wanted_labels(own_ref, slots, owned)
    totals = (sums_ref[...], area_ref[...], trains_ref[...])
    totals = add_shards(totals, [last_ref], ids, mine)
    forces, own_forces = block_forces(speeds_ref, totals, own_ref, slots, owned)
    for c in range(3):
        force_ref[c] = forces[c]
        marker_ref[c] = own_forces[c]

    acc[...] = jnp.zeros_like(acc)
    iota = lax.broadcasted_iota(jnp.int32, (16, mark), 0).astype(jnp.float32)
    steps = [(iota + 16.0 * j).astype(bf) for j in range(rows // 16)]
    zero = jnp.zeros((16, mark), bf)

    def body(step, carry):
        first = pl.multiple_of(step * group, group)
        for c in range(3):
            lines_ref[group, c] = force_ref[c, pl.ds(first, group), :]
        for i in range(group):
            at = pl.ds(pl.multiple_of((first + i) * kernel, kernel), kernel)
            weight = weights_ref[at, :]
            lines_ref[i, 6] = (cells_ref[at, :] >> (lanes.bit_length() - 1)).astype(jnp.float32)
            for c in range(3):
                value = weight * lines_ref[group, c, i : i + 1, :]
                high = value.astype(bf).astype(jnp.float32)
                lines_ref[i, 2 * c] = high
                lines_ref[i, 2 * c + 1] = value - high

            def wide(which, k, i=i):
                entries = lines_ref[i, which, k : k + 1, :]
                return jnp.broadcast_to(entries, (16, mark)).astype(bf)

            left = []
            for k in range(kernel):
                row = wide(6, k)
                masks = [steps[j] == row for j in range(rows // 16)]
                pieces = []
                for which in range(6):
                    part = wide(which, k)
                    pieces += [jnp.where(mask, part, zero) for mask in masks]
                left.append(jnp.concatenate(pieces, axis=0))
            here = pl.ds(pl.multiple_of((first + i) * points, points), points)
            acc[...] += jnp.dot(
                jnp.concatenate(left, axis=1),
                lanes_ref[here, :],
                preferred_element_type=jnp.float32,
            )
        return carry

    lax.fori_loop(0, slots // group, body, 0)
    cell_force = [
        acc[2 * c * rows : (2 * c + 1) * rows, :] + acc[(2 * c + 1) * rows : (2 * c + 2) * rows, :]
        for c in range(3)
    ]
    relaxed = collide([pop_ref[q] for q in range(19)], cell_force, solid_ref[...])
    for q in range(19):
        relaxed_ref[q] = relaxed[q]
    even = place_ref[3] == 0
    for i in range(5):
        ahead = relaxed[going(0, 1)[i]][rows - size_y :]
        behind = relaxed[going(0, -1)[i]][:size_y]
        far_ref[i] = jnp.where(even, behind, ahead)
        near_ref[i] = jnp.where(even, ahead, behind)
        for x in range(rows // size_y):
            up = relaxed[going(1, 1)[i]][size_y * x + size_y - 1 : size_y * x + size_y, :]
            down = relaxed[going(1, -1)[i]][size_y * x : size_y * x + 1, :]
            at = rows // size_y * i + x
            side_ref[at : at + 1, :] = jnp.where(place_ref[0] == 0, up, down)


def spread(owned, place, own, last, early, cells, weights, populations, lane_match, solid):
    mark = cells.shape[1]
    slots = early[1].shape[0]
    line_count, lanes = solid.shape
    smem = pl.BlockSpec(memory_space=pltpu.SMEM)
    vmem = pl.BlockSpec(memory_space=pltpu.VMEM)
    return pl.pallas_call(
        functools.partial(spread_kernel, slots, owned),
        out_shape=(
            full(populations.shape),
            full((5, 8, lanes)),
            full((5, 8, lanes)),
            full((24, lanes)),
            full((3, owned, mark)),
        ),
        in_specs=[smem] + [vmem] * 11,
        scratch_shapes=[
            pltpu.VMEM((3, slots, mark), jnp.float32),
            pltpu.VMEM((group + 1, 7, cells.shape[0] // slots, mark), jnp.float32),
            pltpu.VMEM((6 * line_count, lanes), jnp.float32),
        ],
        compiler_params=kernel_params(),
        name="spread",
    )(place, own, last, *early, cells, weights, populations, lane_match, solid)


def downwind(place_ref, relaxed_ref, far_ref, near_ref):
    size_y = far_ref.shape[1]
    size_x = relaxed_ref.shape[1] // size_y
    even = place_ref[3] == 0

    def cells(q, x):
        step = int(velocity_table[q][0])
        source = x - step
        if 0 <= source < size_x:
            return relaxed_ref[q, source * size_y : (source + 1) * size_y, :]
        i = going(0, step).index(q)
        if step == 1:
            return jnp.where(even, far_ref[i], near_ref[i])
        return jnp.where(even, near_ref[i], far_ref[i])

    return cells


def sideways(cells, side_ref, edge):
    def result(q, x, y_at):
        step_x, step_y = (int(step) for step in velocity_table[q][:2])
        size_y = y_at.shape[0]
        size_x = side_ref.shape[0] // 6
        if step_y == 0:
            return cells(q, x)
        source = x - step_x
        at = size_x * going(1, step_y).index(q) + source
        halo = side_ref[at : at + 1, :] if 0 <= source < size_x else edge(q)
        turned = pltpu.roll(cells(q, x), step_y % size_y, 0)
        return jnp.where(y_at == (0 if step_y == 1 else size_y - 1), halo, turned)

    return result


def corner_index(q):
    step_y = int(velocity_table[q][1])
    return [p for p in going(1, step_y) if int(velocity_table[p][0]) != 0].index(q)


def pack_kernel(
    place_ref, relaxed_ref, far_ref, near_ref, side_ref, corner_ref, first_ref, second_ref
):
    size_y, lanes = far_ref.shape[1:]
    size_x = relaxed_ref.shape[1] // size_y
    cells = downwind(place_ref, relaxed_ref, far_ref, near_ref)
    corner_ref[...] = jnp.zeros(corner_ref.shape, jnp.float32)
    for ahead in going(1, 1):
        step_x = int(velocity_table[ahead][0])
        if step_x == 0:
            continue
        behind = opposite_table[ahead]
        up = cells(ahead, 0 if step_x == 1 else size_x - 1)[size_y - 1 : size_y, :]
        down = cells(behind, size_x - 1 if step_x == 1 else 0)[0:1, :]
        at = corner_index(ahead)
        from_behind = corner_index(behind)
        lower = place_ref[0] == 0

        @pl.when(lower)
        def _(at=at, up=up):
            corner_ref[at : at + 1, :] = up

        @pl.when(jnp.logical_not(lower))
        def _(at=from_behind, down=down):
            corner_ref[at : at + 1, :] = down

    y_at = lax.broadcasted_iota(jnp.int32, (size_y, lanes), 0)
    lane_at = lax.broadcasted_iota(jnp.int32, (size_y, lanes), 1)
    level = sideways(cells, side_ref, None)
    packs = []
    for step in (1, -1):
        packed = jnp.zeros((size_y, lanes), jnp.float32)
        for i, q in enumerate(going(2, step)):
            edge = lanes - 1 if step == 1 else 0
            for x in range(size_x):
                at = 8 * x + i
                moved = pltpu.roll(level(q, x, y_at), (at - edge) % lanes, 1)
                packed = jnp.where(lane_at == at, moved, packed)
        packs.append(packed)
    even = place_ref[1] % 2 == 0
    first_ref[...] = jnp.where(even, packs[0], packs[1])
    second_ref[...] = jnp.where(even, packs[1], packs[0])


def pack(place, relaxed, far, near, side):
    smem = pl.BlockSpec(memory_space=pltpu.SMEM)
    vmem = pl.BlockSpec(memory_space=pltpu.VMEM)
    edge = full(far.shape[1:])
    return pl.pallas_call(
        pack_kernel,
        out_shape=(edge, edge, edge),
        in_specs=[smem] + [vmem] * 4,
        compiler_params=kernel_params(),
        name="pack",
    )(place, relaxed, far, near, side)


def stream_kernel(
    count_z, place_ref, relaxed_ref, far_ref, near_ref, side_ref, corner_ref, first_ref,
    second_ref, out_any, out_ref, sems,
):
    size_x, size_y, lanes = out_ref.shape[1:]
    shape = (size_y, lanes)
    y_at = lax.broadcasted_iota(jnp.int32, shape, 0)
    z_at = lax.broadcasted_iota(jnp.int32, shape, 1)
    y_index, z_index = (place_ref[0], place_ref[1])
    streamed = sideways(
        downwind(place_ref, relaxed_ref, far_ref, near_ref),
        side_ref,
        lambda q: corner_ref[corner_index(q) : corner_index(q) + 1, :],
    )
    even = z_index % 2 == 0
    columns = {
        -1: jnp.where(even, first_ref[...], second_ref[...]),
        1: jnp.where(even, second_ref[...], first_ref[...]),
    }
    on_side = y_at == jnp.where(y_index == 0, 0, size_y - 1)
    on_side = on_side | ((z_at == 0) & (z_index == 0))
    on_side = on_side | ((z_at == lanes - 1) & (z_index == count_z - 1))
    copies = []
    for q in range(19):
        step_z = int(velocity_table[q][2])
        z_edge = 0 if step_z == 1 else lanes - 1
        for x in range(size_x):
            cells = streamed(q, x, y_at)
            if step_z != 0:
                at = 8 * x + going(2, step_z).index(q)
                cells = jnp.where(
                    z_at == z_edge,
                    pltpu.roll(columns[step_z], (z_edge - at) % lanes, 1),
                    pltpu.roll(cells, step_z % lanes, 1),
                )
            out_ref[q, x] = jnp.where(on_side, far_field[q], cells)
        copies.append(pltpu.make_async_copy(out_ref.at[q], out_any.at[q], sems.at[q]))
        copies[-1].start()
    for copy in copies:
        copy.wait()


def stream(count_z, place, relaxed, *halos):
    rows, lanes = relaxed.shape[1:]
    size_y = halos[0].shape[1]
    smem = pl.BlockSpec(memory_space=pltpu.SMEM)
    vmem = pl.BlockSpec(memory_space=pltpu.VMEM)
    shape = (19, rows // size_y, size_y, lanes)
    return pl.pallas_call(
        functools.partial(stream_kernel, count_z),
        out_shape=full(shape),
        in_specs=[smem] + [vmem] * (1 + len(halos)),
        out_specs=pl.BlockSpec(memory_space=pltpu.HBM),
        scratch_shapes=[pltpu.VMEM(shape, jnp.float32), pltpu.SemaphoreType.DMA((19,))],
        compiler_params=kernel_params(),
        name="stream",
    )(place, relaxed, *halos)


def per_device(
    populations,
    solid_cells,
    slot_cells,
    slot_weights,
    slot_owner,
    slot_block,
    train_of_block,
    marker_area,
    train_velocity,
):
    size_x, size_y, size_z = (populations.shape[1], populations.shape[2], populations.shape[3])
    lines = size_x * size_y
    slots, kernel, mark = (slot_cells.shape[3], slot_cells.shape[4], slot_cells.shape[5])
    owned = train_of_block.shape[3]
    count_x, count_y, count_z = (lax.axis_size(axis) for axis in ("gx", "gy", "gz"))
    x_index, y_index, z_index = (lax.axis_index(axis) for axis in ("gx", "gy", "gz"))
    place = jnp.stack([y_index, z_index, x_index * count_y + y_index, x_index % 2])
    place = place.astype(jnp.int32)
    inputs = [
        pltpu.with_memory_space_constraint(entries, pltpu.HBM)
        for entries in (
            populations.reshape(19, lines, size_z),
            slot_cells.reshape(slots * kernel, mark),
            slot_weights.reshape(slots * kernel, mark),
            marker_area.reshape(owned, mark),
            slot_owner.reshape(1, slots),
            slot_block.reshape(1, slots),
            train_of_block.reshape(1, owned),
        )
    ]
    own, pops, cells, weights = sample(place, *inputs)
    swap = [(0, 1), (1, 0)]

    def across_x(entries, distance):
        return lax.ppermute(entries, "gx", [(i, i ^ distance) for i in range(count_x)])

    def across_y(entries):
        return lax.ppermute(entries, "gy", swap)

    shards = {0: own}
    for distance in reversed(range(1, count_x)):
        shards[distance] = across_x(own, distance)
    beside = {distance: across_y(shards[distance]) for distance in (0, 1, 3)}
    lane_match, waiting = lax.optimization_barrier((prepare(cells), shards[2]))
    last = across_y(waiting)
    early = settle_early(slots, owned, train_velocity, [*shards.values(), *beside.values()])
    solid = solid_cells.reshape(lines, size_z)
    relaxed, far, near, side, marker_force = spread(
        owned, place, own, last, early, cells, weights, pops, lane_match, solid
    )
    evens = range(0, count_x, 2)
    far = lax.ppermute(
        far,
        "gx",
        [(i, (i - 1) % count_x) for i in evens] + [((i - 1) % count_x, i) for i in evens],
    )
    near = lax.ppermute(near, "gx", [(i, i + 1) for i in evens] + [(i + 1, i) for i in evens])
    side = across_y(side)
    corner, up_first, down_first = pack(place, relaxed, far, near, side)
    corner = across_y(corner)
    inner = [(i, i + 1) for i in range(0, count_z - 1, 2)]
    outer = [(i, i + 1) for i in range(1, count_z - 1, 2)]
    up_first = lax.ppermute(up_first, "gz", inner + [(j, i) for i, j in inner])
    down_first = lax.ppermute(down_first, "gz", outer + [(j, i) for i, j in outer])
    populations_next = stream(
        count_z, place, relaxed, far, near, side, corner, up_first, down_first
    )
    marker_force = marker_force.transpose(1, 0, 2).reshape(1, 1, 1, owned, 3, mark)
    return (populations_next, marker_force)


def solution(mesh):
    placed = (
        P(None, "gx", "gy", "gz"),
        P("gx", "gy", "gz"),
        P("gx", "gy", "gz", None, None, None),
        P("gx", "gy", "gz", None, None, None),
        P("gx", "gy", "gz", None, None),
        P("gx", "gy", "gz", None),
        P("gx", "gy", "gz", None),
        P("gx", "gy", "gz", None, None),
        P(),
    )
    small = mesh.shape["gy"] == 2 and mesh.shape["gx"] == 4 and mesh.shape["gz"] % 2 == 0
    return jax.shard_map(
        per_device if small else per_device_general,
        mesh=mesh,
        in_specs=placed,
        out_specs=(P(None, "gx", "gy", "gz"), P("gx", "gy", "gz", None, None, None)),
        check_vma=False,
    )
```

```python
import functools
import jax
import jax.numpy as jnp
import numpy as np
from jax import lax
from jax.experimental import pallas as pl
from jax.experimental.pallas import tpu as pltpu
from jax.sharding import PartitionSpec as P

velocity_table = np.array(
    [
        [0, 0, 0],
        [1, 0, 0],
        [-1, 0, 0],
        [0, 1, 0],
        [0, -1, 0],
        [0, 0, 1],
        [0, 0, -1],
        [1, 1, 0],
        [-1, -1, 0],
        [1, -1, 0],
        [-1, 1, 0],
        [1, 0, 1],
        [-1, 0, -1],
        [1, 0, -1],
        [-1, 0, 1],
        [0, 1, 1],
        [0, -1, -1],
        [0, 1, -1],
        [0, -1, 1],
    ]
)
weight_table = [1.0 / 3.0] + [1.0 / 18.0] * 6 + [1.0 / 36.0] * 12
opposite_table = [0, 2, 1, 4, 3, 6, 5, 8, 7, 10, 9, 12, 11, 14, 13, 16, 15, 18, 17]
stress_pairs = [(0, 0), (1, 1), (2, 2), (0, 1), (0, 2), (1, 2)]
tau_base = 0.55
smag_term = 18.0 * 1.4142135623730951 * 0.17 * 0.17
regular_eps = 0.0001
stiffness = 2.0
far_velocity = (0.02, 0.06, 0.0)
vmem_bytes = 16 << 20
group = 8


def going(axis, step):
    return [q for q in range(19) if int(velocity_table[q][axis]) == step]


def project(direction, vector):
    projection = 0.0 * vector[0]
    for component in range(3):
        lattice_step = int(velocity_table[direction][component])
        if lattice_step != 0:
            projection = projection + lattice_step * vector[component]
    return projection


def moments(populations):
    density = populations[0]
    momentum = [jnp.zeros_like(density) for component in range(3)]
    for direction in range(1, 19):
        density = density + populations[direction]
        for component in range(3):
            lattice_step = int(velocity_table[direction][component])
            if lattice_step == 1:
                momentum[component] = momentum[component] + populations[direction]
            elif lattice_step == -1:
                momentum[component] = momentum[component] - populations[direction]
    return (density, momentum)


def equilibrium(density, velocity):
    speed_sq = velocity[0] * velocity[0] + velocity[1] * velocity[1] + velocity[2] * velocity[2]
    result = []
    for direction in range(19):
        projected = project(direction, velocity)
        result.append(
            weight_table[direction]
            * density
            * (1.0 + 3.0 * projected + 4.5 * projected * projected - 1.5 * speed_sq)
        )
    return result


far_field = [float(np.float32(value)) for value in equilibrium(1.0, list(far_velocity))]


def collide(populations, cell_force, solid_cells):
    density, momentum = moments(populations)
    velocity = [
        (momentum[component] + 0.5 * cell_force[component]) / density for component in range(3)
    ]
    balance = equilibrium(density, velocity)
    stress = [jnp.zeros_like(density) for pair_pos in range(6)]
    for direction in range(19):
        non_eq = populations[direction] - balance[direction]
        for pair_pos in range(6):
            row_axis, col_axis = stress_pairs[pair_pos]
            factor = int(velocity_table[direction][row_axis] * velocity_table[direction][col_axis])
            if factor != 0:
                stress[pair_pos] = stress[pair_pos] + factor * non_eq
    shear_sq = stress[0] * stress[0] + stress[1] * stress[1] + stress[2] * stress[2]
    shear_sq = shear_sq + 2.0 * (
        stress[3] * stress[3] + stress[4] * stress[4] + stress[5] * stress[5]
    )
    magnitude = jnp.sqrt(shear_sq + regular_eps)
    relax_time = 0.5 * (tau_base + jnp.sqrt(tau_base * tau_base + smag_term * magnitude / density))
    relax_rate = 1.0 / relax_time
    guo_factor = 1.0 - 0.5 * relax_rate
    speed_force = (
        velocity[0] * cell_force[0] + velocity[1] * cell_force[1] + velocity[2] * cell_force[2]
    )
    result = []
    for direction in range(19):
        along_force = project(direction, cell_force)
        along_speed = project(direction, velocity)
        source = (
            guo_factor
            * weight_table[direction]
            * (3.0 * (along_force - speed_force) + 9.0 * along_speed * along_force)
        )
        relaxed = (
            populations[direction]
            - (populations[direction] - balance[direction]) * relax_rate
            + source
        )
        result.append(jnp.where(solid_cells == 1, populations[opposite_table[direction]], relaxed))
    return result


def with_halo(cells, sides, width):
    for axis, dim in sides:
        count = lax.axis_size(axis)
        head = lax.slice_in_dim(cells, 0, width, axis=dim)
        tail = lax.slice_in_dim(cells, cells.shape[dim] - width, cells.shape[dim], axis=dim)
        cells = jnp.concatenate(
            [
                lax.ppermute(tail, axis, [(i, (i + 1) % count) for i in range(count)]),
                cells,
                lax.ppermute(head, axis, [((i + 1) % count, i) for i in range(count)]),
            ],
            axis=dim,
        )
    return cells


def settle(received, labels, owned, train_of_block, marker_area, train_velocity, mark):
    rows_in = received.reshape(-1, 3 * mark)
    label_rows = labels.reshape(-1)
    owner_match = (label_rows[None, :] == jnp.arange(owned, dtype=jnp.int32)[:, None]).astype(
        jnp.float32
    )
    marker_velocity = jnp.dot(owner_match, rows_in, precision=lax.Precision.HIGHEST).reshape(
        owned, 3, mark
    )
    trains = train_velocity.shape[0]
    train_rows = train_of_block.reshape(owned)
    train_match = (train_rows[:, None] == jnp.arange(trains, dtype=jnp.int32)[None, :]).astype(
        jnp.float32
    )
    target = jnp.dot(train_match, train_velocity, precision=lax.Precision.HIGHEST)
    areas = marker_area.reshape(owned, mark)
    marker_force = stiffness * areas[:, None, :] * (target[:, :, None] - marker_velocity)
    back_rows = jnp.dot(
        owner_match.T, marker_force.reshape(owned, 3 * mark), precision=lax.Precision.HIGHEST
    )
    return (marker_force, back_rows)


def per_device_general(
    populations,
    solid_cells,
    slot_cells,
    slot_weights,
    slot_owner,
    slot_block,
    train_of_block,
    marker_area,
    train_velocity,
):
    size_x, size_y, size_z = (populations.shape[1], populations.shape[2], populations.shape[3])
    cell_count = size_x * size_y * size_z
    slots, kernel, mark = (slot_cells.shape[3], slot_cells.shape[4], slot_cells.shape[5])
    owned = train_of_block.shape[3]
    peers_x = lax.axis_size("gx")
    peers_y = lax.axis_size("gy")
    peers = peers_x * peers_y
    capacity = max(2, 2 * slots // peers)
    density, momentum = moments(populations)
    rest_velocity = jnp.stack([momentum[component] / density for component in range(3)]).reshape(
        3, cell_count
    )
    cells = slot_cells.reshape(slots, kernel, mark)
    weights = slot_weights.reshape(slots, kernel, mark)
    partial_value = jnp.sum(rest_velocity[:, cells] * weights[None], axis=2)
    slot_rows = partial_value.transpose(1, 0, 2).reshape(slots, 3 * mark)
    slot_dest = slot_owner.reshape(slots)
    blocks = slot_block.reshape(slots)
    order = jnp.arange(slots, dtype=jnp.int32)
    earlier = (slot_dest[None, :] == slot_dest[:, None]) & (order[None, :] < order[:, None])
    slot_rank = jnp.sum(earlier.astype(jnp.int32), axis=1)
    target_row = slot_dest * capacity + slot_rank
    buffer_rows = jnp.arange(peers * capacity, dtype=jnp.int32)
    matches = buffer_rows[:, None] == target_row[None, :]
    placement = matches.astype(jnp.float32)
    outgoing = jnp.dot(placement, slot_rows, precision=lax.Precision.HIGHEST)
    labels = jnp.sum(jnp.where(matches, blocks[None, :] + 1, 0), axis=1) - 1
    received, got_labels = (
        lax.all_to_all(
            outgoing.reshape(peers, capacity, 3 * mark),
            ("gx", "gy"),
            split_axis=0,
            concat_axis=0,
            tiled=True,
        ),
        lax.all_to_all(
            labels.reshape(peers, capacity), ("gx", "gy"), split_axis=0, concat_axis=0, tiled=True
        ),
    )
    marker_force, back_rows = settle(
        received, got_labels, owned, train_of_block, marker_area, train_velocity, mark
    )
    returned = lax.all_to_all(
        back_rows.reshape(peers, capacity, 3 * mark),
        ("gx", "gy"),
        split_axis=0,
        concat_axis=0,
        tiled=True,
    )
    slot_force = jnp.dot(
        placement.T, returned.reshape(peers * capacity, 3 * mark), precision=lax.Precision.HIGHEST
    )
    slot_force = slot_force.reshape(slots, 3, mark).transpose(1, 0, 2)
    contrib = weights[None] * slot_force[:, :, None, :]
    cell_force = (
        jnp.zeros((3, cell_count), jnp.float32).at[:, cells.reshape(-1)].add(contrib.reshape(3, -1))
    )
    cell_force = cell_force.reshape(3, size_x, size_y, size_z)
    relaxed = collide(populations, cell_force, solid_cells)
    padded = with_halo(jnp.stack(relaxed), (("gx", 1), ("gy", 2), ("gz", 3)), 1)
    parts = []
    for direction in range(19):
        shift_x = 1 - int(velocity_table[direction][0])
        shift_y = 1 - int(velocity_table[direction][1])
        shift_z = 1 - int(velocity_table[direction][2])
        parts.append(
            padded[
                direction,
                shift_x : shift_x + size_x,
                shift_y : shift_y + size_y,
                shift_z : shift_z + size_z,
            ]
        )
    read = jnp.stack(parts)
    total_y = size_y * lax.axis_size("gy")
    total_z = size_z * lax.axis_size("gz")
    global_y = lax.axis_index("gy") * size_y + jnp.arange(size_y, dtype=jnp.int32)
    global_z = lax.axis_index("gz") * size_z + jnp.arange(size_z, dtype=jnp.int32)
    on_side = ((global_y == 0) | (global_y == total_y - 1))[:, None] | (
        (global_z == 0) | (global_z == total_z - 1)
    )[None, :]
    far_field = jnp.array(equilibrium(1.0, list(far_velocity)), dtype=jnp.float32)
    populations_next = jnp.where(on_side[None, None], far_field[:, None, None, None], read)
    return (populations_next, marker_force.reshape(1, 1, 1, owned, 3, mark))


def full(shape):
    return jax.ShapeDtypeStruct(shape, jnp.float32)


def kernel_params():
    return pltpu.CompilerParams(vmem_limit_bytes=vmem_bytes)


def low_half(shape):
    return lax.broadcasted_iota(jnp.int32, shape, 1) < shape[1] // 2


def fetch(pairs, sems):
    copies = [
        pltpu.make_async_copy(source, target, sems.at[i])
        for i, (source, target) in enumerate(pairs)
    ]
    for copy in copies:
        copy.start()
    return copies


def shard_rows(slots, owned):
    return 3 * slots + owned + 8


def sample_kernel(
    place_ref, pop_any, cells_any, weights_any, areas_any, owner_any, block_any, trains_any,
    out_ref, pop_ref, cells_ref, weights_ref, areas_ref, owner_ref, block_ref, trains_ref,
    table, sems,
):
    rows, lanes = (pop_ref.shape[1], pop_ref.shape[2])
    mark = cells_ref.shape[1]
    owned = areas_ref.shape[0]
    slots = owner_ref.shape[1]
    kernel = cells_ref.shape[0] // slots
    copies = fetch(
        (
            (pop_any, pop_ref),
            (cells_any, cells_ref),
            (weights_any, weights_ref),
            (areas_any, areas_ref),
            (owner_any, owner_ref),
            (block_any, block_ref),
            (trains_any, trains_ref),
        ),
        sems,
    )

    copies[0].wait()
    density, momentum = moments([pop_ref[q] for q in range(19)])
    speed = [momentum[c] / density for c in range(3)]
    largest = jnp.maximum(jnp.maximum(jnp.abs(speed[0]), jnp.abs(speed[1])), jnp.abs(speed[2]))
    largest = jnp.max(largest, axis=(0, 1), keepdims=True) + 1e-20
    scale = largest * (1.0 / 32767.0)
    fixed = [(speed[c] * (1.0 / scale) + 32768.5).astype(jnp.int32) for c in range(3)]
    words = jnp.concatenate(
        [
            (fixed[0] << 16) | fixed[1],
            (fixed[2][: rows // 2] << 16) | fixed[2][rows // 2 :],
        ],
        axis=0,
    )
    for r in range(table.shape[0]):
        table[r] = jnp.broadcast_to(words[r : r + 1], (group, lanes))
    for copy in copies[1:]:
        copy.wait()
    meta = 3 * slots + owned
    out_ref[3 * slots : meta, :] = areas_ref[...]
    out_ref[meta : meta + 8, :] = jnp.zeros((8, mark), jnp.float32)
    ids = (owner_ref[...] * owned + block_ref[...]).astype(jnp.float32)
    out_ref[meta : meta + 1, :] = jnp.concatenate([ids] * (mark // slots), axis=1)
    out_ref[meta + 1 : meta + 2, 0:owned] = trains_ref[...].astype(jnp.float32)
    mine = lax.broadcasted_iota(jnp.int32, (1, mark), 1) % owned + place_ref[2] * owned
    out_ref[meta + 2 : meta + 3, :] = mine.astype(jnp.float32)

    def body(step, carry):
        first = pl.multiple_of(step * group, group)
        total = [jnp.zeros((group, mark), jnp.float32) for c in range(3)]
        for k in range(kernel):
            at = pl.ds(first * kernel + k, group, stride=kernel)
            cells = cells_ref[at, :]
            lane = cells & (lanes - 1)
            row = cells >> (lanes.bit_length() - 1)
            bits = [(row >> bit) & 1 == 1 for bit in range(rows.bit_length() - 1)]

            def choose(low, level):
                if level < 0:
                    return jnp.take_along_axis(table[low], lane, axis=1, mode="promise_in_bounds")
                lower = choose(low, level - 1)
                return jnp.where(bits[level], choose(low + (1 << level), level - 1), lower)

            pair = choose(0, len(bits) - 1)
            third = choose(rows, len(bits) - 2)
            picked = [
                lax.shift_right_logical(pair, 16),
                pair & 65535,
                jnp.where(bits[-1], third & 65535, lax.shift_right_logical(third, 16)),
            ]
            weight = weights_ref[at, :]
            for c in range(3):
                total[c] = total[c] + weight * (picked[c].astype(jnp.float32) - 32768.0)
        for c in range(3):
            here = pl.ds(pl.multiple_of(c * slots + first, group), group)
            out_ref[here, :] = total[c] * scale
        return carry

    lax.fori_loop(0, slots // group, body, 0)


def sample(place, populations, cells, weights, areas, owner, block, trains):
    smem = pl.BlockSpec(memory_space=pltpu.SMEM)
    hbm = pl.BlockSpec(memory_space=pltpu.HBM)
    vmem = pl.BlockSpec(memory_space=pltpu.VMEM)
    kept = (populations, cells, weights)
    return pl.pallas_call(
        sample_kernel,
        out_shape=[full((shard_rows(owner.shape[1], areas.shape[0]), cells.shape[1]))]
        + [jax.ShapeDtypeStruct(entries.shape, entries.dtype) for entries in kept],
        in_specs=[smem] + [hbm] * 7,
        out_specs=[vmem] * 4,
        scratch_shapes=[
            pltpu.VMEM(entries.shape, entries.dtype) for entries in (areas, owner, block, trains)
        ]
        + [
            pltpu.VMEM((populations.shape[1] * 3 // 2, group, populations.shape[2]), jnp.int32),
            pltpu.SemaphoreType.DMA((7,)),
        ],
        compiler_params=kernel_params(),
        name="sample",
    )(place, populations, cells, weights, areas, owner, block, trains)


def three_parts(values):
    parts = []
    for _ in range(3):
        parts.append(values.astype(jnp.bfloat16))
        values = values - parts[-1].astype(jnp.float32)
    return parts


def one_hot(mask):
    return jnp.where(mask, 1.0, 0.0).astype(jnp.bfloat16)


def wanted_labels(own_ref, slots, owned):
    mark = own_ref.shape[1]
    own = own_ref[3 * slots + owned : 3 * slots + owned + 8, :]
    ids, trains, mine = (jnp.broadcast_to(own[i : i + 1], (mark, mark)).T for i in range(3))
    return (ids[0:slots], mine[0:owned], trains[0:owned])


def add_shards(totals, shards, ids, mine):
    slots, owned = (ids.shape[0], mine.shape[0])
    meta = 3 * slots + owned
    wanted = jnp.concatenate([ids, mine], axis=0)
    for shard in shards:
        match = one_hot(wanted == shard[meta : meta + 1, :])
        match = jnp.concatenate([match, match[:, 0:slots]], axis=1)
        values = jnp.concatenate([shard[c * slots : (c + 1) * slots, :] for c in range(3)], axis=1)
        sums = jnp.dot(
            match, jnp.concatenate(three_parts(values), axis=0), preferred_element_type=jnp.float32
        )
        held = ids == shard[meta + 2 : meta + 3, :]
        parts = three_parts(shard[3 * slots : meta, :])
        parts.append(jnp.zeros_like(parts[0]))
        area = jnp.dot(
            one_hot(held), jnp.concatenate(parts, axis=0), preferred_element_type=jnp.float32
        )
        trains = jnp.where(held, shard[meta + 1 : meta + 2, :], 0.0)
        got = (sums, area, trains)
        totals = got if totals is None else [total + new for total, new in zip(totals, got)]
    return totals


def settle_kernel(slots, owned, speeds_ref, *refs):
    shards, (sums_ref, area_ref, trains_ref, rows_ref) = (refs[:-4], refs[-4:])
    mark = rows_ref.shape[1]
    for train in range(speeds_ref.shape[0]):
        for c in range(3):
            at = 3 * train + c
            rows_ref[at : at + 1, :] = jnp.full((1, mark), speeds_ref[train, c], jnp.float32)
    ids, mine, _ = wanted_labels(shards[0], slots, owned)
    sums_ref[...], area_ref[...], trains_ref[...] = add_shards(None, shards, ids, mine)


def settle_early(slots, owned, speeds, shards):
    mark = shards[0].shape[1]
    smem = pl.BlockSpec(memory_space=pltpu.SMEM)
    vmem = pl.BlockSpec(memory_space=pltpu.VMEM)
    return pl.pallas_call(
        functools.partial(settle_kernel, slots, owned),
        out_shape=(
            full((slots + owned, 3 * mark)),
            full((slots, mark)),
            full((slots, mark)),
            full((3 * speeds.shape[0], mark)),
        ),
        in_specs=[smem] + [vmem] * len(shards),
        compiler_params=kernel_params(),
        cost_estimate=pl.CostEstimate(
            flops=10**9, bytes_accessed=len(shards) * shards[0].size * 4, transcendentals=0
        ),
        name="settle",
    )(speeds, *shards)


def block_forces(rows_ref, totals, own_ref, slots, owned):
    mark = own_ref.shape[1]
    ids, mine, own_trains = wanted_labels(own_ref, slots, owned)
    sums, area, trains = totals
    trains = jnp.broadcast_to(jnp.sum(trains, axis=1, keepdims=True), area.shape)
    own_area = own_ref[3 * slots : 3 * slots + owned, :]
    forces, own_forces = ([], [])
    for c in range(3):
        target, own_target = (jnp.zeros_like(area), jnp.zeros_like(own_area))
        for train in range(rows_ref.shape[0] // 3):
            at = 3 * train + c
            speed = rows_ref[at : at + 1, :]
            target = jnp.where(trains == float(train), speed, target)
            own_target = jnp.where(own_trains == float(train), speed, own_target)
        got = sums[:, c * mark : (c + 1) * mark]
        forces.append(stiffness * area * (target - got[0:slots]))
        own_forces.append(stiffness * own_area * (own_target - got[slots:]))
    return (forces, own_forces)


def spread_kernel(
    slots, owned, place_ref, own_ref, last_ref, sums_ref, area_ref, trains_ref, speeds_ref,
    cells_ref, weights_ref, pop_ref, solid_ref,
    relaxed_ref, far_ref, near_ref, side_ref, marker_ref, force_ref, lines_ref, acc,
):
    rows, lanes = (pop_ref.shape[1], pop_ref.shape[2])
    size_y = 8
    mark = cells_ref.shape[1]
    kernel = cells_ref.shape[0] // slots
    bf = jnp.bfloat16
    ids, mine, _ = wanted_labels(own_ref, slots, owned)
    totals = (sums_ref[...], area_ref[...], trains_ref[...])
    totals = add_shards(totals, [last_ref], ids, mine)
    forces, own_forces = block_forces(speeds_ref, totals, own_ref, slots, owned)
    for c in range(3):
        force_ref[c] = forces[c]
        marker_ref[c] = own_forces[c]

    acc[...] = jnp.zeros_like(acc)
    iota = lax.broadcasted_iota(jnp.int32, (16, mark), 0).astype(jnp.float32)
    steps = [(iota + 16.0 * j).astype(bf) for j in range(max(rows, lanes) // 16)]
    one, zero = (jnp.ones((16, mark), bf), jnp.zeros((16, mark), bf))

    def body(step, carry):
        first = pl.multiple_of(step * group, group)
        force = [force_ref[c, pl.ds(first, group), :] for c in range(3)]
        for k in range(kernel):
            at = pl.ds(first * kernel + k, group, stride=kernel)
            cells = cells_ref[at, :]
            weight = weights_ref[at, :]
            lane = (cells & (lanes - 1)).astype(jnp.float32)
            row = (cells >> (lanes.bit_length() - 1)).astype(jnp.float32)
            parts = []
            for c in range(3):
                value = weight * force[c]
                high = value.astype(bf).astype(jnp.float32)
                parts += [high, value - high]
            for which, entries in enumerate([lane, row] + parts):
                lines_ref[k, which] = entries

            def wide(which, i):
                entries = lines_ref[k, which, pl.ds(i, 8, stride=0), :]
                return jnp.concatenate([entries, entries], axis=0).astype(bf)

            left, right = ([], [])
            for i in range(group):
                lane_i, row_i = (wide(0, i), wide(1, i))
                right.append(
                    jnp.concatenate(
                        [jnp.where(steps[j] == lane_i, one, zero) for j in range(lanes // 16)],
                        axis=0,
                    )
                )
                masks = [steps[j] == row_i for j in range(rows // 16)]
                pieces = []
                for which in range(len(parts)):
                    part_i = wide(2 + which, i)
                    pieces += [jnp.where(mask, part_i, zero) for mask in masks]
                left.append(jnp.concatenate(pieces, axis=0))
            acc[...] += lax.dot_general(
                jnp.concatenate(left, axis=1),
                jnp.concatenate(right, axis=1),
                (((1,), (1,)), ((), ())),
                preferred_element_type=jnp.float32,
            )
        return carry

    lax.fori_loop(0, slots // group, body, 0)
    cell_force = [
        acc[2 * c * rows : (2 * c + 1) * rows, :] + acc[(2 * c + 1) * rows : (2 * c + 2) * rows, :]
        for c in range(3)
    ]
    relaxed = collide([pop_ref[q] for q in range(19)], cell_force, solid_ref[...])
    for q in range(19):
        relaxed_ref[q] = relaxed[q]
    even = place_ref[3] == 0
    for i in range(5):
        ahead = relaxed[going(0, 1)[i]][rows - size_y :]
        behind = relaxed[going(0, -1)[i]][:size_y]
        far_ref[i] = jnp.where(even, behind, ahead)
        near_ref[i] = jnp.where(even, ahead, behind)
        for x in range(rows // size_y):
            up = relaxed[going(1, 1)[i]][size_y * x + size_y - 1 : size_y * x + size_y, :]
            down = relaxed[going(1, -1)[i]][size_y * x : size_y * x + 1, :]
            at = rows // size_y * i + x
            side_ref[at : at + 1, :] = jnp.where(place_ref[0] == 0, up, down)


def spread(owned, place, own, last, early, cells, weights, populations, solid):
    mark = cells.shape[1]
    slots = early[1].shape[0]
    line_count, lanes = solid.shape
    smem = pl.BlockSpec(memory_space=pltpu.SMEM)
    vmem = pl.BlockSpec(memory_space=pltpu.VMEM)
    return pl.pallas_call(
        functools.partial(spread_kernel, slots, owned),
        out_shape=(
            full(populations.shape),
            full((5, 8, lanes)),
            full((5, 8, lanes)),
            full((24, lanes)),
            full((3, owned, mark)),
        ),
        in_specs=[smem] + [vmem] * 10,
        scratch_shapes=[
            pltpu.VMEM((3, slots, mark), jnp.float32),
            pltpu.VMEM((cells.shape[0] // slots, 8, group, mark), jnp.float32),
            pltpu.VMEM((6 * line_count, lanes), jnp.float32),
        ],
        compiler_params=kernel_params(),
        name="spread",
    )(place, own, last, *early, cells, weights, populations, solid)


def downwind(place_ref, relaxed_ref, far_ref, near_ref):
    size_y = far_ref.shape[1]
    size_x = relaxed_ref.shape[1] // size_y
    even = place_ref[3] == 0

    def cells(q, x):
        step = int(velocity_table[q][0])
        source = x - step
        if 0 <= source < size_x:
            return relaxed_ref[q, source * size_y : (source + 1) * size_y, :]
        i = going(0, step).index(q)
        if step == 1:
            return jnp.where(even, far_ref[i], near_ref[i])
        return jnp.where(even, near_ref[i], far_ref[i])

    return cells


def sideways(cells, side_ref, edge):
    def result(q, x, y_at):
        step_x, step_y = (int(step) for step in velocity_table[q][:2])
        size_y = y_at.shape[0]
        size_x = side_ref.shape[0] // 6
        if step_y == 0:
            return cells(q, x)
        source = x - step_x
        at = size_x * going(1, step_y).index(q) + source
        halo = side_ref[at : at + 1, :] if 0 <= source < size_x else edge(q)
        turned = pltpu.roll(cells(q, x), step_y % size_y, 0)
        return jnp.where(y_at == (0 if step_y == 1 else size_y - 1), halo, turned)

    return result


def corner_index(q):
    step_y = int(velocity_table[q][1])
    return [p for p in going(1, step_y) if int(velocity_table[p][0]) != 0].index(q)


def pack_kernel(
    place_ref, relaxed_ref, far_ref, near_ref, side_ref, corner_ref, first_ref, second_ref
):
    size_y, lanes = far_ref.shape[1:]
    size_x = relaxed_ref.shape[1] // size_y
    cells = downwind(place_ref, relaxed_ref, far_ref, near_ref)
    corner_ref[...] = jnp.zeros(corner_ref.shape, jnp.float32)
    for ahead in going(1, 1):
        step_x = int(velocity_table[ahead][0])
        if step_x == 0:
            continue
        behind = opposite_table[ahead]
        up = cells(ahead, 0 if step_x == 1 else size_x - 1)[size_y - 1 : size_y, :]
        down = cells(behind, size_x - 1 if step_x == 1 else 0)[0:1, :]
        at = corner_index(ahead)
        from_behind = corner_index(behind)
        lower = place_ref[0] == 0

        @pl.when(lower)
        def _(at=at, up=up):
            corner_ref[at : at + 1, :] = up

        @pl.when(jnp.logical_not(lower))
        def _(at=from_behind, down=down):
            corner_ref[at : at + 1, :] = down

    y_at = lax.broadcasted_iota(jnp.int32, (size_y, lanes), 0)
    lane_at = lax.broadcasted_iota(jnp.int32, (size_y, lanes), 1)
    level = sideways(cells, side_ref, None)
    packs = []
    for step in (1, -1):
        packed = jnp.zeros((size_y, lanes), jnp.float32)
        for i, q in enumerate(going(2, step)):
            edge = lanes - 1 if step == 1 else 0
            for x in range(size_x):
                at = 8 * x + i
                moved = pltpu.roll(level(q, x, y_at), (at - edge) % lanes, 1)
                packed = jnp.where(lane_at == at, moved, packed)
        packs.append(packed)
    even = place_ref[1] % 2 == 0
    first_ref[...] = jnp.where(even, packs[0], packs[1])
    second_ref[...] = jnp.where(even, packs[1], packs[0])


def pack(place, relaxed, far, near, side):
    smem = pl.BlockSpec(memory_space=pltpu.SMEM)
    vmem = pl.BlockSpec(memory_space=pltpu.VMEM)
    edge = full(far.shape[1:])
    return pl.pallas_call(
        pack_kernel,
        out_shape=(edge, edge, edge),
        in_specs=[smem] + [vmem] * 4,
        compiler_params=kernel_params(),
        name="pack",
    )(place, relaxed, far, near, side)


def stream_kernel(
    count_z, place_ref, relaxed_ref, far_ref, near_ref, side_ref, second_ref, corner_ref,
    first_ref, out_any, out_ref, sems,
):
    size_x, size_y, lanes = out_ref.shape[1:]
    shape = (size_y, lanes)
    y_at = lax.broadcasted_iota(jnp.int32, shape, 0)
    z_at = lax.broadcasted_iota(jnp.int32, shape, 1)
    y_index, z_index = (place_ref[0], place_ref[1])
    streamed = sideways(
        downwind(place_ref, relaxed_ref, far_ref, near_ref),
        side_ref,
        lambda q: corner_ref[corner_index(q) : corner_index(q) + 1, :],
    )
    even = z_index % 2 == 0
    columns = {
        -1: jnp.where(even, first_ref[...], second_ref[...]),
        1: jnp.where(even, second_ref[...], first_ref[...]),
    }
    on_side = y_at == jnp.where(y_index == 0, 0, size_y - 1)
    on_side = on_side | ((z_at == 0) & (z_index == 0))
    on_side = on_side | ((z_at == lanes - 1) & (z_index == count_z - 1))
    copies = []
    for q in range(19):
        step_z = int(velocity_table[q][2])
        z_edge = 0 if step_z == 1 else lanes - 1
        for x in range(size_x):
            cells = streamed(q, x, y_at)
            if step_z != 0:
                at = 8 * x + going(2, step_z).index(q)
                cells = jnp.where(
                    z_at == z_edge,
                    pltpu.roll(columns[step_z], (z_edge - at) % lanes, 1),
                    pltpu.roll(cells, step_z % lanes, 1),
                )
            out_ref[q, x] = jnp.where(on_side, far_field[q], cells)
        copies.append(pltpu.make_async_copy(out_ref.at[q], out_any.at[q], sems.at[q]))
        copies[-1].start()
    for copy in copies:
        copy.wait()


def stream(count_z, place, relaxed, *halos):
    rows, lanes = relaxed.shape[1:]
    size_y = halos[0].shape[1]
    smem = pl.BlockSpec(memory_space=pltpu.SMEM)
    vmem = pl.BlockSpec(memory_space=pltpu.VMEM)
    shape = (19, rows // size_y, size_y, lanes)
    return pl.pallas_call(
        functools.partial(stream_kernel, count_z),
        out_shape=full(shape),
        in_specs=[smem] + [vmem] * (1 + len(halos)),
        out_specs=pl.BlockSpec(memory_space=pltpu.HBM),
        scratch_shapes=[pltpu.VMEM(shape, jnp.float32), pltpu.SemaphoreType.DMA((19,))],
        compiler_params=kernel_params(),
        name="stream",
    )(place, relaxed, *halos)


def per_device(
    populations,
    solid_cells,
    slot_cells,
    slot_weights,
    slot_owner,
    slot_block,
    train_of_block,
    marker_area,
    train_velocity,
):
    size_x, size_y, size_z = (populations.shape[1], populations.shape[2], populations.shape[3])
    lines = size_x * size_y
    slots, kernel, mark = (slot_cells.shape[3], slot_cells.shape[4], slot_cells.shape[5])
    owned = train_of_block.shape[3]
    count_x, count_y, count_z = (lax.axis_size(axis) for axis in ("gx", "gy", "gz"))
    x_index, y_index, z_index = (lax.axis_index(axis) for axis in ("gx", "gy", "gz"))
    place = jnp.stack([y_index, z_index, x_index * count_y + y_index, x_index % 2])
    place = place.astype(jnp.int32)
    inputs = [
        pltpu.with_memory_space_constraint(entries, pltpu.HBM)
        for entries in (
            populations.reshape(19, lines, size_z),
            slot_cells.reshape(slots * kernel, mark),
            slot_weights.reshape(slots * kernel, mark),
            marker_area.reshape(owned, mark),
            slot_owner.reshape(1, slots),
            slot_block.reshape(1, slots),
            train_of_block.reshape(1, owned),
        )
    ]
    own, pops, cells, weights = sample(place, *inputs)
    swap = [(0, 1), (1, 0)]

    def across_x(entries, distance):
        return lax.ppermute(entries, "gx", [(i, i ^ distance) for i in range(count_x)])

    def across_y(entries):
        return lax.ppermute(entries, "gy", swap)

    shards = {0: own}
    for distance in reversed(range(1, count_x)):
        shards[distance] = across_x(own, distance)
    beside = {distance: across_y(shards[distance]) for distance in (0, 1, 3, 2)}
    last = beside.pop(2)
    early = settle_early(slots, owned, train_velocity, [*shards.values(), *beside.values()])
    solid = solid_cells.reshape(lines, size_z)
    relaxed, far, near, side, marker_force = spread(
        owned, place, own, last, early, cells, weights, pops, solid
    )
    evens = range(0, count_x, 2)
    far = lax.ppermute(
        far,
        "gx",
        [(i, (i - 1) % count_x) for i in evens] + [((i - 1) % count_x, i) for i in evens],
    )
    near = lax.ppermute(near, "gx", [(i, i + 1) for i in evens] + [(i + 1, i) for i in evens])
    side = across_y(side)
    corner, up_first, down_first = pack(place, relaxed, far, near, side)
    inner = [(i, i + 1) for i in range(0, count_z - 1, 2)]
    outer = [(i, i + 1) for i in range(1, count_z - 1, 2)]
    down_first = lax.ppermute(down_first, "gz", outer + [(j, i) for i, j in outer])
    corner = across_y(corner)
    up_first = lax.ppermute(up_first, "gz", inner + [(j, i) for i, j in inner])
    populations_next = stream(
        count_z, place, relaxed, far, near, side, down_first, corner, up_first
    )
    marker_force = marker_force.transpose(1, 0, 2).reshape(1, 1, 1, owned, 3, mark)
    return (populations_next, marker_force)


def solution(mesh):
    placed = (
        P(None, "gx", "gy", "gz"),
        P("gx", "gy", "gz"),
        P("gx", "gy", "gz", None, None, None),
        P("gx", "gy", "gz", None, None, None),
        P("gx", "gy", "gz", None, None),
        P("gx", "gy", "gz", None),
        P("gx", "gy", "gz", None),
        P("gx", "gy", "gz", None, None),
        P(),
    )
    small = mesh.shape["gy"] == 2 and mesh.shape["gx"] == 4 and mesh.shape["gz"] % 2 == 0
    return jax.shard_map(
        per_device if small else per_device_general,
        mesh=mesh,
        in_specs=placed,
        out_specs=(P(None, "gx", "gy", "gz"), P("gx", "gy", "gz", None, None, None)),
        check_vma=False,
    )
```

```python
import functools
import jax
import jax.numpy as jnp
import numpy as np
from jax import lax
from jax.experimental import pallas as pl
from jax.experimental.pallas import tpu as pltpu
from jax.sharding import PartitionSpec as P

velocity_table = np.array(
    [
        [0, 0, 0],
        [1, 0, 0],
        [-1, 0, 0],
        [0, 1, 0],
        [0, -1, 0],
        [0, 0, 1],
        [0, 0, -1],
        [1, 1, 0],
        [-1, -1, 0],
        [1, -1, 0],
        [-1, 1, 0],
        [1, 0, 1],
        [-1, 0, -1],
        [1, 0, -1],
        [-1, 0, 1],
        [0, 1, 1],
        [0, -1, -1],
        [0, 1, -1],
        [0, -1, 1],
    ]
)
weight_table = [1.0 / 3.0] + [1.0 / 18.0] * 6 + [1.0 / 36.0] * 12
opposite_table = [0, 2, 1, 4, 3, 6, 5, 8, 7, 10, 9, 12, 11, 14, 13, 16, 15, 18, 17]
stress_pairs = [(0, 0), (1, 1), (2, 2), (0, 1), (0, 2), (1, 2)]
tau_base = 0.55
smag_term = 18.0 * 1.4142135623730951 * 0.17 * 0.17
regular_eps = 0.0001
stiffness = 2.0
far_velocity = (0.02, 0.06, 0.0)
vmem_bytes = 16 << 20
group = 8


def going(axis, step):
    return [q for q in range(19) if int(velocity_table[q][axis]) == step]


def project(direction, vector):
    projection = 0.0 * vector[0]
    for component in range(3):
        lattice_step = int(velocity_table[direction][component])
        if lattice_step != 0:
            projection = projection + lattice_step * vector[component]
    return projection


def moments(populations):
    density = populations[0]
    momentum = [jnp.zeros_like(density) for component in range(3)]
    for direction in range(1, 19):
        density = density + populations[direction]
        for component in range(3):
            lattice_step = int(velocity_table[direction][component])
            if lattice_step == 1:
                momentum[component] = momentum[component] + populations[direction]
            elif lattice_step == -1:
                momentum[component] = momentum[component] - populations[direction]
    return (density, momentum)


def equilibrium(density, velocity):
    speed_sq = velocity[0] * velocity[0] + velocity[1] * velocity[1] + velocity[2] * velocity[2]
    result = []
    for direction in range(19):
        projected = project(direction, velocity)
        result.append(
            weight_table[direction]
            * density
            * (1.0 + 3.0 * projected + 4.5 * projected * projected - 1.5 * speed_sq)
        )
    return result


far_field = [float(np.float32(value)) for value in equilibrium(1.0, list(far_velocity))]


def collide(populations, cell_force, solid_cells):
    density, momentum = moments(populations)
    velocity = [
        (momentum[component] + 0.5 * cell_force[component]) / density for component in range(3)
    ]
    balance = equilibrium(density, velocity)
    stress = [jnp.zeros_like(density) for pair_pos in range(6)]
    for direction in range(19):
        non_eq = populations[direction] - balance[direction]
        for pair_pos in range(6):
            row_axis, col_axis = stress_pairs[pair_pos]
            factor = int(velocity_table[direction][row_axis] * velocity_table[direction][col_axis])
            if factor != 0:
                stress[pair_pos] = stress[pair_pos] + factor * non_eq
    shear_sq = stress[0] * stress[0] + stress[1] * stress[1] + stress[2] * stress[2]
    shear_sq = shear_sq + 2.0 * (
        stress[3] * stress[3] + stress[4] * stress[4] + stress[5] * stress[5]
    )
    magnitude = jnp.sqrt(shear_sq + regular_eps)
    relax_time = 0.5 * (tau_base + jnp.sqrt(tau_base * tau_base + smag_term * magnitude / density))
    relax_rate = 1.0 / relax_time
    guo_factor = 1.0 - 0.5 * relax_rate
    speed_force = (
        velocity[0] * cell_force[0] + velocity[1] * cell_force[1] + velocity[2] * cell_force[2]
    )
    result = []
    for direction in range(19):
        along_force = project(direction, cell_force)
        along_speed = project(direction, velocity)
        source = (
            guo_factor
            * weight_table[direction]
            * (3.0 * (along_force - speed_force) + 9.0 * along_speed * along_force)
        )
        relaxed = (
            populations[direction]
            - (populations[direction] - balance[direction]) * relax_rate
            + source
        )
        result.append(jnp.where(solid_cells == 1, populations[opposite_table[direction]], relaxed))
    return result


def with_halo(cells, sides, width):
    for axis, dim in sides:
        count = lax.axis_size(axis)
        head = lax.slice_in_dim(cells, 0, width, axis=dim)
        tail = lax.slice_in_dim(cells, cells.shape[dim] - width, cells.shape[dim], axis=dim)
        cells = jnp.concatenate(
            [
                lax.ppermute(tail, axis, [(i, (i + 1) % count) for i in range(count)]),
                cells,
                lax.ppermute(head, axis, [((i + 1) % count, i) for i in range(count)]),
            ],
            axis=dim,
        )
    return cells


def settle(received, labels, owned, train_of_block, marker_area, train_velocity, mark):
    rows_in = received.reshape(-1, 3 * mark)
    label_rows = labels.reshape(-1)
    owner_match = (label_rows[None, :] == jnp.arange(owned, dtype=jnp.int32)[:, None]).astype(
        jnp.float32
    )
    marker_velocity = jnp.dot(owner_match, rows_in, precision=lax.Precision.HIGHEST).reshape(
        owned, 3, mark
    )
    trains = train_velocity.shape[0]
    train_rows = train_of_block.reshape(owned)
    train_match = (train_rows[:, None] == jnp.arange(trains, dtype=jnp.int32)[None, :]).astype(
        jnp.float32
    )
    target = jnp.dot(train_match, train_velocity, precision=lax.Precision.HIGHEST)
    areas = marker_area.reshape(owned, mark)
    marker_force = stiffness * areas[:, None, :] * (target[:, :, None] - marker_velocity)
    back_rows = jnp.dot(
        owner_match.T, marker_force.reshape(owned, 3 * mark), precision=lax.Precision.HIGHEST
    )
    return (marker_force, back_rows)


def per_device_general(
    populations,
    solid_cells,
    slot_cells,
    slot_weights,
    slot_owner,
    slot_block,
    train_of_block,
    marker_area,
    train_velocity,
):
    size_x, size_y, size_z = (populations.shape[1], populations.shape[2], populations.shape[3])
    cell_count = size_x * size_y * size_z
    slots, kernel, mark = (slot_cells.shape[3], slot_cells.shape[4], slot_cells.shape[5])
    owned = train_of_block.shape[3]
    peers_x = lax.axis_size("gx")
    peers_y = lax.axis_size("gy")
    peers = peers_x * peers_y
    capacity = max(2, 2 * slots // peers)
    density, momentum = moments(populations)
    rest_velocity = jnp.stack([momentum[component] / density for component in range(3)]).reshape(
        3, cell_count
    )
    cells = slot_cells.reshape(slots, kernel, mark)
    weights = slot_weights.reshape(slots, kernel, mark)
    partial_value = jnp.sum(rest_velocity[:, cells] * weights[None], axis=2)
    slot_rows = partial_value.transpose(1, 0, 2).reshape(slots, 3 * mark)
    slot_dest = slot_owner.reshape(slots)
    blocks = slot_block.reshape(slots)
    order = jnp.arange(slots, dtype=jnp.int32)
    earlier = (slot_dest[None, :] == slot_dest[:, None]) & (order[None, :] < order[:, None])
    slot_rank = jnp.sum(earlier.astype(jnp.int32), axis=1)
    target_row = slot_dest * capacity + slot_rank
    buffer_rows = jnp.arange(peers * capacity, dtype=jnp.int32)
    matches = buffer_rows[:, None] == target_row[None, :]
    placement = matches.astype(jnp.float32)
    outgoing = jnp.dot(placement, slot_rows, precision=lax.Precision.HIGHEST)
    labels = jnp.sum(jnp.where(matches, blocks[None, :] + 1, 0), axis=1) - 1
    received, got_labels = (
        lax.all_to_all(
            outgoing.reshape(peers, capacity, 3 * mark),
            ("gx", "gy"),
            split_axis=0,
            concat_axis=0,
            tiled=True,
        ),
        lax.all_to_all(
            labels.reshape(peers, capacity), ("gx", "gy"), split_axis=0, concat_axis=0, tiled=True
        ),
    )
    marker_force, back_rows = settle(
        received, got_labels, owned, train_of_block, marker_area, train_velocity, mark
    )
    returned = lax.all_to_all(
        back_rows.reshape(peers, capacity, 3 * mark),
        ("gx", "gy"),
        split_axis=0,
        concat_axis=0,
        tiled=True,
    )
    slot_force = jnp.dot(
        placement.T, returned.reshape(peers * capacity, 3 * mark), precision=lax.Precision.HIGHEST
    )
    slot_force = slot_force.reshape(slots, 3, mark).transpose(1, 0, 2)
    contrib = weights[None] * slot_force[:, :, None, :]
    cell_force = (
        jnp.zeros((3, cell_count), jnp.float32).at[:, cells.reshape(-1)].add(contrib.reshape(3, -1))
    )
    cell_force = cell_force.reshape(3, size_x, size_y, size_z)
    relaxed = collide(populations, cell_force, solid_cells)
    padded = with_halo(jnp.stack(relaxed), (("gx", 1), ("gy", 2), ("gz", 3)), 1)
    parts = []
    for direction in range(19):
        shift_x = 1 - int(velocity_table[direction][0])
        shift_y = 1 - int(velocity_table[direction][1])
        shift_z = 1 - int(velocity_table[direction][2])
        parts.append(
            padded[
                direction,
                shift_x : shift_x + size_x,
                shift_y : shift_y + size_y,
                shift_z : shift_z + size_z,
            ]
        )
    read = jnp.stack(parts)
    total_y = size_y * lax.axis_size("gy")
    total_z = size_z * lax.axis_size("gz")
    global_y = lax.axis_index("gy") * size_y + jnp.arange(size_y, dtype=jnp.int32)
    global_z = lax.axis_index("gz") * size_z + jnp.arange(size_z, dtype=jnp.int32)
    on_side = ((global_y == 0) | (global_y == total_y - 1))[:, None] | (
        (global_z == 0) | (global_z == total_z - 1)
    )[None, :]
    far_field = jnp.array(equilibrium(1.0, list(far_velocity)), dtype=jnp.float32)
    populations_next = jnp.where(on_side[None, None], far_field[:, None, None, None], read)
    return (populations_next, marker_force.reshape(1, 1, 1, owned, 3, mark))


def full(shape):
    return jax.ShapeDtypeStruct(shape, jnp.float32)


def kernel_params():
    return pltpu.CompilerParams(vmem_limit_bytes=vmem_bytes)


def low_half(shape):
    return lax.broadcasted_iota(jnp.int32, shape, 1) < shape[1] // 2


def fetch(pairs, sems):
    copies = [
        pltpu.make_async_copy(source, target, sems.at[i])
        for i, (source, target) in enumerate(pairs)
    ]
    for copy in copies:
        copy.start()
    return copies


def shard_rows(slots, owned):
    return 8 + owned + 3 * slots


def sample_kernel(
    place_ref, pop_any, cells_any, weights_any, areas_any, owner_any, block_any, trains_any,
    out_ref, pop_ref, cells_ref, weights_ref, areas_ref, owner_ref, block_ref, trains_ref,
    table, sems,
):
    rows, lanes = (pop_ref.shape[1], pop_ref.shape[2])
    mark = cells_ref.shape[1]
    owned = areas_ref.shape[0]
    slots = owner_ref.shape[1]
    kernel = cells_ref.shape[0] // slots
    copies = fetch(
        (
            (pop_any, pop_ref),
            (cells_any, cells_ref),
            (weights_any, weights_ref),
            (areas_any, areas_ref),
            (owner_any, owner_ref),
            (block_any, block_ref),
            (trains_any, trains_ref),
        ),
        sems,
    )

    copies[0].wait()
    density, momentum = moments([pop_ref[q] for q in range(19)])
    speed = [momentum[c] / density for c in range(3)]
    largest = jnp.maximum(jnp.maximum(jnp.abs(speed[0]), jnp.abs(speed[1])), jnp.abs(speed[2]))
    largest = jnp.max(largest, axis=(0, 1), keepdims=True) + 1e-20
    scale = largest * (1.0 / 32767.0)
    fixed = [(speed[c] * (1.0 / scale) + 32768.5).astype(jnp.int32) for c in range(3)]
    words = jnp.concatenate(
        [
            (fixed[0] << 16) | fixed[1],
            (fixed[2][: rows // 2] << 16) | fixed[2][rows // 2 :],
        ],
        axis=0,
    )
    for r in range(table.shape[0]):
        table[r] = jnp.broadcast_to(words[r : r + 1], (group, lanes))
    for copy in copies[1:]:
        copy.wait()
    out_ref[8 : 8 + owned, :] = areas_ref[...]
    out_ref[0:8, :] = jnp.zeros((8, mark), jnp.float32)
    ids = (owner_ref[...] * owned + block_ref[...]).astype(jnp.float32)
    out_ref[0:1, :] = jnp.concatenate([ids] * (mark // slots), axis=1)
    out_ref[1:2, 0:owned] = trains_ref[...].astype(jnp.float32)
    mine = lax.broadcasted_iota(jnp.int32, (1, mark), 1) % owned + place_ref[2] * owned
    out_ref[2:3, :] = mine.astype(jnp.float32)

    def body(step, carry):
        first = pl.multiple_of(step * group, group)
        total = [jnp.zeros((group, mark), jnp.float32) for c in range(3)]
        for k in range(kernel):
            at = pl.ds(first * kernel + k, group, stride=kernel)
            cells = cells_ref[at, :]
            lane = cells & (lanes - 1)
            row = cells >> (lanes.bit_length() - 1)
            bits = [(row >> bit) & 1 == 1 for bit in range(rows.bit_length() - 1)]

            def choose(low, level):
                if level < 0:
                    return jnp.take_along_axis(table[low], lane, axis=1, mode="promise_in_bounds")
                lower = choose(low, level - 1)
                return jnp.where(bits[level], choose(low + (1 << level), level - 1), lower)

            pair = choose(0, len(bits) - 1)
            third = choose(rows, len(bits) - 2)
            picked = [
                lax.shift_right_logical(pair, 16),
                pair & 65535,
                jnp.where(bits[-1], third & 65535, lax.shift_right_logical(third, 16)),
            ]
            weight = weights_ref[at, :]
            for c in range(3):
                total[c] = total[c] + weight * (picked[c].astype(jnp.float32) - 32768.0)
        for c in range(3):
            here = pl.ds(pl.multiple_of(8 + owned + c * slots + first, group), group)
            out_ref[here, :] = total[c] * scale
        return carry

    lax.fori_loop(0, slots // group, body, 0)


def sample(place, populations, cells, weights, areas, owner, block, trains):
    smem = pl.BlockSpec(memory_space=pltpu.SMEM)
    hbm = pl.BlockSpec(memory_space=pltpu.HBM)
    vmem = pl.BlockSpec(memory_space=pltpu.VMEM)
    kept = (populations, cells, weights)
    count = shard_rows(owner.shape[1], areas.shape[0])
    return pl.pallas_call(
        sample_kernel,
        out_shape=[full((count, cells.shape[1]))]
        + [jax.ShapeDtypeStruct(entries.shape, entries.dtype) for entries in kept],
        in_specs=[smem] + [hbm] * 7,
        out_specs=[vmem] * 4,
        scratch_shapes=[
            pltpu.VMEM(entries.shape, entries.dtype) for entries in (areas, owner, block, trains)
        ]
        + [
            pltpu.VMEM((populations.shape[1] * 3 // 2, group, populations.shape[2]), jnp.int32),
            pltpu.SemaphoreType.DMA((7,)),
        ],
        compiler_params=kernel_params(),
        name="sample",
    )(place, populations, cells, weights, areas, owner, block, trains)


def three_parts(values):
    parts = []
    for _ in range(3):
        parts.append(values.astype(jnp.bfloat16))
        values = values - parts[-1].astype(jnp.float32)
    return parts


def one_hot(mask):
    return jnp.where(mask, 1.0, 0.0).astype(jnp.bfloat16)


def wanted_labels(own_ref, slots, owned):
    mark = own_ref.shape[1]
    own = own_ref[0:8, :]
    ids, trains, mine = (jnp.broadcast_to(own[i : i + 1], (mark, mark)).T for i in range(3))
    return (ids[0:slots], mine[0:owned], trains[0:owned])


def add_shards(totals, shards, ids, mine):
    slots, owned = (ids.shape[0], mine.shape[0])
    wanted = jnp.concatenate([ids, mine], axis=0)
    for shard in shards:
        match = one_hot(wanted == shard[0:1, :])
        match = jnp.concatenate([match, match[:, 0:slots]], axis=1)
        starts = [8 + owned + c * slots for c in range(3)]
        values = jnp.concatenate([shard[at : at + slots, :] for at in starts], axis=1)
        sums = jnp.dot(
            match, jnp.concatenate(three_parts(values), axis=0), preferred_element_type=jnp.float32
        )
        held = ids == shard[2:3, :]
        parts = three_parts(shard[8 : 8 + owned, :])
        parts.append(jnp.zeros_like(parts[0]))
        area = jnp.dot(
            one_hot(held), jnp.concatenate(parts, axis=0), preferred_element_type=jnp.float32
        )
        got = (sums, area, jnp.where(held, shard[1:2, :], 0.0))
        totals = got if totals is None else [total + new for total, new in zip(totals, got)]
    return totals


def settle_kernel(slots, owned, speeds_ref, *refs):
    *shards, sums_ref, area_ref, trains_ref, rows_ref = refs
    mark = rows_ref.shape[1]
    for train in range(speeds_ref.shape[0]):
        for c in range(3):
            at = 3 * train + c
            rows_ref[at : at + 1, :] = jnp.full((1, mark), speeds_ref[train, c], jnp.float32)
    ids, mine, _ = wanted_labels(shards[0], slots, owned)
    sums_ref[...], area_ref[...], trains_ref[...] = add_shards(None, shards, ids, mine)


def settle_early(slots, owned, speeds, shards):
    mark = shards[0].shape[1]
    smem = pl.BlockSpec(memory_space=pltpu.SMEM)
    vmem = pl.BlockSpec(memory_space=pltpu.VMEM)
    return pl.pallas_call(
        functools.partial(settle_kernel, slots, owned),
        out_shape=(
            full((slots + owned, 3 * mark)),
            full((slots, mark)),
            full((slots, mark)),
            full((3 * speeds.shape[0], mark)),
        ),
        in_specs=[smem] + [vmem] * len(shards),
        compiler_params=kernel_params(),
        cost_estimate=pl.CostEstimate(
            flops=10**9, bytes_accessed=len(shards) * shards[0].size * 4, transcendentals=0
        ),
        name="settle",
    )(speeds, *shards)


def block_forces(rows_ref, totals, own_ref, slots, owned):
    mark = own_ref.shape[1]
    ids, mine, own_trains = wanted_labels(own_ref, slots, owned)
    sums, area, trains = totals
    trains = jnp.broadcast_to(jnp.sum(trains, axis=1, keepdims=True), area.shape)
    own_area = own_ref[8 : 8 + owned, :]
    forces, own_forces = ([], [])
    for c in range(3):
        target, own_target = (jnp.zeros_like(area), jnp.zeros_like(own_area))
        for train in range(rows_ref.shape[0] // 3):
            at = 3 * train + c
            speed = rows_ref[at : at + 1, :]
            target = jnp.where(trains == float(train), speed, target)
            own_target = jnp.where(own_trains == float(train), speed, own_target)
        got = sums[:, c * mark : (c + 1) * mark]
        forces.append(stiffness * area * (target - got[0:slots]))
        own_forces.append(stiffness * own_area * (own_target - got[slots:]))
    return (forces, own_forces)


def spread_kernel(
    slots, owned, place_ref, own_ref, last_ref, sums_ref, area_ref, trains_ref, speeds_ref,
    cells_ref, weights_ref, pop_ref, solid_ref,
    relaxed_ref, far_ref, near_ref, side_ref, marker_any, marker_ref, force_ref, lines_ref, acc,
    sem,
):
    rows, lanes = (pop_ref.shape[1], pop_ref.shape[2])
    size_y = 8
    mark = cells_ref.shape[1]
    kernel = cells_ref.shape[0] // slots
    bf = jnp.bfloat16
    ids, mine, _ = wanted_labels(own_ref, slots, owned)
    totals = add_shards((sums_ref[...], area_ref[...], trains_ref[...]), [last_ref], ids, mine)
    forces, own_forces = block_forces(speeds_ref, totals, own_ref, slots, owned)
    for c in range(3):
        force_ref[c] = forces[c]
        marker_ref[c] = own_forces[c]
    marker_copy = pltpu.make_async_copy(marker_ref, marker_any, sem)
    marker_copy.start()

    acc[...] = jnp.zeros_like(acc)
    iota = lax.broadcasted_iota(jnp.int32, (16, mark), 0).astype(jnp.float32)
    steps = [(iota + 16.0 * j).astype(bf) for j in range(max(rows, lanes) // 16)]
    one, zero = (jnp.ones((16, mark), bf), jnp.zeros((16, mark), bf))

    def body(step, carry):
        first = pl.multiple_of(step * group, group)
        force = [force_ref[c, pl.ds(first, group), :] for c in range(3)]
        for k in range(kernel):
            at = pl.ds(first * kernel + k, group, stride=kernel)
            cells = cells_ref[at, :]
            weight = weights_ref[at, :]
            lane = (cells & (lanes - 1)).astype(jnp.float32)
            row = (cells >> (lanes.bit_length() - 1)).astype(jnp.float32)
            parts = []
            for c in range(3):
                value = weight * force[c]
                high = value.astype(bf).astype(jnp.float32)
                parts += [high, value - high]
            for which, entries in enumerate([lane, row] + parts):
                lines_ref[k, which] = entries

            def wide(which, i):
                entries = lines_ref[k, which, pl.ds(i, 8, stride=0), :]
                return jnp.concatenate([entries, entries], axis=0).astype(bf)

            left, right = ([], [])
            for i in range(group):
                lane_i, row_i = (wide(0, i), wide(1, i))
                right.append(
                    jnp.concatenate(
                        [jnp.where(steps[j] == lane_i, one, zero) for j in range(lanes // 16)],
                        axis=0,
                    )
                )
                masks = [steps[j] == row_i for j in range(rows // 16)]
                pieces = []
                for which in range(len(parts)):
                    part_i = wide(2 + which, i)
                    pieces += [jnp.where(mask, part_i, zero) for mask in masks]
                left.append(jnp.concatenate(pieces, axis=0))
            acc[...] += lax.dot_general(
                jnp.concatenate(left, axis=1),
                jnp.concatenate(right, axis=1),
                (((1,), (1,)), ((), ())),
                preferred_element_type=jnp.float32,
            )
        return carry

    lax.fori_loop(0, slots // group, body, 0)
    cell_force = [
        acc[2 * c * rows : (2 * c + 1) * rows, :] + acc[(2 * c + 1) * rows : (2 * c + 2) * rows, :]
        for c in range(3)
    ]
    relaxed = collide([pop_ref[q] for q in range(19)], cell_force, solid_ref[...])
    for q in range(19):
        relaxed_ref[q] = relaxed[q]
    even = place_ref[3] == 0
    for i in range(5):
        ahead = relaxed[going(0, 1)[i]][rows - size_y :]
        behind = relaxed[going(0, -1)[i]][:size_y]
        far_ref[i] = jnp.where(even, behind, ahead)
        near_ref[i] = jnp.where(even, ahead, behind)
        for x in range(rows // size_y):
            up = relaxed[going(1, 1)[i]][size_y * x + size_y - 1 : size_y * x + size_y, :]
            down = relaxed[going(1, -1)[i]][size_y * x : size_y * x + 1, :]
            at = rows // size_y * i + x
            side_ref[at : at + 1, :] = jnp.where(place_ref[0] == 0, up, down)
    marker_copy.wait()


def spread(owned, place, own, last, early, cells, weights, populations, solid):
    mark = cells.shape[1]
    slots = early[1].shape[0]
    line_count, lanes = solid.shape
    smem = pl.BlockSpec(memory_space=pltpu.SMEM)
    vmem = pl.BlockSpec(memory_space=pltpu.VMEM)
    return pl.pallas_call(
        functools.partial(spread_kernel, slots, owned),
        out_shape=(
            full(populations.shape),
            full((5, 8, lanes)),
            full((5, 8, lanes)),
            full((24, lanes)),
            full((3, owned, mark)),
        ),
        in_specs=[smem] + [vmem] * 10,
        out_specs=[vmem] * 4 + [pl.BlockSpec(memory_space=pltpu.HBM)],
        scratch_shapes=[
            pltpu.VMEM((3, owned, mark), jnp.float32),
            pltpu.VMEM((3, slots, mark), jnp.float32),
            pltpu.VMEM((cells.shape[0] // slots, 8, group, mark), jnp.float32),
            pltpu.VMEM((6 * line_count, lanes), jnp.float32),
            pltpu.SemaphoreType.DMA,
        ],
        compiler_params=kernel_params(),
        name="spread",
    )(place, own, last, *early, cells, weights, populations, solid)


def downwind(place_ref, relaxed_ref, far_ref, near_ref):
    size_y = far_ref.shape[1]
    size_x = relaxed_ref.shape[1] // size_y
    even = place_ref[3] == 0

    def cells(q, x):
        step = int(velocity_table[q][0])
        source = x - step
        if 0 <= source < size_x:
            return relaxed_ref[q, source * size_y : (source + 1) * size_y, :]
        i = going(0, step).index(q)
        if step == 1:
            return jnp.where(even, far_ref[i], near_ref[i])
        return jnp.where(even, near_ref[i], far_ref[i])

    return cells


def sideways(cells, side_ref, edge):
    def result(q, x, y_at):
        step_x, step_y = (int(step) for step in velocity_table[q][:2])
        size_y = y_at.shape[0]
        size_x = side_ref.shape[0] // 6
        if step_y == 0:
            return cells(q, x)
        source = x - step_x
        at = size_x * going(1, step_y).index(q) + source
        halo = side_ref[at : at + 1, :] if 0 <= source < size_x else edge(q)
        turned = pltpu.roll(cells(q, x), step_y % size_y, 0)
        return jnp.where(y_at == (0 if step_y == 1 else size_y - 1), halo, turned)

    return result


def corner_index(q):
    step_y = int(velocity_table[q][1])
    return [p for p in going(1, step_y) if int(velocity_table[p][0]) != 0].index(q)


def pack_kernel(
    place_ref, relaxed_ref, far_ref, near_ref, side_ref, corner_ref, first_ref, second_ref
):
    size_y, lanes = far_ref.shape[1:]
    size_x = relaxed_ref.shape[1] // size_y
    cells = downwind(place_ref, relaxed_ref, far_ref, near_ref)
    corner_ref[...] = jnp.zeros(corner_ref.shape, jnp.float32)
    for ahead in going(1, 1):
        step_x = int(velocity_table[ahead][0])
        if step_x == 0:
            continue
        behind = opposite_table[ahead]
        up = cells(ahead, 0 if step_x == 1 else size_x - 1)[size_y - 1 : size_y, :]
        down = cells(behind, size_x - 1 if step_x == 1 else 0)[0:1, :]
        at = corner_index(ahead)
        from_behind = corner_index(behind)
        lower = place_ref[0] == 0

        @pl.when(lower)
        def _(at=at, up=up):
            corner_ref[at : at + 1, :] = up

        @pl.when(jnp.logical_not(lower))
        def _(at=from_behind, down=down):
            corner_ref[at : at + 1, :] = down

    y_at = lax.broadcasted_iota(jnp.int32, (size_y, lanes), 0)
    lane_at = lax.broadcasted_iota(jnp.int32, (size_y, lanes), 1)
    level = sideways(cells, side_ref, None)
    packs = []
    for step in (1, -1):
        packed = jnp.zeros((size_y, lanes), jnp.float32)
        for i, q in enumerate(going(2, step)):
            edge = lanes - 1 if step == 1 else 0
            for x in range(size_x):
                at = 8 * x + i
                moved = pltpu.roll(level(q, x, y_at), (at - edge) % lanes, 1)
                packed = jnp.where(lane_at == at, moved, packed)
        packs.append(packed)
    even = place_ref[1] % 2 == 0
    first_ref[...] = jnp.where(even, packs[0], packs[1])
    second_ref[...] = jnp.where(even, packs[1], packs[0])


def pack(place, relaxed, far, near, side):
    smem = pl.BlockSpec(memory_space=pltpu.SMEM)
    vmem = pl.BlockSpec(memory_space=pltpu.VMEM)
    edge = full(far.shape[1:])
    return pl.pallas_call(
        pack_kernel,
        out_shape=(edge, edge, edge),
        in_specs=[smem] + [vmem] * 4,
        compiler_params=kernel_params(),
        name="pack",
    )(place, relaxed, far, near, side)


def stream_kernel(
    count_z, place_ref, relaxed_ref, far_ref, near_ref, side_ref, second_ref, corner_ref,
    first_ref, out_any, out_ref, sems,
):
    size_x, size_y, lanes = out_ref.shape[1:]
    shape = (size_y, lanes)
    y_at = lax.broadcasted_iota(jnp.int32, shape, 0)
    z_at = lax.broadcasted_iota(jnp.int32, shape, 1)
    y_index, z_index = (place_ref[0], place_ref[1])
    streamed = sideways(
        downwind(place_ref, relaxed_ref, far_ref, near_ref),
        side_ref,
        lambda q: corner_ref[corner_index(q) : corner_index(q) + 1, :],
    )
    even = z_index % 2 == 0
    columns = {
        -1: jnp.where(even, first_ref[...], second_ref[...]),
        1: jnp.where(even, second_ref[...], first_ref[...]),
    }
    on_side = y_at == jnp.where(y_index == 0, 0, size_y - 1)
    on_side = on_side | ((z_at == 0) & (z_index == 0))
    on_side = on_side | ((z_at == lanes - 1) & (z_index == count_z - 1))
    copies = []
    for q in range(19):
        step_z = int(velocity_table[q][2])
        z_edge = 0 if step_z == 1 else lanes - 1
        for x in range(size_x):
            cells = streamed(q, x, y_at)
            if step_z != 0:
                at = 8 * x + going(2, step_z).index(q)
                cells = jnp.where(
                    z_at == z_edge,
                    pltpu.roll(columns[step_z], (z_edge - at) % lanes, 1),
                    pltpu.roll(cells, step_z % lanes, 1),
                )
            out_ref[q, x] = jnp.where(on_side, far_field[q], cells)
        copies.append(pltpu.make_async_copy(out_ref.at[q], out_any.at[q], sems.at[q]))
        copies[-1].start()
    for copy in copies:
        copy.wait()


def stream(count_z, place, relaxed, *halos):
    rows, lanes = relaxed.shape[1:]
    size_y = halos[0].shape[1]
    smem = pl.BlockSpec(memory_space=pltpu.SMEM)
    vmem = pl.BlockSpec(memory_space=pltpu.VMEM)
    shape = (19, rows // size_y, size_y, lanes)
    return pl.pallas_call(
        functools.partial(stream_kernel, count_z),
        out_shape=full(shape),
        in_specs=[smem] + [vmem] * (1 + len(halos)),
        out_specs=pl.BlockSpec(memory_space=pltpu.HBM),
        scratch_shapes=[pltpu.VMEM(shape, jnp.float32), pltpu.SemaphoreType.DMA((19,))],
        compiler_params=kernel_params(),
        name="stream",
    )(place, relaxed, *halos)


def per_device(
    populations,
    solid_cells,
    slot_cells,
    slot_weights,
    slot_owner,
    slot_block,
    train_of_block,
    marker_area,
    train_velocity,
):
    size_x, size_y, size_z = (populations.shape[1], populations.shape[2], populations.shape[3])
    lines = size_x * size_y
    slots, kernel, mark = (slot_cells.shape[3], slot_cells.shape[4], slot_cells.shape[5])
    owned = train_of_block.shape[3]
    count_x, count_y, count_z = (lax.axis_size(axis) for axis in ("gx", "gy", "gz"))
    x_index, y_index, z_index = (lax.axis_index(axis) for axis in ("gx", "gy", "gz"))
    place = jnp.stack([y_index, z_index, x_index * count_y + y_index, x_index % 2])
    place = place.astype(jnp.int32)
    inputs = [
        pltpu.with_memory_space_constraint(entries, pltpu.HBM)
        for entries in (
            populations.reshape(19, lines, size_z),
            slot_cells.reshape(slots * kernel, mark),
            slot_weights.reshape(slots * kernel, mark),
            marker_area.reshape(owned, mark),
            slot_owner.reshape(1, slots),
            slot_block.reshape(1, slots),
            train_of_block.reshape(1, owned),
        )
    ]
    own, pops, cells, weights = sample(place, *inputs)
    swap = [(0, 1), (1, 0)]

    def across_x(entries, distance):
        return lax.ppermute(entries, "gx", [(i, i ^ distance) for i in range(count_x)])

    def across_y(entries):
        return lax.ppermute(entries, "gy", swap)

    third, first = (across_x(own, distance) for distance in (3, 1))
    beside = across_y(own)
    third_beside = across_y(lax.optimization_barrier((third, beside))[0])
    second = across_x(third, 1)
    first_beside = across_y(first)
    last = across_x(third_beside, 1)
    whole = [own, first, third, second, beside, first_beside, third_beside]
    early = settle_early(slots, owned, train_velocity, whole)
    solid = solid_cells.reshape(lines, size_z)
    relaxed, far, near, side, marker_force = spread(
        owned, place, own, last, early, cells, weights, pops, solid
    )
    evens = range(0, count_x, 2)
    far = lax.ppermute(
        far,
        "gx",
        [(i, (i - 1) % count_x) for i in evens] + [((i - 1) % count_x, i) for i in evens],
    )
    near = lax.ppermute(near, "gx", [(i, i + 1) for i in evens] + [(i + 1, i) for i in evens])
    side = across_y(side)
    corner, up_first, down_first = pack(place, relaxed, far, near, side)
    inner = [(i, i + 1) for i in range(0, count_z - 1, 2)]
    outer = [(i, i + 1) for i in range(1, count_z - 1, 2)]
    down_first = lax.ppermute(down_first, "gz", outer + [(j, i) for i, j in outer])
    corner = across_y(corner)
    up_first = lax.ppermute(up_first, "gz", inner + [(j, i) for i, j in inner])
    populations_next = stream(
        count_z, place, relaxed, far, near, side, down_first, corner, up_first
    )
    marker_force = marker_force.transpose(1, 0, 2).reshape(1, 1, 1, owned, 3, mark)
    return (populations_next, marker_force)


def solution(mesh):
    placed = (
        P(None, "gx", "gy", "gz"),
        P("gx", "gy", "gz"),
        P("gx", "gy", "gz", None, None, None),
        P("gx", "gy", "gz", None, None, None),
        P("gx", "gy", "gz", None, None),
        P("gx", "gy", "gz", None),
        P("gx", "gy", "gz", None),
        P("gx", "gy", "gz", None, None),
        P(),
    )
    small = mesh.shape["gy"] == 2 and mesh.shape["gx"] == 4 and mesh.shape["gz"] % 2 == 0
    return jax.shard_map(
        per_device if small else per_device_general,
        mesh=mesh,
        in_specs=placed,
        out_specs=(P(None, "gx", "gy", "gz"), P("gx", "gy", "gz", None, None, None)),
        check_vma=False,
    )
```

```python
import functools
import jax
import jax.numpy as jnp
import numpy as np
from jax import lax
from jax.experimental import pallas as pl
from jax.experimental.pallas import tpu as pltpu
from jax.sharding import PartitionSpec as P

velocity_table = np.array(
    [
        [0, 0, 0],
        [1, 0, 0],
        [-1, 0, 0],
        [0, 1, 0],
        [0, -1, 0],
        [0, 0, 1],
        [0, 0, -1],
        [1, 1, 0],
        [-1, -1, 0],
        [1, -1, 0],
        [-1, 1, 0],
        [1, 0, 1],
        [-1, 0, -1],
        [1, 0, -1],
        [-1, 0, 1],
        [0, 1, 1],
        [0, -1, -1],
        [0, 1, -1],
        [0, -1, 1],
    ]
)
weight_table = [1.0 / 3.0] + [1.0 / 18.0] * 6 + [1.0 / 36.0] * 12
opposite_table = [0, 2, 1, 4, 3, 6, 5, 8, 7, 10, 9, 12, 11, 14, 13, 16, 15, 18, 17]
stress_pairs = [(0, 0), (1, 1), (2, 2), (0, 1), (0, 2), (1, 2)]
tau_base = 0.55
smag_term = 18.0 * 1.4142135623730951 * 0.17 * 0.17
regular_eps = 0.0001
stiffness = 2.0
far_velocity = (0.02, 0.06, 0.0)
vmem_bytes = 16 << 20
group = 8


def going(axis, step):
    return [q for q in range(19) if int(velocity_table[q][axis]) == step]


def project(direction, vector):
    projection = 0.0 * vector[0]
    for component in range(3):
        lattice_step = int(velocity_table[direction][component])
        if lattice_step != 0:
            projection = projection + lattice_step * vector[component]
    return projection


def moments(populations):
    density = populations[0]
    momentum = [jnp.zeros_like(density) for component in range(3)]
    for direction in range(1, 19):
        density = density + populations[direction]
        for component in range(3):
            lattice_step = int(velocity_table[direction][component])
            if lattice_step == 1:
                momentum[component] = momentum[component] + populations[direction]
            elif lattice_step == -1:
                momentum[component] = momentum[component] - populations[direction]
    return (density, momentum)


def equilibrium(density, velocity):
    speed_sq = velocity[0] * velocity[0] + velocity[1] * velocity[1] + velocity[2] * velocity[2]
    result = []
    for direction in range(19):
        projected = project(direction, velocity)
        result.append(
            weight_table[direction]
            * density
            * (1.0 + 3.0 * projected + 4.5 * projected * projected - 1.5 * speed_sq)
        )
    return result


far_field = [float(np.float32(value)) for value in equilibrium(1.0, list(far_velocity))]


def collide(populations, cell_force, solid_cells):
    density, momentum = moments(populations)
    velocity = [
        (momentum[component] + 0.5 * cell_force[component]) / density for component in range(3)
    ]
    balance = equilibrium(density, velocity)
    stress = [jnp.zeros_like(density) for pair_pos in range(6)]
    for direction in range(19):
        non_eq = populations[direction] - balance[direction]
        for pair_pos in range(6):
            row_axis, col_axis = stress_pairs[pair_pos]
            factor = int(velocity_table[direction][row_axis] * velocity_table[direction][col_axis])
            if factor != 0:
                stress[pair_pos] = stress[pair_pos] + factor * non_eq
    shear_sq = stress[0] * stress[0] + stress[1] * stress[1] + stress[2] * stress[2]
    shear_sq = shear_sq + 2.0 * (
        stress[3] * stress[3] + stress[4] * stress[4] + stress[5] * stress[5]
    )
    magnitude = jnp.sqrt(shear_sq + regular_eps)
    relax_time = 0.5 * (tau_base + jnp.sqrt(tau_base * tau_base + smag_term * magnitude / density))
    relax_rate = 1.0 / relax_time
    guo_factor = 1.0 - 0.5 * relax_rate
    speed_force = (
        velocity[0] * cell_force[0] + velocity[1] * cell_force[1] + velocity[2] * cell_force[2]
    )
    result = []
    for direction in range(19):
        along_force = project(direction, cell_force)
        along_speed = project(direction, velocity)
        source = (
            guo_factor
            * weight_table[direction]
            * (3.0 * (along_force - speed_force) + 9.0 * along_speed * along_force)
        )
        relaxed = (
            populations[direction]
            - (populations[direction] - balance[direction]) * relax_rate
            + source
        )
        result.append(jnp.where(solid_cells == 1, populations[opposite_table[direction]], relaxed))
    return result


def with_halo(cells, sides, width):
    for axis, dim in sides:
        count = lax.axis_size(axis)
        head = lax.slice_in_dim(cells, 0, width, axis=dim)
        tail = lax.slice_in_dim(cells, cells.shape[dim] - width, cells.shape[dim], axis=dim)
        cells = jnp.concatenate(
            [
                lax.ppermute(tail, axis, [(i, (i + 1) % count) for i in range(count)]),
                cells,
                lax.ppermute(head, axis, [((i + 1) % count, i) for i in range(count)]),
            ],
            axis=dim,
        )
    return cells


def settle(received, labels, owned, train_of_block, marker_area, train_velocity, mark):
    rows_in = received.reshape(-1, 3 * mark)
    label_rows = labels.reshape(-1)
    owner_match = (label_rows[None, :] == jnp.arange(owned, dtype=jnp.int32)[:, None]).astype(
        jnp.float32
    )
    marker_velocity = jnp.dot(owner_match, rows_in, precision=lax.Precision.HIGHEST).reshape(
        owned, 3, mark
    )
    trains = train_velocity.shape[0]
    train_rows = train_of_block.reshape(owned)
    train_match = (train_rows[:, None] == jnp.arange(trains, dtype=jnp.int32)[None, :]).astype(
        jnp.float32
    )
    target = jnp.dot(train_match, train_velocity, precision=lax.Precision.HIGHEST)
    areas = marker_area.reshape(owned, mark)
    marker_force = stiffness * areas[:, None, :] * (target[:, :, None] - marker_velocity)
    back_rows = jnp.dot(
        owner_match.T, marker_force.reshape(owned, 3 * mark), precision=lax.Precision.HIGHEST
    )
    return (marker_force, back_rows)


def per_device_general(
    populations,
    solid_cells,
    slot_cells,
    slot_weights,
    slot_owner,
    slot_block,
    train_of_block,
    marker_area,
    train_velocity,
):
    size_x, size_y, size_z = (populations.shape[1], populations.shape[2], populations.shape[3])
    cell_count = size_x * size_y * size_z
    slots, kernel, mark = (slot_cells.shape[3], slot_cells.shape[4], slot_cells.shape[5])
    owned = train_of_block.shape[3]
    peers_x = lax.axis_size("gx")
    peers_y = lax.axis_size("gy")
    peers = peers_x * peers_y
    capacity = max(2, 2 * slots // peers)
    density, momentum = moments(populations)
    rest_velocity = jnp.stack([momentum[component] / density for component in range(3)]).reshape(
        3, cell_count
    )
    cells = slot_cells.reshape(slots, kernel, mark)
    weights = slot_weights.reshape(slots, kernel, mark)
    partial_value = jnp.sum(rest_velocity[:, cells] * weights[None], axis=2)
    slot_rows = partial_value.transpose(1, 0, 2).reshape(slots, 3 * mark)
    slot_dest = slot_owner.reshape(slots)
    blocks = slot_block.reshape(slots)
    order = jnp.arange(slots, dtype=jnp.int32)
    earlier = (slot_dest[None, :] == slot_dest[:, None]) & (order[None, :] < order[:, None])
    slot_rank = jnp.sum(earlier.astype(jnp.int32), axis=1)
    target_row = slot_dest * capacity + slot_rank
    buffer_rows = jnp.arange(peers * capacity, dtype=jnp.int32)
    matches = buffer_rows[:, None] == target_row[None, :]
    placement = matches.astype(jnp.float32)
    outgoing = jnp.dot(placement, slot_rows, precision=lax.Precision.HIGHEST)
    labels = jnp.sum(jnp.where(matches, blocks[None, :] + 1, 0), axis=1) - 1
    received, got_labels = (
        lax.all_to_all(
            outgoing.reshape(peers, capacity, 3 * mark),
            ("gx", "gy"),
            split_axis=0,
            concat_axis=0,
            tiled=True,
        ),
        lax.all_to_all(
            labels.reshape(peers, capacity), ("gx", "gy"), split_axis=0, concat_axis=0, tiled=True
        ),
    )
    marker_force, back_rows = settle(
        received, got_labels, owned, train_of_block, marker_area, train_velocity, mark
    )
    returned = lax.all_to_all(
        back_rows.reshape(peers, capacity, 3 * mark),
        ("gx", "gy"),
        split_axis=0,
        concat_axis=0,
        tiled=True,
    )
    slot_force = jnp.dot(
        placement.T, returned.reshape(peers * capacity, 3 * mark), precision=lax.Precision.HIGHEST
    )
    slot_force = slot_force.reshape(slots, 3, mark).transpose(1, 0, 2)
    contrib = weights[None] * slot_force[:, :, None, :]
    cell_force = (
        jnp.zeros((3, cell_count), jnp.float32).at[:, cells.reshape(-1)].add(contrib.reshape(3, -1))
    )
    cell_force = cell_force.reshape(3, size_x, size_y, size_z)
    relaxed = collide(populations, cell_force, solid_cells)
    padded = with_halo(jnp.stack(relaxed), (("gx", 1), ("gy", 2), ("gz", 3)), 1)
    parts = []
    for direction in range(19):
        shift_x = 1 - int(velocity_table[direction][0])
        shift_y = 1 - int(velocity_table[direction][1])
        shift_z = 1 - int(velocity_table[direction][2])
        parts.append(
            padded[
                direction,
                shift_x : shift_x + size_x,
                shift_y : shift_y + size_y,
                shift_z : shift_z + size_z,
            ]
        )
    read = jnp.stack(parts)
    total_y = size_y * lax.axis_size("gy")
    total_z = size_z * lax.axis_size("gz")
    global_y = lax.axis_index("gy") * size_y + jnp.arange(size_y, dtype=jnp.int32)
    global_z = lax.axis_index("gz") * size_z + jnp.arange(size_z, dtype=jnp.int32)
    on_side = ((global_y == 0) | (global_y == total_y - 1))[:, None] | (
        (global_z == 0) | (global_z == total_z - 1)
    )[None, :]
    far_field = jnp.array(equilibrium(1.0, list(far_velocity)), dtype=jnp.float32)
    populations_next = jnp.where(on_side[None, None], far_field[:, None, None, None], read)
    return (populations_next, marker_force.reshape(1, 1, 1, owned, 3, mark))


def full(shape):
    return jax.ShapeDtypeStruct(shape, jnp.float32)


def kernel_params():
    return pltpu.CompilerParams(vmem_limit_bytes=vmem_bytes)


def low_half(shape):
    return lax.broadcasted_iota(jnp.int32, shape, 1) < shape[1] // 2


def fetch(pairs, sems):
    copies = [
        pltpu.make_async_copy(source, target, sems.at[i])
        for i, (source, target) in enumerate(pairs)
    ]
    for copy in copies:
        copy.start()
    return copies


def shard_rows(slots, owned):
    return 8 + owned + 3 * slots


def sample_kernel(
    place_ref, pop_any, cells_any, weights_any, areas_any, owner_any, block_any, trains_any,
    out_ref, pop_ref, cells_ref, weights_ref, areas_ref, owner_ref, block_ref, trains_ref,
    table, sems,
):
    rows, lanes = (pop_ref.shape[1], pop_ref.shape[2])
    mark = cells_ref.shape[1]
    owned = areas_ref.shape[0]
    slots = owner_ref.shape[1]
    kernel = cells_ref.shape[0] // slots
    planes = [pl.ds(at, min(5, 19 - at)) for at in range(0, 19, 5)]
    halves = [pl.ds(at, slots * kernel // 2) for at in (0, slots * kernel // 2)]
    copies = fetch(
        (
            *((pop_any.at[part], pop_ref.at[part]) for part in planes),
            *((cells_any.at[part], cells_ref.at[part]) for part in halves),
            *((weights_any.at[part], weights_ref.at[part]) for part in halves),
            (areas_any, areas_ref),
            (owner_any, owner_ref),
            (block_any, block_ref),
            (trains_any, trains_ref),
        ),
        sems,
    )

    for copy in copies[: len(planes)]:
        copy.wait()
    density, momentum = moments([pop_ref[q] for q in range(19)])
    speed = [momentum[c] / density for c in range(3)]
    largest = jnp.maximum(jnp.maximum(jnp.abs(speed[0]), jnp.abs(speed[1])), jnp.abs(speed[2]))
    largest = jnp.max(largest, axis=(0, 1), keepdims=True) + 1e-20
    scale = largest * (1.0 / 32767.0)
    fixed = [(speed[c] * (1.0 / scale) + 32768.5).astype(jnp.int32) for c in range(3)]
    words = jnp.concatenate(
        [
            (fixed[0] << 16) | fixed[1],
            (fixed[2][: rows // 2] << 16) | fixed[2][rows // 2 :],
        ],
        axis=0,
    )
    for r in range(table.shape[0]):
        table[r] = jnp.broadcast_to(words[r : r + 1], (group, lanes))
    for copy in copies[len(planes) :]:
        copy.wait()
    out_ref[8 : 8 + owned, :] = areas_ref[...]
    out_ref[0:8, :] = jnp.zeros((8, mark), jnp.float32)
    ids = (owner_ref[...] * owned + block_ref[...]).astype(jnp.float32)
    out_ref[0:1, :] = jnp.concatenate([ids] * (mark // slots), axis=1)
    out_ref[1:2, 0:owned] = trains_ref[...].astype(jnp.float32)
    mine = lax.broadcasted_iota(jnp.int32, (1, mark), 1) % owned + place_ref[2] * owned
    out_ref[2:3, :] = mine.astype(jnp.float32)

    def body(step, carry):
        first = pl.multiple_of(step * group, group)
        total = [jnp.zeros((group, mark), jnp.float32) for c in range(3)]
        for k in range(kernel):
            at = pl.ds(first * kernel + k, group, stride=kernel)
            cells = cells_ref[at, :]
            lane = cells & (lanes - 1)
            row = cells >> (lanes.bit_length() - 1)
            bits = [(row >> bit) & 1 == 1 for bit in range(rows.bit_length() - 1)]

            def choose(low, level):
                if level < 0:
                    return jnp.take_along_axis(table[low], lane, axis=1, mode="promise_in_bounds")
                lower = choose(low, level - 1)
                return jnp.where(bits[level], choose(low + (1 << level), level - 1), lower)

            pair = choose(0, len(bits) - 1)
            third = choose(rows, len(bits) - 2)
            picked = [
                lax.shift_right_logical(pair, 16),
                pair & 65535,
                jnp.where(bits[-1], third & 65535, lax.shift_right_logical(third, 16)),
            ]
            weight = weights_ref[at, :]
            for c in range(3):
                total[c] = total[c] + weight * (picked[c].astype(jnp.float32) - 32768.0)
        for c in range(3):
            here = pl.ds(pl.multiple_of(8 + owned + c * slots + first, group), group)
            out_ref[here, :] = total[c] * scale
        return carry

    lax.fori_loop(0, slots // group, body, 0)


def sample(place, populations, cells, weights, areas, owner, block, trains):
    smem = pl.BlockSpec(memory_space=pltpu.SMEM)
    hbm = pl.BlockSpec(memory_space=pltpu.HBM)
    vmem = pl.BlockSpec(memory_space=pltpu.VMEM)
    kept = (populations, cells, weights)
    count = shard_rows(owner.shape[1], areas.shape[0])
    return pl.pallas_call(
        sample_kernel,
        out_shape=[full((count, cells.shape[1]))]
        + [jax.ShapeDtypeStruct(entries.shape, entries.dtype) for entries in kept],
        in_specs=[smem] + [hbm] * 7,
        out_specs=[vmem] * 4,
        scratch_shapes=[
            pltpu.VMEM(entries.shape, entries.dtype) for entries in (areas, owner, block, trains)
        ]
        + [
            pltpu.VMEM((populations.shape[1] * 3 // 2, group, populations.shape[2]), jnp.int32),
            pltpu.SemaphoreType.DMA((12,)),
        ],
        compiler_params=kernel_params(),
        name="sample",
    )(place, populations, cells, weights, areas, owner, block, trains)


def three_parts(values):
    parts = []
    for _ in range(3):
        parts.append(values.astype(jnp.bfloat16))
        values = values - parts[-1].astype(jnp.float32)
    return parts


def one_hot(mask):
    return jnp.where(mask, 1.0, 0.0).astype(jnp.bfloat16)


def wanted_labels(own_ref, slots, owned):
    mark = own_ref.shape[1]
    own = own_ref[0:8, :]
    ids, trains, mine = (jnp.broadcast_to(own[i : i + 1], (mark, mark)).T for i in range(3))
    return (ids[0:slots], mine[0:owned], trains[0:owned])


def add_shards(totals, shards, ids, mine):
    slots, owned = (ids.shape[0], mine.shape[0])
    wanted = jnp.concatenate([ids, mine], axis=0)
    for shard in shards:
        match = one_hot(wanted == shard[0:1, :])
        match = jnp.concatenate([match, match[:, 0:slots]], axis=1)
        starts = [8 + owned + c * slots for c in range(3)]
        values = jnp.concatenate([shard[at : at + slots, :] for at in starts], axis=1)
        sums = jnp.dot(
            match, jnp.concatenate(three_parts(values), axis=0), preferred_element_type=jnp.float32
        )
        held = ids == shard[2:3, :]
        parts = three_parts(shard[8 : 8 + owned, :])
        parts.append(jnp.zeros_like(parts[0]))
        area = jnp.dot(
            one_hot(held), jnp.concatenate(parts, axis=0), preferred_element_type=jnp.float32
        )
        got = (sums, area, jnp.where(held, shard[1:2, :], 0.0))
        totals = got if totals is None else [total + new for total, new in zip(totals, got)]
    return totals


def settle_kernel(slots, owned, speeds_ref, *refs):
    *shards, sums_ref, area_ref, trains_ref, rows_ref = refs
    mark = rows_ref.shape[1]
    for train in range(speeds_ref.shape[0]):
        for c in range(3):
            at = 3 * train + c
            rows_ref[at : at + 1, :] = jnp.full((1, mark), speeds_ref[train, c], jnp.float32)
    ids, mine, _ = wanted_labels(shards[0], slots, owned)
    sums_ref[...], area_ref[...], trains_ref[...] = add_shards(None, shards, ids, mine)


def settle_early(slots, owned, speeds, shards):
    mark = shards[0].shape[1]
    smem = pl.BlockSpec(memory_space=pltpu.SMEM)
    vmem = pl.BlockSpec(memory_space=pltpu.VMEM)
    return pl.pallas_call(
        functools.partial(settle_kernel, slots, owned),
        out_shape=(
            full((slots + owned, 3 * mark)),
            full((slots, mark)),
            full((slots, mark)),
            full((3 * speeds.shape[0], mark)),
        ),
        in_specs=[smem] + [vmem] * len(shards),
        compiler_params=kernel_params(),
        cost_estimate=pl.CostEstimate(
            flops=10**9, bytes_accessed=len(shards) * shards[0].size * 4, transcendentals=0
        ),
        name="settle",
    )(speeds, *shards)


def block_forces(rows_ref, totals, own_ref, slots, owned):
    mark = own_ref.shape[1]
    ids, mine, own_trains = wanted_labels(own_ref, slots, owned)
    sums, area, trains = totals
    trains = jnp.broadcast_to(jnp.sum(trains, axis=1, keepdims=True), area.shape)
    own_area = own_ref[8 : 8 + owned, :]
    forces, own_forces = ([], [])
    for c in range(3):
        target, own_target = (jnp.zeros_like(area), jnp.zeros_like(own_area))
        for train in range(rows_ref.shape[0] // 3):
            at = 3 * train + c
            speed = rows_ref[at : at + 1, :]
            target = jnp.where(trains == float(train), speed, target)
            own_target = jnp.where(own_trains == float(train), speed, own_target)
        got = sums[:, c * mark : (c + 1) * mark]
        forces.append(stiffness * area * (target - got[0:slots]))
        own_forces.append(stiffness * own_area * (own_target - got[slots:]))
    return (forces, own_forces)


def spread_kernel(
    slots, owned, place_ref, own_ref, last_ref, sums_ref, area_ref, trains_ref, speeds_ref,
    cells_ref, weights_ref, pop_ref, solid_ref,
    relaxed_ref, far_ref, near_ref, side_ref, marker_any, marker_ref, force_ref, lines_ref, acc,
    sem,
):
    rows, lanes = (pop_ref.shape[1], pop_ref.shape[2])
    size_y = 8
    mark = cells_ref.shape[1]
    kernel = cells_ref.shape[0] // slots
    bf = jnp.bfloat16
    ids, mine, _ = wanted_labels(own_ref, slots, owned)
    totals = add_shards((sums_ref[...], area_ref[...], trains_ref[...]), [last_ref], ids, mine)
    forces, own_forces = block_forces(speeds_ref, totals, own_ref, slots, owned)
    for c in range(3):
        force_ref[c] = forces[c]
        marker_ref[c] = own_forces[c]
    marker_copy = pltpu.make_async_copy(marker_ref, marker_any, sem)
    marker_copy.start()

    acc[...] = jnp.zeros_like(acc)
    iota = lax.broadcasted_iota(jnp.int32, (16, mark), 0).astype(jnp.float32)
    steps = [(iota + 16.0 * j).astype(bf) for j in range(max(rows, lanes) // 16)]
    one, zero = (jnp.ones((16, mark), bf), jnp.zeros((16, mark), bf))

    def body(step, carry):
        first = pl.multiple_of(step * group, group)
        force = [force_ref[c, pl.ds(first, group), :] for c in range(3)]
        left, right = ([], [])
        for k in range(kernel):
            at = pl.ds(first * kernel + k, group, stride=kernel)
            cells = cells_ref[at, :]
            weight = weights_ref[at, :]
            lane = (cells & (lanes - 1)).astype(jnp.float32)
            row = (cells >> (lanes.bit_length() - 1)).astype(jnp.float32)
            parts = []
            for c in range(3):
                value = weight * force[c]
                high = value.astype(bf).astype(jnp.float32)
                parts += [high, value - high]
            for which, entries in enumerate([lane, row] + parts):
                lines_ref[k, which] = entries

            def wide(which, i, k=k):
                entries = lines_ref[k, which, pl.ds(i, 8, stride=0), :]
                return jnp.concatenate([entries, entries], axis=0).astype(bf)

            for i in range(group):
                lane_i, row_i = (wide(0, i), wide(1, i))
                right.append(
                    jnp.concatenate(
                        [jnp.where(steps[j] == lane_i, one, zero) for j in range(lanes // 16)],
                        axis=0,
                    )
                )
                masks = [steps[j] == row_i for j in range(rows // 16)]
                pieces = []
                for which in range(len(parts)):
                    part_i = wide(2 + which, i)
                    pieces += [jnp.where(mask, part_i, zero) for mask in masks]
                left.append(jnp.concatenate(pieces, axis=0))
        acc[...] += lax.dot_general(
            jnp.concatenate(left, axis=1),
            jnp.concatenate(right, axis=1),
            (((1,), (1,)), ((), ())),
            preferred_element_type=jnp.float32,
        )
        return carry

    lax.fori_loop(0, slots // group, body, 0)
    cell_force = [
        acc[2 * c * rows : (2 * c + 1) * rows, :] + acc[(2 * c + 1) * rows : (2 * c + 2) * rows, :]
        for c in range(3)
    ]
    relaxed = collide([pop_ref[q] for q in range(19)], cell_force, solid_ref[...])
    for q in range(19):
        relaxed_ref[q] = relaxed[q]
    even = place_ref[3] == 0
    for i in range(5):
        ahead = relaxed[going(0, 1)[i]][rows - size_y :]
        behind = relaxed[going(0, -1)[i]][:size_y]
        far_ref[i] = jnp.where(even, behind, ahead)
        near_ref[i] = jnp.where(even, ahead, behind)
        for x in range(rows // size_y):
            up = relaxed[going(1, 1)[i]][size_y * x + size_y - 1 : size_y * x + size_y, :]
            down = relaxed[going(1, -1)[i]][size_y * x : size_y * x + 1, :]
            at = rows // size_y * i + x
            side_ref[at : at + 1, :] = jnp.where(place_ref[0] == 0, up, down)
    marker_copy.wait()


def spread(owned, place, own, last, early, cells, weights, populations, solid):
    mark = cells.shape[1]
    slots = early[1].shape[0]
    line_count, lanes = solid.shape
    smem = pl.BlockSpec(memory_space=pltpu.SMEM)
    vmem = pl.BlockSpec(memory_space=pltpu.VMEM)
    return pl.pallas_call(
        functools.partial(spread_kernel, slots, owned),
        out_shape=(
            full(populations.shape),
            full((5, 8, lanes)),
            full((5, 8, lanes)),
            full((24, lanes)),
            full((3, owned, mark)),
        ),
        in_specs=[smem] + [vmem] * 10,
        out_specs=[vmem] * 4 + [pl.BlockSpec(memory_space=pltpu.HBM)],
        scratch_shapes=[
            pltpu.VMEM((3, owned, mark), jnp.float32),
            pltpu.VMEM((3, slots, mark), jnp.float32),
            pltpu.VMEM((cells.shape[0] // slots, 8, group, mark), jnp.float32),
            pltpu.VMEM((6 * line_count, lanes), jnp.float32),
            pltpu.SemaphoreType.DMA,
        ],
        compiler_params=kernel_params(),
        name="spread",
    )(place, own, last, *early, cells, weights, populations, solid)


def downwind(place_ref, relaxed_ref, far_ref, near_ref):
    size_y = far_ref.shape[1]
    size_x = relaxed_ref.shape[1] // size_y
    even = place_ref[3] == 0

    def cells(q, x):
        step = int(velocity_table[q][0])
        source = x - step
        if 0 <= source < size_x:
            return relaxed_ref[q, source * size_y : (source + 1) * size_y, :]
        i = going(0, step).index(q)
        if step == 1:
            return jnp.where(even, far_ref[i], near_ref[i])
        return jnp.where(even, near_ref[i], far_ref[i])

    return cells


def sideways(cells, side_ref, edge):
    def result(q, x, y_at):
        step_x, step_y = (int(step) for step in velocity_table[q][:2])
        size_y = y_at.shape[0]
        size_x = side_ref.shape[0] // 6
        if step_y == 0:
            return cells(q, x)
        source = x - step_x
        at = size_x * going(1, step_y).index(q) + source
        halo = side_ref[at : at + 1, :] if 0 <= source < size_x else edge(q)
        turned = pltpu.roll(cells(q, x), step_y % size_y, 0)
        return jnp.where(y_at == (0 if step_y == 1 else size_y - 1), halo, turned)

    return result


def corner_index(q):
    step_y = int(velocity_table[q][1])
    return [p for p in going(1, step_y) if int(velocity_table[p][0]) != 0].index(q)


def pack_kernel(
    place_ref, relaxed_ref, far_ref, near_ref, side_ref, corner_ref, first_ref, second_ref
):
    size_y, lanes = far_ref.shape[1:]
    size_x = relaxed_ref.shape[1] // size_y
    cells = downwind(place_ref, relaxed_ref, far_ref, near_ref)
    corner_ref[...] = jnp.zeros(corner_ref.shape, jnp.float32)
    for ahead in going(1, 1):
        step_x = int(velocity_table[ahead][0])
        if step_x == 0:
            continue
        behind = opposite_table[ahead]
        up = cells(ahead, 0 if step_x == 1 else size_x - 1)[size_y - 1 : size_y, :]
        down = cells(behind, size_x - 1 if step_x == 1 else 0)[0:1, :]
        at = corner_index(ahead)
        from_behind = corner_index(behind)
        lower = place_ref[0] == 0

        @pl.when(lower)
        def _(at=at, up=up):
            corner_ref[at : at + 1, :] = up

        @pl.when(jnp.logical_not(lower))
        def _(at=from_behind, down=down):
            corner_ref[at : at + 1, :] = down

    y_at = lax.broadcasted_iota(jnp.int32, (size_y, lanes), 0)
    lane_at = lax.broadcasted_iota(jnp.int32, (size_y, lanes), 1)
    level = sideways(cells, side_ref, None)
    packs = []
    for step in (1, -1):
        packed = jnp.zeros((size_y, lanes), jnp.float32)
        for i, q in enumerate(going(2, step)):
            edge = lanes - 1 if step == 1 else 0
            for x in range(size_x):
                at = 8 * x + i
                moved = pltpu.roll(level(q, x, y_at), (at - edge) % lanes, 1)
                packed = jnp.where(lane_at == at, moved, packed)
        packs.append(packed)
    even = place_ref[1] % 2 == 0
    first_ref[...] = jnp.where(even, packs[0], packs[1])
    second_ref[...] = jnp.where(even, packs[1], packs[0])


def pack(place, relaxed, far, near, side):
    smem = pl.BlockSpec(memory_space=pltpu.SMEM)
    vmem = pl.BlockSpec(memory_space=pltpu.VMEM)
    edge = full(far.shape[1:])
    return pl.pallas_call(
        pack_kernel,
        out_shape=(edge, edge, edge),
        in_specs=[smem] + [vmem] * 4,
        compiler_params=kernel_params(),
        name="pack",
    )(place, relaxed, far, near, side)


def stream_kernel(
    count_z, place_ref, relaxed_ref, far_ref, near_ref, side_ref, second_ref, corner_ref,
    first_ref, out_any, out_ref, sems,
):
    size_x, size_y, lanes = out_ref.shape[1:]
    shape = (size_y, lanes)
    y_at = lax.broadcasted_iota(jnp.int32, shape, 0)
    z_at = lax.broadcasted_iota(jnp.int32, shape, 1)
    y_index, z_index = (place_ref[0], place_ref[1])
    streamed = sideways(
        downwind(place_ref, relaxed_ref, far_ref, near_ref),
        side_ref,
        lambda q: corner_ref[corner_index(q) : corner_index(q) + 1, :],
    )
    even = z_index % 2 == 0
    columns = {
        -1: jnp.where(even, first_ref[...], second_ref[...]),
        1: jnp.where(even, second_ref[...], first_ref[...]),
    }
    on_side = y_at == jnp.where(y_index == 0, 0, size_y - 1)
    on_side = on_side | ((z_at == 0) & (z_index == 0))
    on_side = on_side | ((z_at == lanes - 1) & (z_index == count_z - 1))
    copies = []
    for q in range(19):
        step_z = int(velocity_table[q][2])
        z_edge = 0 if step_z == 1 else lanes - 1
        for x in range(size_x):
            cells = streamed(q, x, y_at)
            if step_z != 0:
                at = 8 * x + going(2, step_z).index(q)
                cells = jnp.where(
                    z_at == z_edge,
                    pltpu.roll(columns[step_z], (z_edge - at) % lanes, 1),
                    pltpu.roll(cells, step_z % lanes, 1),
                )
            out_ref[q, x] = jnp.where(on_side, far_field[q], cells)
        copies.append(pltpu.make_async_copy(out_ref.at[q], out_any.at[q], sems.at[q]))
        copies[-1].start()
    for copy in copies:
        copy.wait()


def stream(count_z, place, relaxed, *halos):
    rows, lanes = relaxed.shape[1:]
    size_y = halos[0].shape[1]
    smem = pl.BlockSpec(memory_space=pltpu.SMEM)
    vmem = pl.BlockSpec(memory_space=pltpu.VMEM)
    shape = (19, rows // size_y, size_y, lanes)
    return pl.pallas_call(
        functools.partial(stream_kernel, count_z),
        out_shape=full(shape),
        in_specs=[smem] + [vmem] * (1 + len(halos)),
        out_specs=pl.BlockSpec(memory_space=pltpu.HBM),
        scratch_shapes=[pltpu.VMEM(shape, jnp.float32), pltpu.SemaphoreType.DMA((19,))],
        compiler_params=kernel_params(),
        name="stream",
    )(place, relaxed, *halos)


def per_device(
    populations,
    solid_cells,
    slot_cells,
    slot_weights,
    slot_owner,
    slot_block,
    train_of_block,
    marker_area,
    train_velocity,
):
    size_x, size_y, size_z = (populations.shape[1], populations.shape[2], populations.shape[3])
    lines = size_x * size_y
    slots, kernel, mark = (slot_cells.shape[3], slot_cells.shape[4], slot_cells.shape[5])
    owned = train_of_block.shape[3]
    count_x, count_y, count_z = (lax.axis_size(axis) for axis in ("gx", "gy", "gz"))
    x_index, y_index, z_index = (lax.axis_index(axis) for axis in ("gx", "gy", "gz"))
    place = jnp.stack([y_index, z_index, x_index * count_y + y_index, x_index % 2])
    place = place.astype(jnp.int32)
    inputs = [
        pltpu.with_memory_space_constraint(entries, pltpu.HBM)
        for entries in (
            populations.reshape(19, lines, size_z),
            slot_cells.reshape(slots * kernel, mark),
            slot_weights.reshape(slots * kernel, mark),
            marker_area.reshape(owned, mark),
            slot_owner.reshape(1, slots),
            slot_block.reshape(1, slots),
            train_of_block.reshape(1, owned),
        )
    ]
    own, pops, cells, weights = sample(place, *inputs)
    swap = [(0, 1), (1, 0)]

    def across_x(entries, distance):
        return lax.ppermute(entries, "gx", [(i, i ^ distance) for i in range(count_x)])

    def across_y(entries):
        return lax.ppermute(entries, "gy", swap)

    third, first = (across_x(own, distance) for distance in (3, 1))
    beside = across_y(own)
    third_beside = across_y(lax.optimization_barrier((third, beside))[0])
    second = across_x(third, 1)
    first_beside = across_y(first)
    last = across_x(third_beside, 1)
    whole = [own, first, third, second, beside, first_beside, third_beside]
    early = settle_early(slots, owned, train_velocity, whole)
    solid = solid_cells.reshape(lines, size_z)
    relaxed, far, near, side, marker_force = spread(
        owned, place, own, last, early, cells, weights, pops, solid
    )
    evens = range(0, count_x, 2)
    far = lax.ppermute(
        far,
        "gx",
        [(i, (i - 1) % count_x) for i in evens] + [((i - 1) % count_x, i) for i in evens],
    )
    near = lax.ppermute(near, "gx", [(i, i + 1) for i in evens] + [(i + 1, i) for i in evens])
    side = across_y(side)
    corner, up_first, down_first = pack(place, relaxed, far, near, side)
    inner = [(i, i + 1) for i in range(0, count_z - 1, 2)]
    outer = [(i, i + 1) for i in range(1, count_z - 1, 2)]
    down_first = lax.ppermute(down_first, "gz", outer + [(j, i) for i, j in outer])
    corner = across_y(corner)
    up_first = lax.ppermute(up_first, "gz", inner + [(j, i) for i, j in inner])
    populations_next = stream(
        count_z, place, relaxed, far, near, side, down_first, corner, up_first
    )
    marker_force = marker_force.transpose(1, 0, 2).reshape(1, 1, 1, owned, 3, mark)
    return (populations_next, marker_force)


def solution(mesh):
    placed = (
        P(None, "gx", "gy", "gz"),
        P("gx", "gy", "gz"),
        P("gx", "gy", "gz", None, None, None),
        P("gx", "gy", "gz", None, None, None),
        P("gx", "gy", "gz", None, None),
        P("gx", "gy", "gz", None),
        P("gx", "gy", "gz", None),
        P("gx", "gy", "gz", None, None),
        P(),
    )
    small = mesh.shape["gy"] == 2 and mesh.shape["gx"] == 4 and mesh.shape["gz"] % 2 == 0
    return jax.shard_map(
        per_device if small else per_device_general,
        mesh=mesh,
        in_specs=placed,
        out_specs=(P(None, "gx", "gy", "gz"), P("gx", "gy", "gz", None, None, None)),
        check_vma=False,
    )
```

```python
import functools
import jax
import jax.numpy as jnp
import numpy as np
from jax import lax
from jax.experimental import pallas as pl
from jax.experimental.pallas import tpu as pltpu
from jax.sharding import PartitionSpec as P

velocity_table = np.array(
    [
        [0, 0, 0],
        [1, 0, 0],
        [-1, 0, 0],
        [0, 1, 0],
        [0, -1, 0],
        [0, 0, 1],
        [0, 0, -1],
        [1, 1, 0],
        [-1, -1, 0],
        [1, -1, 0],
        [-1, 1, 0],
        [1, 0, 1],
        [-1, 0, -1],
        [1, 0, -1],
        [-1, 0, 1],
        [0, 1, 1],
        [0, -1, -1],
        [0, 1, -1],
        [0, -1, 1],
    ]
)
weight_table = [1.0 / 3.0] + [1.0 / 18.0] * 6 + [1.0 / 36.0] * 12
opposite_table = [0, 2, 1, 4, 3, 6, 5, 8, 7, 10, 9, 12, 11, 14, 13, 16, 15, 18, 17]
stress_pairs = [(0, 0), (1, 1), (2, 2), (0, 1), (0, 2), (1, 2)]
tau_base = 0.55
smag_term = 18.0 * 1.4142135623730951 * 0.17 * 0.17
regular_eps = 0.0001
stiffness = 2.0
far_velocity = (0.02, 0.06, 0.0)
vmem_bytes = 16 << 20
group = 8


def going(axis, step):
    return [q for q in range(19) if int(velocity_table[q][axis]) == step]


def project(direction, vector):
    projection = 0.0 * vector[0]
    for component in range(3):
        lattice_step = int(velocity_table[direction][component])
        if lattice_step != 0:
            projection = projection + lattice_step * vector[component]
    return projection


def moments(populations):
    density = populations[0]
    momentum = [jnp.zeros_like(density) for component in range(3)]
    for direction in range(1, 19):
        density = density + populations[direction]
        for component in range(3):
            lattice_step = int(velocity_table[direction][component])
            if lattice_step == 1:
                momentum[component] = momentum[component] + populations[direction]
            elif lattice_step == -1:
                momentum[component] = momentum[component] - populations[direction]
    return (density, momentum)


def equilibrium(density, velocity):
    speed_sq = velocity[0] * velocity[0] + velocity[1] * velocity[1] + velocity[2] * velocity[2]
    result = []
    for direction in range(19):
        projected = project(direction, velocity)
        result.append(
            weight_table[direction]
            * density
            * (1.0 + 3.0 * projected + 4.5 * projected * projected - 1.5 * speed_sq)
        )
    return result


far_field = [float(np.float32(value)) for value in equilibrium(1.0, list(far_velocity))]


def collide(populations, cell_force, solid_cells):
    density, momentum = moments(populations)
    velocity = [
        (momentum[component] + 0.5 * cell_force[component]) / density for component in range(3)
    ]
    balance = equilibrium(density, velocity)
    stress = [jnp.zeros_like(density) for pair_pos in range(6)]
    for direction in range(19):
        non_eq = populations[direction] - balance[direction]
        for pair_pos in range(6):
            row_axis, col_axis = stress_pairs[pair_pos]
            factor = int(velocity_table[direction][row_axis] * velocity_table[direction][col_axis])
            if factor != 0:
                stress[pair_pos] = stress[pair_pos] + factor * non_eq
    shear_sq = stress[0] * stress[0] + stress[1] * stress[1] + stress[2] * stress[2]
    shear_sq = shear_sq + 2.0 * (
        stress[3] * stress[3] + stress[4] * stress[4] + stress[5] * stress[5]
    )
    magnitude = jnp.sqrt(shear_sq + regular_eps)
    relax_time = 0.5 * (tau_base + jnp.sqrt(tau_base * tau_base + smag_term * magnitude / density))
    relax_rate = 1.0 / relax_time
    guo_factor = 1.0 - 0.5 * relax_rate
    speed_force = (
        velocity[0] * cell_force[0] + velocity[1] * cell_force[1] + velocity[2] * cell_force[2]
    )
    result = []
    for direction in range(19):
        along_force = project(direction, cell_force)
        along_speed = project(direction, velocity)
        source = (
            guo_factor
            * weight_table[direction]
            * (3.0 * (along_force - speed_force) + 9.0 * along_speed * along_force)
        )
        relaxed = (
            populations[direction]
            - (populations[direction] - balance[direction]) * relax_rate
            + source
        )
        result.append(jnp.where(solid_cells == 1, populations[opposite_table[direction]], relaxed))
    return result


def with_halo(cells, sides, width):
    for axis, dim in sides:
        count = lax.axis_size(axis)
        head = lax.slice_in_dim(cells, 0, width, axis=dim)
        tail = lax.slice_in_dim(cells, cells.shape[dim] - width, cells.shape[dim], axis=dim)
        cells = jnp.concatenate(
            [
                lax.ppermute(tail, axis, [(i, (i + 1) % count) for i in range(count)]),
                cells,
                lax.ppermute(head, axis, [((i + 1) % count, i) for i in range(count)]),
            ],
            axis=dim,
        )
    return cells


def settle(received, labels, owned, train_of_block, marker_area, train_velocity, mark):
    rows_in = received.reshape(-1, 3 * mark)
    label_rows = labels.reshape(-1)
    owner_match = (label_rows[None, :] == jnp.arange(owned, dtype=jnp.int32)[:, None]).astype(
        jnp.float32
    )
    marker_velocity = jnp.dot(owner_match, rows_in, precision=lax.Precision.HIGHEST).reshape(
        owned, 3, mark
    )
    trains = train_velocity.shape[0]
    train_rows = train_of_block.reshape(owned)
    train_match = (train_rows[:, None] == jnp.arange(trains, dtype=jnp.int32)[None, :]).astype(
        jnp.float32
    )
    target = jnp.dot(train_match, train_velocity, precision=lax.Precision.HIGHEST)
    areas = marker_area.reshape(owned, mark)
    marker_force = stiffness * areas[:, None, :] * (target[:, :, None] - marker_velocity)
    back_rows = jnp.dot(
        owner_match.T, marker_force.reshape(owned, 3 * mark), precision=lax.Precision.HIGHEST
    )
    return (marker_force, back_rows)


def per_device_general(
    populations,
    solid_cells,
    slot_cells,
    slot_weights,
    slot_owner,
    slot_block,
    train_of_block,
    marker_area,
    train_velocity,
):
    size_x, size_y, size_z = (populations.shape[1], populations.shape[2], populations.shape[3])
    cell_count = size_x * size_y * size_z
    slots, kernel, mark = (slot_cells.shape[3], slot_cells.shape[4], slot_cells.shape[5])
    owned = train_of_block.shape[3]
    peers_x = lax.axis_size("gx")
    peers_y = lax.axis_size("gy")
    peers = peers_x * peers_y
    capacity = max(2, 2 * slots // peers)
    density, momentum = moments(populations)
    rest_velocity = jnp.stack([momentum[component] / density for component in range(3)]).reshape(
        3, cell_count
    )
    cells = slot_cells.reshape(slots, kernel, mark)
    weights = slot_weights.reshape(slots, kernel, mark)
    partial_value = jnp.sum(rest_velocity[:, cells] * weights[None], axis=2)
    slot_rows = partial_value.transpose(1, 0, 2).reshape(slots, 3 * mark)
    slot_dest = slot_owner.reshape(slots)
    blocks = slot_block.reshape(slots)
    order = jnp.arange(slots, dtype=jnp.int32)
    earlier = (slot_dest[None, :] == slot_dest[:, None]) & (order[None, :] < order[:, None])
    slot_rank = jnp.sum(earlier.astype(jnp.int32), axis=1)
    target_row = slot_dest * capacity + slot_rank
    buffer_rows = jnp.arange(peers * capacity, dtype=jnp.int32)
    matches = buffer_rows[:, None] == target_row[None, :]
    placement = matches.astype(jnp.float32)
    outgoing = jnp.dot(placement, slot_rows, precision=lax.Precision.HIGHEST)
    labels = jnp.sum(jnp.where(matches, blocks[None, :] + 1, 0), axis=1) - 1
    received, got_labels = (
        lax.all_to_all(
            outgoing.reshape(peers, capacity, 3 * mark),
            ("gx", "gy"),
            split_axis=0,
            concat_axis=0,
            tiled=True,
        ),
        lax.all_to_all(
            labels.reshape(peers, capacity), ("gx", "gy"), split_axis=0, concat_axis=0, tiled=True
        ),
    )
    marker_force, back_rows = settle(
        received, got_labels, owned, train_of_block, marker_area, train_velocity, mark
    )
    returned = lax.all_to_all(
        back_rows.reshape(peers, capacity, 3 * mark),
        ("gx", "gy"),
        split_axis=0,
        concat_axis=0,
        tiled=True,
    )
    slot_force = jnp.dot(
        placement.T, returned.reshape(peers * capacity, 3 * mark), precision=lax.Precision.HIGHEST
    )
    slot_force = slot_force.reshape(slots, 3, mark).transpose(1, 0, 2)
    contrib = weights[None] * slot_force[:, :, None, :]
    cell_force = (
        jnp.zeros((3, cell_count), jnp.float32).at[:, cells.reshape(-1)].add(contrib.reshape(3, -1))
    )
    cell_force = cell_force.reshape(3, size_x, size_y, size_z)
    relaxed = collide(populations, cell_force, solid_cells)
    padded = with_halo(jnp.stack(relaxed), (("gx", 1), ("gy", 2), ("gz", 3)), 1)
    parts = []
    for direction in range(19):
        shift_x = 1 - int(velocity_table[direction][0])
        shift_y = 1 - int(velocity_table[direction][1])
        shift_z = 1 - int(velocity_table[direction][2])
        parts.append(
            padded[
                direction,
                shift_x : shift_x + size_x,
                shift_y : shift_y + size_y,
                shift_z : shift_z + size_z,
            ]
        )
    read = jnp.stack(parts)
    total_y = size_y * lax.axis_size("gy")
    total_z = size_z * lax.axis_size("gz")
    global_y = lax.axis_index("gy") * size_y + jnp.arange(size_y, dtype=jnp.int32)
    global_z = lax.axis_index("gz") * size_z + jnp.arange(size_z, dtype=jnp.int32)
    on_side = ((global_y == 0) | (global_y == total_y - 1))[:, None] | (
        (global_z == 0) | (global_z == total_z - 1)
    )[None, :]
    far_field = jnp.array(equilibrium(1.0, list(far_velocity)), dtype=jnp.float32)
    populations_next = jnp.where(on_side[None, None], far_field[:, None, None, None], read)
    return (populations_next, marker_force.reshape(1, 1, 1, owned, 3, mark))


def full(shape):
    return jax.ShapeDtypeStruct(shape, jnp.float32)


def kernel_params():
    return pltpu.CompilerParams(vmem_limit_bytes=vmem_bytes)


def low_half(shape):
    return lax.broadcasted_iota(jnp.int32, shape, 1) < shape[1] // 2


def fetch(pairs, sems):
    copies = [
        pltpu.make_async_copy(source, target, sems.at[i])
        for i, (source, target) in enumerate(pairs)
    ]
    for copy in copies:
        copy.start()
    return copies


def shard_rows(slots, owned):
    return 8 + owned + 3 * slots


def sample_kernel(
    place_ref, pop_any, cells_any, weights_any, areas_any, owner_any, block_any, trains_any,
    out_ref, pop_ref, cells_ref, weights_ref, areas_ref, owner_ref, block_ref, trains_ref,
    table, sems,
):
    rows, lanes = (pop_ref.shape[1], pop_ref.shape[2])
    mark = cells_ref.shape[1]
    owned = areas_ref.shape[0]
    slots = owner_ref.shape[1]
    kernel = cells_ref.shape[0] // slots
    copies = fetch(
        (
            (pop_any, pop_ref),
            (cells_any, cells_ref),
            (weights_any, weights_ref),
            (areas_any, areas_ref),
            (owner_any, owner_ref),
            (block_any, block_ref),
            (trains_any, trains_ref),
        ),
        sems,
    )

    copies[0].wait()
    density, momentum = moments([pop_ref[q] for q in range(19)])
    speed = [momentum[c] / density for c in range(3)]
    largest = jnp.maximum(jnp.maximum(jnp.abs(speed[0]), jnp.abs(speed[1])), jnp.abs(speed[2]))
    largest = jnp.max(largest, axis=(0, 1), keepdims=True) + 1e-20
    scale = largest * (1.0 / 32767.0)
    fixed = [(speed[c] * (1.0 / scale) + 32768.5).astype(jnp.int32) for c in range(3)]
    words = jnp.concatenate(
        [
            (fixed[0] << 16) | fixed[1],
            (fixed[2][: rows // 2] << 16) | fixed[2][rows // 2 :],
        ],
        axis=0,
    )
    for r in range(table.shape[0]):
        table[r] = jnp.broadcast_to(words[r : r + 1], (group, lanes))
    for copy in copies[1:]:
        copy.wait()
    out_ref[8 : 8 + owned, :] = areas_ref[...]
    out_ref[0:8, :] = jnp.zeros((8, mark), jnp.float32)
    ids = (owner_ref[...] * owned + block_ref[...]).astype(jnp.float32)
    out_ref[0:1, :] = jnp.concatenate([ids] * (mark // slots), axis=1)
    out_ref[1:2, 0:owned] = trains_ref[...].astype(jnp.float32)
    mine = lax.broadcasted_iota(jnp.int32, (1, mark), 1) % owned + place_ref[2] * owned
    out_ref[2:3, :] = mine.astype(jnp.float32)

    def body(step, carry):
        first = pl.multiple_of(step * group, group)
        total = [jnp.zeros((group, mark), jnp.float32) for c in range(3)]
        for k in range(kernel):
            at = pl.ds(first * kernel + k, group, stride=kernel)
            cells = cells_ref[at, :]
            lane = cells & (lanes - 1)
            row = cells >> (lanes.bit_length() - 1)
            bits = [(row >> bit) & 1 == 1 for bit in range(rows.bit_length() - 1)]

            def choose(low, level):
                if level < 0:
                    return jnp.take_along_axis(table[low], lane, axis=1, mode="promise_in_bounds")
                lower = choose(low, level - 1)
                return jnp.where(bits[level], choose(low + (1 << level), level - 1), lower)

            pair = choose(0, len(bits) - 1)
            third = choose(rows, len(bits) - 2)
            picked = [
                lax.shift_right_logical(pair, 16),
                pair & 65535,
                jnp.where(bits[-1], third & 65535, lax.shift_right_logical(third, 16)),
            ]
            weight = weights_ref[at, :]
            for c in range(3):
                total[c] = total[c] + weight * (picked[c].astype(jnp.float32) - 32768.0)
        for c in range(3):
            here = pl.ds(pl.multiple_of(8 + owned + c * slots + first, group), group)
            out_ref[here, :] = total[c] * scale
        return carry

    lax.fori_loop(0, slots // group, body, 0)


def sample(place, populations, cells, weights, areas, owner, block, trains):
    smem = pl.BlockSpec(memory_space=pltpu.SMEM)
    hbm = pl.BlockSpec(memory_space=pltpu.HBM)
    vmem = pl.BlockSpec(memory_space=pltpu.VMEM)
    kept = (populations, cells, weights)
    count = shard_rows(owner.shape[1], areas.shape[0])
    return pl.pallas_call(
        sample_kernel,
        out_shape=[full((count, cells.shape[1]))]
        + [jax.ShapeDtypeStruct(entries.shape, entries.dtype) for entries in kept],
        in_specs=[smem] + [hbm] * 7,
        out_specs=[vmem] * 4,
        scratch_shapes=[
            pltpu.VMEM(entries.shape, entries.dtype) for entries in (areas, owner, block, trains)
        ]
        + [
            pltpu.VMEM((populations.shape[1] * 3 // 2, group, populations.shape[2]), jnp.int32),
            pltpu.SemaphoreType.DMA((7,)),
        ],
        compiler_params=kernel_params(),
        name="sample",
    )(place, populations, cells, weights, areas, owner, block, trains)


def three_parts(values):
    parts = []
    for _ in range(3):
        parts.append(values.astype(jnp.bfloat16))
        values = values - parts[-1].astype(jnp.float32)
    return parts


def one_hot(mask):
    return jnp.where(mask, 1.0, 0.0).astype(jnp.bfloat16)


def wanted_labels(own_ref, slots, owned):
    mark = own_ref.shape[1]
    own = own_ref[0:8, :]
    ids, trains, mine = (jnp.broadcast_to(own[i : i + 1], (mark, mark)).T for i in range(3))
    return (ids[0:slots], mine[0:owned], trains[0:owned])


def add_shards(totals, shards, ids, mine):
    slots, owned = (ids.shape[0], mine.shape[0])
    wanted = jnp.concatenate([ids, mine], axis=0)
    for shard in shards:
        match = one_hot(wanted == shard[0:1, :])
        match = jnp.concatenate([match, match[:, 0:slots]], axis=1)
        starts = [8 + owned + c * slots for c in range(3)]
        values = jnp.concatenate([shard[at : at + slots, :] for at in starts], axis=1)
        sums = jnp.dot(
            match, jnp.concatenate(three_parts(values), axis=0), preferred_element_type=jnp.float32
        )
        held = ids == shard[2:3, :]
        parts = three_parts(shard[8 : 8 + owned, :])
        parts.append(jnp.zeros_like(parts[0]))
        area = jnp.dot(
            one_hot(held), jnp.concatenate(parts, axis=0), preferred_element_type=jnp.float32
        )
        got = (sums, area, jnp.where(held, shard[1:2, :], 0.0))
        totals = got if totals is None else [total + new for total, new in zip(totals, got)]
    return totals


def settle_kernel(slots, owned, speeds_ref, *refs):
    *shards, sums_ref, area_ref, trains_ref, rows_ref = refs
    mark = rows_ref.shape[1]
    for train in range(speeds_ref.shape[0]):
        for c in range(3):
            at = 3 * train + c
            rows_ref[at : at + 1, :] = jnp.full((1, mark), speeds_ref[train, c], jnp.float32)
    ids, mine, _ = wanted_labels(shards[0], slots, owned)
    sums_ref[...], area_ref[...], trains_ref[...] = add_shards(None, shards, ids, mine)


def settle_early(slots, owned, speeds, shards):
    mark = shards[0].shape[1]
    smem = pl.BlockSpec(memory_space=pltpu.SMEM)
    vmem = pl.BlockSpec(memory_space=pltpu.VMEM)
    return pl.pallas_call(
        functools.partial(settle_kernel, slots, owned),
        out_shape=(
            full((slots + owned, 3 * mark)),
            full((slots, mark)),
            full((slots, mark)),
            full((3 * speeds.shape[0], mark)),
        ),
        in_specs=[smem] + [vmem] * len(shards),
        compiler_params=kernel_params(),
        cost_estimate=pl.CostEstimate(
            flops=10**9, bytes_accessed=len(shards) * shards[0].size * 4, transcendentals=0
        ),
        name="settle",
    )(speeds, *shards)


def block_forces(rows_ref, totals, own_ref, slots, owned):
    mark = own_ref.shape[1]
    ids, mine, own_trains = wanted_labels(own_ref, slots, owned)
    sums, area, trains = totals
    trains = jnp.broadcast_to(jnp.sum(trains, axis=1, keepdims=True), area.shape)
    own_area = own_ref[8 : 8 + owned, :]
    forces, own_forces = ([], [])
    for c in range(3):
        target, own_target = (jnp.zeros_like(area), jnp.zeros_like(own_area))
        for train in range(rows_ref.shape[0] // 3):
            at = 3 * train + c
            speed = rows_ref[at : at + 1, :]
            target = jnp.where(trains == float(train), speed, target)
            own_target = jnp.where(own_trains == float(train), speed, own_target)
        got = sums[:, c * mark : (c + 1) * mark]
        forces.append(stiffness * area * (target - got[0:slots]))
        own_forces.append(stiffness * own_area * (own_target - got[slots:]))
    return (forces, own_forces)


def spread_kernel(
    slots, owned, place_ref, own_ref, last_ref, sums_ref, area_ref, trains_ref, speeds_ref,
    cells_ref, weights_ref, pop_ref, solid_ref,
    relaxed_ref, far_ref, near_ref, side_ref, marker_any, marker_ref, force_ref, lines_ref, acc,
    sem,
):
    rows, lanes = (pop_ref.shape[1], pop_ref.shape[2])
    size_y = 8
    mark = cells_ref.shape[1]
    kernel = cells_ref.shape[0] // slots
    bf = jnp.bfloat16
    ids, mine, _ = wanted_labels(own_ref, slots, owned)
    totals = add_shards((sums_ref[...], area_ref[...], trains_ref[...]), [last_ref], ids, mine)
    forces, own_forces = block_forces(speeds_ref, totals, own_ref, slots, owned)
    for c in range(3):
        force_ref[c] = forces[c]
        marker_ref[c] = own_forces[c]
    marker_copy = pltpu.make_async_copy(marker_ref, marker_any, sem)
    marker_copy.start()

    acc[...] = jnp.zeros_like(acc)
    iota = lax.broadcasted_iota(jnp.int32, (16, mark), 0).astype(jnp.float32)
    steps = [(iota + 16.0 * j).astype(bf) for j in range(max(rows, lanes) // 16)]
    one, zero = (jnp.ones((16, mark), bf), jnp.zeros((16, mark), bf))

    def body(step, carry):
        first = pl.multiple_of(step * group, group)
        force = [force_ref[c, pl.ds(first, group), :] for c in range(3)]
        for k in range(kernel):
            at = pl.ds(first * kernel + k, group, stride=kernel)
            cells = cells_ref[at, :]
            weight = weights_ref[at, :]
            lane = (cells & (lanes - 1)).astype(jnp.float32)
            row = (cells >> (lanes.bit_length() - 1)).astype(jnp.float32)
            parts = []
            for c in range(3):
                value = weight * force[c]
                high = value.astype(bf).astype(jnp.float32)
                parts += [high, value - high]
            for which, entries in enumerate([lane, row] + parts):
                lines_ref[k, which] = entries

            def wide(which, i):
                entries = lines_ref[k, which, pl.ds(i, 8, stride=0), :]
                return jnp.concatenate([entries, entries], axis=0).astype(bf)

            left, right = ([], [])
            for i in range(group):
                lane_i, row_i = (wide(0, i), wide(1, i))
                right.append(
                    jnp.concatenate(
                        [jnp.where(steps[j] == lane_i, one, zero) for j in range(lanes // 16)],
                        axis=0,
                    )
                )
                masks = [steps[j] == row_i for j in range(rows // 16)]
                pieces = []
                for which in range(len(parts)):
                    part_i = wide(2 + which, i)
                    pieces += [jnp.where(mask, part_i, zero) for mask in masks]
                left.append(jnp.concatenate(pieces, axis=0))
            acc[...] += lax.dot_general(
                jnp.concatenate(left, axis=1),
                jnp.concatenate(right, axis=1),
                (((1,), (1,)), ((), ())),
                preferred_element_type=jnp.float32,
            )
        return carry

    lax.fori_loop(0, slots // group, body, 0)
    cell_force = [
        acc[2 * c * rows : (2 * c + 1) * rows, :] + acc[(2 * c + 1) * rows : (2 * c + 2) * rows, :]
        for c in range(3)
    ]
    relaxed = collide([pop_ref[q] for q in range(19)], cell_force, solid_ref[...])
    for q in range(19):
        relaxed_ref[q] = relaxed[q]
    even = place_ref[3] == 0
    for i in range(5):
        ahead = relaxed[going(0, 1)[i]][rows - size_y :]
        behind = relaxed[going(0, -1)[i]][:size_y]
        far_ref[i] = jnp.where(even, behind, ahead)
        near_ref[i] = jnp.where(even, ahead, behind)
        for x in range(rows // size_y):
            up = relaxed[going(1, 1)[i]][size_y * x + size_y - 1 : size_y * x + size_y, :]
            down = relaxed[going(1, -1)[i]][size_y * x : size_y * x + 1, :]
            at = rows // size_y * i + x
            side_ref[at : at + 1, :] = jnp.where(place_ref[0] == 0, up, down)
    marker_copy.wait()


def spread(owned, place, own, last, early, cells, weights, populations, solid):
    mark = cells.shape[1]
    slots = early[1].shape[0]
    line_count, lanes = solid.shape
    smem = pl.BlockSpec(memory_space=pltpu.SMEM)
    vmem = pl.BlockSpec(memory_space=pltpu.VMEM)
    return pl.pallas_call(
        functools.partial(spread_kernel, slots, owned),
        out_shape=(
            full(populations.shape),
            full((5, 8, lanes)),
            full((5, 8, lanes)),
            full((24, lanes)),
            full((3, owned, mark)),
        ),
        in_specs=[smem] + [vmem] * 10,
        out_specs=[vmem] * 4 + [pl.BlockSpec(memory_space=pltpu.HBM)],
        scratch_shapes=[
            pltpu.VMEM((3, owned, mark), jnp.float32),
            pltpu.VMEM((3, slots, mark), jnp.float32),
            pltpu.VMEM((cells.shape[0] // slots, 8, group, mark), jnp.float32),
            pltpu.VMEM((6 * line_count, lanes), jnp.float32),
            pltpu.SemaphoreType.DMA,
        ],
        compiler_params=kernel_params(),
        name="spread",
    )(place, own, last, *early, cells, weights, populations, solid)


def downwind(place_ref, relaxed_ref, far_ref, near_ref):
    size_y = far_ref.shape[1]
    size_x = relaxed_ref.shape[1] // size_y
    even = place_ref[3] == 0

    def cells(q, x):
        step = int(velocity_table[q][0])
        source = x - step
        if 0 <= source < size_x:
            return relaxed_ref[q, source * size_y : (source + 1) * size_y, :]
        i = going(0, step).index(q)
        if step == 1:
            return jnp.where(even, far_ref[i], near_ref[i])
        return jnp.where(even, near_ref[i], far_ref[i])

    return cells


def sideways(cells, side_ref, edge):
    def result(q, x, y_at):
        step_x, step_y = (int(step) for step in velocity_table[q][:2])
        size_y = y_at.shape[0]
        size_x = side_ref.shape[0] // 6
        if step_y == 0:
            return cells(q, x)
        source = x - step_x
        at = size_x * going(1, step_y).index(q) + source
        halo = side_ref[at : at + 1, :] if 0 <= source < size_x else edge(q)
        turned = pltpu.roll(cells(q, x), step_y % size_y, 0)
        return jnp.where(y_at == (0 if step_y == 1 else size_y - 1), halo, turned)

    return result


def corner_index(q):
    step_y = int(velocity_table[q][1])
    return [p for p in going(1, step_y) if int(velocity_table[p][0]) != 0].index(q)


def pack_kernel(
    place_ref, relaxed_ref, far_ref, near_ref, side_ref, corner_ref, first_ref, second_ref
):
    size_y, lanes = far_ref.shape[1:]
    size_x = relaxed_ref.shape[1] // size_y
    cells = downwind(place_ref, relaxed_ref, far_ref, near_ref)
    corner_ref[...] = jnp.zeros(corner_ref.shape, jnp.float32)
    for ahead in going(1, 1):
        step_x = int(velocity_table[ahead][0])
        if step_x == 0:
            continue
        behind = opposite_table[ahead]
        up = cells(ahead, 0 if step_x == 1 else size_x - 1)[size_y - 1 : size_y, :]
        down = cells(behind, size_x - 1 if step_x == 1 else 0)[0:1, :]
        at = corner_index(ahead)
        from_behind = corner_index(behind)
        lower = place_ref[0] == 0

        @pl.when(lower)
        def _(at=at, up=up):
            corner_ref[at : at + 1, :] = up

        @pl.when(jnp.logical_not(lower))
        def _(at=from_behind, down=down):
            corner_ref[at : at + 1, :] = down

    y_at = lax.broadcasted_iota(jnp.int32, (size_y, lanes), 0)
    lane_at = lax.broadcasted_iota(jnp.int32, (size_y, lanes), 1)
    level = sideways(cells, side_ref, None)
    packs = []
    for step in (1, -1):
        packed = jnp.zeros((size_y, lanes), jnp.float32)
        for i, q in enumerate(going(2, step)):
            edge = lanes - 1 if step == 1 else 0
            for x in range(size_x):
                at = 8 * x + i
                moved = pltpu.roll(level(q, x, y_at), (at - edge) % lanes, 1)
                packed = jnp.where(lane_at == at, moved, packed)
        packs.append(packed)
    even = place_ref[1] % 2 == 0
    first_ref[...] = jnp.where(even, packs[0], packs[1])
    second_ref[...] = jnp.where(even, packs[1], packs[0])


def pack(place, relaxed, far, near, side):
    smem = pl.BlockSpec(memory_space=pltpu.SMEM)
    vmem = pl.BlockSpec(memory_space=pltpu.VMEM)
    edge = full(far.shape[1:])
    return pl.pallas_call(
        pack_kernel,
        out_shape=(edge, edge, edge),
        in_specs=[smem] + [vmem] * 4,
        compiler_params=kernel_params(),
        name="pack",
    )(place, relaxed, far, near, side)


def stream_kernel(
    count_z, place_ref, relaxed_ref, far_ref, near_ref, side_ref, second_ref, corner_ref,
    first_ref, out_any, out_ref, sems,
):
    size_x, size_y, lanes = out_ref.shape[1:]
    shape = (size_y, lanes)
    y_at = lax.broadcasted_iota(jnp.int32, shape, 0)
    z_at = lax.broadcasted_iota(jnp.int32, shape, 1)
    y_index, z_index = (place_ref[0], place_ref[1])
    streamed = sideways(
        downwind(place_ref, relaxed_ref, far_ref, near_ref),
        side_ref,
        lambda q: corner_ref[corner_index(q) : corner_index(q) + 1, :],
    )
    even = z_index % 2 == 0
    columns = {
        -1: jnp.where(even, first_ref[...], second_ref[...]),
        1: jnp.where(even, second_ref[...], first_ref[...]),
    }
    on_side = y_at == jnp.where(y_index == 0, 0, size_y - 1)
    on_side = on_side | ((z_at == 0) & (z_index == 0))
    on_side = on_side | ((z_at == lanes - 1) & (z_index == count_z - 1))
    copies = []
    for q in range(19):
        step_z = int(velocity_table[q][2])
        z_edge = 0 if step_z == 1 else lanes - 1
        for x in range(size_x):
            cells = streamed(q, x, y_at)
            if step_z != 0:
                at = 8 * x + going(2, step_z).index(q)
                cells = jnp.where(
                    z_at == z_edge,
                    pltpu.roll(columns[step_z], (z_edge - at) % lanes, 1),
                    pltpu.roll(cells, step_z % lanes, 1),
                )
            out_ref[q, x] = jnp.where(on_side, far_field[q], cells)
        copies.append(pltpu.make_async_copy(out_ref.at[q], out_any.at[q], sems.at[q]))
        copies[-1].start()
    for copy in copies:
        copy.wait()


def stream(count_z, place, relaxed, *halos):
    rows, lanes = relaxed.shape[1:]
    size_y = halos[0].shape[1]
    smem = pl.BlockSpec(memory_space=pltpu.SMEM)
    vmem = pl.BlockSpec(memory_space=pltpu.VMEM)
    shape = (19, rows // size_y, size_y, lanes)
    return pl.pallas_call(
        functools.partial(stream_kernel, count_z),
        out_shape=full(shape),
        in_specs=[smem] + [vmem] * (1 + len(halos)),
        out_specs=pl.BlockSpec(memory_space=pltpu.HBM),
        scratch_shapes=[pltpu.VMEM(shape, jnp.float32), pltpu.SemaphoreType.DMA((19,))],
        compiler_params=kernel_params(),
        name="stream",
    )(place, relaxed, *halos)


def per_device(
    populations,
    solid_cells,
    slot_cells,
    slot_weights,
    slot_owner,
    slot_block,
    train_of_block,
    marker_area,
    train_velocity,
):
    size_x, size_y, size_z = (populations.shape[1], populations.shape[2], populations.shape[3])
    lines = size_x * size_y
    slots, kernel, mark = (slot_cells.shape[3], slot_cells.shape[4], slot_cells.shape[5])
    owned = train_of_block.shape[3]
    count_x, count_y, count_z = (lax.axis_size(axis) for axis in ("gx", "gy", "gz"))
    x_index, y_index, z_index = (lax.axis_index(axis) for axis in ("gx", "gy", "gz"))
    place = jnp.stack([y_index, z_index, x_index * count_y + y_index, x_index % 2])
    place = place.astype(jnp.int32)
    inputs = [
        pltpu.with_memory_space_constraint(entries, pltpu.HBM)
        for entries in (
            populations.reshape(19, lines, size_z),
            slot_cells.reshape(slots * kernel, mark),
            slot_weights.reshape(slots * kernel, mark),
            marker_area.reshape(owned, mark),
            slot_owner.reshape(1, slots),
            slot_block.reshape(1, slots),
            train_of_block.reshape(1, owned),
        )
    ]
    own, pops, cells, weights = sample(place, *inputs)
    swap = [(0, 1), (1, 0)]

    def across_x(entries, distance):
        return lax.ppermute(entries, "gx", [(i, i ^ distance) for i in range(count_x)])

    def across_y(entries):
        return lax.ppermute(entries, "gy", swap)

    third, first = (across_x(own, distance) for distance in (3, 1))
    beside = across_y(own)
    first_beside = across_x(beside, 1)
    third_beside = across_y(lax.optimization_barrier((third, beside, first))[0])
    second = across_x(lax.optimization_barrier((third, first_beside))[0], 1)
    last = across_x(third_beside, 1)
    whole = [own, first, third, second, beside, first_beside, third_beside]
    early = settle_early(slots, owned, train_velocity, whole)
    solid = solid_cells.reshape(lines, size_z)
    relaxed, far, near, side, marker_force = spread(
        owned, place, own, last, early, cells, weights, pops, solid
    )
    evens = range(0, count_x, 2)
    far = lax.ppermute(
        far,
        "gx",
        [(i, (i - 1) % count_x) for i in evens] + [((i - 1) % count_x, i) for i in evens],
    )
    near = lax.ppermute(near, "gx", [(i, i + 1) for i in evens] + [(i + 1, i) for i in evens])
    side = across_y(side)
    corner, up_first, down_first = pack(place, relaxed, far, near, side)
    inner = [(i, i + 1) for i in range(0, count_z - 1, 2)]
    outer = [(i, i + 1) for i in range(1, count_z - 1, 2)]
    down_first = lax.ppermute(down_first, "gz", outer + [(j, i) for i, j in outer])
    corner = across_y(corner)
    up_first = lax.ppermute(up_first, "gz", inner + [(j, i) for i, j in inner])
    populations_next = stream(
        count_z, place, relaxed, far, near, side, down_first, corner, up_first
    )
    marker_force = marker_force.transpose(1, 0, 2).reshape(1, 1, 1, owned, 3, mark)
    return (populations_next, marker_force)


def solution(mesh):
    placed = (
        P(None, "gx", "gy", "gz"),
        P("gx", "gy", "gz"),
        P("gx", "gy", "gz", None, None, None),
        P("gx", "gy", "gz", None, None, None),
        P("gx", "gy", "gz", None, None),
        P("gx", "gy", "gz", None),
        P("gx", "gy", "gz", None),
        P("gx", "gy", "gz", None, None),
        P(),
    )
    small = mesh.shape["gy"] == 2 and mesh.shape["gx"] == 4 and mesh.shape["gz"] % 2 == 0
    return jax.shard_map(
        per_device if small else per_device_general,
        mesh=mesh,
        in_specs=placed,
        out_specs=(P(None, "gx", "gy", "gz"), P("gx", "gy", "gz", None, None, None)),
        check_vma=False,
    )
```

```python
import functools
import jax
import jax.numpy as jnp
import numpy as np
from jax import lax
from jax.experimental import pallas as pl
from jax.experimental.pallas import tpu as pltpu
from jax.sharding import PartitionSpec as P

velocity_table = np.array(
    [
        [0, 0, 0],
        [1, 0, 0],
        [-1, 0, 0],
        [0, 1, 0],
        [0, -1, 0],
        [0, 0, 1],
        [0, 0, -1],
        [1, 1, 0],
        [-1, -1, 0],
        [1, -1, 0],
        [-1, 1, 0],
        [1, 0, 1],
        [-1, 0, -1],
        [1, 0, -1],
        [-1, 0, 1],
        [0, 1, 1],
        [0, -1, -1],
        [0, 1, -1],
        [0, -1, 1],
    ]
)
weight_table = [1.0 / 3.0] + [1.0 / 18.0] * 6 + [1.0 / 36.0] * 12
opposite_table = [0, 2, 1, 4, 3, 6, 5, 8, 7, 10, 9, 12, 11, 14, 13, 16, 15, 18, 17]
stress_pairs = [(0, 0), (1, 1), (2, 2), (0, 1), (0, 2), (1, 2)]
tau_base = 0.55
smag_term = 18.0 * 1.4142135623730951 * 0.17 * 0.17
regular_eps = 0.0001
stiffness = 2.0
far_velocity = (0.02, 0.06, 0.0)
vmem_bytes = 16 << 20
group = 8
fine = jnp.float8_e4m3fn


def going(axis, step):
    return [q for q in range(19) if int(velocity_table[q][axis]) == step]


def project(direction, vector):
    projection = 0.0 * vector[0]
    for component in range(3):
        lattice_step = int(velocity_table[direction][component])
        if lattice_step != 0:
            projection = projection + lattice_step * vector[component]
    return projection


def moments(populations):
    density = populations[0]
    momentum = [jnp.zeros_like(density) for component in range(3)]
    for direction in range(1, 19):
        density = density + populations[direction]
        for component in range(3):
            lattice_step = int(velocity_table[direction][component])
            if lattice_step == 1:
                momentum[component] = momentum[component] + populations[direction]
            elif lattice_step == -1:
                momentum[component] = momentum[component] - populations[direction]
    return (density, momentum)


def equilibrium(density, velocity):
    speed_sq = velocity[0] * velocity[0] + velocity[1] * velocity[1] + velocity[2] * velocity[2]
    result = []
    for direction in range(19):
        projected = project(direction, velocity)
        result.append(
            weight_table[direction]
            * density
            * (1.0 + 3.0 * projected + 4.5 * projected * projected - 1.5 * speed_sq)
        )
    return result


far_field = [float(np.float32(value)) for value in equilibrium(1.0, list(far_velocity))]


def collide(populations, cell_force, solid_cells):
    density, momentum = moments(populations)
    velocity = [
        (momentum[component] + 0.5 * cell_force[component]) / density for component in range(3)
    ]
    balance = equilibrium(density, velocity)
    stress = [jnp.zeros_like(density) for pair_pos in range(6)]
    for direction in range(19):
        non_eq = populations[direction] - balance[direction]
        for pair_pos in range(6):
            row_axis, col_axis = stress_pairs[pair_pos]
            factor = int(velocity_table[direction][row_axis] * velocity_table[direction][col_axis])
            if factor != 0:
                stress[pair_pos] = stress[pair_pos] + factor * non_eq
    shear_sq = stress[0] * stress[0] + stress[1] * stress[1] + stress[2] * stress[2]
    shear_sq = shear_sq + 2.0 * (
        stress[3] * stress[3] + stress[4] * stress[4] + stress[5] * stress[5]
    )
    magnitude = jnp.sqrt(shear_sq + regular_eps)
    relax_time = 0.5 * (tau_base + jnp.sqrt(tau_base * tau_base + smag_term * magnitude / density))
    relax_rate = 1.0 / relax_time
    guo_factor = 1.0 - 0.5 * relax_rate
    speed_force = (
        velocity[0] * cell_force[0] + velocity[1] * cell_force[1] + velocity[2] * cell_force[2]
    )
    result = []
    for direction in range(19):
        along_force = project(direction, cell_force)
        along_speed = project(direction, velocity)
        source = (
            guo_factor
            * weight_table[direction]
            * (3.0 * (along_force - speed_force) + 9.0 * along_speed * along_force)
        )
        relaxed = (
            populations[direction]
            - (populations[direction] - balance[direction]) * relax_rate
            + source
        )
        result.append(jnp.where(solid_cells == 1, populations[opposite_table[direction]], relaxed))
    return result


def with_halo(cells, sides, width):
    for axis, dim in sides:
        count = lax.axis_size(axis)
        head = lax.slice_in_dim(cells, 0, width, axis=dim)
        tail = lax.slice_in_dim(cells, cells.shape[dim] - width, cells.shape[dim], axis=dim)
        cells = jnp.concatenate(
            [
                lax.ppermute(tail, axis, [(i, (i + 1) % count) for i in range(count)]),
                cells,
                lax.ppermute(head, axis, [((i + 1) % count, i) for i in range(count)]),
            ],
            axis=dim,
        )
    return cells


def settle(received, labels, owned, train_of_block, marker_area, train_velocity, mark):
    rows_in = received.reshape(-1, 3 * mark)
    label_rows = labels.reshape(-1)
    owner_match = (label_rows[None, :] == jnp.arange(owned, dtype=jnp.int32)[:, None]).astype(
        jnp.float32
    )
    marker_velocity = jnp.dot(owner_match, rows_in, precision=lax.Precision.HIGHEST).reshape(
        owned, 3, mark
    )
    trains = train_velocity.shape[0]
    train_rows = train_of_block.reshape(owned)
    train_match = (train_rows[:, None] == jnp.arange(trains, dtype=jnp.int32)[None, :]).astype(
        jnp.float32
    )
    target = jnp.dot(train_match, train_velocity, precision=lax.Precision.HIGHEST)
    areas = marker_area.reshape(owned, mark)
    marker_force = stiffness * areas[:, None, :] * (target[:, :, None] - marker_velocity)
    back_rows = jnp.dot(
        owner_match.T, marker_force.reshape(owned, 3 * mark), precision=lax.Precision.HIGHEST
    )
    return (marker_force, back_rows)


def per_device_general(
    populations,
    solid_cells,
    slot_cells,
    slot_weights,
    slot_owner,
    slot_block,
    train_of_block,
    marker_area,
    train_velocity,
):
    size_x, size_y, size_z = (populations.shape[1], populations.shape[2], populations.shape[3])
    cell_count = size_x * size_y * size_z
    slots, kernel, mark = (slot_cells.shape[3], slot_cells.shape[4], slot_cells.shape[5])
    owned = train_of_block.shape[3]
    peers_x = lax.axis_size("gx")
    peers_y = lax.axis_size("gy")
    peers = peers_x * peers_y
    capacity = max(2, 2 * slots // peers)
    density, momentum = moments(populations)
    rest_velocity = jnp.stack([momentum[component] / density for component in range(3)]).reshape(
        3, cell_count
    )
    cells = slot_cells.reshape(slots, kernel, mark)
    weights = slot_weights.reshape(slots, kernel, mark)
    partial_value = jnp.sum(rest_velocity[:, cells] * weights[None], axis=2)
    slot_rows = partial_value.transpose(1, 0, 2).reshape(slots, 3 * mark)
    slot_dest = slot_owner.reshape(slots)
    blocks = slot_block.reshape(slots)
    order = jnp.arange(slots, dtype=jnp.int32)
    earlier = (slot_dest[None, :] == slot_dest[:, None]) & (order[None, :] < order[:, None])
    slot_rank = jnp.sum(earlier.astype(jnp.int32), axis=1)
    target_row = slot_dest * capacity + slot_rank
    buffer_rows = jnp.arange(peers * capacity, dtype=jnp.int32)
    matches = buffer_rows[:, None] == target_row[None, :]
    placement = matches.astype(jnp.float32)
    outgoing = jnp.dot(placement, slot_rows, precision=lax.Precision.HIGHEST)
    labels = jnp.sum(jnp.where(matches, blocks[None, :] + 1, 0), axis=1) - 1
    received, got_labels = (
        lax.all_to_all(
            outgoing.reshape(peers, capacity, 3 * mark),
            ("gx", "gy"),
            split_axis=0,
            concat_axis=0,
            tiled=True,
        ),
        lax.all_to_all(
            labels.reshape(peers, capacity), ("gx", "gy"), split_axis=0, concat_axis=0, tiled=True
        ),
    )
    marker_force, back_rows = settle(
        received, got_labels, owned, train_of_block, marker_area, train_velocity, mark
    )
    returned = lax.all_to_all(
        back_rows.reshape(peers, capacity, 3 * mark),
        ("gx", "gy"),
        split_axis=0,
        concat_axis=0,
        tiled=True,
    )
    slot_force = jnp.dot(
        placement.T, returned.reshape(peers * capacity, 3 * mark), precision=lax.Precision.HIGHEST
    )
    slot_force = slot_force.reshape(slots, 3, mark).transpose(1, 0, 2)
    contrib = weights[None] * slot_force[:, :, None, :]
    cell_force = (
        jnp.zeros((3, cell_count), jnp.float32).at[:, cells.reshape(-1)].add(contrib.reshape(3, -1))
    )
    cell_force = cell_force.reshape(3, size_x, size_y, size_z)
    relaxed = collide(populations, cell_force, solid_cells)
    padded = with_halo(jnp.stack(relaxed), (("gx", 1), ("gy", 2), ("gz", 3)), 1)
    parts = []
    for direction in range(19):
        shift_x = 1 - int(velocity_table[direction][0])
        shift_y = 1 - int(velocity_table[direction][1])
        shift_z = 1 - int(velocity_table[direction][2])
        parts.append(
            padded[
                direction,
                shift_x : shift_x + size_x,
                shift_y : shift_y + size_y,
                shift_z : shift_z + size_z,
            ]
        )
    read = jnp.stack(parts)
    total_y = size_y * lax.axis_size("gy")
    total_z = size_z * lax.axis_size("gz")
    global_y = lax.axis_index("gy") * size_y + jnp.arange(size_y, dtype=jnp.int32)
    global_z = lax.axis_index("gz") * size_z + jnp.arange(size_z, dtype=jnp.int32)
    on_side = ((global_y == 0) | (global_y == total_y - 1))[:, None] | (
        (global_z == 0) | (global_z == total_z - 1)
    )[None, :]
    far_field = jnp.array(equilibrium(1.0, list(far_velocity)), dtype=jnp.float32)
    populations_next = jnp.where(on_side[None, None], far_field[:, None, None, None], read)
    return (populations_next, marker_force.reshape(1, 1, 1, owned, 3, mark))


def full(shape):
    return jax.ShapeDtypeStruct(shape, jnp.float32)


def kernel_params():
    return pltpu.CompilerParams(vmem_limit_bytes=vmem_bytes)


def low_half(shape):
    return lax.broadcasted_iota(jnp.int32, shape, 1) < shape[1] // 2


def fetch(pairs, sems):
    copies = [
        pltpu.make_async_copy(source, target, sems.at[i])
        for i, (source, target) in enumerate(pairs)
    ]
    for copy in copies:
        copy.start()
    return copies


def shard_rows(slots, owned):
    return 8 + owned + 3 * slots


def sample_kernel(
    place_ref, pop_any, cells_any, weights_any, areas_any, owner_any, block_any, trains_any,
    out_ref, pop_ref, cells_ref, weights_ref, areas_ref, owner_ref, block_ref, trains_ref,
    table, sems,
):
    rows, lanes = (pop_ref.shape[1], pop_ref.shape[2])
    mark = cells_ref.shape[1]
    owned = areas_ref.shape[0]
    slots = owner_ref.shape[1]
    kernel = cells_ref.shape[0] // slots
    copies = fetch(
        (
            (pop_any, pop_ref),
            (cells_any, cells_ref),
            (weights_any, weights_ref),
            (areas_any, areas_ref),
            (owner_any, owner_ref),
            (block_any, block_ref),
            (trains_any, trains_ref),
        ),
        sems,
    )

    copies[0].wait()
    density, momentum = moments([pop_ref[q] for q in range(19)])
    speed = [momentum[c] / density for c in range(3)]
    largest = jnp.maximum(jnp.maximum(jnp.abs(speed[0]), jnp.abs(speed[1])), jnp.abs(speed[2]))
    largest = jnp.max(largest, axis=(0, 1), keepdims=True) + 1e-20
    scale = largest * (1.0 / 32767.0)
    fixed = [(speed[c] * (1.0 / scale) + 32768.5).astype(jnp.int32) for c in range(3)]
    words = jnp.concatenate(
        [
            (fixed[0] << 16) | fixed[1],
            (fixed[2][: rows // 2] << 16) | fixed[2][rows // 2 :],
        ],
        axis=0,
    )
    for r in range(table.shape[0]):
        table[r] = jnp.broadcast_to(words[r : r + 1], (group, lanes))
    for copy in copies[1:]:
        copy.wait()
    out_ref[8 : 8 + owned, :] = areas_ref[...]
    out_ref[0:8, :] = jnp.zeros((8, mark), jnp.float32)
    ids = (owner_ref[...] * owned + block_ref[...]).astype(jnp.float32)
    out_ref[0:1, :] = jnp.concatenate([ids] * (mark // slots), axis=1)
    out_ref[1:2, 0:owned] = trains_ref[...].astype(jnp.float32)
    mine = lax.broadcasted_iota(jnp.int32, (1, mark), 1) % owned + place_ref[2] * owned
    out_ref[2:3, :] = mine.astype(jnp.float32)

    def body(step, carry):
        first = pl.multiple_of(step * group, group)
        total = [jnp.zeros((group, mark), jnp.float32) for c in range(3)]
        for k in range(kernel):
            at = pl.ds(first * kernel + k, group, stride=kernel)
            cells = cells_ref[at, :]
            lane = cells & (lanes - 1)
            row = cells >> (lanes.bit_length() - 1)
            bits = [(row >> bit) & 1 == 1 for bit in range(rows.bit_length() - 1)]

            def choose(low, level):
                if level < 0:
                    return jnp.take_along_axis(table[low], lane, axis=1, mode="promise_in_bounds")
                lower = choose(low, level - 1)
                return jnp.where(bits[level], choose(low + (1 << level), level - 1), lower)

            pair = choose(0, len(bits) - 1)
            third = choose(rows, len(bits) - 2)
            picked = [
                lax.shift_right_logical(pair, 16),
                pair & 65535,
                jnp.where(bits[-1], third & 65535, lax.shift_right_logical(third, 16)),
            ]
            weight = weights_ref[at, :]
            for c in range(3):
                total[c] = total[c] + weight * (picked[c].astype(jnp.float32) - 32768.0)
        for c in range(3):
            here = pl.ds(pl.multiple_of(8 + owned + c * slots + first, group), group)
            out_ref[here, :] = total[c] * scale
        return carry

    lax.fori_loop(0, slots // group, body, 0)


def sample(place, populations, cells, weights, areas, owner, block, trains):
    smem = pl.BlockSpec(memory_space=pltpu.SMEM)
    hbm = pl.BlockSpec(memory_space=pltpu.HBM)
    vmem = pl.BlockSpec(memory_space=pltpu.VMEM)
    kept = (populations, cells, weights)
    count = shard_rows(owner.shape[1], areas.shape[0])
    return pl.pallas_call(
        sample_kernel,
        out_shape=[full((count, cells.shape[1]))]
        + [jax.ShapeDtypeStruct(entries.shape, entries.dtype) for entries in kept],
        in_specs=[smem] + [hbm] * 7,
        out_specs=[vmem] * 4,
        scratch_shapes=[
            pltpu.VMEM(entries.shape, entries.dtype) for entries in (areas, owner, block, trains)
        ]
        + [
            pltpu.VMEM((populations.shape[1] * 3 // 2, group, populations.shape[2]), jnp.int32),
            pltpu.SemaphoreType.DMA((7,)),
        ],
        compiler_params=kernel_params(),
        name="sample",
    )(place, populations, cells, weights, areas, owner, block, trains)


def three_parts(values):
    parts = []
    for _ in range(3):
        parts.append(values.astype(jnp.bfloat16))
        values = values - parts[-1].astype(jnp.float32)
    return parts


def one_hot(mask):
    return jnp.where(mask, 1.0, 0.0).astype(jnp.bfloat16)


def wanted_labels(own_ref, slots, owned):
    mark = own_ref.shape[1]
    own = own_ref[0:8, :]
    ids, trains, mine = (jnp.broadcast_to(own[i : i + 1], (mark, mark)).T for i in range(3))
    return (ids[0:slots], mine[0:owned], trains[0:owned])


def add_shards(totals, shards, ids, mine):
    slots, owned = (ids.shape[0], mine.shape[0])
    wanted = jnp.concatenate([ids, mine], axis=0)
    for shard in shards:
        match = one_hot(wanted == shard[0:1, :])
        match = jnp.concatenate([match, match[:, 0:slots]], axis=1)
        starts = [8 + owned + c * slots for c in range(3)]
        values = jnp.concatenate([shard[at : at + slots, :] for at in starts], axis=1)
        sums = jnp.dot(
            match, jnp.concatenate(three_parts(values), axis=0), preferred_element_type=jnp.float32
        )
        held = ids == shard[2:3, :]
        parts = three_parts(shard[8 : 8 + owned, :])
        parts.append(jnp.zeros_like(parts[0]))
        area = jnp.dot(
            one_hot(held), jnp.concatenate(parts, axis=0), preferred_element_type=jnp.float32
        )
        got = (sums, area, jnp.where(held, shard[1:2, :], 0.0))
        totals = got if totals is None else [total + new for total, new in zip(totals, got)]
    return totals


def settle_kernel(slots, owned, speeds_ref, *refs):
    *shards, sums_ref, area_ref, trains_ref, rows_ref = refs
    mark = rows_ref.shape[1]
    for train in range(speeds_ref.shape[0]):
        for c in range(3):
            at = 3 * train + c
            rows_ref[at : at + 1, :] = jnp.full((1, mark), speeds_ref[train, c], jnp.float32)
    ids, mine, _ = wanted_labels(shards[0], slots, owned)
    sums_ref[...], area_ref[...], trains_ref[...] = add_shards(None, shards, ids, mine)


def settle_early(slots, owned, speeds, shards):
    mark = shards[0].shape[1]
    smem = pl.BlockSpec(memory_space=pltpu.SMEM)
    vmem = pl.BlockSpec(memory_space=pltpu.VMEM)
    return pl.pallas_call(
        functools.partial(settle_kernel, slots, owned),
        out_shape=(
            full((slots + owned, 3 * mark)),
            full((slots, mark)),
            full((slots, mark)),
            full((3 * speeds.shape[0], mark)),
        ),
        in_specs=[smem] + [vmem] * len(shards),
        compiler_params=kernel_params(),
        cost_estimate=pl.CostEstimate(
            flops=10**9, bytes_accessed=len(shards) * shards[0].size * 4, transcendentals=0
        ),
        name="settle",
    )(speeds, *shards)


def block_forces(rows_ref, totals, own_ref, slots, owned):
    mark = own_ref.shape[1]
    ids, mine, own_trains = wanted_labels(own_ref, slots, owned)
    sums, area, trains = totals
    trains = jnp.broadcast_to(jnp.sum(trains, axis=1, keepdims=True), area.shape)
    own_area = own_ref[8 : 8 + owned, :]
    forces, own_forces = ([], [])
    for c in range(3):
        target, own_target = (jnp.zeros_like(area), jnp.zeros_like(own_area))
        for train in range(rows_ref.shape[0] // 3):
            at = 3 * train + c
            speed = rows_ref[at : at + 1, :]
            target = jnp.where(trains == float(train), speed, target)
            own_target = jnp.where(own_trains == float(train), speed, own_target)
        got = sums[:, c * mark : (c + 1) * mark]
        forces.append(stiffness * area * (target - got[0:slots]))
        own_forces.append(stiffness * own_area * (own_target - got[slots:]))
    return (forces, own_forces)


def spread_kernel(
    slots, owned, place_ref, own_ref, last_ref, sums_ref, area_ref, trains_ref, speeds_ref,
    cells_ref, weights_ref, pop_ref, solid_ref,
    relaxed_ref, far_ref, near_ref, side_ref, marker_any, marker_ref, force_ref, lines_ref, acc,
    sem,
):
    rows, lanes = (pop_ref.shape[1], pop_ref.shape[2])
    size_y = 8
    mark = cells_ref.shape[1]
    kernel = cells_ref.shape[0] // slots
    bf = jnp.bfloat16
    ids, mine, _ = wanted_labels(own_ref, slots, owned)
    totals = add_shards((sums_ref[...], area_ref[...], trains_ref[...]), [last_ref], ids, mine)
    forces, own_forces = block_forces(speeds_ref, totals, own_ref, slots, owned)
    largest = jnp.maximum(jnp.maximum(jnp.abs(forces[0]), jnp.abs(forces[1])), jnp.abs(forces[2]))
    largest = jnp.maximum(jnp.max(largest, axis=(0, 1), keepdims=True), 1e-20)
    scale = (224.0 * 16.0) / largest
    for c in range(3):
        force_ref[c] = forces[c] * scale
        marker_ref[c] = own_forces[c]
    marker_copy = pltpu.make_async_copy(marker_ref, marker_any, sem)
    marker_copy.start()

    acc[...] = jnp.zeros_like(acc)
    iota = lax.broadcasted_iota(jnp.int32, (16, mark), 0).astype(jnp.float32)
    steps = [(iota + 16.0 * j).astype(bf) for j in range(max(rows, lanes) // 16)]
    one, zero = (jnp.ones((16, mark), bf), jnp.zeros((16, mark), bf))

    def body(step, carry):
        first = pl.multiple_of(step * group, group)
        force = [force_ref[c, pl.ds(first, group), :] for c in range(3)]
        for k in range(kernel):
            at = pl.ds(first * kernel + k, group, stride=kernel)
            cells = cells_ref[at, :]
            weight = weights_ref[at, :]
            lane = (cells & (lanes - 1)).astype(jnp.float32)
            row = (cells >> (lanes.bit_length() - 1)).astype(jnp.float32)
            parts = []
            for c in range(3):
                value = weight * force[c]
                for _ in range(3):
                    parts.append(value.astype(fine).astype(jnp.float32))
                    value = (value - parts[-1]) * 16.0
            for which, entries in enumerate([lane, row] + parts):
                lines_ref[k, which] = entries

            def wide(which, i):
                entries = lines_ref[k, which, pl.ds(i, 8, stride=0), :]
                return jnp.concatenate([entries, entries], axis=0).astype(bf)

            left, right = ([], [])
            for i in range(group):
                lane_i, row_i = (wide(0, i), wide(1, i))
                match = [jnp.where(steps[j] == lane_i, one, zero) for j in range(lanes // 16)]
                right.append(jnp.concatenate(match, axis=0).astype(fine))
                masks = [steps[j] == row_i for j in range(rows // 16)]
                pieces = []
                for which in range(len(parts)):
                    part_i = wide(2 + which, i)
                    piece = [jnp.where(mask, part_i, zero) for mask in masks]
                    pieces.append(jnp.concatenate(piece, axis=0).astype(fine))
                left.append(jnp.concatenate(pieces, axis=0))
            acc[...] += lax.dot_general(
                jnp.concatenate(left, axis=1),
                jnp.concatenate(right, axis=1),
                (((1,), (1,)), ((), ())),
                preferred_element_type=jnp.float32,
            )
        return carry

    lax.fori_loop(0, slots // group, body, 0)
    cell_force = []
    for c in range(3):
        total = acc[3 * c * rows : (3 * c + 1) * rows, :]
        total = total + acc[(3 * c + 1) * rows : (3 * c + 2) * rows, :] * (1.0 / 16.0)
        total = total + acc[(3 * c + 2) * rows : (3 * c + 3) * rows, :] * (1.0 / 256.0)
        cell_force.append(total * (1.0 / scale))
    relaxed = collide([pop_ref[q] for q in range(19)], cell_force, solid_ref[...])
    for q in range(19):
        relaxed_ref[q] = relaxed[q]
    even = place_ref[3] == 0
    for i in range(5):
        ahead = relaxed[going(0, 1)[i]][rows - size_y :]
        behind = relaxed[going(0, -1)[i]][:size_y]
        far_ref[i] = jnp.where(even, behind, ahead)
        near_ref[i] = jnp.where(even, ahead, behind)
        for x in range(rows // size_y):
            up = relaxed[going(1, 1)[i]][size_y * x + size_y - 1 : size_y * x + size_y, :]
            down = relaxed[going(1, -1)[i]][size_y * x : size_y * x + 1, :]
            at = rows // size_y * i + x
            side_ref[at : at + 1, :] = jnp.where(place_ref[0] == 0, up, down)
    marker_copy.wait()


def spread(owned, place, own, last, early, cells, weights, populations, solid):
    mark = cells.shape[1]
    slots = early[1].shape[0]
    line_count, lanes = solid.shape
    smem = pl.BlockSpec(memory_space=pltpu.SMEM)
    vmem = pl.BlockSpec(memory_space=pltpu.VMEM)
    return pl.pallas_call(
        functools.partial(spread_kernel, slots, owned),
        out_shape=(
            full(populations.shape),
            full((5, 8, lanes)),
            full((5, 8, lanes)),
            full((24, lanes)),
            full((3, owned, mark)),
        ),
        in_specs=[smem] + [vmem] * 10,
        out_specs=[vmem] * 4 + [pl.BlockSpec(memory_space=pltpu.HBM)],
        scratch_shapes=[
            pltpu.VMEM((3, owned, mark), jnp.float32),
            pltpu.VMEM((3, slots, mark), jnp.float32),
            pltpu.VMEM((cells.shape[0] // slots, 11, group, mark), jnp.float32),
            pltpu.VMEM((9 * line_count, lanes), jnp.float32),
            pltpu.SemaphoreType.DMA,
        ],
        compiler_params=kernel_params(),
        name="spread",
    )(place, own, last, *early, cells, weights, populations, solid)


def downwind(place_ref, relaxed_ref, far_ref, near_ref):
    size_y = far_ref.shape[1]
    size_x = relaxed_ref.shape[1] // size_y
    even = place_ref[3] == 0

    def cells(q, x):
        step = int(velocity_table[q][0])
        source = x - step
        if 0 <= source < size_x:
            return relaxed_ref[q, source * size_y : (source + 1) * size_y, :]
        i = going(0, step).index(q)
        if step == 1:
            return jnp.where(even, far_ref[i], near_ref[i])
        return jnp.where(even, near_ref[i], far_ref[i])

    return cells


def sideways(cells, side_ref, edge):
    def result(q, x, y_at):
        step_x, step_y = (int(step) for step in velocity_table[q][:2])
        size_y = y_at.shape[0]
        size_x = side_ref.shape[0] // 6
        if step_y == 0:
            return cells(q, x)
        source = x - step_x
        at = size_x * going(1, step_y).index(q) + source
        halo = side_ref[at : at + 1, :] if 0 <= source < size_x else edge(q)
        turned = pltpu.roll(cells(q, x), step_y % size_y, 0)
        return jnp.where(y_at == (0 if step_y == 1 else size_y - 1), halo, turned)

    return result


def corner_index(q):
    step_y = int(velocity_table[q][1])
    return [p for p in going(1, step_y) if int(velocity_table[p][0]) != 0].index(q)


def pack_kernel(
    place_ref, relaxed_ref, far_ref, near_ref, side_ref, corner_ref, first_ref, second_ref
):
    size_y, lanes = far_ref.shape[1:]
    size_x = relaxed_ref.shape[1] // size_y
    cells = downwind(place_ref, relaxed_ref, far_ref, near_ref)
    corner_ref[...] = jnp.zeros(corner_ref.shape, jnp.float32)
    for ahead in going(1, 1):
        step_x = int(velocity_table[ahead][0])
        if step_x == 0:
            continue
        behind = opposite_table[ahead]
        up = cells(ahead, 0 if step_x == 1 else size_x - 1)[size_y - 1 : size_y, :]
        down = cells(behind, size_x - 1 if step_x == 1 else 0)[0:1, :]
        at = corner_index(ahead)
        from_behind = corner_index(behind)
        lower = place_ref[0] == 0

        @pl.when(lower)
        def _(at=at, up=up):
            corner_ref[at : at + 1, :] = up

        @pl.when(jnp.logical_not(lower))
        def _(at=from_behind, down=down):
            corner_ref[at : at + 1, :] = down

    y_at = lax.broadcasted_iota(jnp.int32, (size_y, lanes), 0)
    lane_at = lax.broadcasted_iota(jnp.int32, (size_y, lanes), 1)
    level = sideways(cells, side_ref, None)
    packs = []
    for step in (1, -1):
        packed = jnp.zeros((size_y, lanes), jnp.float32)
        for i, q in enumerate(going(2, step)):
            edge = lanes - 1 if step == 1 else 0
            for x in range(size_x):
                at = 8 * x + i
                moved = pltpu.roll(level(q, x, y_at), (at - edge) % lanes, 1)
                packed = jnp.where(lane_at == at, moved, packed)
        packs.append(packed)
    even = place_ref[1] % 2 == 0
    first_ref[...] = jnp.where(even, packs[0], packs[1])
    second_ref[...] = jnp.where(even, packs[1], packs[0])


def pack(place, relaxed, far, near, side):
    smem = pl.BlockSpec(memory_space=pltpu.SMEM)
    vmem = pl.BlockSpec(memory_space=pltpu.VMEM)
    edge = full(far.shape[1:])
    return pl.pallas_call(
        pack_kernel,
        out_shape=(edge, edge, edge),
        in_specs=[smem] + [vmem] * 4,
        compiler_params=kernel_params(),
        name="pack",
    )(place, relaxed, far, near, side)


def stream_kernel(
    count_z, place_ref, relaxed_ref, far_ref, near_ref, side_ref, second_ref, corner_ref,
    first_ref, out_any, out_ref, sems,
):
    size_x, size_y, lanes = out_ref.shape[1:]
    shape = (size_y, lanes)
    y_at = lax.broadcasted_iota(jnp.int32, shape, 0)
    z_at = lax.broadcasted_iota(jnp.int32, shape, 1)
    y_index, z_index = (place_ref[0], place_ref[1])
    streamed = sideways(
        downwind(place_ref, relaxed_ref, far_ref, near_ref),
        side_ref,
        lambda q: corner_ref[corner_index(q) : corner_index(q) + 1, :],
    )
    even = z_index % 2 == 0
    columns = {
        -1: jnp.where(even, first_ref[...], second_ref[...]),
        1: jnp.where(even, second_ref[...], first_ref[...]),
    }
    on_side = y_at == jnp.where(y_index == 0, 0, size_y - 1)
    on_side = on_side | ((z_at == 0) & (z_index == 0))
    on_side = on_side | ((z_at == lanes - 1) & (z_index == count_z - 1))
    copies = []
    for q in range(19):
        step_z = int(velocity_table[q][2])
        z_edge = 0 if step_z == 1 else lanes - 1
        for x in range(size_x):
            cells = streamed(q, x, y_at)
            if step_z != 0:
                at = 8 * x + going(2, step_z).index(q)
                cells = jnp.where(
                    z_at == z_edge,
                    pltpu.roll(columns[step_z], (z_edge - at) % lanes, 1),
                    pltpu.roll(cells, step_z % lanes, 1),
                )
            out_ref[q, x] = jnp.where(on_side, far_field[q], cells)
        copies.append(pltpu.make_async_copy(out_ref.at[q], out_any.at[q], sems.at[q]))
        copies[-1].start()
    for copy in copies:
        copy.wait()


def stream(count_z, place, relaxed, *halos):
    rows, lanes = relaxed.shape[1:]
    size_y = halos[0].shape[1]
    smem = pl.BlockSpec(memory_space=pltpu.SMEM)
    vmem = pl.BlockSpec(memory_space=pltpu.VMEM)
    shape = (19, rows // size_y, size_y, lanes)
    return pl.pallas_call(
        functools.partial(stream_kernel, count_z),
        out_shape=full(shape),
        in_specs=[smem] + [vmem] * (1 + len(halos)),
        out_specs=pl.BlockSpec(memory_space=pltpu.HBM),
        scratch_shapes=[pltpu.VMEM(shape, jnp.float32), pltpu.SemaphoreType.DMA((19,))],
        compiler_params=kernel_params(),
        name="stream",
    )(place, relaxed, *halos)


def per_device(
    populations,
    solid_cells,
    slot_cells,
    slot_weights,
    slot_owner,
    slot_block,
    train_of_block,
    marker_area,
    train_velocity,
):
    size_x, size_y, size_z = (populations.shape[1], populations.shape[2], populations.shape[3])
    lines = size_x * size_y
    slots, kernel, mark = (slot_cells.shape[3], slot_cells.shape[4], slot_cells.shape[5])
    owned = train_of_block.shape[3]
    count_x, count_y, count_z = (lax.axis_size(axis) for axis in ("gx", "gy", "gz"))
    x_index, y_index, z_index = (lax.axis_index(axis) for axis in ("gx", "gy", "gz"))
    place = jnp.stack([y_index, z_index, x_index * count_y + y_index, x_index % 2])
    place = place.astype(jnp.int32)
    inputs = [
        pltpu.with_memory_space_constraint(entries, pltpu.HBM)
        for entries in (
            populations.reshape(19, lines, size_z),
            slot_cells.reshape(slots * kernel, mark),
            slot_weights.reshape(slots * kernel, mark),
            marker_area.reshape(owned, mark),
            slot_owner.reshape(1, slots),
            slot_block.reshape(1, slots),
            train_of_block.reshape(1, owned),
        )
    ]
    own, pops, cells, weights = sample(place, *inputs)
    swap = [(0, 1), (1, 0)]

    def across_x(entries, distance):
        return lax.ppermute(entries, "gx", [(i, i ^ distance) for i in range(count_x)])

    def across_y(entries):
        return lax.ppermute(entries, "gy", swap)

    third, first = (across_x(own, distance) for distance in (3, 1))
    beside = across_y(own)
    third_beside = across_y(lax.optimization_barrier((third, beside))[0])
    second = across_x(third, 1)
    first_beside = across_y(first)
    last = across_x(third_beside, 1)
    whole = [own, first, third, second, beside, first_beside, third_beside]
    early = settle_early(slots, owned, train_velocity, whole)
    solid = solid_cells.reshape(lines, size_z)
    relaxed, far, near, side, marker_force = spread(
        owned, place, own, last, early, cells, weights, pops, solid
    )
    evens = range(0, count_x, 2)
    far = lax.ppermute(
        far,
        "gx",
        [(i, (i - 1) % count_x) for i in evens] + [((i - 1) % count_x, i) for i in evens],
    )
    near = lax.ppermute(near, "gx", [(i, i + 1) for i in evens] + [(i + 1, i) for i in evens])
    side = across_y(side)
    corner, up_first, down_first = pack(place, relaxed, far, near, side)
    inner = [(i, i + 1) for i in range(0, count_z - 1, 2)]
    outer = [(i, i + 1) for i in range(1, count_z - 1, 2)]
    down_first = lax.ppermute(down_first, "gz", outer + [(j, i) for i, j in outer])
    corner = across_y(corner)
    up_first = lax.ppermute(up_first, "gz", inner + [(j, i) for i, j in inner])
    populations_next = stream(
        count_z, place, relaxed, far, near, side, down_first, corner, up_first
    )
    marker_force = marker_force.transpose(1, 0, 2).reshape(1, 1, 1, owned, 3, mark)
    return (populations_next, marker_force)


def solution(mesh):
    placed = (
        P(None, "gx", "gy", "gz"),
        P("gx", "gy", "gz"),
        P("gx", "gy", "gz", None, None, None),
        P("gx", "gy", "gz", None, None, None),
        P("gx", "gy", "gz", None, None),
        P("gx", "gy", "gz", None),
        P("gx", "gy", "gz", None),
        P("gx", "gy", "gz", None, None),
        P(),
    )
    small = mesh.shape["gy"] == 2 and mesh.shape["gx"] == 4 and mesh.shape["gz"] % 2 == 0
    return jax.shard_map(
        per_device if small else per_device_general,
        mesh=mesh,
        in_specs=placed,
        out_specs=(P(None, "gx", "gy", "gz"), P("gx", "gy", "gz", None, None, None)),
        check_vma=False,
    )
```

```python
import functools
import jax
import jax.numpy as jnp
import numpy as np
from jax import lax
from jax.experimental import pallas as pl
from jax.experimental.pallas import tpu as pltpu
from jax.sharding import PartitionSpec as P

velocity_table = np.array(
    [
        [0, 0, 0],
        [1, 0, 0],
        [-1, 0, 0],
        [0, 1, 0],
        [0, -1, 0],
        [0, 0, 1],
        [0, 0, -1],
        [1, 1, 0],
        [-1, -1, 0],
        [1, -1, 0],
        [-1, 1, 0],
        [1, 0, 1],
        [-1, 0, -1],
        [1, 0, -1],
        [-1, 0, 1],
        [0, 1, 1],
        [0, -1, -1],
        [0, 1, -1],
        [0, -1, 1],
    ]
)
weight_table = [1.0 / 3.0] + [1.0 / 18.0] * 6 + [1.0 / 36.0] * 12
opposite_table = [0, 2, 1, 4, 3, 6, 5, 8, 7, 10, 9, 12, 11, 14, 13, 16, 15, 18, 17]
stress_pairs = [(0, 0), (1, 1), (2, 2), (0, 1), (0, 2), (1, 2)]
tau_base = 0.55
smag_term = 18.0 * 1.4142135623730951 * 0.17 * 0.17
regular_eps = 0.0001
stiffness = 2.0
far_velocity = (0.02, 0.06, 0.0)
vmem_bytes = 16 << 20
group = 8
fine = jnp.float8_e4m3fn


def going(axis, step):
    return [q for q in range(19) if int(velocity_table[q][axis]) == step]


def project(direction, vector):
    projection = 0.0 * vector[0]
    for component in range(3):
        lattice_step = int(velocity_table[direction][component])
        if lattice_step != 0:
            projection = projection + lattice_step * vector[component]
    return projection


def moments(populations):
    density = populations[0]
    momentum = [jnp.zeros_like(density) for component in range(3)]
    for direction in range(1, 19):
        density = density + populations[direction]
        for component in range(3):
            lattice_step = int(velocity_table[direction][component])
            if lattice_step == 1:
                momentum[component] = momentum[component] + populations[direction]
            elif lattice_step == -1:
                momentum[component] = momentum[component] - populations[direction]
    return (density, momentum)


def equilibrium(density, velocity):
    speed_sq = velocity[0] * velocity[0] + velocity[1] * velocity[1] + velocity[2] * velocity[2]
    result = []
    for direction in range(19):
        projected = project(direction, velocity)
        result.append(
            weight_table[direction]
            * density
            * (1.0 + 3.0 * projected + 4.5 * projected * projected - 1.5 * speed_sq)
        )
    return result


far_field = [float(np.float32(value)) for value in equilibrium(1.0, list(far_velocity))]


def collide(populations, cell_force, solid_cells):
    density, momentum = moments(populations)
    velocity = [
        (momentum[component] + 0.5 * cell_force[component]) / density for component in range(3)
    ]
    balance = equilibrium(density, velocity)
    stress = [jnp.zeros_like(density) for pair_pos in range(6)]
    for direction in range(19):
        non_eq = populations[direction] - balance[direction]
        for pair_pos in range(6):
            row_axis, col_axis = stress_pairs[pair_pos]
            factor = int(velocity_table[direction][row_axis] * velocity_table[direction][col_axis])
            if factor != 0:
                stress[pair_pos] = stress[pair_pos] + factor * non_eq
    shear_sq = stress[0] * stress[0] + stress[1] * stress[1] + stress[2] * stress[2]
    shear_sq = shear_sq + 2.0 * (
        stress[3] * stress[3] + stress[4] * stress[4] + stress[5] * stress[5]
    )
    magnitude = jnp.sqrt(shear_sq + regular_eps)
    relax_time = 0.5 * (tau_base + jnp.sqrt(tau_base * tau_base + smag_term * magnitude / density))
    relax_rate = 1.0 / relax_time
    guo_factor = 1.0 - 0.5 * relax_rate
    speed_force = (
        velocity[0] * cell_force[0] + velocity[1] * cell_force[1] + velocity[2] * cell_force[2]
    )
    result = []
    for direction in range(19):
        along_force = project(direction, cell_force)
        along_speed = project(direction, velocity)
        source = (
            guo_factor
            * weight_table[direction]
            * (3.0 * (along_force - speed_force) + 9.0 * along_speed * along_force)
        )
        relaxed = (
            populations[direction]
            - (populations[direction] - balance[direction]) * relax_rate
            + source
        )
        result.append(jnp.where(solid_cells == 1, populations[opposite_table[direction]], relaxed))
    return result


def with_halo(cells, sides, width):
    for axis, dim in sides:
        count = lax.axis_size(axis)
        head = lax.slice_in_dim(cells, 0, width, axis=dim)
        tail = lax.slice_in_dim(cells, cells.shape[dim] - width, cells.shape[dim], axis=dim)
        cells = jnp.concatenate(
            [
                lax.ppermute(tail, axis, [(i, (i + 1) % count) for i in range(count)]),
                cells,
                lax.ppermute(head, axis, [((i + 1) % count, i) for i in range(count)]),
            ],
            axis=dim,
        )
    return cells


def settle(received, labels, owned, train_of_block, marker_area, train_velocity, mark):
    rows_in = received.reshape(-1, 3 * mark)
    label_rows = labels.reshape(-1)
    owner_match = (label_rows[None, :] == jnp.arange(owned, dtype=jnp.int32)[:, None]).astype(
        jnp.float32
    )
    marker_velocity = jnp.dot(owner_match, rows_in, precision=lax.Precision.HIGHEST).reshape(
        owned, 3, mark
    )
    trains = train_velocity.shape[0]
    train_rows = train_of_block.reshape(owned)
    train_match = (train_rows[:, None] == jnp.arange(trains, dtype=jnp.int32)[None, :]).astype(
        jnp.float32
    )
    target = jnp.dot(train_match, train_velocity, precision=lax.Precision.HIGHEST)
    areas = marker_area.reshape(owned, mark)
    marker_force = stiffness * areas[:, None, :] * (target[:, :, None] - marker_velocity)
    back_rows = jnp.dot(
        owner_match.T, marker_force.reshape(owned, 3 * mark), precision=lax.Precision.HIGHEST
    )
    return (marker_force, back_rows)


def per_device_general(
    populations,
    solid_cells,
    slot_cells,
    slot_weights,
    slot_owner,
    slot_block,
    train_of_block,
    marker_area,
    train_velocity,
):
    size_x, size_y, size_z = (populations.shape[1], populations.shape[2], populations.shape[3])
    cell_count = size_x * size_y * size_z
    slots, kernel, mark = (slot_cells.shape[3], slot_cells.shape[4], slot_cells.shape[5])
    owned = train_of_block.shape[3]
    peers_x = lax.axis_size("gx")
    peers_y = lax.axis_size("gy")
    peers = peers_x * peers_y
    capacity = max(2, 2 * slots // peers)
    density, momentum = moments(populations)
    rest_velocity = jnp.stack([momentum[component] / density for component in range(3)]).reshape(
        3, cell_count
    )
    cells = slot_cells.reshape(slots, kernel, mark)
    weights = slot_weights.reshape(slots, kernel, mark)
    partial_value = jnp.sum(rest_velocity[:, cells] * weights[None], axis=2)
    slot_rows = partial_value.transpose(1, 0, 2).reshape(slots, 3 * mark)
    slot_dest = slot_owner.reshape(slots)
    blocks = slot_block.reshape(slots)
    order = jnp.arange(slots, dtype=jnp.int32)
    earlier = (slot_dest[None, :] == slot_dest[:, None]) & (order[None, :] < order[:, None])
    slot_rank = jnp.sum(earlier.astype(jnp.int32), axis=1)
    target_row = slot_dest * capacity + slot_rank
    buffer_rows = jnp.arange(peers * capacity, dtype=jnp.int32)
    matches = buffer_rows[:, None] == target_row[None, :]
    placement = matches.astype(jnp.float32)
    outgoing = jnp.dot(placement, slot_rows, precision=lax.Precision.HIGHEST)
    labels = jnp.sum(jnp.where(matches, blocks[None, :] + 1, 0), axis=1) - 1
    received, got_labels = (
        lax.all_to_all(
            outgoing.reshape(peers, capacity, 3 * mark),
            ("gx", "gy"),
            split_axis=0,
            concat_axis=0,
            tiled=True,
        ),
        lax.all_to_all(
            labels.reshape(peers, capacity), ("gx", "gy"), split_axis=0, concat_axis=0, tiled=True
        ),
    )
    marker_force, back_rows = settle(
        received, got_labels, owned, train_of_block, marker_area, train_velocity, mark
    )
    returned = lax.all_to_all(
        back_rows.reshape(peers, capacity, 3 * mark),
        ("gx", "gy"),
        split_axis=0,
        concat_axis=0,
        tiled=True,
    )
    slot_force = jnp.dot(
        placement.T, returned.reshape(peers * capacity, 3 * mark), precision=lax.Precision.HIGHEST
    )
    slot_force = slot_force.reshape(slots, 3, mark).transpose(1, 0, 2)
    contrib = weights[None] * slot_force[:, :, None, :]
    cell_force = (
        jnp.zeros((3, cell_count), jnp.float32).at[:, cells.reshape(-1)].add(contrib.reshape(3, -1))
    )
    cell_force = cell_force.reshape(3, size_x, size_y, size_z)
    relaxed = collide(populations, cell_force, solid_cells)
    padded = with_halo(jnp.stack(relaxed), (("gx", 1), ("gy", 2), ("gz", 3)), 1)
    parts = []
    for direction in range(19):
        shift_x = 1 - int(velocity_table[direction][0])
        shift_y = 1 - int(velocity_table[direction][1])
        shift_z = 1 - int(velocity_table[direction][2])
        parts.append(
            padded[
                direction,
                shift_x : shift_x + size_x,
                shift_y : shift_y + size_y,
                shift_z : shift_z + size_z,
            ]
        )
    read = jnp.stack(parts)
    total_y = size_y * lax.axis_size("gy")
    total_z = size_z * lax.axis_size("gz")
    global_y = lax.axis_index("gy") * size_y + jnp.arange(size_y, dtype=jnp.int32)
    global_z = lax.axis_index("gz") * size_z + jnp.arange(size_z, dtype=jnp.int32)
    on_side = ((global_y == 0) | (global_y == total_y - 1))[:, None] | (
        (global_z == 0) | (global_z == total_z - 1)
    )[None, :]
    far_field = jnp.array(equilibrium(1.0, list(far_velocity)), dtype=jnp.float32)
    populations_next = jnp.where(on_side[None, None], far_field[:, None, None, None], read)
    return (populations_next, marker_force.reshape(1, 1, 1, owned, 3, mark))


def full(shape):
    return jax.ShapeDtypeStruct(shape, jnp.float32)


def kernel_params():
    return pltpu.CompilerParams(vmem_limit_bytes=vmem_bytes)


def low_half(shape):
    return lax.broadcasted_iota(jnp.int32, shape, 1) < shape[1] // 2


def fetch(pairs, sems):
    copies = [
        pltpu.make_async_copy(source, target, sems.at[i])
        for i, (source, target) in enumerate(pairs)
    ]
    for copy in copies:
        copy.start()
    return copies


def shard_rows(slots, owned):
    return 8 + owned + 3 * slots


def sample_kernel(
    place_ref, pop_any, cells_any, weights_any, areas_any, owner_any, block_any, trains_any,
    out_ref, pop_ref, cells_ref, weights_ref, areas_ref, owner_ref, block_ref, trains_ref,
    table, sems,
):
    rows, lanes = (pop_ref.shape[1], pop_ref.shape[2])
    mark = cells_ref.shape[1]
    owned = areas_ref.shape[0]
    slots = owner_ref.shape[1]
    kernel = cells_ref.shape[0] // slots
    copies = fetch(
        (
            (pop_any, pop_ref),
            (cells_any, cells_ref),
            (weights_any, weights_ref),
            (areas_any, areas_ref),
            (owner_any, owner_ref),
            (block_any, block_ref),
            (trains_any, trains_ref),
        ),
        sems,
    )

    copies[0].wait()
    density, momentum = moments([pop_ref[q] for q in range(19)])
    speed = [momentum[c] / density for c in range(3)]
    largest = jnp.maximum(jnp.maximum(jnp.abs(speed[0]), jnp.abs(speed[1])), jnp.abs(speed[2]))
    largest = jnp.max(largest, axis=(0, 1), keepdims=True) + 1e-20
    scale = largest * (1.0 / 32767.0)
    fixed = [(speed[c] * (1.0 / scale) + 32768.5).astype(jnp.int32) for c in range(3)]
    words = jnp.concatenate(
        [
            (fixed[0] << 16) | fixed[1],
            (fixed[2][: rows // 2] << 16) | fixed[2][rows // 2 :],
        ],
        axis=0,
    )
    for r in range(table.shape[0]):
        table[r] = jnp.broadcast_to(words[r : r + 1], (group, lanes))
    for copy in copies[1:]:
        copy.wait()
    out_ref[8 : 8 + owned, :] = areas_ref[...]
    out_ref[0:8, :] = jnp.zeros((8, mark), jnp.float32)
    ids = (owner_ref[...] * owned + block_ref[...]).astype(jnp.float32)
    out_ref[0:1, :] = jnp.concatenate([ids] * (mark // slots), axis=1)
    out_ref[1:2, 0:owned] = trains_ref[...].astype(jnp.float32)
    mine = lax.broadcasted_iota(jnp.int32, (1, mark), 1) % owned + place_ref[2] * owned
    out_ref[2:3, :] = mine.astype(jnp.float32)

    def body(step, carry):
        first = pl.multiple_of(step * group, group)
        total = [jnp.zeros((group, mark), jnp.float32) for c in range(3)]
        for k in range(kernel):
            at = pl.ds(first * kernel + k, group, stride=kernel)
            cells = cells_ref[at, :]
            lane = cells & (lanes - 1)
            row = cells >> (lanes.bit_length() - 1)
            bits = [(row >> bit) & 1 == 1 for bit in range(rows.bit_length() - 1)]

            def choose(low, level):
                if level < 0:
                    return jnp.take_along_axis(table[low], lane, axis=1, mode="promise_in_bounds")
                lower = choose(low, level - 1)
                return jnp.where(bits[level], choose(low + (1 << level), level - 1), lower)

            pair = choose(0, len(bits) - 1)
            third = choose(rows, len(bits) - 2)
            picked = [
                lax.shift_right_logical(pair, 16),
                pair & 65535,
                jnp.where(bits[-1], third & 65535, lax.shift_right_logical(third, 16)),
            ]
            weight = weights_ref[at, :]
            for c in range(3):
                total[c] = total[c] + weight * (picked[c].astype(jnp.float32) - 32768.0)
        for c in range(3):
            here = pl.ds(pl.multiple_of(8 + owned + c * slots + first, group), group)
            out_ref[here, :] = total[c] * scale
        return carry

    lax.fori_loop(0, slots // group, body, 0)


def sample(place, populations, cells, weights, areas, owner, block, trains):
    smem = pl.BlockSpec(memory_space=pltpu.SMEM)
    hbm = pl.BlockSpec(memory_space=pltpu.HBM)
    vmem = pl.BlockSpec(memory_space=pltpu.VMEM)
    kept = (populations, cells, weights)
    count = shard_rows(owner.shape[1], areas.shape[0])
    return pl.pallas_call(
        sample_kernel,
        out_shape=[full((count, cells.shape[1]))]
        + [jax.ShapeDtypeStruct(entries.shape, entries.dtype) for entries in kept],
        in_specs=[smem] + [hbm] * 7,
        out_specs=[vmem] * 4,
        scratch_shapes=[
            pltpu.VMEM(entries.shape, entries.dtype) for entries in (areas, owner, block, trains)
        ]
        + [
            pltpu.VMEM((populations.shape[1] * 3 // 2, group, populations.shape[2]), jnp.int32),
            pltpu.SemaphoreType.DMA((7,)),
        ],
        compiler_params=kernel_params(),
        name="sample",
    )(place, populations, cells, weights, areas, owner, block, trains)


def three_parts(values):
    parts = []
    for _ in range(3):
        parts.append(values.astype(jnp.bfloat16))
        values = values - parts[-1].astype(jnp.float32)
    return parts


def one_hot(mask):
    return jnp.where(mask, 1.0, 0.0).astype(jnp.bfloat16)


def wanted_labels(own_ref, slots, owned):
    mark = own_ref.shape[1]
    own = own_ref[0:8, :]
    ids, trains, mine = (jnp.broadcast_to(own[i : i + 1], (mark, mark)).T for i in range(3))
    return (ids[0:slots], mine[0:owned], trains[0:owned])


def add_shards(totals, shards, ids, mine):
    slots, owned = (ids.shape[0], mine.shape[0])
    wanted = jnp.concatenate([ids, mine], axis=0)
    for shard in shards:
        match = one_hot(wanted == shard[0:1, :])
        match = jnp.concatenate([match, match[:, 0:slots]], axis=1)
        starts = [8 + owned + c * slots for c in range(3)]
        values = jnp.concatenate([shard[at : at + slots, :] for at in starts], axis=1)
        sums = jnp.dot(
            match, jnp.concatenate(three_parts(values), axis=0), preferred_element_type=jnp.float32
        )
        held = ids == shard[2:3, :]
        parts = three_parts(shard[8 : 8 + owned, :])
        parts.append(jnp.zeros_like(parts[0]))
        area = jnp.dot(
            one_hot(held), jnp.concatenate(parts, axis=0), preferred_element_type=jnp.float32
        )
        got = (sums, area, jnp.where(held, shard[1:2, :], 0.0))
        totals = got if totals is None else [total + new for total, new in zip(totals, got)]
    return totals


def settle_kernel(slots, owned, speeds_ref, *refs):
    *shards, sums_ref, area_ref, trains_ref, rows_ref = refs
    mark = rows_ref.shape[1]
    for train in range(speeds_ref.shape[0]):
        for c in range(3):
            at = 3 * train + c
            rows_ref[at : at + 1, :] = jnp.full((1, mark), speeds_ref[train, c], jnp.float32)
    ids, mine, _ = wanted_labels(shards[0], slots, owned)
    sums_ref[...], area_ref[...], trains_ref[...] = add_shards(None, shards, ids, mine)


def settle_early(slots, owned, speeds, shards):
    mark = shards[0].shape[1]
    smem = pl.BlockSpec(memory_space=pltpu.SMEM)
    vmem = pl.BlockSpec(memory_space=pltpu.VMEM)
    return pl.pallas_call(
        functools.partial(settle_kernel, slots, owned),
        out_shape=(
            full((slots + owned, 3 * mark)),
            full((slots, mark)),
            full((slots, mark)),
            full((3 * speeds.shape[0], mark)),
        ),
        in_specs=[smem] + [vmem] * len(shards),
        compiler_params=kernel_params(),
        cost_estimate=pl.CostEstimate(
            flops=10**9, bytes_accessed=len(shards) * shards[0].size * 4, transcendentals=0
        ),
        name="settle",
    )(speeds, *shards)


def block_forces(rows_ref, totals, own_ref, slots, owned):
    mark = own_ref.shape[1]
    ids, mine, own_trains = wanted_labels(own_ref, slots, owned)
    sums, area, trains = totals
    trains = jnp.broadcast_to(jnp.sum(trains, axis=1, keepdims=True), area.shape)
    own_area = own_ref[8 : 8 + owned, :]
    forces, own_forces = ([], [])
    for c in range(3):
        target, own_target = (jnp.zeros_like(area), jnp.zeros_like(own_area))
        for train in range(rows_ref.shape[0] // 3):
            at = 3 * train + c
            speed = rows_ref[at : at + 1, :]
            target = jnp.where(trains == float(train), speed, target)
            own_target = jnp.where(own_trains == float(train), speed, own_target)
        got = sums[:, c * mark : (c + 1) * mark]
        forces.append(stiffness * area * (target - got[0:slots]))
        own_forces.append(stiffness * own_area * (own_target - got[slots:]))
    return (forces, own_forces)


def spread_kernel(
    slots, owned, place_ref, own_ref, last_ref, sums_ref, area_ref, trains_ref, speeds_ref,
    cells_ref, weights_ref, pop_ref, solid_ref,
    relaxed_ref, far_ref, near_ref, side_ref, marker_any, marker_ref, force_ref, lines_ref, acc,
    sem,
):
    rows, lanes = (pop_ref.shape[1], pop_ref.shape[2])
    size_y = 8
    mark = cells_ref.shape[1]
    kernel = cells_ref.shape[0] // slots
    bf = jnp.bfloat16
    ids, mine, _ = wanted_labels(own_ref, slots, owned)
    totals = add_shards((sums_ref[...], area_ref[...], trains_ref[...]), [last_ref], ids, mine)
    forces, own_forces = block_forces(speeds_ref, totals, own_ref, slots, owned)
    largest = jnp.maximum(jnp.maximum(jnp.abs(forces[0]), jnp.abs(forces[1])), jnp.abs(forces[2]))
    largest = jnp.maximum(jnp.max(largest, axis=(0, 1), keepdims=True), 1e-20)
    scale = (224.0 * 16.0) / largest
    for c in range(3):
        force_ref[c] = forces[c] * scale
        marker_ref[c] = own_forces[c]
    marker_copy = pltpu.make_async_copy(marker_ref, marker_any, sem)
    marker_copy.start()

    acc[...] = jnp.zeros_like(acc)
    iota = lax.broadcasted_iota(jnp.int32, (16, mark), 0).astype(jnp.float32)
    steps = [(iota + 16.0 * j).astype(bf) for j in range(max(rows, lanes) // 16)]
    one, zero = (jnp.ones((16, mark), bf), jnp.zeros((16, mark), bf))

    def body(step, carry):
        first = pl.multiple_of(step * group, group)
        force = [force_ref[c, pl.ds(first, group), :] for c in range(3)]
        for k in range(kernel):
            at = pl.ds(first * kernel + k, group, stride=kernel)
            cells = cells_ref[at, :]
            weight = weights_ref[at, :]
            lane = (cells & (lanes - 1)).astype(jnp.float32)
            row = (cells >> (lanes.bit_length() - 1)).astype(jnp.float32)
            parts = []
            for c in range(3):
                value = weight * force[c]
                for _ in range(3):
                    parts.append(value.astype(fine).astype(jnp.float32))
                    value = (value - parts[-1]) * 16.0
            for which, entries in enumerate([lane, row] + parts):
                lines_ref[k, which] = entries

            def wide(which, i):
                entries = lines_ref[k, which, pl.ds(i, 8, stride=0), :]
                return jnp.concatenate([entries, entries], axis=0).astype(bf)

            left, right = ([], [])
            for i in range(group):
                lane_i, row_i = (wide(0, i), wide(1, i))
                match = [jnp.where(steps[j] == lane_i, one, zero) for j in range(lanes // 16)]
                right.append(jnp.concatenate(match, axis=0).astype(fine))
                masks = [steps[j] == row_i for j in range(rows // 16)]
                pieces = []
                for which in range(len(parts)):
                    part_i = wide(2 + which, i)
                    piece = [jnp.where(mask, part_i, zero) for mask in masks]
                    pieces.append(jnp.concatenate(piece, axis=0).astype(fine))
                left.append(jnp.concatenate(pieces, axis=0))
            acc[...] += lax.dot_general(
                jnp.concatenate(left, axis=1),
                jnp.concatenate(right, axis=1),
                (((1,), (1,)), ((), ())),
                preferred_element_type=jnp.float32,
            )
        return carry

    lax.fori_loop(0, slots // group, body, 0)
    cell_force = []
    for c in range(3):
        total = acc[3 * c * rows : (3 * c + 1) * rows, :]
        total = total + acc[(3 * c + 1) * rows : (3 * c + 2) * rows, :] * (1.0 / 16.0)
        total = total + acc[(3 * c + 2) * rows : (3 * c + 3) * rows, :] * (1.0 / 256.0)
        cell_force.append(total * (1.0 / scale))
    relaxed = collide([pop_ref[q] for q in range(19)], cell_force, solid_ref[...])
    for q in range(19):
        relaxed_ref[q] = relaxed[q]
    even = place_ref[3] == 0
    for i in range(5):
        ahead = relaxed[going(0, 1)[i]][rows - size_y :]
        behind = relaxed[going(0, -1)[i]][:size_y]
        far_ref[i] = jnp.where(even, behind, ahead)
        near_ref[i] = jnp.where(even, ahead, behind)
        for x in range(rows // size_y):
            up = relaxed[going(1, 1)[i]][size_y * x + size_y - 1 : size_y * x + size_y, :]
            down = relaxed[going(1, -1)[i]][size_y * x : size_y * x + 1, :]
            side_ref[i, x : x + 1, :] = jnp.where(place_ref[0] == 0, up, down)
    marker_copy.wait()


def spread(owned, place, own, last, early, cells, weights, populations, solid):
    mark = cells.shape[1]
    slots = early[1].shape[0]
    line_count, lanes = solid.shape
    smem = pl.BlockSpec(memory_space=pltpu.SMEM)
    vmem = pl.BlockSpec(memory_space=pltpu.VMEM)
    return pl.pallas_call(
        functools.partial(spread_kernel, slots, owned),
        out_shape=(
            full(populations.shape),
            full((5, 8, lanes)),
            full((5, 8, lanes)),
            full((5, 8, lanes)),
            full((3, owned, mark)),
        ),
        in_specs=[smem] + [vmem] * 10,
        out_specs=[vmem] * 4 + [pl.BlockSpec(memory_space=pltpu.HBM)],
        scratch_shapes=[
            pltpu.VMEM((3, owned, mark), jnp.float32),
            pltpu.VMEM((3, slots, mark), jnp.float32),
            pltpu.VMEM((cells.shape[0] // slots, 11, group, mark), jnp.float32),
            pltpu.VMEM((9 * line_count, lanes), jnp.float32),
            pltpu.SemaphoreType.DMA,
        ],
        compiler_params=kernel_params(),
        name="spread",
    )(place, own, last, *early, cells, weights, populations, solid)


def downwind(place_ref, relaxed_ref, far_ref, near_ref):
    size_y = far_ref.shape[1]
    size_x = relaxed_ref.shape[1] // size_y
    even = place_ref[3] == 0

    def cells(q, x):
        step = int(velocity_table[q][0])
        source = x - step
        if 0 <= source < size_x:
            return relaxed_ref[q, source * size_y : (source + 1) * size_y, :]
        i = going(0, step).index(q)
        if step == 1:
            return jnp.where(even, far_ref[i], near_ref[i])
        return jnp.where(even, near_ref[i], far_ref[i])

    return cells


def sideways(size_x, cells, side_ref, edge):
    def result(q, x, y_at):
        step_x, step_y = (int(step) for step in velocity_table[q][:2])
        size_y = y_at.shape[0]
        if step_y == 0:
            return cells(q, x)
        source = x - step_x
        if 0 <= source < size_x:
            halo = side_ref[going(1, step_y).index(q), source : source + 1, :]
        else:
            halo = edge(q)
        turned = pltpu.roll(cells(q, x), step_y % size_y, 0)
        return jnp.where(y_at == (0 if step_y == 1 else size_y - 1), halo, turned)

    return result


def corner_index(q):
    step_y = int(velocity_table[q][1])
    return [p for p in going(1, step_y) if int(velocity_table[p][0]) != 0].index(q)


def pack_kernel(
    place_ref, relaxed_ref, far_ref, side_ref, near_ref, corner_ref, first_ref, second_ref
):
    size_y, lanes = far_ref.shape[1:]
    size_x = relaxed_ref.shape[1] // size_y
    cells = downwind(place_ref, relaxed_ref, far_ref, near_ref)
    corner_ref[...] = jnp.zeros(corner_ref.shape, jnp.float32)
    for ahead in going(1, 1):
        step_x = int(velocity_table[ahead][0])
        if step_x == 0:
            continue
        behind = opposite_table[ahead]
        up = cells(ahead, 0 if step_x == 1 else size_x - 1)[size_y - 1 : size_y, :]
        down = cells(behind, size_x - 1 if step_x == 1 else 0)[0:1, :]
        at = corner_index(ahead)
        from_behind = corner_index(behind)
        lower = place_ref[0] == 0

        @pl.when(lower)
        def _(at=at, up=up):
            corner_ref[at : at + 1, :] = up

        @pl.when(jnp.logical_not(lower))
        def _(at=from_behind, down=down):
            corner_ref[at : at + 1, :] = down

    y_at = lax.broadcasted_iota(jnp.int32, (size_y, lanes), 0)
    lane_at = lax.broadcasted_iota(jnp.int32, (size_y, lanes), 1)
    level = sideways(size_x, cells, side_ref, None)
    packs = []
    for step in (1, -1):
        packed = jnp.zeros((size_y, lanes), jnp.float32)
        for i, q in enumerate(going(2, step)):
            edge = lanes - 1 if step == 1 else 0
            for x in range(size_x):
                at = 8 * x + i
                moved = pltpu.roll(level(q, x, y_at), (at - edge) % lanes, 1)
                packed = jnp.where(lane_at == at, moved, packed)
        packs.append(packed)
    even = place_ref[1] % 2 == 0
    first_ref[...] = jnp.where(even, packs[0], packs[1])
    second_ref[...] = jnp.where(even, packs[1], packs[0])


def pack(place, relaxed, far, side, near):
    smem = pl.BlockSpec(memory_space=pltpu.SMEM)
    vmem = pl.BlockSpec(memory_space=pltpu.VMEM)
    edge = full(far.shape[1:])
    return pl.pallas_call(
        pack_kernel,
        out_shape=(edge, edge, edge),
        in_specs=[smem] + [vmem] * 4,
        compiler_params=kernel_params(),
        name="pack",
    )(place, relaxed, far, side, near)


def stream_kernel(
    count_z, place_ref, relaxed_ref, far_ref, side_ref, near_ref, second_ref, corner_ref,
    first_ref, out_any, out_ref, sems,
):
    size_x, size_y, lanes = out_ref.shape[1:]
    shape = (size_y, lanes)
    y_at = lax.broadcasted_iota(jnp.int32, shape, 0)
    z_at = lax.broadcasted_iota(jnp.int32, shape, 1)
    y_index, z_index = (place_ref[0], place_ref[1])
    streamed = sideways(
        size_x,
        downwind(place_ref, relaxed_ref, far_ref, near_ref),
        side_ref,
        lambda q: corner_ref[corner_index(q) : corner_index(q) + 1, :],
    )
    even = z_index % 2 == 0
    columns = {
        -1: jnp.where(even, first_ref[...], second_ref[...]),
        1: jnp.where(even, second_ref[...], first_ref[...]),
    }
    on_side = y_at == jnp.where(y_index == 0, 0, size_y - 1)
    on_side = on_side | ((z_at == 0) & (z_index == 0))
    on_side = on_side | ((z_at == lanes - 1) & (z_index == count_z - 1))
    copies = []
    for q in range(19):
        step_z = int(velocity_table[q][2])
        z_edge = 0 if step_z == 1 else lanes - 1
        for x in range(size_x):
            cells = streamed(q, x, y_at)
            if step_z != 0:
                at = 8 * x + going(2, step_z).index(q)
                cells = jnp.where(
                    z_at == z_edge,
                    pltpu.roll(columns[step_z], (z_edge - at) % lanes, 1),
                    pltpu.roll(cells, step_z % lanes, 1),
                )
            out_ref[q, x] = jnp.where(on_side, far_field[q], cells)
        copies.append(pltpu.make_async_copy(out_ref.at[q], out_any.at[q], sems.at[q]))
        copies[-1].start()
    for copy in copies:
        copy.wait()


def stream(count_z, place, relaxed, *halos):
    rows, lanes = relaxed.shape[1:]
    size_y = halos[0].shape[1]
    smem = pl.BlockSpec(memory_space=pltpu.SMEM)
    vmem = pl.BlockSpec(memory_space=pltpu.VMEM)
    shape = (19, rows // size_y, size_y, lanes)
    return pl.pallas_call(
        functools.partial(stream_kernel, count_z),
        out_shape=full(shape),
        in_specs=[smem] + [vmem] * (1 + len(halos)),
        out_specs=pl.BlockSpec(memory_space=pltpu.HBM),
        scratch_shapes=[pltpu.VMEM(shape, jnp.float32), pltpu.SemaphoreType.DMA((19,))],
        compiler_params=kernel_params(),
        name="stream",
    )(place, relaxed, *halos)


def per_device(
    populations,
    solid_cells,
    slot_cells,
    slot_weights,
    slot_owner,
    slot_block,
    train_of_block,
    marker_area,
    train_velocity,
):
    size_x, size_y, size_z = (populations.shape[1], populations.shape[2], populations.shape[3])
    lines = size_x * size_y
    slots, kernel, mark = (slot_cells.shape[3], slot_cells.shape[4], slot_cells.shape[5])
    owned = train_of_block.shape[3]
    count_x, count_y, count_z = (lax.axis_size(axis) for axis in ("gx", "gy", "gz"))
    x_index, y_index, z_index = (lax.axis_index(axis) for axis in ("gx", "gy", "gz"))
    place = jnp.stack([y_index, z_index, x_index * count_y + y_index, x_index % 2])
    place = place.astype(jnp.int32)
    inputs = [
        pltpu.with_memory_space_constraint(entries, pltpu.HBM)
        for entries in (
            populations.reshape(19, lines, size_z),
            slot_cells.reshape(slots * kernel, mark),
            slot_weights.reshape(slots * kernel, mark),
            marker_area.reshape(owned, mark),
            slot_owner.reshape(1, slots),
            slot_block.reshape(1, slots),
            train_of_block.reshape(1, owned),
        )
    ]
    own, pops, cells, weights = sample(place, *inputs)
    swap = [(0, 1), (1, 0)]

    def across_x(entries, distance):
        return lax.ppermute(entries, "gx", [(i, i ^ distance) for i in range(count_x)])

    def across_y(entries):
        return lax.ppermute(entries, "gy", swap)

    third, first = (across_x(own, distance) for distance in (3, 1))
    beside = across_y(own)
    third_beside = across_y(lax.optimization_barrier((third, beside))[0])
    second = across_x(third, 1)
    first_beside = across_y(first)
    last = across_x(third_beside, 1)
    whole = [own, first, third, second, beside, first_beside, third_beside]
    early = settle_early(slots, owned, train_velocity, whole)
    solid = solid_cells.reshape(lines, size_z)
    relaxed, far, near, side, marker_force = spread(
        owned, place, own, last, early, cells, weights, pops, solid
    )
    evens = range(0, count_x, 2)
    far = lax.ppermute(
        far,
        "gx",
        [(i, (i - 1) % count_x) for i in evens] + [((i - 1) % count_x, i) for i in evens],
    )
    side = across_y(side)
    near = lax.ppermute(near, "gx", [(i, i + 1) for i in evens] + [(i + 1, i) for i in evens])
    corner, up_first, down_first = pack(place, relaxed, far, side, near)
    inner = [(i, i + 1) for i in range(0, count_z - 1, 2)]
    outer = [(i, i + 1) for i in range(1, count_z - 1, 2)]
    down_first = lax.ppermute(down_first, "gz", outer + [(j, i) for i, j in outer])
    corner = across_y(corner)
    up_first = lax.ppermute(up_first, "gz", inner + [(j, i) for i, j in inner])
    populations_next = stream(
        count_z, place, relaxed, far, side, near, down_first, corner, up_first
    )
    marker_force = marker_force.transpose(1, 0, 2).reshape(1, 1, 1, owned, 3, mark)
    return (populations_next, marker_force)


def solution(mesh):
    placed = (
        P(None, "gx", "gy", "gz"),
        P("gx", "gy", "gz"),
        P("gx", "gy", "gz", None, None, None),
        P("gx", "gy", "gz", None, None, None),
        P("gx", "gy", "gz", None, None),
        P("gx", "gy", "gz", None),
        P("gx", "gy", "gz", None),
        P("gx", "gy", "gz", None, None),
        P(),
    )
    small = mesh.shape["gy"] == 2 and mesh.shape["gx"] == 4 and mesh.shape["gz"] % 2 == 0
    return jax.shard_map(
        per_device if small else per_device_general,
        mesh=mesh,
        in_specs=placed,
        out_specs=(P(None, "gx", "gy", "gz"), P("gx", "gy", "gz", None, None, None)),
        check_vma=False,
    )
```

```python
import functools
import jax
import jax.numpy as jnp
import numpy as np
from jax import lax
from jax.experimental import pallas as pl
from jax.experimental.pallas import tpu as pltpu
from jax.sharding import PartitionSpec as P

velocity_table = np.array(
    [
        [0, 0, 0],
        [1, 0, 0],
        [-1, 0, 0],
        [0, 1, 0],
        [0, -1, 0],
        [0, 0, 1],
        [0, 0, -1],
        [1, 1, 0],
        [-1, -1, 0],
        [1, -1, 0],
        [-1, 1, 0],
        [1, 0, 1],
        [-1, 0, -1],
        [1, 0, -1],
        [-1, 0, 1],
        [0, 1, 1],
        [0, -1, -1],
        [0, 1, -1],
        [0, -1, 1],
    ]
)
weight_table = [1.0 / 3.0] + [1.0 / 18.0] * 6 + [1.0 / 36.0] * 12
opposite_table = [0, 2, 1, 4, 3, 6, 5, 8, 7, 10, 9, 12, 11, 14, 13, 16, 15, 18, 17]
stress_pairs = [(0, 0), (1, 1), (2, 2), (0, 1), (0, 2), (1, 2)]
tau_base = 0.55
smag_term = 18.0 * 1.4142135623730951 * 0.17 * 0.17
regular_eps = 0.0001
stiffness = 2.0
far_velocity = (0.02, 0.06, 0.0)
vmem_bytes = 16 << 20
group = 8
fine = jnp.float8_e4m3fn


def going(axis, step):
    return [q for q in range(19) if int(velocity_table[q][axis]) == step]


def project(direction, vector):
    projection = 0.0 * vector[0]
    for component in range(3):
        lattice_step = int(velocity_table[direction][component])
        if lattice_step != 0:
            projection = projection + lattice_step * vector[component]
    return projection


def moments(populations):
    density = populations[0]
    momentum = [jnp.zeros_like(density) for component in range(3)]
    for direction in range(1, 19):
        density = density + populations[direction]
        for component in range(3):
            lattice_step = int(velocity_table[direction][component])
            if lattice_step == 1:
                momentum[component] = momentum[component] + populations[direction]
            elif lattice_step == -1:
                momentum[component] = momentum[component] - populations[direction]
    return (density, momentum)


def equilibrium(density, velocity):
    speed_sq = velocity[0] * velocity[0] + velocity[1] * velocity[1] + velocity[2] * velocity[2]
    result = []
    for direction in range(19):
        projected = project(direction, velocity)
        result.append(
            weight_table[direction]
            * density
            * (1.0 + 3.0 * projected + 4.5 * projected * projected - 1.5 * speed_sq)
        )
    return result


far_field = [float(np.float32(value)) for value in equilibrium(1.0, list(far_velocity))]


def collide(populations, cell_force, solid_cells):
    density, momentum = moments(populations)
    velocity = [
        (momentum[component] + 0.5 * cell_force[component]) / density for component in range(3)
    ]
    balance = equilibrium(density, velocity)
    stress = [jnp.zeros_like(density) for pair_pos in range(6)]
    for direction in range(19):
        non_eq = populations[direction] - balance[direction]
        for pair_pos in range(6):
            row_axis, col_axis = stress_pairs[pair_pos]
            factor = int(velocity_table[direction][row_axis] * velocity_table[direction][col_axis])
            if factor != 0:
                stress[pair_pos] = stress[pair_pos] + factor * non_eq
    shear_sq = stress[0] * stress[0] + stress[1] * stress[1] + stress[2] * stress[2]
    shear_sq = shear_sq + 2.0 * (
        stress[3] * stress[3] + stress[4] * stress[4] + stress[5] * stress[5]
    )
    magnitude = jnp.sqrt(shear_sq + regular_eps)
    relax_time = 0.5 * (tau_base + jnp.sqrt(tau_base * tau_base + smag_term * magnitude / density))
    relax_rate = 1.0 / relax_time
    guo_factor = 1.0 - 0.5 * relax_rate
    speed_force = (
        velocity[0] * cell_force[0] + velocity[1] * cell_force[1] + velocity[2] * cell_force[2]
    )
    result = []
    for direction in range(19):
        along_force = project(direction, cell_force)
        along_speed = project(direction, velocity)
        source = (
            guo_factor
            * weight_table[direction]
            * (3.0 * (along_force - speed_force) + 9.0 * along_speed * along_force)
        )
        relaxed = (
            populations[direction]
            - (populations[direction] - balance[direction]) * relax_rate
            + source
        )
        result.append(jnp.where(solid_cells == 1, populations[opposite_table[direction]], relaxed))
    return result


def with_halo(cells, sides, width):
    for axis, dim in sides:
        count = lax.axis_size(axis)
        head = lax.slice_in_dim(cells, 0, width, axis=dim)
        tail = lax.slice_in_dim(cells, cells.shape[dim] - width, cells.shape[dim], axis=dim)
        cells = jnp.concatenate(
            [
                lax.ppermute(tail, axis, [(i, (i + 1) % count) for i in range(count)]),
                cells,
                lax.ppermute(head, axis, [((i + 1) % count, i) for i in range(count)]),
            ],
            axis=dim,
        )
    return cells


def settle(received, labels, owned, train_of_block, marker_area, train_velocity, mark):
    rows_in = received.reshape(-1, 3 * mark)
    label_rows = labels.reshape(-1)
    owner_match = (label_rows[None, :] == jnp.arange(owned, dtype=jnp.int32)[:, None]).astype(
        jnp.float32
    )
    marker_velocity = jnp.dot(owner_match, rows_in, precision=lax.Precision.HIGHEST).reshape(
        owned, 3, mark
    )
    trains = train_velocity.shape[0]
    train_rows = train_of_block.reshape(owned)
    train_match = (train_rows[:, None] == jnp.arange(trains, dtype=jnp.int32)[None, :]).astype(
        jnp.float32
    )
    target = jnp.dot(train_match, train_velocity, precision=lax.Precision.HIGHEST)
    areas = marker_area.reshape(owned, mark)
    marker_force = stiffness * areas[:, None, :] * (target[:, :, None] - marker_velocity)
    back_rows = jnp.dot(
        owner_match.T, marker_force.reshape(owned, 3 * mark), precision=lax.Precision.HIGHEST
    )
    return (marker_force, back_rows)


def per_device_general(
    populations,
    solid_cells,
    slot_cells,
    slot_weights,
    slot_owner,
    slot_block,
    train_of_block,
    marker_area,
    train_velocity,
):
    size_x, size_y, size_z = (populations.shape[1], populations.shape[2], populations.shape[3])
    cell_count = size_x * size_y * size_z
    slots, kernel, mark = (slot_cells.shape[3], slot_cells.shape[4], slot_cells.shape[5])
    owned = train_of_block.shape[3]
    peers_x = lax.axis_size("gx")
    peers_y = lax.axis_size("gy")
    peers = peers_x * peers_y
    capacity = max(2, 2 * slots // peers)
    density, momentum = moments(populations)
    rest_velocity = jnp.stack([momentum[component] / density for component in range(3)]).reshape(
        3, cell_count
    )
    cells = slot_cells.reshape(slots, kernel, mark)
    weights = slot_weights.reshape(slots, kernel, mark)
    partial_value = jnp.sum(rest_velocity[:, cells] * weights[None], axis=2)
    slot_rows = partial_value.transpose(1, 0, 2).reshape(slots, 3 * mark)
    slot_dest = slot_owner.reshape(slots)
    blocks = slot_block.reshape(slots)
    order = jnp.arange(slots, dtype=jnp.int32)
    earlier = (slot_dest[None, :] == slot_dest[:, None]) & (order[None, :] < order[:, None])
    slot_rank = jnp.sum(earlier.astype(jnp.int32), axis=1)
    target_row = slot_dest * capacity + slot_rank
    buffer_rows = jnp.arange(peers * capacity, dtype=jnp.int32)
    matches = buffer_rows[:, None] == target_row[None, :]
    placement = matches.astype(jnp.float32)
    outgoing = jnp.dot(placement, slot_rows, precision=lax.Precision.HIGHEST)
    labels = jnp.sum(jnp.where(matches, blocks[None, :] + 1, 0), axis=1) - 1
    received, got_labels = (
        lax.all_to_all(
            outgoing.reshape(peers, capacity, 3 * mark),
            ("gx", "gy"),
            split_axis=0,
            concat_axis=0,
            tiled=True,
        ),
        lax.all_to_all(
            labels.reshape(peers, capacity), ("gx", "gy"), split_axis=0, concat_axis=0, tiled=True
        ),
    )
    marker_force, back_rows = settle(
        received, got_labels, owned, train_of_block, marker_area, train_velocity, mark
    )
    returned = lax.all_to_all(
        back_rows.reshape(peers, capacity, 3 * mark),
        ("gx", "gy"),
        split_axis=0,
        concat_axis=0,
        tiled=True,
    )
    slot_force = jnp.dot(
        placement.T, returned.reshape(peers * capacity, 3 * mark), precision=lax.Precision.HIGHEST
    )
    slot_force = slot_force.reshape(slots, 3, mark).transpose(1, 0, 2)
    contrib = weights[None] * slot_force[:, :, None, :]
    cell_force = (
        jnp.zeros((3, cell_count), jnp.float32).at[:, cells.reshape(-1)].add(contrib.reshape(3, -1))
    )
    cell_force = cell_force.reshape(3, size_x, size_y, size_z)
    relaxed = collide(populations, cell_force, solid_cells)
    padded = with_halo(jnp.stack(relaxed), (("gx", 1), ("gy", 2), ("gz", 3)), 1)
    parts = []
    for direction in range(19):
        shift_x = 1 - int(velocity_table[direction][0])
        shift_y = 1 - int(velocity_table[direction][1])
        shift_z = 1 - int(velocity_table[direction][2])
        parts.append(
            padded[
                direction,
                shift_x : shift_x + size_x,
                shift_y : shift_y + size_y,
                shift_z : shift_z + size_z,
            ]
        )
    read = jnp.stack(parts)
    total_y = size_y * lax.axis_size("gy")
    total_z = size_z * lax.axis_size("gz")
    global_y = lax.axis_index("gy") * size_y + jnp.arange(size_y, dtype=jnp.int32)
    global_z = lax.axis_index("gz") * size_z + jnp.arange(size_z, dtype=jnp.int32)
    on_side = ((global_y == 0) | (global_y == total_y - 1))[:, None] | (
        (global_z == 0) | (global_z == total_z - 1)
    )[None, :]
    far_field = jnp.array(equilibrium(1.0, list(far_velocity)), dtype=jnp.float32)
    populations_next = jnp.where(on_side[None, None], far_field[:, None, None, None], read)
    return (populations_next, marker_force.reshape(1, 1, 1, owned, 3, mark))


def full(shape):
    return jax.ShapeDtypeStruct(shape, jnp.float32)


def kernel_params():
    return pltpu.CompilerParams(vmem_limit_bytes=vmem_bytes)


def low_half(shape):
    return lax.broadcasted_iota(jnp.int32, shape, 1) < shape[1] // 2


def fetch(pairs, sems):
    copies = [
        pltpu.make_async_copy(source, target, sems.at[i])
        for i, (source, target) in enumerate(pairs)
    ]
    for copy in copies:
        copy.start()
    return copies


def shard_rows(slots, owned):
    return 8 + owned + 3 * slots


def sample_kernel(
    place_ref, pop_any, cells_any, weights_any, areas_any, owner_any, block_any, trains_any,
    out_ref, pop_ref, cells_ref, weights_ref, areas_ref, owner_ref, block_ref, trains_ref,
    table, sems,
):
    rows, lanes = (pop_ref.shape[1], pop_ref.shape[2])
    mark = cells_ref.shape[1]
    owned = areas_ref.shape[0]
    slots = owner_ref.shape[1]
    kernel = cells_ref.shape[0] // slots
    copies = fetch(
        (
            (pop_any, pop_ref),
            (cells_any, cells_ref),
            (weights_any, weights_ref),
            (areas_any, areas_ref),
            (owner_any, owner_ref),
            (block_any, block_ref),
            (trains_any, trains_ref),
        ),
        sems,
    )

    copies[0].wait()
    density, momentum = moments([pop_ref[q] for q in range(19)])
    speed = [momentum[c] / density for c in range(3)]
    largest = jnp.maximum(jnp.maximum(jnp.abs(speed[0]), jnp.abs(speed[1])), jnp.abs(speed[2]))
    largest = jnp.max(largest, axis=(0, 1), keepdims=True) + 1e-20
    scale = largest * (1.0 / 32767.0)
    fixed = [(speed[c] * (1.0 / scale) + 32768.5).astype(jnp.int32) for c in range(3)]
    words = jnp.concatenate(
        [
            (fixed[0] << 16) | fixed[1],
            (fixed[2][: rows // 2] << 16) | fixed[2][rows // 2 :],
        ],
        axis=0,
    )
    for r in range(table.shape[0]):
        table[r] = jnp.broadcast_to(words[r : r + 1], (group, lanes))
    for copy in copies[1:]:
        copy.wait()
    out_ref[8 : 8 + owned, :] = areas_ref[...]
    out_ref[0:8, :] = jnp.zeros((8, mark), jnp.float32)
    ids = (owner_ref[...] * owned + block_ref[...]).astype(jnp.float32)
    out_ref[0:1, :] = jnp.concatenate([ids] * (mark // slots), axis=1)
    out_ref[1:2, 0:owned] = trains_ref[...].astype(jnp.float32)
    mine = lax.broadcasted_iota(jnp.int32, (1, mark), 1) % owned + place_ref[2] * owned
    out_ref[2:3, :] = mine.astype(jnp.float32)

    def body(step, carry):
        first = pl.multiple_of(step * group, group)
        total = [jnp.zeros((group, mark), jnp.float32) for c in range(3)]
        for k in range(kernel):
            at = pl.ds(first * kernel + k, group, stride=kernel)
            cells = cells_ref[at, :]
            lane = cells & (lanes - 1)
            row = cells >> (lanes.bit_length() - 1)
            bits = [(row >> bit) & 1 == 1 for bit in range(rows.bit_length() - 1)]

            def choose(low, level):
                if level < 0:
                    return jnp.take_along_axis(table[low], lane, axis=1, mode="promise_in_bounds")
                lower = choose(low, level - 1)
                return jnp.where(bits[level], choose(low + (1 << level), level - 1), lower)

            pair = choose(0, len(bits) - 1)
            third = choose(rows, len(bits) - 2)
            picked = [
                lax.shift_right_logical(pair, 16),
                pair & 65535,
                jnp.where(bits[-1], third & 65535, lax.shift_right_logical(third, 16)),
            ]
            weight = weights_ref[at, :]
            for c in range(3):
                total[c] = total[c] + weight * (picked[c].astype(jnp.float32) - 32768.0)
        for c in range(3):
            here = pl.ds(pl.multiple_of(8 + owned + c * slots + first, group), group)
            out_ref[here, :] = total[c] * scale
        return carry

    lax.fori_loop(0, slots // group, body, 0)


def sample(place, populations, cells, weights, areas, owner, block, trains):
    smem = pl.BlockSpec(memory_space=pltpu.SMEM)
    hbm = pl.BlockSpec(memory_space=pltpu.HBM)
    vmem = pl.BlockSpec(memory_space=pltpu.VMEM)
    kept = (populations, cells, weights)
    count = shard_rows(owner.shape[1], areas.shape[0])
    return pl.pallas_call(
        sample_kernel,
        out_shape=[full((count, cells.shape[1]))]
        + [jax.ShapeDtypeStruct(entries.shape, entries.dtype) for entries in kept],
        in_specs=[smem] + [hbm] * 7,
        out_specs=[vmem] * 4,
        scratch_shapes=[
            pltpu.VMEM(entries.shape, entries.dtype) for entries in (areas, owner, block, trains)
        ]
        + [
            pltpu.VMEM((populations.shape[1] * 3 // 2, group, populations.shape[2]), jnp.int32),
            pltpu.SemaphoreType.DMA((7,)),
        ],
        compiler_params=kernel_params(),
        name="sample",
    )(place, populations, cells, weights, areas, owner, block, trains)


def three_parts(values):
    parts = []
    for _ in range(3):
        parts.append(values.astype(jnp.bfloat16))
        values = values - parts[-1].astype(jnp.float32)
    return parts


def one_hot(mask):
    return jnp.where(mask, 1.0, 0.0).astype(jnp.bfloat16)


def wanted_labels(own_ref, slots, owned):
    mark = own_ref.shape[1]
    own = own_ref[0:8, :]
    ids, trains, mine = (jnp.broadcast_to(own[i : i + 1], (mark, mark)).T for i in range(3))
    return (ids[0:slots], mine[0:owned], trains[0:owned])


def add_shards(totals, shards, ids, mine):
    slots, owned = (ids.shape[0], mine.shape[0])
    wanted = jnp.concatenate([ids, mine], axis=0)
    for shard in shards:
        match = one_hot(wanted == shard[0:1, :])
        match = jnp.concatenate([match, match[:, 0:slots]], axis=1)
        starts = [8 + owned + c * slots for c in range(3)]
        values = jnp.concatenate([shard[at : at + slots, :] for at in starts], axis=1)
        sums = jnp.dot(
            match, jnp.concatenate(three_parts(values), axis=0), preferred_element_type=jnp.float32
        )
        held = ids == shard[2:3, :]
        parts = three_parts(shard[8 : 8 + owned, :])
        parts.append(jnp.zeros_like(parts[0]))
        area = jnp.dot(
            one_hot(held), jnp.concatenate(parts, axis=0), preferred_element_type=jnp.float32
        )
        got = (sums, area, jnp.where(held, shard[1:2, :], 0.0))
        totals = got if totals is None else [total + new for total, new in zip(totals, got)]
    return totals


def settle_kernel(slots, owned, speeds_ref, *refs):
    *shards, sums_ref, area_ref, trains_ref, rows_ref, labels_ref = refs
    mark = rows_ref.shape[1]
    for train in range(speeds_ref.shape[0]):
        for c in range(3):
            at = 3 * train + c
            rows_ref[at : at + 1, :] = jnp.full((1, mark), speeds_ref[train, c], jnp.float32)
    ids, mine, own_trains = wanted_labels(shards[0], slots, owned)
    labels_ref[...] = jnp.concatenate([ids, mine, own_trains], axis=0)
    sums_ref[...], area_ref[...], trains_ref[...] = add_shards(None, shards, ids, mine)


def settle_early(slots, owned, speeds, shards):
    mark = shards[0].shape[1]
    smem = pl.BlockSpec(memory_space=pltpu.SMEM)
    vmem = pl.BlockSpec(memory_space=pltpu.VMEM)
    return pl.pallas_call(
        functools.partial(settle_kernel, slots, owned),
        out_shape=(
            full((slots + owned, 3 * mark)),
            full((slots, mark)),
            full((slots, mark)),
            full((3 * speeds.shape[0], mark)),
            full((slots + 2 * owned, mark)),
        ),
        in_specs=[smem] + [vmem] * len(shards),
        compiler_params=kernel_params(),
        cost_estimate=pl.CostEstimate(
            flops=10**9, bytes_accessed=len(shards) * shards[0].size * 4, transcendentals=0
        ),
        name="settle",
    )(speeds, *shards)


def block_forces(rows_ref, totals, own_ref, own_trains):
    mark = own_ref.shape[1]
    sums, area, trains = totals
    slots, owned = (area.shape[0], own_trains.shape[0])
    trains = jnp.broadcast_to(jnp.sum(trains, axis=1, keepdims=True), area.shape)
    own_area = own_ref[8 : 8 + owned, :]
    forces, own_forces = ([], [])
    for c in range(3):
        target, own_target = (jnp.zeros_like(area), jnp.zeros_like(own_area))
        for train in range(rows_ref.shape[0] // 3):
            at = 3 * train + c
            speed = rows_ref[at : at + 1, :]
            target = jnp.where(trains == float(train), speed, target)
            own_target = jnp.where(own_trains == float(train), speed, own_target)
        got = sums[:, c * mark : (c + 1) * mark]
        forces.append(stiffness * area * (target - got[0:slots]))
        own_forces.append(stiffness * own_area * (own_target - got[slots:]))
    return (forces, own_forces)


def spread_kernel(
    slots, owned, place_ref, own_ref, last_ref, sums_ref, area_ref, trains_ref, speeds_ref,
    labels_ref,
    cells_ref, weights_ref, pop_ref, solid_ref,
    relaxed_ref, far_ref, near_ref, side_ref, marker_any, marker_ref, force_ref, lines_ref, acc,
    sem,
):
    rows, lanes = (pop_ref.shape[1], pop_ref.shape[2])
    size_y = 8
    mark = cells_ref.shape[1]
    kernel = cells_ref.shape[0] // slots
    bf = jnp.bfloat16
    ids = labels_ref[0:slots]
    mine, own_trains = (labels_ref[at : at + owned] for at in (slots, slots + owned))
    totals = add_shards((sums_ref[...], area_ref[...], trains_ref[...]), [last_ref], ids, mine)
    forces, own_forces = block_forces(speeds_ref, totals, own_ref, own_trains)
    largest = jnp.maximum(jnp.maximum(jnp.abs(forces[0]), jnp.abs(forces[1])), jnp.abs(forces[2]))
    largest = jnp.maximum(jnp.max(largest, axis=(0, 1), keepdims=True), 1e-20)
    scale = (224.0 * 16.0) / largest
    for c in range(3):
        force_ref[c] = forces[c] * scale
        marker_ref[c] = own_forces[c]
    marker_copy = pltpu.make_async_copy(marker_ref, marker_any, sem)
    marker_copy.start()

    acc[...] = jnp.zeros_like(acc)
    iota = lax.broadcasted_iota(jnp.int32, (16, mark), 0).astype(jnp.float32)
    steps = [(iota + 16.0 * j).astype(bf) for j in range(max(rows, lanes) // 16)]
    one, zero = (jnp.ones((16, mark), bf), jnp.zeros((16, mark), bf))

    def body(step, carry):
        first = pl.multiple_of(step * group, group)
        force = [force_ref[c, pl.ds(first, group), :] for c in range(3)]
        for k in range(kernel):
            at = pl.ds(first * kernel + k, group, stride=kernel)
            cells = cells_ref[at, :]
            weight = weights_ref[at, :]
            lane = (cells & (lanes - 1)).astype(jnp.float32)
            row = (cells >> (lanes.bit_length() - 1)).astype(jnp.float32)
            parts = []
            for c in range(3):
                value = weight * force[c]
                for _ in range(3):
                    parts.append(value.astype(fine).astype(jnp.float32))
                    value = (value - parts[-1]) * 16.0
            for which, entries in enumerate([lane, row] + parts):
                lines_ref[k, which] = entries

            def wide(which, i):
                entries = lines_ref[k, which, pl.ds(i, 8, stride=0), :]
                return jnp.concatenate([entries, entries], axis=0).astype(bf)

            left, right = ([], [])
            for i in range(group):
                lane_i, row_i = (wide(0, i), wide(1, i))
                match = [jnp.where(steps[j] == lane_i, one, zero) for j in range(lanes // 16)]
                right.append(jnp.concatenate(match, axis=0).astype(fine))
                masks = [steps[j] == row_i for j in range(rows // 16)]
                pieces = []
                for which in range(len(parts)):
                    part_i = wide(2 + which, i)
                    piece = [jnp.where(mask, part_i, zero) for mask in masks]
                    pieces.append(jnp.concatenate(piece, axis=0).astype(fine))
                left.append(jnp.concatenate(pieces, axis=0))
            acc[...] += lax.dot_general(
                jnp.concatenate(left, axis=1),
                jnp.concatenate(right, axis=1),
                (((1,), (1,)), ((), ())),
                preferred_element_type=jnp.float32,
            )
        return carry

    lax.fori_loop(0, slots // group, body, 0)
    cell_force = []
    for c in range(3):
        total = acc[3 * c * rows : (3 * c + 1) * rows, :]
        total = total + acc[(3 * c + 1) * rows : (3 * c + 2) * rows, :] * (1.0 / 16.0)
        total = total + acc[(3 * c + 2) * rows : (3 * c + 3) * rows, :] * (1.0 / 256.0)
        cell_force.append(total * (1.0 / scale))
    relaxed = collide([pop_ref[q] for q in range(19)], cell_force, solid_ref[...])
    for q in range(19):
        relaxed_ref[q] = relaxed[q]
    even = place_ref[3] == 0
    for i in range(5):
        ahead = relaxed[going(0, 1)[i]][rows - size_y :]
        behind = relaxed[going(0, -1)[i]][:size_y]
        far_ref[i] = jnp.where(even, behind, ahead)
        near_ref[i] = jnp.where(even, ahead, behind)
        for x in range(rows // size_y):
            up = relaxed[going(1, 1)[i]][size_y * x + size_y - 1 : size_y * x + size_y, :]
            down = relaxed[going(1, -1)[i]][size_y * x : size_y * x + 1, :]
            at = rows // size_y * i + x
            side_ref[at : at + 1, :] = jnp.where(place_ref[0] == 0, up, down)
    marker_copy.wait()


def spread(owned, place, own, last, early, cells, weights, populations, solid):
    mark = cells.shape[1]
    slots = early[1].shape[0]
    line_count, lanes = solid.shape
    smem = pl.BlockSpec(memory_space=pltpu.SMEM)
    vmem = pl.BlockSpec(memory_space=pltpu.VMEM)
    return pl.pallas_call(
        functools.partial(spread_kernel, slots, owned),
        out_shape=(
            full(populations.shape),
            full((5, 8, lanes)),
            full((5, 8, lanes)),
            full((24, lanes)),
            full((3, owned, mark)),
        ),
        in_specs=[smem] + [vmem] * 11,
        out_specs=[vmem] * 4 + [pl.BlockSpec(memory_space=pltpu.HBM)],
        scratch_shapes=[
            pltpu.VMEM((3, owned, mark), jnp.float32),
            pltpu.VMEM((3, slots, mark), jnp.float32),
            pltpu.VMEM((cells.shape[0] // slots, 11, group, mark), jnp.float32),
            pltpu.VMEM((9 * line_count, lanes), jnp.float32),
            pltpu.SemaphoreType.DMA,
        ],
        compiler_params=kernel_params(),
        name="spread",
    )(place, own, last, *early, cells, weights, populations, solid)


def downwind(place_ref, relaxed_ref, far_ref, near_ref):
    size_y = far_ref.shape[1]
    size_x = relaxed_ref.shape[1] // size_y
    even = place_ref[3] == 0

    def cells(q, x):
        step = int(velocity_table[q][0])
        source = x - step
        if 0 <= source < size_x:
            return relaxed_ref[q, source * size_y : (source + 1) * size_y, :]
        i = going(0, step).index(q)
        if step == 1:
            return jnp.where(even, far_ref[i], near_ref[i])
        return jnp.where(even, near_ref[i], far_ref[i])

    return cells


def sideways(cells, side_ref, edge):
    def result(q, x, y_at):
        step_x, step_y = (int(step) for step in velocity_table[q][:2])
        size_y = y_at.shape[0]
        size_x = side_ref.shape[0] // 6
        if step_y == 0:
            return cells(q, x)
        source = x - step_x
        at = size_x * going(1, step_y).index(q) + source
        halo = side_ref[at : at + 1, :] if 0 <= source < size_x else edge(q)
        turned = pltpu.roll(cells(q, x), step_y % size_y, 0)
        return jnp.where(y_at == (0 if step_y == 1 else size_y - 1), halo, turned)

    return result


def corner_index(q):
    step_y = int(velocity_table[q][1])
    return [p for p in going(1, step_y) if int(velocity_table[p][0]) != 0].index(q)


def pack_kernel(
    place_ref, relaxed_ref, far_ref, near_ref, side_ref, corner_ref, first_ref, second_ref
):
    size_y, lanes = far_ref.shape[1:]
    size_x = relaxed_ref.shape[1] // size_y
    cells = downwind(place_ref, relaxed_ref, far_ref, near_ref)
    corner_ref[...] = jnp.zeros(corner_ref.shape, jnp.float32)
    for ahead in going(1, 1):
        step_x = int(velocity_table[ahead][0])
        if step_x == 0:
            continue
        behind = opposite_table[ahead]
        up = cells(ahead, 0 if step_x == 1 else size_x - 1)[size_y - 1 : size_y, :]
        down = cells(behind, size_x - 1 if step_x == 1 else 0)[0:1, :]
        at = corner_index(ahead)
        from_behind = corner_index(behind)
        lower = place_ref[0] == 0

        @pl.when(lower)
        def _(at=at, up=up):
            corner_ref[at : at + 1, :] = up

        @pl.when(jnp.logical_not(lower))
        def _(at=from_behind, down=down):
            corner_ref[at : at + 1, :] = down

    y_at = lax.broadcasted_iota(jnp.int32, (size_y, lanes), 0)
    lane_at = lax.broadcasted_iota(jnp.int32, (size_y, lanes), 1)
    level = sideways(cells, side_ref, None)
    packs = []
    for step in (1, -1):
        packed = jnp.zeros((size_y, lanes), jnp.float32)
        for i, q in enumerate(going(2, step)):
            edge = lanes - 1 if step == 1 else 0
            for x in range(size_x):
                at = 8 * x + i
                moved = pltpu.roll(level(q, x, y_at), (at - edge) % lanes, 1)
                packed = jnp.where(lane_at == at, moved, packed)
        packs.append(packed)
    even = place_ref[1] % 2 == 0
    first_ref[...] = jnp.where(even, packs[0], packs[1])
    second_ref[...] = jnp.where(even, packs[1], packs[0])


def pack(place, relaxed, far, near, side):
    smem = pl.BlockSpec(memory_space=pltpu.SMEM)
    vmem = pl.BlockSpec(memory_space=pltpu.VMEM)
    edge = full(far.shape[1:])
    return pl.pallas_call(
        pack_kernel,
        out_shape=(edge, edge, edge),
        in_specs=[smem] + [vmem] * 4,
        compiler_params=kernel_params(),
        name="pack",
    )(place, relaxed, far, near, side)


def stream_kernel(
    count_z, place_ref, relaxed_ref, far_ref, near_ref, side_ref, second_ref, corner_ref,
    first_ref, out_any, out_ref, sems,
):
    size_x, size_y, lanes = out_ref.shape[1:]
    shape = (size_y, lanes)
    y_at = lax.broadcasted_iota(jnp.int32, shape, 0)
    z_at = lax.broadcasted_iota(jnp.int32, shape, 1)
    y_index, z_index = (place_ref[0], place_ref[1])
    streamed = sideways(
        downwind(place_ref, relaxed_ref, far_ref, near_ref),
        side_ref,
        lambda q: corner_ref[corner_index(q) : corner_index(q) + 1, :],
    )
    even = z_index % 2 == 0
    columns = {
        -1: jnp.where(even, first_ref[...], second_ref[...]),
        1: jnp.where(even, second_ref[...], first_ref[...]),
    }
    on_side = y_at == jnp.where(y_index == 0, 0, size_y - 1)
    on_side = on_side | ((z_at == 0) & (z_index == 0))
    on_side = on_side | ((z_at == lanes - 1) & (z_index == count_z - 1))
    copies = []
    for q in range(19):
        step_z = int(velocity_table[q][2])
        z_edge = 0 if step_z == 1 else lanes - 1
        for x in range(size_x):
            cells = streamed(q, x, y_at)
            if step_z != 0:
                at = 8 * x + going(2, step_z).index(q)
                cells = jnp.where(
                    z_at == z_edge,
                    pltpu.roll(columns[step_z], (z_edge - at) % lanes, 1),
                    pltpu.roll(cells, step_z % lanes, 1),
                )
            out_ref[q, x] = jnp.where(on_side, far_field[q], cells)
        copies.append(pltpu.make_async_copy(out_ref.at[q], out_any.at[q], sems.at[q]))
        copies[-1].start()
    for copy in copies:
        copy.wait()


def stream(count_z, place, relaxed, *halos):
    rows, lanes = relaxed.shape[1:]
    size_y = halos[0].shape[1]
    smem = pl.BlockSpec(memory_space=pltpu.SMEM)
    vmem = pl.BlockSpec(memory_space=pltpu.VMEM)
    shape = (19, rows // size_y, size_y, lanes)
    return pl.pallas_call(
        functools.partial(stream_kernel, count_z),
        out_shape=full(shape),
        in_specs=[smem] + [vmem] * (1 + len(halos)),
        out_specs=pl.BlockSpec(memory_space=pltpu.HBM),
        scratch_shapes=[pltpu.VMEM(shape, jnp.float32), pltpu.SemaphoreType.DMA((19,))],
        compiler_params=kernel_params(),
        name="stream",
    )(place, relaxed, *halos)


def per_device(
    populations,
    solid_cells,
    slot_cells,
    slot_weights,
    slot_owner,
    slot_block,
    train_of_block,
    marker_area,
    train_velocity,
):
    size_x, size_y, size_z = (populations.shape[1], populations.shape[2], populations.shape[3])
    lines = size_x * size_y
    slots, kernel, mark = (slot_cells.shape[3], slot_cells.shape[4], slot_cells.shape[5])
    owned = train_of_block.shape[3]
    count_x, count_y, count_z = (lax.axis_size(axis) for axis in ("gx", "gy", "gz"))
    x_index, y_index, z_index = (lax.axis_index(axis) for axis in ("gx", "gy", "gz"))
    place = jnp.stack([y_index, z_index, x_index * count_y + y_index, x_index % 2])
    place = place.astype(jnp.int32)
    inputs = [
        pltpu.with_memory_space_constraint(entries, pltpu.HBM)
        for entries in (
            populations.reshape(19, lines, size_z),
            slot_cells.reshape(slots * kernel, mark),
            slot_weights.reshape(slots * kernel, mark),
            marker_area.reshape(owned, mark),
            slot_owner.reshape(1, slots),
            slot_block.reshape(1, slots),
            train_of_block.reshape(1, owned),
        )
    ]
    own, pops, cells, weights = sample(place, *inputs)
    swap = [(0, 1), (1, 0)]

    def across_x(entries, distance):
        return lax.ppermute(entries, "gx", [(i, i ^ distance) for i in range(count_x)])

    def across_y(entries):
        return lax.ppermute(entries, "gy", swap)

    third, first = (across_x(own, distance) for distance in (3, 1))
    beside = across_y(own)
    third_beside = across_y(third)
    second = across_x(lax.optimization_barrier((third, beside))[0], 1)
    first_beside = across_y(first)
    last = across_x(third_beside, 1)
    whole = [own, first, third, second, beside, first_beside, third_beside]
    early = settle_early(slots, owned, train_velocity, whole)
    solid = solid_cells.reshape(lines, size_z)
    relaxed, far, near, side, marker_force = spread(
        owned, place, own, last, early, cells, weights, pops, solid
    )
    evens = range(0, count_x, 2)
    far = lax.ppermute(
        far,
        "gx",
        [(i, (i - 1) % count_x) for i in evens] + [((i - 1) % count_x, i) for i in evens],
    )
    near = lax.ppermute(near, "gx", [(i, i + 1) for i in evens] + [(i + 1, i) for i in evens])
    side = across_y(side)
    corner, up_first, down_first = pack(place, relaxed, far, near, side)
    inner = [(i, i + 1) for i in range(0, count_z - 1, 2)]
    outer = [(i, i + 1) for i in range(1, count_z - 1, 2)]
    down_first = lax.ppermute(down_first, "gz", outer + [(j, i) for i, j in outer])
    corner = across_y(corner)
    up_first = lax.ppermute(up_first, "gz", inner + [(j, i) for i, j in inner])
    populations_next = stream(
        count_z, place, relaxed, far, near, side, down_first, corner, up_first
    )
    marker_force = marker_force.transpose(1, 0, 2).reshape(1, 1, 1, owned, 3, mark)
    return (populations_next, marker_force)


def solution(mesh):
    placed = (
        P(None, "gx", "gy", "gz"),
        P("gx", "gy", "gz"),
        P("gx", "gy", "gz", None, None, None),
        P("gx", "gy", "gz", None, None, None),
        P("gx", "gy", "gz", None, None),
        P("gx", "gy", "gz", None),
        P("gx", "gy", "gz", None),
        P("gx", "gy", "gz", None, None),
        P(),
    )
    small = mesh.shape["gy"] == 2 and mesh.shape["gx"] == 4 and mesh.shape["gz"] % 2 == 0
    return jax.shard_map(
        per_device if small else per_device_general,
        mesh=mesh,
        in_specs=placed,
        out_specs=(P(None, "gx", "gy", "gz"), P("gx", "gy", "gz", None, None, None)),
        check_vma=False,
    )
```

```python
import functools
import jax
import jax.numpy as jnp
import numpy as np
from jax import lax
from jax.experimental import pallas as pl
from jax.experimental.pallas import tpu as pltpu
from jax.sharding import PartitionSpec as P

velocity_table = np.array(
    [
        [0, 0, 0],
        [1, 0, 0],
        [-1, 0, 0],
        [0, 1, 0],
        [0, -1, 0],
        [0, 0, 1],
        [0, 0, -1],
        [1, 1, 0],
        [-1, -1, 0],
        [1, -1, 0],
        [-1, 1, 0],
        [1, 0, 1],
        [-1, 0, -1],
        [1, 0, -1],
        [-1, 0, 1],
        [0, 1, 1],
        [0, -1, -1],
        [0, 1, -1],
        [0, -1, 1],
    ]
)
weight_table = [1.0 / 3.0] + [1.0 / 18.0] * 6 + [1.0 / 36.0] * 12
opposite_table = [0, 2, 1, 4, 3, 6, 5, 8, 7, 10, 9, 12, 11, 14, 13, 16, 15, 18, 17]
stress_pairs = [(0, 0), (1, 1), (2, 2), (0, 1), (0, 2), (1, 2)]
tau_base = 0.55
smag_term = 18.0 * 1.4142135623730951 * 0.17 * 0.17
regular_eps = 0.0001
stiffness = 2.0
far_velocity = (0.02, 0.06, 0.0)
vmem_bytes = 16 << 20
group = 8
fine = jnp.float8_e4m3fn


def going(axis, step):
    return [q for q in range(19) if int(velocity_table[q][axis]) == step]


def project(direction, vector):
    projection = 0.0 * vector[0]
    for component in range(3):
        lattice_step = int(velocity_table[direction][component])
        if lattice_step != 0:
            projection = projection + lattice_step * vector[component]
    return projection


def moments(populations):
    density = populations[0]
    momentum = [jnp.zeros_like(density) for component in range(3)]
    for direction in range(1, 19):
        density = density + populations[direction]
        for component in range(3):
            lattice_step = int(velocity_table[direction][component])
            if lattice_step == 1:
                momentum[component] = momentum[component] + populations[direction]
            elif lattice_step == -1:
                momentum[component] = momentum[component] - populations[direction]
    return (density, momentum)


def equilibrium(density, velocity):
    speed_sq = velocity[0] * velocity[0] + velocity[1] * velocity[1] + velocity[2] * velocity[2]
    result = []
    for direction in range(19):
        projected = project(direction, velocity)
        result.append(
            weight_table[direction]
            * density
            * (1.0 + 3.0 * projected + 4.5 * projected * projected - 1.5 * speed_sq)
        )
    return result


far_field = [float(np.float32(value)) for value in equilibrium(1.0, list(far_velocity))]


def collide(populations, cell_force, solid_cells):
    density, momentum = moments(populations)
    velocity = [
        (momentum[component] + 0.5 * cell_force[component]) / density for component in range(3)
    ]
    balance = equilibrium(density, velocity)
    stress = [jnp.zeros_like(density) for pair_pos in range(6)]
    for direction in range(19):
        non_eq = populations[direction] - balance[direction]
        for pair_pos in range(6):
            row_axis, col_axis = stress_pairs[pair_pos]
            factor = int(velocity_table[direction][row_axis] * velocity_table[direction][col_axis])
            if factor != 0:
                stress[pair_pos] = stress[pair_pos] + factor * non_eq
    shear_sq = stress[0] * stress[0] + stress[1] * stress[1] + stress[2] * stress[2]
    shear_sq = shear_sq + 2.0 * (
        stress[3] * stress[3] + stress[4] * stress[4] + stress[5] * stress[5]
    )
    magnitude = jnp.sqrt(shear_sq + regular_eps)
    relax_time = 0.5 * (tau_base + jnp.sqrt(tau_base * tau_base + smag_term * magnitude / density))
    relax_rate = 1.0 / relax_time
    guo_factor = 1.0 - 0.5 * relax_rate
    speed_force = (
        velocity[0] * cell_force[0] + velocity[1] * cell_force[1] + velocity[2] * cell_force[2]
    )
    result = []
    for direction in range(19):
        along_force = project(direction, cell_force)
        along_speed = project(direction, velocity)
        source = (
            guo_factor
            * weight_table[direction]
            * (3.0 * (along_force - speed_force) + 9.0 * along_speed * along_force)
        )
        relaxed = (
            populations[direction]
            - (populations[direction] - balance[direction]) * relax_rate
            + source
        )
        result.append(jnp.where(solid_cells == 1, populations[opposite_table[direction]], relaxed))
    return result


def with_halo(cells, sides, width):
    for axis, dim in sides:
        count = lax.axis_size(axis)
        head = lax.slice_in_dim(cells, 0, width, axis=dim)
        tail = lax.slice_in_dim(cells, cells.shape[dim] - width, cells.shape[dim], axis=dim)
        cells = jnp.concatenate(
            [
                lax.ppermute(tail, axis, [(i, (i + 1) % count) for i in range(count)]),
                cells,
                lax.ppermute(head, axis, [((i + 1) % count, i) for i in range(count)]),
            ],
            axis=dim,
        )
    return cells


def settle(received, labels, owned, train_of_block, marker_area, train_velocity, mark):
    rows_in = received.reshape(-1, 3 * mark)
    label_rows = labels.reshape(-1)
    owner_match = (label_rows[None, :] == jnp.arange(owned, dtype=jnp.int32)[:, None]).astype(
        jnp.float32
    )
    marker_velocity = jnp.dot(owner_match, rows_in, precision=lax.Precision.HIGHEST).reshape(
        owned, 3, mark
    )
    trains = train_velocity.shape[0]
    train_rows = train_of_block.reshape(owned)
    train_match = (train_rows[:, None] == jnp.arange(trains, dtype=jnp.int32)[None, :]).astype(
        jnp.float32
    )
    target = jnp.dot(train_match, train_velocity, precision=lax.Precision.HIGHEST)
    areas = marker_area.reshape(owned, mark)
    marker_force = stiffness * areas[:, None, :] * (target[:, :, None] - marker_velocity)
    back_rows = jnp.dot(
        owner_match.T, marker_force.reshape(owned, 3 * mark), precision=lax.Precision.HIGHEST
    )
    return (marker_force, back_rows)


def per_device_general(
    populations,
    solid_cells,
    slot_cells,
    slot_weights,
    slot_owner,
    slot_block,
    train_of_block,
    marker_area,
    train_velocity,
):
    size_x, size_y, size_z = (populations.shape[1], populations.shape[2], populations.shape[3])
    cell_count = size_x * size_y * size_z
    slots, kernel, mark = (slot_cells.shape[3], slot_cells.shape[4], slot_cells.shape[5])
    owned = train_of_block.shape[3]
    peers_x = lax.axis_size("gx")
    peers_y = lax.axis_size("gy")
    peers = peers_x * peers_y
    capacity = max(2, 2 * slots // peers)
    density, momentum = moments(populations)
    rest_velocity = jnp.stack([momentum[component] / density for component in range(3)]).reshape(
        3, cell_count
    )
    cells = slot_cells.reshape(slots, kernel, mark)
    weights = slot_weights.reshape(slots, kernel, mark)
    partial_value = jnp.sum(rest_velocity[:, cells] * weights[None], axis=2)
    slot_rows = partial_value.transpose(1, 0, 2).reshape(slots, 3 * mark)
    slot_dest = slot_owner.reshape(slots)
    blocks = slot_block.reshape(slots)
    order = jnp.arange(slots, dtype=jnp.int32)
    earlier = (slot_dest[None, :] == slot_dest[:, None]) & (order[None, :] < order[:, None])
    slot_rank = jnp.sum(earlier.astype(jnp.int32), axis=1)
    target_row = slot_dest * capacity + slot_rank
    buffer_rows = jnp.arange(peers * capacity, dtype=jnp.int32)
    matches = buffer_rows[:, None] == target_row[None, :]
    placement = matches.astype(jnp.float32)
    outgoing = jnp.dot(placement, slot_rows, precision=lax.Precision.HIGHEST)
    labels = jnp.sum(jnp.where(matches, blocks[None, :] + 1, 0), axis=1) - 1
    received, got_labels = (
        lax.all_to_all(
            outgoing.reshape(peers, capacity, 3 * mark),
            ("gx", "gy"),
            split_axis=0,
            concat_axis=0,
            tiled=True,
        ),
        lax.all_to_all(
            labels.reshape(peers, capacity), ("gx", "gy"), split_axis=0, concat_axis=0, tiled=True
        ),
    )
    marker_force, back_rows = settle(
        received, got_labels, owned, train_of_block, marker_area, train_velocity, mark
    )
    returned = lax.all_to_all(
        back_rows.reshape(peers, capacity, 3 * mark),
        ("gx", "gy"),
        split_axis=0,
        concat_axis=0,
        tiled=True,
    )
    slot_force = jnp.dot(
        placement.T, returned.reshape(peers * capacity, 3 * mark), precision=lax.Precision.HIGHEST
    )
    slot_force = slot_force.reshape(slots, 3, mark).transpose(1, 0, 2)
    contrib = weights[None] * slot_force[:, :, None, :]
    cell_force = (
        jnp.zeros((3, cell_count), jnp.float32).at[:, cells.reshape(-1)].add(contrib.reshape(3, -1))
    )
    cell_force = cell_force.reshape(3, size_x, size_y, size_z)
    relaxed = collide(populations, cell_force, solid_cells)
    padded = with_halo(jnp.stack(relaxed), (("gx", 1), ("gy", 2), ("gz", 3)), 1)
    parts = []
    for direction in range(19):
        shift_x = 1 - int(velocity_table[direction][0])
        shift_y = 1 - int(velocity_table[direction][1])
        shift_z = 1 - int(velocity_table[direction][2])
        parts.append(
            padded[
                direction,
                shift_x : shift_x + size_x,
                shift_y : shift_y + size_y,
                shift_z : shift_z + size_z,
            ]
        )
    read = jnp.stack(parts)
    total_y = size_y * lax.axis_size("gy")
    total_z = size_z * lax.axis_size("gz")
    global_y = lax.axis_index("gy") * size_y + jnp.arange(size_y, dtype=jnp.int32)
    global_z = lax.axis_index("gz") * size_z + jnp.arange(size_z, dtype=jnp.int32)
    on_side = ((global_y == 0) | (global_y == total_y - 1))[:, None] | (
        (global_z == 0) | (global_z == total_z - 1)
    )[None, :]
    far_field = jnp.array(equilibrium(1.0, list(far_velocity)), dtype=jnp.float32)
    populations_next = jnp.where(on_side[None, None], far_field[:, None, None, None], read)
    return (populations_next, marker_force.reshape(1, 1, 1, owned, 3, mark))


def full(shape):
    return jax.ShapeDtypeStruct(shape, jnp.float32)


def kernel_params():
    return pltpu.CompilerParams(vmem_limit_bytes=vmem_bytes)


def low_half(shape):
    return lax.broadcasted_iota(jnp.int32, shape, 1) < shape[1] // 2


def fetch(pairs, sems):
    copies = [
        pltpu.make_async_copy(source, target, sems.at[i])
        for i, (source, target) in enumerate(pairs)
    ]
    for copy in copies:
        copy.start()
    return copies


def shard_rows(slots, owned):
    return 8 + owned + 3 * slots


def sample_kernel(
    place_ref, pop_any, cells_any, weights_any, areas_any, owner_any, block_any, trains_any,
    out_ref, pop_ref, cells_ref, weights_ref, areas_ref, owner_ref, block_ref, trains_ref,
    table, sems,
):
    rows, lanes = (pop_ref.shape[1], pop_ref.shape[2])
    mark = cells_ref.shape[1]
    owned = areas_ref.shape[0]
    slots = owner_ref.shape[1]
    kernel = cells_ref.shape[0] // slots
    copies = fetch(
        (
            (pop_any, pop_ref),
            (cells_any, cells_ref),
            (weights_any, weights_ref),
            (areas_any, areas_ref),
            (owner_any, owner_ref),
            (block_any, block_ref),
            (trains_any, trains_ref),
        ),
        sems,
    )

    copies[0].wait()
    density, momentum = moments([pop_ref[q] for q in range(19)])
    speed = [momentum[c] / density for c in range(3)]
    largest = jnp.maximum(jnp.maximum(jnp.abs(speed[0]), jnp.abs(speed[1])), jnp.abs(speed[2]))
    largest = jnp.max(largest, axis=(0, 1), keepdims=True) + 1e-20
    scale = largest * (1.0 / 32767.0)
    fixed = [(speed[c] * (1.0 / scale) + 32768.5).astype(jnp.int32) for c in range(3)]
    words = jnp.concatenate(
        [
            (fixed[0] << 16) | fixed[1],
            (fixed[2][: rows // 2] << 16) | fixed[2][rows // 2 :],
        ],
        axis=0,
    )
    for r in range(table.shape[0]):
        table[r] = jnp.broadcast_to(words[r : r + 1], (group, lanes))
    for copy in copies[1:]:
        copy.wait()
    out_ref[8 : 8 + owned, :] = areas_ref[...]
    out_ref[0:8, :] = jnp.zeros((8, mark), jnp.float32)
    ids = (owner_ref[...] * owned + block_ref[...]).astype(jnp.float32)
    out_ref[0:1, :] = jnp.concatenate([ids] * (mark // slots), axis=1)
    out_ref[1:2, 0:owned] = trains_ref[...].astype(jnp.float32)
    mine = lax.broadcasted_iota(jnp.int32, (1, mark), 1) % owned + place_ref[2] * owned
    out_ref[2:3, :] = mine.astype(jnp.float32)

    def body(step, carry):
        first = pl.multiple_of(step * group, group)
        total = [jnp.zeros((group, mark), jnp.float32) for c in range(3)]
        for k in range(kernel):
            at = pl.ds(first * kernel + k, group, stride=kernel)
            cells = cells_ref[at, :]
            lane = cells & (lanes - 1)
            row = cells >> (lanes.bit_length() - 1)
            bits = [(row >> bit) & 1 == 1 for bit in range(rows.bit_length() - 1)]

            def choose(low, level):
                if level < 0:
                    return jnp.take_along_axis(table[low], lane, axis=1, mode="promise_in_bounds")
                lower = choose(low, level - 1)
                return jnp.where(bits[level], choose(low + (1 << level), level - 1), lower)

            pair = choose(0, len(bits) - 1)
            third = choose(rows, len(bits) - 2)
            picked = [
                lax.shift_right_logical(pair, 16),
                pair & 65535,
                jnp.where(bits[-1], third & 65535, lax.shift_right_logical(third, 16)),
            ]
            weight = weights_ref[at, :]
            for c in range(3):
                total[c] = total[c] + weight * (picked[c].astype(jnp.float32) - 32768.0)
        for c in range(3):
            here = pl.ds(pl.multiple_of(8 + owned + c * slots + first, group), group)
            out_ref[here, :] = total[c] * scale
        return carry

    lax.fori_loop(0, slots // group, body, 0)


def sample(place, populations, cells, weights, areas, owner, block, trains):
    smem = pl.BlockSpec(memory_space=pltpu.SMEM)
    hbm = pl.BlockSpec(memory_space=pltpu.HBM)
    vmem = pl.BlockSpec(memory_space=pltpu.VMEM)
    kept = (populations, cells, weights)
    count = shard_rows(owner.shape[1], areas.shape[0])
    return pl.pallas_call(
        sample_kernel,
        out_shape=[full((count, cells.shape[1]))]
        + [jax.ShapeDtypeStruct(entries.shape, entries.dtype) for entries in kept],
        in_specs=[smem] + [hbm] * 7,
        out_specs=[vmem] * 4,
        scratch_shapes=[
            pltpu.VMEM(entries.shape, entries.dtype) for entries in (areas, owner, block, trains)
        ]
        + [
            pltpu.VMEM((populations.shape[1] * 3 // 2, group, populations.shape[2]), jnp.int32),
            pltpu.SemaphoreType.DMA((7,)),
        ],
        compiler_params=kernel_params(),
        name="sample",
    )(place, populations, cells, weights, areas, owner, block, trains)


def three_parts(values):
    parts = []
    for _ in range(3):
        parts.append(values.astype(jnp.bfloat16))
        values = values - parts[-1].astype(jnp.float32)
    return parts


def one_hot(mask):
    return jnp.where(mask, 1.0, 0.0).astype(jnp.bfloat16)


def wanted_labels(own_ref, slots, owned):
    mark = own_ref.shape[1]
    own = own_ref[0:8, :]
    ids, trains, mine = (jnp.broadcast_to(own[i : i + 1], (mark, mark)).T for i in range(3))
    return (ids[0:slots], mine[0:owned], trains[0:owned])


def add_shards(totals, shards, ids, mine):
    slots, owned = (ids.shape[0], mine.shape[0])
    wanted = jnp.concatenate([ids, mine], axis=0)
    for shard in shards:
        match = one_hot(wanted == shard[0:1, :])
        match = jnp.concatenate([match, match[:, 0:slots]], axis=1)
        starts = [8 + owned + c * slots for c in range(3)]
        values = jnp.concatenate([shard[at : at + slots, :] for at in starts], axis=1)
        sums = jnp.dot(
            match, jnp.concatenate(three_parts(values), axis=0), preferred_element_type=jnp.float32
        )
        held = ids == shard[2:3, :]
        parts = three_parts(shard[8 : 8 + owned, :])
        parts.append(jnp.zeros_like(parts[0]))
        area = jnp.dot(
            one_hot(held), jnp.concatenate(parts, axis=0), preferred_element_type=jnp.float32
        )
        got = (sums, area, jnp.where(held, shard[1:2, :], 0.0))
        totals = got if totals is None else [total + new for total, new in zip(totals, got)]
    return totals


def settle_kernel(slots, owned, speeds_ref, *refs):
    *shards, sums_ref, area_ref, trains_ref, rows_ref, labels_ref = refs
    mark = rows_ref.shape[1]
    for train in range(speeds_ref.shape[0]):
        for c in range(3):
            at = 3 * train + c
            rows_ref[at : at + 1, :] = jnp.full((1, mark), speeds_ref[train, c], jnp.float32)
    ids, mine, own_trains = wanted_labels(shards[0], slots, owned)
    labels_ref[...] = jnp.concatenate([ids, mine, own_trains], axis=0)
    sums_ref[...], area_ref[...], trains_ref[...] = add_shards(None, shards, ids, mine)


def settle_early(slots, owned, speeds, shards):
    mark = shards[0].shape[1]
    smem = pl.BlockSpec(memory_space=pltpu.SMEM)
    vmem = pl.BlockSpec(memory_space=pltpu.VMEM)
    return pl.pallas_call(
        functools.partial(settle_kernel, slots, owned),
        out_shape=(
            full((slots + owned, 3 * mark)),
            full((slots, mark)),
            full((slots, mark)),
            full((3 * speeds.shape[0], mark)),
            full((slots + 2 * owned, mark)),
        ),
        in_specs=[smem] + [vmem] * len(shards),
        compiler_params=kernel_params(),
        cost_estimate=pl.CostEstimate(
            flops=10**9, bytes_accessed=len(shards) * shards[0].size * 4, transcendentals=0
        ),
        name="settle",
    )(speeds, *shards)


def block_forces(rows_ref, totals, own_ref, own_trains):
    mark = own_ref.shape[1]
    sums, area, trains = totals
    slots, owned = (area.shape[0], own_trains.shape[0])
    trains = jnp.broadcast_to(jnp.sum(trains, axis=1, keepdims=True), area.shape)
    own_area = own_ref[8 : 8 + owned, :]
    forces, own_forces = ([], [])
    for c in range(3):
        target, own_target = (jnp.zeros_like(area), jnp.zeros_like(own_area))
        for train in range(rows_ref.shape[0] // 3):
            at = 3 * train + c
            speed = rows_ref[at : at + 1, :]
            target = jnp.where(trains == float(train), speed, target)
            own_target = jnp.where(own_trains == float(train), speed, own_target)
        got = sums[:, c * mark : (c + 1) * mark]
        forces.append(stiffness * area * (target - got[0:slots]))
        own_forces.append(stiffness * own_area * (own_target - got[slots:]))
    return (forces, own_forces)


def spread_kernel(
    slots, owned, place_ref, own_ref, last_ref, sums_ref, area_ref, trains_ref, speeds_ref,
    labels_ref,
    cells_ref, weights_ref, pop_ref, solid_ref,
    relaxed_ref, far_ref, near_ref, side_ref, marker_any, marker_ref, force_ref, lines_ref, acc,
    sem,
):
    rows, lanes = (pop_ref.shape[1], pop_ref.shape[2])
    size_y = 8
    mark = cells_ref.shape[1]
    kernel = cells_ref.shape[0] // slots
    bf = jnp.bfloat16
    ids = labels_ref[0:slots]
    mine, own_trains = (labels_ref[at : at + owned] for at in (slots, slots + owned))
    totals = add_shards((sums_ref[...], area_ref[...], trains_ref[...]), [last_ref], ids, mine)
    forces, own_forces = block_forces(speeds_ref, totals, own_ref, own_trains)
    largest = jnp.maximum(jnp.maximum(jnp.abs(forces[0]), jnp.abs(forces[1])), jnp.abs(forces[2]))
    largest = jnp.maximum(jnp.max(largest, axis=(0, 1), keepdims=True), 1e-20)
    scale = (224.0 * 16.0) / largest
    for c in range(3):
        force_ref[c] = forces[c] * scale
        marker_ref[c] = own_forces[c]
    marker_copy = pltpu.make_async_copy(marker_ref, marker_any, sem)
    marker_copy.start()

    acc[...] = jnp.zeros_like(acc)
    iota = lax.broadcasted_iota(jnp.int32, (16, mark), 0).astype(jnp.float32)
    steps = [(iota + 16.0 * j).astype(bf) for j in range(max(rows, lanes) // 16)]
    one, zero = (jnp.ones((16, mark), bf), jnp.zeros((16, mark), bf))

    def body(step, carry):
        first = pl.multiple_of(step * group, group)
        force = [force_ref[c, pl.ds(first, group), :] for c in range(3)]
        for k in range(kernel):
            at = pl.ds(first * kernel + k, group, stride=kernel)
            cells = cells_ref[at, :]
            weight = weights_ref[at, :]
            lane = (cells & (lanes - 1)).astype(jnp.float32)
            row = (cells >> (lanes.bit_length() - 1)).astype(jnp.float32)
            parts = []
            for c in range(3):
                value = weight * force[c]
                for _ in range(3):
                    parts.append(value.astype(fine).astype(jnp.float32))
                    value = (value - parts[-1]) * 16.0
            for which, entries in enumerate([lane, row] + parts):
                lines_ref[k, which] = entries

            def wide(which, i):
                entries = lines_ref[k, which, pl.ds(i, 8, stride=0), :]
                return jnp.concatenate([entries, entries], axis=0).astype(bf)

            left, right = ([], [])
            for i in range(group):
                lane_i, row_i = (wide(0, i), wide(1, i))
                match = [jnp.where(steps[j] == lane_i, one, zero) for j in range(lanes // 16)]
                right.append(jnp.concatenate(match, axis=0).astype(fine))
                masks = [steps[j] == row_i for j in range(rows // 16)]
                pieces = []
                for which in range(len(parts)):
                    part_i = wide(2 + which, i)
                    piece = [jnp.where(mask, part_i, zero) for mask in masks]
                    pieces.append(jnp.concatenate(piece, axis=0).astype(fine))
                left.append(jnp.concatenate(pieces, axis=0))
            acc[...] += lax.dot_general(
                jnp.concatenate(left, axis=1),
                jnp.concatenate(right, axis=1),
                (((1,), (1,)), ((), ())),
                preferred_element_type=jnp.float32,
            )
        return carry

    lax.fori_loop(0, slots // group, body, 0)
    cell_force = []
    for c in range(3):
        total = acc[3 * c * rows : (3 * c + 1) * rows, :]
        total = total + acc[(3 * c + 1) * rows : (3 * c + 2) * rows, :] * (1.0 / 16.0)
        total = total + acc[(3 * c + 2) * rows : (3 * c + 3) * rows, :] * (1.0 / 256.0)
        cell_force.append(total * (1.0 / scale))
    relaxed = collide([pop_ref[q] for q in range(19)], cell_force, solid_ref[...])
    for q in range(19):
        relaxed_ref[q] = relaxed[q]
    even = place_ref[3] == 0
    for i in range(5):
        ahead = relaxed[going(0, 1)[i]][rows - size_y :]
        behind = relaxed[going(0, -1)[i]][:size_y]
        far_ref[i] = jnp.where(even, behind, ahead)
        near_ref[i] = jnp.where(even, ahead, behind)
        for x in range(rows // size_y):
            up = relaxed[going(1, 1)[i]][size_y * x + size_y - 1 : size_y * x + size_y, :]
            down = relaxed[going(1, -1)[i]][size_y * x : size_y * x + 1, :]
            at = rows // size_y * i + x
            side_ref[at : at + 1, :] = jnp.where(place_ref[0] == 0, up, down)
    marker_copy.wait()


def spread(owned, place, own, last, early, cells, weights, populations, solid):
    mark = cells.shape[1]
    slots = early[1].shape[0]
    line_count, lanes = solid.shape
    smem = pl.BlockSpec(memory_space=pltpu.SMEM)
    vmem = pl.BlockSpec(memory_space=pltpu.VMEM)
    return pl.pallas_call(
        functools.partial(spread_kernel, slots, owned),
        out_shape=(
            full(populations.shape),
            full((5, 8, lanes)),
            full((5, 8, lanes)),
            full((24, lanes)),
            full((3, owned, mark)),
        ),
        in_specs=[smem] + [vmem] * 11,
        out_specs=[vmem] * 4 + [pl.BlockSpec(memory_space=pltpu.HBM)],
        scratch_shapes=[
            pltpu.VMEM((3, owned, mark), jnp.float32),
            pltpu.VMEM((3, slots, mark), jnp.float32),
            pltpu.VMEM((cells.shape[0] // slots, 11, group, mark), jnp.float32),
            pltpu.VMEM((9 * line_count, lanes), jnp.float32),
            pltpu.SemaphoreType.DMA,
        ],
        compiler_params=kernel_params(),
        name="spread",
    )(place, own, last, *early, cells, weights, populations, solid)


def downwind(place_ref, relaxed_ref, far_ref, near_ref):
    size_y = far_ref.shape[1]
    size_x = relaxed_ref.shape[1] // size_y
    even = place_ref[3] == 0

    def cells(q, x):
        step = int(velocity_table[q][0])
        source = x - step
        if 0 <= source < size_x:
            return relaxed_ref[q, source * size_y : (source + 1) * size_y, :]
        i = going(0, step).index(q)
        if step == 1:
            return jnp.where(even, far_ref[i], near_ref[i])
        return jnp.where(even, near_ref[i], far_ref[i])

    return cells


def sideways(cells, side_ref, edge):
    def result(q, x, y_at):
        step_x, step_y = (int(step) for step in velocity_table[q][:2])
        size_y = y_at.shape[0]
        size_x = side_ref.shape[0] // 6
        if step_y == 0:
            return cells(q, x)
        source = x - step_x
        at = size_x * going(1, step_y).index(q) + source
        halo = side_ref[at : at + 1, :] if 0 <= source < size_x else edge(q)
        turned = pltpu.roll(cells(q, x), step_y % size_y, 0)
        return jnp.where(y_at == (0 if step_y == 1 else size_y - 1), halo, turned)

    return result


def corner_index(q):
    step_y = int(velocity_table[q][1])
    return [p for p in going(1, step_y) if int(velocity_table[p][0]) != 0].index(q)


def pack_kernel(
    place_ref, relaxed_ref, far_ref, near_ref, side_ref, corner_ref, first_ref, second_ref
):
    size_y, lanes = far_ref.shape[1:]
    size_x = relaxed_ref.shape[1] // size_y
    cells = downwind(place_ref, relaxed_ref, far_ref, near_ref)
    corner_ref[...] = jnp.zeros(corner_ref.shape, jnp.float32)
    for ahead in going(1, 1):
        step_x = int(velocity_table[ahead][0])
        if step_x == 0:
            continue
        behind = opposite_table[ahead]
        up = cells(ahead, 0 if step_x == 1 else size_x - 1)[size_y - 1 : size_y, :]
        down = cells(behind, size_x - 1 if step_x == 1 else 0)[0:1, :]
        at = corner_index(ahead)
        from_behind = corner_index(behind)
        lower = place_ref[0] == 0

        @pl.when(lower)
        def _(at=at, up=up):
            corner_ref[at : at + 1, :] = up

        @pl.when(jnp.logical_not(lower))
        def _(at=from_behind, down=down):
            corner_ref[at : at + 1, :] = down

    y_at = lax.broadcasted_iota(jnp.int32, (size_y, lanes), 0)
    lane_at = lax.broadcasted_iota(jnp.int32, (size_y, lanes), 1)
    level = sideways(cells, side_ref, None)
    packs = []
    for step in (1, -1):
        packed = jnp.zeros((size_y, lanes), jnp.float32)
        for i, q in enumerate(going(2, step)):
            edge = lanes - 1 if step == 1 else 0
            for x in range(size_x):
                at = 8 * x + i
                moved = pltpu.roll(level(q, x, y_at), (at - edge) % lanes, 1)
                packed = jnp.where(lane_at == at, moved, packed)
        packs.append(packed)
    even = place_ref[1] % 2 == 0
    first_ref[...] = jnp.where(even, packs[0], packs[1])
    second_ref[...] = jnp.where(even, packs[1], packs[0])


def pack(place, relaxed, far, near, side):
    smem = pl.BlockSpec(memory_space=pltpu.SMEM)
    vmem = pl.BlockSpec(memory_space=pltpu.VMEM)
    edge = full(far.shape[1:])
    return pl.pallas_call(
        pack_kernel,
        out_shape=(edge, edge, edge),
        in_specs=[smem] + [vmem] * 4,
        compiler_params=kernel_params(),
        name="pack",
    )(place, relaxed, far, near, side)


def stream_kernel(
    count_z, place_ref, relaxed_ref, far_ref, near_ref, side_ref, second_ref, corner_ref,
    first_ref, out_any, out_ref, sems,
):
    size_x, size_y, lanes = out_ref.shape[1:]
    shape = (size_y, lanes)
    y_at = lax.broadcasted_iota(jnp.int32, shape, 0)
    z_at = lax.broadcasted_iota(jnp.int32, shape, 1)
    y_index, z_index = (place_ref[0], place_ref[1])
    streamed = sideways(
        downwind(place_ref, relaxed_ref, far_ref, near_ref),
        side_ref,
        lambda q: corner_ref[corner_index(q) : corner_index(q) + 1, :],
    )
    even = z_index % 2 == 0
    columns = {
        -1: jnp.where(even, first_ref[...], second_ref[...]),
        1: jnp.where(even, second_ref[...], first_ref[...]),
    }
    on_side = y_at == jnp.where(y_index == 0, 0, size_y - 1)
    on_side = on_side | ((z_at == 0) & (z_index == 0))
    on_side = on_side | ((z_at == lanes - 1) & (z_index == count_z - 1))
    copies = []
    for q in range(19):
        step_z = int(velocity_table[q][2])
        z_edge = 0 if step_z == 1 else lanes - 1
        for x in range(size_x):
            cells = streamed(q, x, y_at)
            if step_z != 0:
                at = 8 * x + going(2, step_z).index(q)
                cells = jnp.where(
                    z_at == z_edge,
                    pltpu.roll(columns[step_z], (z_edge - at) % lanes, 1),
                    pltpu.roll(cells, step_z % lanes, 1),
                )
            out_ref[q, x] = jnp.where(on_side, far_field[q], cells)
        copies.append(pltpu.make_async_copy(out_ref.at[q], out_any.at[q], sems.at[q]))
        copies[-1].start()
    for copy in copies:
        copy.wait()


def stream(count_z, place, relaxed, *halos):
    rows, lanes = relaxed.shape[1:]
    size_y = halos[0].shape[1]
    smem = pl.BlockSpec(memory_space=pltpu.SMEM)
    vmem = pl.BlockSpec(memory_space=pltpu.VMEM)
    shape = (19, rows // size_y, size_y, lanes)
    return pl.pallas_call(
        functools.partial(stream_kernel, count_z),
        out_shape=full(shape),
        in_specs=[smem] + [vmem] * (1 + len(halos)),
        out_specs=pl.BlockSpec(memory_space=pltpu.HBM),
        scratch_shapes=[pltpu.VMEM(shape, jnp.float32), pltpu.SemaphoreType.DMA((19,))],
        compiler_params=kernel_params(),
        name="stream",
    )(place, relaxed, *halos)


def per_device(
    populations,
    solid_cells,
    slot_cells,
    slot_weights,
    slot_owner,
    slot_block,
    train_of_block,
    marker_area,
    train_velocity,
):
    size_x, size_y, size_z = (populations.shape[1], populations.shape[2], populations.shape[3])
    lines = size_x * size_y
    slots, kernel, mark = (slot_cells.shape[3], slot_cells.shape[4], slot_cells.shape[5])
    owned = train_of_block.shape[3]
    count_x, count_y, count_z = (lax.axis_size(axis) for axis in ("gx", "gy", "gz"))
    x_index, y_index, z_index = (lax.axis_index(axis) for axis in ("gx", "gy", "gz"))
    place = jnp.stack([y_index, z_index, x_index * count_y + y_index, x_index % 2])
    place = place.astype(jnp.int32)
    inputs = [
        pltpu.with_memory_space_constraint(entries, pltpu.HBM)
        for entries in (
            populations.reshape(19, lines, size_z),
            slot_cells.reshape(slots * kernel, mark),
            slot_weights.reshape(slots * kernel, mark),
            marker_area.reshape(owned, mark),
            slot_owner.reshape(1, slots),
            slot_block.reshape(1, slots),
            train_of_block.reshape(1, owned),
        )
    ]
    own, pops, cells, weights = sample(place, *inputs)
    swap = [(0, 1), (1, 0)]

    def across_x(entries, distance):
        return lax.ppermute(entries, "gx", [(i, i ^ distance) for i in range(count_x)])

    def across_y(entries):
        return lax.ppermute(entries, "gy", swap)

    second, first = (across_x(own, distance) for distance in (2, 1))
    beside = across_y(own)
    second_beside = across_y(second)
    third = across_x(lax.optimization_barrier((second, beside))[0], 1)
    first_beside = across_y(first)
    last = across_x(second_beside, 1)
    whole = [own, first, second, third, beside, first_beside, second_beside]
    early = settle_early(slots, owned, train_velocity, whole)
    solid = solid_cells.reshape(lines, size_z)
    relaxed, far, near, side, marker_force = spread(
        owned, place, own, last, early, cells, weights, pops, solid
    )
    evens = range(0, count_x, 2)
    far = lax.ppermute(
        far,
        "gx",
        [(i, (i - 1) % count_x) for i in evens] + [((i - 1) % count_x, i) for i in evens],
    )
    near = lax.ppermute(near, "gx", [(i, i + 1) for i in evens] + [(i + 1, i) for i in evens])
    side = across_y(side)
    corner, up_first, down_first = pack(place, relaxed, far, near, side)
    inner = [(i, i + 1) for i in range(0, count_z - 1, 2)]
    outer = [(i, i + 1) for i in range(1, count_z - 1, 2)]
    down_first = lax.ppermute(down_first, "gz", outer + [(j, i) for i, j in outer])
    corner = across_y(corner)
    up_first = lax.ppermute(up_first, "gz", inner + [(j, i) for i, j in inner])
    populations_next = stream(
        count_z, place, relaxed, far, near, side, down_first, corner, up_first
    )
    marker_force = marker_force.transpose(1, 0, 2).reshape(1, 1, 1, owned, 3, mark)
    return (populations_next, marker_force)


def solution(mesh):
    placed = (
        P(None, "gx", "gy", "gz"),
        P("gx", "gy", "gz"),
        P("gx", "gy", "gz", None, None, None),
        P("gx", "gy", "gz", None, None, None),
        P("gx", "gy", "gz", None, None),
        P("gx", "gy", "gz", None),
        P("gx", "gy", "gz", None),
        P("gx", "gy", "gz", None, None),
        P(),
    )
    small = mesh.shape["gy"] == 2 and mesh.shape["gx"] == 4 and mesh.shape["gz"] % 2 == 0
    return jax.shard_map(
        per_device if small else per_device_general,
        mesh=mesh,
        in_specs=placed,
        out_specs=(P(None, "gx", "gy", "gz"), P("gx", "gy", "gz", None, None, None)),
        check_vma=False,
    )
```

```python
import functools
import jax
import jax.numpy as jnp
import numpy as np
from jax import lax
from jax.experimental import pallas as pl
from jax.experimental.pallas import tpu as pltpu
from jax.sharding import PartitionSpec as P

velocity_table = np.array(
    [
        [0, 0, 0],
        [1, 0, 0],
        [-1, 0, 0],
        [0, 1, 0],
        [0, -1, 0],
        [0, 0, 1],
        [0, 0, -1],
        [1, 1, 0],
        [-1, -1, 0],
        [1, -1, 0],
        [-1, 1, 0],
        [1, 0, 1],
        [-1, 0, -1],
        [1, 0, -1],
        [-1, 0, 1],
        [0, 1, 1],
        [0, -1, -1],
        [0, 1, -1],
        [0, -1, 1],
    ]
)
weight_table = [1.0 / 3.0] + [1.0 / 18.0] * 6 + [1.0 / 36.0] * 12
opposite_table = [0, 2, 1, 4, 3, 6, 5, 8, 7, 10, 9, 12, 11, 14, 13, 16, 15, 18, 17]
stress_pairs = [(0, 0), (1, 1), (2, 2), (0, 1), (0, 2), (1, 2)]
tau_base = 0.55
smag_term = 18.0 * 1.4142135623730951 * 0.17 * 0.17
regular_eps = 0.0001
stiffness = 2.0
far_velocity = (0.02, 0.06, 0.0)
vmem_bytes = 16 << 20
group = 8
fine = jnp.float8_e4m3fn
matrix_points = 2


def going(axis, step):
    return [q for q in range(19) if int(velocity_table[q][axis]) == step]


def project(direction, vector):
    projection = 0.0 * vector[0]
    for component in range(3):
        lattice_step = int(velocity_table[direction][component])
        if lattice_step != 0:
            projection = projection + lattice_step * vector[component]
    return projection


def moments(populations):
    density = populations[0]
    momentum = [jnp.zeros_like(density) for component in range(3)]
    for direction in range(1, 19):
        density = density + populations[direction]
        for component in range(3):
            lattice_step = int(velocity_table[direction][component])
            if lattice_step == 1:
                momentum[component] = momentum[component] + populations[direction]
            elif lattice_step == -1:
                momentum[component] = momentum[component] - populations[direction]
    return (density, momentum)


def equilibrium(density, velocity):
    speed_sq = velocity[0] * velocity[0] + velocity[1] * velocity[1] + velocity[2] * velocity[2]
    result = []
    for direction in range(19):
        projected = project(direction, velocity)
        result.append(
            weight_table[direction]
            * density
            * (1.0 + 3.0 * projected + 4.5 * projected * projected - 1.5 * speed_sq)
        )
    return result


far_field = [float(np.float32(value)) for value in equilibrium(1.0, list(far_velocity))]


def collide(populations, cell_force, solid_cells):
    density, momentum = moments(populations)
    velocity = [
        (momentum[component] + 0.5 * cell_force[component]) / density for component in range(3)
    ]
    balance = equilibrium(density, velocity)
    stress = [jnp.zeros_like(density) for pair_pos in range(6)]
    for direction in range(19):
        non_eq = populations[direction] - balance[direction]
        for pair_pos in range(6):
            row_axis, col_axis = stress_pairs[pair_pos]
            factor = int(velocity_table[direction][row_axis] * velocity_table[direction][col_axis])
            if factor != 0:
                stress[pair_pos] = stress[pair_pos] + factor * non_eq
    shear_sq = stress[0] * stress[0] + stress[1] * stress[1] + stress[2] * stress[2]
    shear_sq = shear_sq + 2.0 * (
        stress[3] * stress[3] + stress[4] * stress[4] + stress[5] * stress[5]
    )
    magnitude = jnp.sqrt(shear_sq + regular_eps)
    relax_time = 0.5 * (tau_base + jnp.sqrt(tau_base * tau_base + smag_term * magnitude / density))
    relax_rate = 1.0 / relax_time
    guo_factor = 1.0 - 0.5 * relax_rate
    speed_force = (
        velocity[0] * cell_force[0] + velocity[1] * cell_force[1] + velocity[2] * cell_force[2]
    )
    result = []
    for direction in range(19):
        along_force = project(direction, cell_force)
        along_speed = project(direction, velocity)
        source = (
            guo_factor
            * weight_table[direction]
            * (3.0 * (along_force - speed_force) + 9.0 * along_speed * along_force)
        )
        relaxed = (
            populations[direction]
            - (populations[direction] - balance[direction]) * relax_rate
            + source
        )
        result.append(jnp.where(solid_cells == 1, populations[opposite_table[direction]], relaxed))
    return result


def with_halo(cells, sides, width):
    for axis, dim in sides:
        count = lax.axis_size(axis)
        head = lax.slice_in_dim(cells, 0, width, axis=dim)
        tail = lax.slice_in_dim(cells, cells.shape[dim] - width, cells.shape[dim], axis=dim)
        cells = jnp.concatenate(
            [
                lax.ppermute(tail, axis, [(i, (i + 1) % count) for i in range(count)]),
                cells,
                lax.ppermute(head, axis, [((i + 1) % count, i) for i in range(count)]),
            ],
            axis=dim,
        )
    return cells


def settle(received, labels, owned, train_of_block, marker_area, train_velocity, mark):
    rows_in = received.reshape(-1, 3 * mark)
    label_rows = labels.reshape(-1)
    owner_match = (label_rows[None, :] == jnp.arange(owned, dtype=jnp.int32)[:, None]).astype(
        jnp.float32
    )
    marker_velocity = jnp.dot(owner_match, rows_in, precision=lax.Precision.HIGHEST).reshape(
        owned, 3, mark
    )
    trains = train_velocity.shape[0]
    train_rows = train_of_block.reshape(owned)
    train_match = (train_rows[:, None] == jnp.arange(trains, dtype=jnp.int32)[None, :]).astype(
        jnp.float32
    )
    target = jnp.dot(train_match, train_velocity, precision=lax.Precision.HIGHEST)
    areas = marker_area.reshape(owned, mark)
    marker_force = stiffness * areas[:, None, :] * (target[:, :, None] - marker_velocity)
    back_rows = jnp.dot(
        owner_match.T, marker_force.reshape(owned, 3 * mark), precision=lax.Precision.HIGHEST
    )
    return (marker_force, back_rows)


def per_device_general(
    populations,
    solid_cells,
    slot_cells,
    slot_weights,
    slot_owner,
    slot_block,
    train_of_block,
    marker_area,
    train_velocity,
):
    size_x, size_y, size_z = (populations.shape[1], populations.shape[2], populations.shape[3])
    cell_count = size_x * size_y * size_z
    slots, kernel, mark = (slot_cells.shape[3], slot_cells.shape[4], slot_cells.shape[5])
    owned = train_of_block.shape[3]
    peers_x = lax.axis_size("gx")
    peers_y = lax.axis_size("gy")
    peers = peers_x * peers_y
    capacity = max(2, 2 * slots // peers)
    density, momentum = moments(populations)
    rest_velocity = jnp.stack([momentum[component] / density for component in range(3)]).reshape(
        3, cell_count
    )
    cells = slot_cells.reshape(slots, kernel, mark)
    weights = slot_weights.reshape(slots, kernel, mark)
    partial_value = jnp.sum(rest_velocity[:, cells] * weights[None], axis=2)
    slot_rows = partial_value.transpose(1, 0, 2).reshape(slots, 3 * mark)
    slot_dest = slot_owner.reshape(slots)
    blocks = slot_block.reshape(slots)
    order = jnp.arange(slots, dtype=jnp.int32)
    earlier = (slot_dest[None, :] == slot_dest[:, None]) & (order[None, :] < order[:, None])
    slot_rank = jnp.sum(earlier.astype(jnp.int32), axis=1)
    target_row = slot_dest * capacity + slot_rank
    buffer_rows = jnp.arange(peers * capacity, dtype=jnp.int32)
    matches = buffer_rows[:, None] == target_row[None, :]
    placement = matches.astype(jnp.float32)
    outgoing = jnp.dot(placement, slot_rows, precision=lax.Precision.HIGHEST)
    labels = jnp.sum(jnp.where(matches, blocks[None, :] + 1, 0), axis=1) - 1
    received, got_labels = (
        lax.all_to_all(
            outgoing.reshape(peers, capacity, 3 * mark),
            ("gx", "gy"),
            split_axis=0,
            concat_axis=0,
            tiled=True,
        ),
        lax.all_to_all(
            labels.reshape(peers, capacity), ("gx", "gy"), split_axis=0, concat_axis=0, tiled=True
        ),
    )
    marker_force, back_rows = settle(
        received, got_labels, owned, train_of_block, marker_area, train_velocity, mark
    )
    returned = lax.all_to_all(
        back_rows.reshape(peers, capacity, 3 * mark),
        ("gx", "gy"),
        split_axis=0,
        concat_axis=0,
        tiled=True,
    )
    slot_force = jnp.dot(
        placement.T, returned.reshape(peers * capacity, 3 * mark), precision=lax.Precision.HIGHEST
    )
    slot_force = slot_force.reshape(slots, 3, mark).transpose(1, 0, 2)
    contrib = weights[None] * slot_force[:, :, None, :]
    cell_force = (
        jnp.zeros((3, cell_count), jnp.float32).at[:, cells.reshape(-1)].add(contrib.reshape(3, -1))
    )
    cell_force = cell_force.reshape(3, size_x, size_y, size_z)
    relaxed = collide(populations, cell_force, solid_cells)
    padded = with_halo(jnp.stack(relaxed), (("gx", 1), ("gy", 2), ("gz", 3)), 1)
    parts = []
    for direction in range(19):
        shift_x = 1 - int(velocity_table[direction][0])
        shift_y = 1 - int(velocity_table[direction][1])
        shift_z = 1 - int(velocity_table[direction][2])
        parts.append(
            padded[
                direction,
                shift_x : shift_x + size_x,
                shift_y : shift_y + size_y,
                shift_z : shift_z + size_z,
            ]
        )
    read = jnp.stack(parts)
    total_y = size_y * lax.axis_size("gy")
    total_z = size_z * lax.axis_size("gz")
    global_y = lax.axis_index("gy") * size_y + jnp.arange(size_y, dtype=jnp.int32)
    global_z = lax.axis_index("gz") * size_z + jnp.arange(size_z, dtype=jnp.int32)
    on_side = ((global_y == 0) | (global_y == total_y - 1))[:, None] | (
        (global_z == 0) | (global_z == total_z - 1)
    )[None, :]
    far_field = jnp.array(equilibrium(1.0, list(far_velocity)), dtype=jnp.float32)
    populations_next = jnp.where(on_side[None, None], far_field[:, None, None, None], read)
    return (populations_next, marker_force.reshape(1, 1, 1, owned, 3, mark))


def full(shape):
    return jax.ShapeDtypeStruct(shape, jnp.float32)


def kernel_params():
    return pltpu.CompilerParams(vmem_limit_bytes=vmem_bytes)


def low_half(shape):
    return lax.broadcasted_iota(jnp.int32, shape, 1) < shape[1] // 2


def fetch(pairs, sems):
    copies = [
        pltpu.make_async_copy(source, target, sems.at[i])
        for i, (source, target) in enumerate(pairs)
    ]
    for copy in copies:
        copy.start()
    return copies


def shard_rows(slots, owned):
    return 8 + owned + 3 * slots


def sample_kernel(
    place_ref, pop_any, cells_any, weights_any, areas_any, owner_any, block_any, trains_any,
    out_ref, pop_ref, cells_ref, weights_ref, areas_ref, owner_ref, block_ref, trains_ref,
    table, parts_ref, lines_ref, spread_ref, sems,
):
    rows, lanes = (pop_ref.shape[1], pop_ref.shape[2])
    mark = cells_ref.shape[1]
    owned = areas_ref.shape[0]
    slots = owner_ref.shape[1]
    kernel = cells_ref.shape[0] // slots
    copies = fetch(
        (
            (pop_any, pop_ref),
            (cells_any, cells_ref),
            (weights_any, weights_ref),
            (areas_any, areas_ref),
            (owner_any, owner_ref),
            (block_any, block_ref),
            (trains_any, trains_ref),
        ),
        sems,
    )

    copies[0].wait()
    density, momentum = moments([pop_ref[q] for q in range(19)])
    speed = [momentum[c] / density for c in range(3)]
    largest = jnp.maximum(jnp.maximum(jnp.abs(speed[0]), jnp.abs(speed[1])), jnp.abs(speed[2]))
    largest = jnp.max(largest, axis=(0, 1), keepdims=True) + 1e-20
    scale = largest * (1.0 / 32767.0)
    fixed = [(speed[c] * (1.0 / scale) + 32768.5).astype(jnp.int32) for c in range(3)]
    words = jnp.concatenate(
        [
            (fixed[0] << 16) | fixed[1],
            (fixed[2][: rows // 2] << 16) | fixed[2][rows // 2 :],
        ],
        axis=0,
    )
    for r in range(table.shape[0]):
        table[r] = jnp.broadcast_to(words[r : r + 1], (group, lanes))
    for c in range(3):
        value = speed[c] * (224.0 / largest)
        for part in range(4):
            piece = value.astype(fine)
            parts_ref[c * rows : (c + 1) * rows, part * lanes : (part + 1) * lanes] = piece
            value = value - piece.astype(jnp.float32)
    for copy in copies[1:]:
        copy.wait()
    out_ref[8 : 8 + owned, :] = areas_ref[...]
    out_ref[0:8, :] = jnp.zeros((8, mark), jnp.float32)
    ids = (owner_ref[...] * owned + block_ref[...]).astype(jnp.float32)
    out_ref[0:1, :] = jnp.concatenate([ids] * (mark // slots), axis=1)
    out_ref[1:2, 0:owned] = trains_ref[...].astype(jnp.float32)
    mine = lax.broadcasted_iota(jnp.int32, (1, mark), 1) % owned + place_ref[2] * owned
    out_ref[2:3, :] = mine.astype(jnp.float32)

    bf = jnp.bfloat16
    iota = lax.broadcasted_iota(jnp.int32, (16, mark), 0).astype(jnp.float32)
    steps = [(iota + 16.0 * j).astype(bf) for j in range(lanes // 16)]
    line_at = [iota[0:8] + 8.0 * j for j in range(rows // 8)]
    one, zero = (jnp.ones((16, mark), bf), jnp.zeros((16, mark), bf))

    def by_matrix(first):
        for which, k in enumerate(range(kernel - matrix_points, kernel)):
            at = pl.ds(first * kernel + k, group, stride=kernel)
            cells = cells_ref[at, :]
            lines_ref[which, 0] = (cells & (lanes - 1)).astype(jnp.float32)
            lines_ref[which, 1] = (cells >> (lanes.bit_length() - 1)).astype(jnp.float32)
            lines_ref[which, 2] = weights_ref[at, :]
        for i in range(group):
            sums = [jnp.zeros((8, mark), jnp.float32) for c in range(3)]
            for which in range(matrix_points):
                lane, row, weight = (
                    lines_ref[which, entry, pl.ds(i, 8, stride=0), :] for entry in range(3)
                )
                lane = jnp.concatenate([lane, lane], axis=0).astype(bf)
                match = [jnp.where(step == lane, one, zero) for step in steps]
                match = jnp.concatenate(match, axis=0).astype(fine)
                got = jnp.dot(
                    parts_ref[...],
                    jnp.concatenate([match] * 4, axis=0),
                    preferred_element_type=jnp.float32,
                )
                for j in range(rows // 8):
                    share = jnp.where(line_at[j] == row, weight, 0.0)
                    for c in range(3):
                        here = c * rows + 8 * j
                        sums[c] = sums[c] + share * got[here : here + 8]
            for c in range(3):
                spread_ref[c, 8 * i : 8 * i + 8, :] = sums[c]
        result = []
        for c in range(3):
            total = spread_ref[c, pl.ds(0, group, stride=8), :]
            for j in range(1, 8):
                total = total + spread_ref[c, pl.ds(j, group, stride=8), :]
            result.append(total)
        return result

    def body(step, carry):
        first = pl.multiple_of(step * group, group)
        total = [jnp.zeros((group, mark), jnp.float32) for c in range(3)]
        other = by_matrix(first)
        for k in range(kernel - matrix_points):
            at = pl.ds(first * kernel + k, group, stride=kernel)
            cells = cells_ref[at, :]
            lane = cells & (lanes - 1)
            row = cells >> (lanes.bit_length() - 1)
            bits = [(row >> bit) & 1 == 1 for bit in range(rows.bit_length() - 1)]

            def choose(low, level):
                if level < 0:
                    return jnp.take_along_axis(table[low], lane, axis=1, mode="promise_in_bounds")
                lower = choose(low, level - 1)
                return jnp.where(bits[level], choose(low + (1 << level), level - 1), lower)

            pair = choose(0, len(bits) - 1)
            third = choose(rows, len(bits) - 2)
            picked = [
                lax.shift_right_logical(pair, 16),
                pair & 65535,
                jnp.where(bits[-1], third & 65535, lax.shift_right_logical(third, 16)),
            ]
            weight = weights_ref[at, :]
            for c in range(3):
                total[c] = total[c] + weight * (picked[c].astype(jnp.float32) - 32768.0)
        for c in range(3):
            here = pl.ds(pl.multiple_of(8 + owned + c * slots + first, group), group)
            out_ref[here, :] = total[c] * scale + other[c] * (largest * (1.0 / 224.0))
        return carry

    lax.fori_loop(0, slots // group, body, 0)


def sample(place, populations, cells, weights, areas, owner, block, trains):
    smem = pl.BlockSpec(memory_space=pltpu.SMEM)
    hbm = pl.BlockSpec(memory_space=pltpu.HBM)
    vmem = pl.BlockSpec(memory_space=pltpu.VMEM)
    kept = (populations, cells, weights)
    count = shard_rows(owner.shape[1], areas.shape[0])
    return pl.pallas_call(
        sample_kernel,
        out_shape=[full((count, cells.shape[1]))]
        + [jax.ShapeDtypeStruct(entries.shape, entries.dtype) for entries in kept],
        in_specs=[smem] + [hbm] * 7,
        out_specs=[vmem] * 4,
        scratch_shapes=[
            pltpu.VMEM(entries.shape, entries.dtype) for entries in (areas, owner, block, trains)
        ]
        + [
            pltpu.VMEM((populations.shape[1] * 3 // 2, group, populations.shape[2]), jnp.int32),
            pltpu.VMEM((3 * populations.shape[1], 4 * populations.shape[2]), fine),
            pltpu.VMEM((matrix_points, 3, group, cells.shape[1]), jnp.float32),
            pltpu.VMEM((3, 8 * group, cells.shape[1]), jnp.float32),
            pltpu.SemaphoreType.DMA((7,)),
        ],
        compiler_params=kernel_params(),
        name="sample",
    )(place, populations, cells, weights, areas, owner, block, trains)


def three_parts(values):
    parts = []
    for _ in range(3):
        parts.append(values.astype(jnp.bfloat16))
        values = values - parts[-1].astype(jnp.float32)
    return parts


def one_hot(mask):
    return jnp.where(mask, 1.0, 0.0).astype(jnp.bfloat16)


def wanted_labels(own_ref, slots, owned):
    mark = own_ref.shape[1]
    own = own_ref[0:8, :]
    ids, trains, mine = (jnp.broadcast_to(own[i : i + 1], (mark, mark)).T for i in range(3))
    return (ids[0:slots], mine[0:owned], trains[0:owned])


def add_shards(totals, shards, ids, mine):
    slots, owned = (ids.shape[0], mine.shape[0])
    wanted = jnp.concatenate([ids, mine], axis=0)
    for shard in shards:
        match = one_hot(wanted == shard[0:1, :])
        match = jnp.concatenate([match, match[:, 0:slots]], axis=1)
        starts = [8 + owned + c * slots for c in range(3)]
        values = jnp.concatenate([shard[at : at + slots, :] for at in starts], axis=1)
        sums = jnp.dot(
            match, jnp.concatenate(three_parts(values), axis=0), preferred_element_type=jnp.float32
        )
        held = ids == shard[2:3, :]
        parts = three_parts(shard[8 : 8 + owned, :])
        parts.append(jnp.zeros_like(parts[0]))
        area = jnp.dot(
            one_hot(held), jnp.concatenate(parts, axis=0), preferred_element_type=jnp.float32
        )
        got = (sums, area, jnp.where(held, shard[1:2, :], 0.0))
        totals = got if totals is None else [total + new for total, new in zip(totals, got)]
    return totals


def settle_kernel(slots, owned, speeds_ref, *refs):
    *shards, sums_ref, area_ref, trains_ref, rows_ref, labels_ref = refs
    mark = rows_ref.shape[1]
    for train in range(speeds_ref.shape[0]):
        for c in range(3):
            at = 3 * train + c
            rows_ref[at : at + 1, :] = jnp.full((1, mark), speeds_ref[train, c], jnp.float32)
    ids, mine, own_trains = wanted_labels(shards[0], slots, owned)
    labels_ref[...] = jnp.concatenate([ids, mine, own_trains], axis=0)
    sums_ref[...], area_ref[...], trains_ref[...] = add_shards(None, shards, ids, mine)


def settle_early(slots, owned, speeds, shards):
    mark = shards[0].shape[1]
    smem = pl.BlockSpec(memory_space=pltpu.SMEM)
    vmem = pl.BlockSpec(memory_space=pltpu.VMEM)
    return pl.pallas_call(
        functools.partial(settle_kernel, slots, owned),
        out_shape=(
            full((slots + owned, 3 * mark)),
            full((slots, mark)),
            full((slots, mark)),
            full((3 * speeds.shape[0], mark)),
            full((slots + 2 * owned, mark)),
        ),
        in_specs=[smem] + [vmem] * len(shards),
        compiler_params=kernel_params(),
        cost_estimate=pl.CostEstimate(
            flops=10**9, bytes_accessed=len(shards) * shards[0].size * 4, transcendentals=0
        ),
        name="settle",
    )(speeds, *shards)


def block_forces(rows_ref, totals, own_ref, own_trains):
    mark = own_ref.shape[1]
    sums, area, trains = totals
    slots, owned = (area.shape[0], own_trains.shape[0])
    trains = jnp.broadcast_to(jnp.sum(trains, axis=1, keepdims=True), area.shape)
    own_area = own_ref[8 : 8 + owned, :]
    forces, own_forces = ([], [])
    for c in range(3):
        target, own_target = (jnp.zeros_like(area), jnp.zeros_like(own_area))
        for train in range(rows_ref.shape[0] // 3):
            at = 3 * train + c
            speed = rows_ref[at : at + 1, :]
            target = jnp.where(trains == float(train), speed, target)
            own_target = jnp.where(own_trains == float(train), speed, own_target)
        got = sums[:, c * mark : (c + 1) * mark]
        forces.append(stiffness * area * (target - got[0:slots]))
        own_forces.append(stiffness * own_area * (own_target - got[slots:]))
    return (forces, own_forces)


def spread_kernel(
    slots, owned, place_ref, own_ref, last_ref, sums_ref, area_ref, trains_ref, speeds_ref,
    labels_ref,
    cells_ref, weights_ref, pop_ref, solid_ref,
    relaxed_ref, far_ref, near_ref, side_ref, marker_any, marker_ref, force_ref, lines_ref, acc,
    sem,
):
    rows, lanes = (pop_ref.shape[1], pop_ref.shape[2])
    size_y = 8
    mark = cells_ref.shape[1]
    kernel = cells_ref.shape[0] // slots
    bf = jnp.bfloat16
    ids = labels_ref[0:slots]
    mine, own_trains = (labels_ref[at : at + owned] for at in (slots, slots + owned))
    totals = add_shards((sums_ref[...], area_ref[...], trains_ref[...]), [last_ref], ids, mine)
    forces, own_forces = block_forces(speeds_ref, totals, own_ref, own_trains)
    largest = jnp.maximum(jnp.maximum(jnp.abs(forces[0]), jnp.abs(forces[1])), jnp.abs(forces[2]))
    largest = jnp.maximum(jnp.max(largest, axis=(0, 1), keepdims=True), 1e-20)
    scale = (224.0 * 16.0) / largest
    for c in range(3):
        force_ref[c] = forces[c] * scale
        marker_ref[c] = own_forces[c]
    marker_copy = pltpu.make_async_copy(marker_ref, marker_any, sem)
    marker_copy.start()

    acc[...] = jnp.zeros_like(acc)
    iota = lax.broadcasted_iota(jnp.int32, (16, mark), 0).astype(jnp.float32)
    steps = [(iota + 16.0 * j).astype(bf) for j in range(max(rows, lanes) // 16)]
    one, zero = (jnp.ones((16, mark), bf), jnp.zeros((16, mark), bf))

    def body(step, carry):
        first = pl.multiple_of(step * group, group)
        force = [force_ref[c, pl.ds(first, group), :] for c in range(3)]
        for k in range(kernel):
            at = pl.ds(first * kernel + k, group, stride=kernel)
            cells = cells_ref[at, :]
            weight = weights_ref[at, :]
            lane = (cells & (lanes - 1)).astype(jnp.float32)
            row = (cells >> (lanes.bit_length() - 1)).astype(jnp.float32)
            parts = []
            for c in range(3):
                value = weight * force[c]
                for _ in range(3):
                    parts.append(value.astype(fine).astype(jnp.float32))
                    value = (value - parts[-1]) * 16.0
            for which, entries in enumerate([lane, row] + parts):
                lines_ref[k, which] = entries

            def wide(which, i):
                entries = lines_ref[k, which, pl.ds(i, 8, stride=0), :]
                return jnp.concatenate([entries, entries], axis=0).astype(bf)

            left, right = ([], [])
            for i in range(group):
                lane_i, row_i = (wide(0, i), wide(1, i))
                match = [jnp.where(steps[j] == lane_i, one, zero) for j in range(lanes // 16)]
                right.append(jnp.concatenate(match, axis=0).astype(fine))
                masks = [steps[j] == row_i for j in range(rows // 16)]
                pieces = []
                for which in range(len(parts)):
                    part_i = wide(2 + which, i)
                    piece = [jnp.where(mask, part_i, zero) for mask in masks]
                    pieces.append(jnp.concatenate(piece, axis=0).astype(fine))
                left.append(jnp.concatenate(pieces, axis=0))
            acc[...] += lax.dot_general(
                jnp.concatenate(left, axis=1),
                jnp.concatenate(right, axis=1),
                (((1,), (1,)), ((), ())),
                preferred_element_type=jnp.float32,
            )
        return carry

    lax.fori_loop(0, slots // group, body, 0)
    cell_force = []
    for c in range(3):
        total = acc[3 * c * rows : (3 * c + 1) * rows, :]
        total = total + acc[(3 * c + 1) * rows : (3 * c + 2) * rows, :] * (1.0 / 16.0)
        total = total + acc[(3 * c + 2) * rows : (3 * c + 3) * rows, :] * (1.0 / 256.0)
        cell_force.append(total * (1.0 / scale))
    relaxed = collide([pop_ref[q] for q in range(19)], cell_force, solid_ref[...])
    for q in range(19):
        relaxed_ref[q] = relaxed[q]
    even = place_ref[3] == 0
    for i in range(5):
        ahead = relaxed[going(0, 1)[i]][rows - size_y :]
        behind = relaxed[going(0, -1)[i]][:size_y]
        far_ref[i] = jnp.where(even, behind, ahead)
        near_ref[i] = jnp.where(even, ahead, behind)
        for x in range(rows // size_y):
            up = relaxed[going(1, 1)[i]][size_y * x + size_y - 1 : size_y * x + size_y, :]
            down = relaxed[going(1, -1)[i]][size_y * x : size_y * x + 1, :]
            at = rows // size_y * i + x
            side_ref[at : at + 1, :] = jnp.where(place_ref[0] == 0, up, down)
    marker_copy.wait()


def spread(owned, place, own, last, early, cells, weights, populations, solid):
    mark = cells.shape[1]
    slots = early[1].shape[0]
    line_count, lanes = solid.shape
    smem = pl.BlockSpec(memory_space=pltpu.SMEM)
    vmem = pl.BlockSpec(memory_space=pltpu.VMEM)
    return pl.pallas_call(
        functools.partial(spread_kernel, slots, owned),
        out_shape=(
            full(populations.shape),
            full((5, 8, lanes)),
            full((5, 8, lanes)),
            full((24, lanes)),
            full((3, owned, mark)),
        ),
        in_specs=[smem] + [vmem] * 11,
        out_specs=[vmem] * 4 + [pl.BlockSpec(memory_space=pltpu.HBM)],
        scratch_shapes=[
            pltpu.VMEM((3, owned, mark), jnp.float32),
            pltpu.VMEM((3, slots, mark), jnp.float32),
            pltpu.VMEM((cells.shape[0] // slots, 11, group, mark), jnp.float32),
            pltpu.VMEM((9 * line_count, lanes), jnp.float32),
            pltpu.SemaphoreType.DMA,
        ],
        compiler_params=kernel_params(),
        name="spread",
    )(place, own, last, *early, cells, weights, populations, solid)


def downwind(place_ref, relaxed_ref, far_ref, near_ref):
    size_y = far_ref.shape[1]
    size_x = relaxed_ref.shape[1] // size_y
    even = place_ref[3] == 0

    def cells(q, x):
        step = int(velocity_table[q][0])
        source = x - step
        if 0 <= source < size_x:
            return relaxed_ref[q, source * size_y : (source + 1) * size_y, :]
        i = going(0, step).index(q)
        if step == 1:
            return jnp.where(even, far_ref[i], near_ref[i])
        return jnp.where(even, near_ref[i], far_ref[i])

    return cells


def sideways(cells, side_ref, edge):
    def result(q, x, y_at):
        step_x, step_y = (int(step) for step in velocity_table[q][:2])
        size_y = y_at.shape[0]
        size_x = side_ref.shape[0] // 6
        if step_y == 0:
            return cells(q, x)
        source = x - step_x
        at = size_x * going(1, step_y).index(q) + source
        halo = side_ref[at : at + 1, :] if 0 <= source < size_x else edge(q)
        turned = pltpu.roll(cells(q, x), step_y % size_y, 0)
        return jnp.where(y_at == (0 if step_y == 1 else size_y - 1), halo, turned)

    return result


def corner_index(q):
    step_y = int(velocity_table[q][1])
    return [p for p in going(1, step_y) if int(velocity_table[p][0]) != 0].index(q)


def pack_kernel(
    place_ref, relaxed_ref, far_ref, near_ref, side_ref, corner_ref, first_ref, second_ref
):
    size_y, lanes = far_ref.shape[1:]
    size_x = relaxed_ref.shape[1] // size_y
    cells = downwind(place_ref, relaxed_ref, far_ref, near_ref)
    corner_ref[...] = jnp.zeros(corner_ref.shape, jnp.float32)
    for ahead in going(1, 1):
        step_x = int(velocity_table[ahead][0])
        if step_x == 0:
            continue
        behind = opposite_table[ahead]
        up = cells(ahead, 0 if step_x == 1 else size_x - 1)[size_y - 1 : size_y, :]
        down = cells(behind, size_x - 1 if step_x == 1 else 0)[0:1, :]
        at = corner_index(ahead)
        from_behind = corner_index(behind)
        lower = place_ref[0] == 0

        @pl.when(lower)
        def _(at=at, up=up):
            corner_ref[at : at + 1, :] = up

        @pl.when(jnp.logical_not(lower))
        def _(at=from_behind, down=down):
            corner_ref[at : at + 1, :] = down

    y_at = lax.broadcasted_iota(jnp.int32, (size_y, lanes), 0)
    lane_at = lax.broadcasted_iota(jnp.int32, (size_y, lanes), 1)
    level = sideways(cells, side_ref, None)
    packs = []
    for step in (1, -1):
        packed = jnp.zeros((size_y, lanes), jnp.float32)
        for i, q in enumerate(going(2, step)):
            edge = lanes - 1 if step == 1 else 0
            for x in range(size_x):
                at = 8 * x + i
                moved = pltpu.roll(level(q, x, y_at), (at - edge) % lanes, 1)
                packed = jnp.where(lane_at == at, moved, packed)
        packs.append(packed)
    even = place_ref[1] % 2 == 0
    first_ref[...] = jnp.where(even, packs[0], packs[1])
    second_ref[...] = jnp.where(even, packs[1], packs[0])


def pack(place, relaxed, far, near, side):
    smem = pl.BlockSpec(memory_space=pltpu.SMEM)
    vmem = pl.BlockSpec(memory_space=pltpu.VMEM)
    edge = full(far.shape[1:])
    return pl.pallas_call(
        pack_kernel,
        out_shape=(edge, edge, edge),
        in_specs=[smem] + [vmem] * 4,
        compiler_params=kernel_params(),
        name="pack",
    )(place, relaxed, far, near, side)


def stream_kernel(
    count_z, place_ref, relaxed_ref, far_ref, near_ref, side_ref, second_ref, corner_ref,
    first_ref, out_any, out_ref, sems,
):
    size_x, size_y, lanes = out_ref.shape[1:]
    shape = (size_y, lanes)
    y_at = lax.broadcasted_iota(jnp.int32, shape, 0)
    z_at = lax.broadcasted_iota(jnp.int32, shape, 1)
    y_index, z_index = (place_ref[0], place_ref[1])
    streamed = sideways(
        downwind(place_ref, relaxed_ref, far_ref, near_ref),
        side_ref,
        lambda q: corner_ref[corner_index(q) : corner_index(q) + 1, :],
    )
    even = z_index % 2 == 0
    columns = {
        -1: jnp.where(even, first_ref[...], second_ref[...]),
        1: jnp.where(even, second_ref[...], first_ref[...]),
    }
    on_side = y_at == jnp.where(y_index == 0, 0, size_y - 1)
    on_side = on_side | ((z_at == 0) & (z_index == 0))
    on_side = on_side | ((z_at == lanes - 1) & (z_index == count_z - 1))
    copies = []
    for q in range(19):
        step_z = int(velocity_table[q][2])
        z_edge = 0 if step_z == 1 else lanes - 1
        for x in range(size_x):
            cells = streamed(q, x, y_at)
            if step_z != 0:
                at = 8 * x + going(2, step_z).index(q)
                cells = jnp.where(
                    z_at == z_edge,
                    pltpu.roll(columns[step_z], (z_edge - at) % lanes, 1),
                    pltpu.roll(cells, step_z % lanes, 1),
                )
            out_ref[q, x] = jnp.where(on_side, far_field[q], cells)
        copies.append(pltpu.make_async_copy(out_ref.at[q], out_any.at[q], sems.at[q]))
        copies[-1].start()
    for copy in copies:
        copy.wait()


def stream(count_z, place, relaxed, *halos):
    rows, lanes = relaxed.shape[1:]
    size_y = halos[0].shape[1]
    smem = pl.BlockSpec(memory_space=pltpu.SMEM)
    vmem = pl.BlockSpec(memory_space=pltpu.VMEM)
    shape = (19, rows // size_y, size_y, lanes)
    return pl.pallas_call(
        functools.partial(stream_kernel, count_z),
        out_shape=full(shape),
        in_specs=[smem] + [vmem] * (1 + len(halos)),
        out_specs=pl.BlockSpec(memory_space=pltpu.HBM),
        scratch_shapes=[pltpu.VMEM(shape, jnp.float32), pltpu.SemaphoreType.DMA((19,))],
        compiler_params=kernel_params(),
        name="stream",
    )(place, relaxed, *halos)


def per_device(
    populations,
    solid_cells,
    slot_cells,
    slot_weights,
    slot_owner,
    slot_block,
    train_of_block,
    marker_area,
    train_velocity,
):
    size_x, size_y, size_z = (populations.shape[1], populations.shape[2], populations.shape[3])
    lines = size_x * size_y
    slots, kernel, mark = (slot_cells.shape[3], slot_cells.shape[4], slot_cells.shape[5])
    owned = train_of_block.shape[3]
    count_x, count_y, count_z = (lax.axis_size(axis) for axis in ("gx", "gy", "gz"))
    x_index, y_index, z_index = (lax.axis_index(axis) for axis in ("gx", "gy", "gz"))
    place = jnp.stack([y_index, z_index, x_index * count_y + y_index, x_index % 2])
    place = place.astype(jnp.int32)
    inputs = [
        pltpu.with_memory_space_constraint(entries, pltpu.HBM)
        for entries in (
            populations.reshape(19, lines, size_z),
            slot_cells.reshape(slots * kernel, mark),
            slot_weights.reshape(slots * kernel, mark),
            marker_area.reshape(owned, mark),
            slot_owner.reshape(1, slots),
            slot_block.reshape(1, slots),
            train_of_block.reshape(1, owned),
        )
    ]
    own, pops, cells, weights = sample(place, *inputs)
    swap = [(0, 1), (1, 0)]

    def across_x(entries, distance):
        return lax.ppermute(entries, "gx", [(i, i ^ distance) for i in range(count_x)])

    def across_y(entries):
        return lax.ppermute(entries, "gy", swap)

    third, first = (across_x(own, distance) for distance in (3, 1))
    beside = across_y(own)
    third_beside = across_y(third)
    second = across_x(lax.optimization_barrier((third, beside))[0], 1)
    first_beside = across_y(first)
    last = across_x(third_beside, 1)
    whole = [own, first, third, second, beside, first_beside, third_beside]
    early = settle_early(slots, owned, train_velocity, whole)
    solid = solid_cells.reshape(lines, size_z)
    relaxed, far, near, side, marker_force = spread(
        owned, place, own, last, early, cells, weights, pops, solid
    )
    evens = range(0, count_x, 2)
    far = lax.ppermute(
        far,
        "gx",
        [(i, (i - 1) % count_x) for i in evens] + [((i - 1) % count_x, i) for i in evens],
    )
    near = lax.ppermute(near, "gx", [(i, i + 1) for i in evens] + [(i + 1, i) for i in evens])
    side = across_y(side)
    corner, up_first, down_first = pack(place, relaxed, far, near, side)
    inner = [(i, i + 1) for i in range(0, count_z - 1, 2)]
    outer = [(i, i + 1) for i in range(1, count_z - 1, 2)]
    down_first = lax.ppermute(down_first, "gz", outer + [(j, i) for i, j in outer])
    corner = across_y(corner)
    up_first = lax.ppermute(up_first, "gz", inner + [(j, i) for i, j in inner])
    populations_next = stream(
        count_z, place, relaxed, far, near, side, down_first, corner, up_first
    )
    marker_force = marker_force.transpose(1, 0, 2).reshape(1, 1, 1, owned, 3, mark)
    return (populations_next, marker_force)


def solution(mesh):
    placed = (
        P(None, "gx", "gy", "gz"),
        P("gx", "gy", "gz"),
        P("gx", "gy", "gz", None, None, None),
        P("gx", "gy", "gz", None, None, None),
        P("gx", "gy", "gz", None, None),
        P("gx", "gy", "gz", None),
        P("gx", "gy", "gz", None),
        P("gx", "gy", "gz", None, None),
        P(),
    )
    small = mesh.shape["gy"] == 2 and mesh.shape["gx"] == 4 and mesh.shape["gz"] % 2 == 0
    return jax.shard_map(
        per_device if small else per_device_general,
        mesh=mesh,
        in_specs=placed,
        out_specs=(P(None, "gx", "gy", "gz"), P("gx", "gy", "gz", None, None, None)),
        check_vma=False,
    )
```

```python
import functools
import jax
import jax.numpy as jnp
import numpy as np
from jax import lax
from jax.experimental import pallas as pl
from jax.experimental.pallas import tpu as pltpu
from jax.sharding import PartitionSpec as P

velocity_table = np.array(
    [
        [0, 0, 0],
        [1, 0, 0],
        [-1, 0, 0],
        [0, 1, 0],
        [0, -1, 0],
        [0, 0, 1],
        [0, 0, -1],
        [1, 1, 0],
        [-1, -1, 0],
        [1, -1, 0],
        [-1, 1, 0],
        [1, 0, 1],
        [-1, 0, -1],
        [1, 0, -1],
        [-1, 0, 1],
        [0, 1, 1],
        [0, -1, -1],
        [0, 1, -1],
        [0, -1, 1],
    ]
)
weight_table = [1.0 / 3.0] + [1.0 / 18.0] * 6 + [1.0 / 36.0] * 12
opposite_table = [0, 2, 1, 4, 3, 6, 5, 8, 7, 10, 9, 12, 11, 14, 13, 16, 15, 18, 17]
stress_pairs = [(0, 0), (1, 1), (2, 2), (0, 1), (0, 2), (1, 2)]
tau_base = 0.55
smag_term = 18.0 * 1.4142135623730951 * 0.17 * 0.17
regular_eps = 0.0001
stiffness = 2.0
far_velocity = (0.02, 0.06, 0.0)
vmem_bytes = 16 << 20
group = 8
fine = jnp.float8_e4m3fn
matrix_points = 3


def going(axis, step):
    return [q for q in range(19) if int(velocity_table[q][axis]) == step]


def project(direction, vector):
    projection = 0.0 * vector[0]
    for component in range(3):
        lattice_step = int(velocity_table[direction][component])
        if lattice_step != 0:
            projection = projection + lattice_step * vector[component]
    return projection


def moments(populations):
    density = populations[0]
    momentum = [jnp.zeros_like(density) for component in range(3)]
    for direction in range(1, 19):
        density = density + populations[direction]
        for component in range(3):
            lattice_step = int(velocity_table[direction][component])
            if lattice_step == 1:
                momentum[component] = momentum[component] + populations[direction]
            elif lattice_step == -1:
                momentum[component] = momentum[component] - populations[direction]
    return (density, momentum)


def equilibrium(density, velocity):
    speed_sq = velocity[0] * velocity[0] + velocity[1] * velocity[1] + velocity[2] * velocity[2]
    result = []
    for direction in range(19):
        projected = project(direction, velocity)
        result.append(
            weight_table[direction]
            * density
            * (1.0 + 3.0 * projected + 4.5 * projected * projected - 1.5 * speed_sq)
        )
    return result


far_field = [float(np.float32(value)) for value in equilibrium(1.0, list(far_velocity))]


def collide(populations, cell_force, solid_cells):
    density, momentum = moments(populations)
    velocity = [
        (momentum[component] + 0.5 * cell_force[component]) / density for component in range(3)
    ]
    balance = equilibrium(density, velocity)
    stress = [jnp.zeros_like(density) for pair_pos in range(6)]
    for direction in range(19):
        non_eq = populations[direction] - balance[direction]
        for pair_pos in range(6):
            row_axis, col_axis = stress_pairs[pair_pos]
            factor = int(velocity_table[direction][row_axis] * velocity_table[direction][col_axis])
            if factor != 0:
                stress[pair_pos] = stress[pair_pos] + factor * non_eq
    shear_sq = stress[0] * stress[0] + stress[1] * stress[1] + stress[2] * stress[2]
    shear_sq = shear_sq + 2.0 * (
        stress[3] * stress[3] + stress[4] * stress[4] + stress[5] * stress[5]
    )
    magnitude = jnp.sqrt(shear_sq + regular_eps)
    relax_time = 0.5 * (tau_base + jnp.sqrt(tau_base * tau_base + smag_term * magnitude / density))
    relax_rate = 1.0 / relax_time
    guo_factor = 1.0 - 0.5 * relax_rate
    speed_force = (
        velocity[0] * cell_force[0] + velocity[1] * cell_force[1] + velocity[2] * cell_force[2]
    )
    result = []
    for direction in range(19):
        along_force = project(direction, cell_force)
        along_speed = project(direction, velocity)
        source = (
            guo_factor
            * weight_table[direction]
            * (3.0 * (along_force - speed_force) + 9.0 * along_speed * along_force)
        )
        relaxed = (
            populations[direction]
            - (populations[direction] - balance[direction]) * relax_rate
            + source
        )
        result.append(jnp.where(solid_cells == 1, populations[opposite_table[direction]], relaxed))
    return result


def with_halo(cells, sides, width):
    for axis, dim in sides:
        count = lax.axis_size(axis)
        head = lax.slice_in_dim(cells, 0, width, axis=dim)
        tail = lax.slice_in_dim(cells, cells.shape[dim] - width, cells.shape[dim], axis=dim)
        cells = jnp.concatenate(
            [
                lax.ppermute(tail, axis, [(i, (i + 1) % count) for i in range(count)]),
                cells,
                lax.ppermute(head, axis, [((i + 1) % count, i) for i in range(count)]),
            ],
            axis=dim,
        )
    return cells


def settle(received, labels, owned, train_of_block, marker_area, train_velocity, mark):
    rows_in = received.reshape(-1, 3 * mark)
    label_rows = labels.reshape(-1)
    owner_match = (label_rows[None, :] == jnp.arange(owned, dtype=jnp.int32)[:, None]).astype(
        jnp.float32
    )
    marker_velocity = jnp.dot(owner_match, rows_in, precision=lax.Precision.HIGHEST).reshape(
        owned, 3, mark
    )
    trains = train_velocity.shape[0]
    train_rows = train_of_block.reshape(owned)
    train_match = (train_rows[:, None] == jnp.arange(trains, dtype=jnp.int32)[None, :]).astype(
        jnp.float32
    )
    target = jnp.dot(train_match, train_velocity, precision=lax.Precision.HIGHEST)
    areas = marker_area.reshape(owned, mark)
    marker_force = stiffness * areas[:, None, :] * (target[:, :, None] - marker_velocity)
    back_rows = jnp.dot(
        owner_match.T, marker_force.reshape(owned, 3 * mark), precision=lax.Precision.HIGHEST
    )
    return (marker_force, back_rows)


def per_device_general(
    populations,
    solid_cells,
    slot_cells,
    slot_weights,
    slot_owner,
    slot_block,
    train_of_block,
    marker_area,
    train_velocity,
):
    size_x, size_y, size_z = (populations.shape[1], populations.shape[2], populations.shape[3])
    cell_count = size_x * size_y * size_z
    slots, kernel, mark = (slot_cells.shape[3], slot_cells.shape[4], slot_cells.shape[5])
    owned = train_of_block.shape[3]
    peers_x = lax.axis_size("gx")
    peers_y = lax.axis_size("gy")
    peers = peers_x * peers_y
    capacity = max(2, 2 * slots // peers)
    density, momentum = moments(populations)
    rest_velocity = jnp.stack([momentum[component] / density for component in range(3)]).reshape(
        3, cell_count
    )
    cells = slot_cells.reshape(slots, kernel, mark)
    weights = slot_weights.reshape(slots, kernel, mark)
    partial_value = jnp.sum(rest_velocity[:, cells] * weights[None], axis=2)
    slot_rows = partial_value.transpose(1, 0, 2).reshape(slots, 3 * mark)
    slot_dest = slot_owner.reshape(slots)
    blocks = slot_block.reshape(slots)
    order = jnp.arange(slots, dtype=jnp.int32)
    earlier = (slot_dest[None, :] == slot_dest[:, None]) & (order[None, :] < order[:, None])
    slot_rank = jnp.sum(earlier.astype(jnp.int32), axis=1)
    target_row = slot_dest * capacity + slot_rank
    buffer_rows = jnp.arange(peers * capacity, dtype=jnp.int32)
    matches = buffer_rows[:, None] == target_row[None, :]
    placement = matches.astype(jnp.float32)
    outgoing = jnp.dot(placement, slot_rows, precision=lax.Precision.HIGHEST)
    labels = jnp.sum(jnp.where(matches, blocks[None, :] + 1, 0), axis=1) - 1
    received, got_labels = (
        lax.all_to_all(
            outgoing.reshape(peers, capacity, 3 * mark),
            ("gx", "gy"),
            split_axis=0,
            concat_axis=0,
            tiled=True,
        ),
        lax.all_to_all(
            labels.reshape(peers, capacity), ("gx", "gy"), split_axis=0, concat_axis=0, tiled=True
        ),
    )
    marker_force, back_rows = settle(
        received, got_labels, owned, train_of_block, marker_area, train_velocity, mark
    )
    returned = lax.all_to_all(
        back_rows.reshape(peers, capacity, 3 * mark),
        ("gx", "gy"),
        split_axis=0,
        concat_axis=0,
        tiled=True,
    )
    slot_force = jnp.dot(
        placement.T, returned.reshape(peers * capacity, 3 * mark), precision=lax.Precision.HIGHEST
    )
    slot_force = slot_force.reshape(slots, 3, mark).transpose(1, 0, 2)
    contrib = weights[None] * slot_force[:, :, None, :]
    cell_force = (
        jnp.zeros((3, cell_count), jnp.float32).at[:, cells.reshape(-1)].add(contrib.reshape(3, -1))
    )
    cell_force = cell_force.reshape(3, size_x, size_y, size_z)
    relaxed = collide(populations, cell_force, solid_cells)
    padded = with_halo(jnp.stack(relaxed), (("gx", 1), ("gy", 2), ("gz", 3)), 1)
    parts = []
    for direction in range(19):
        shift_x = 1 - int(velocity_table[direction][0])
        shift_y = 1 - int(velocity_table[direction][1])
        shift_z = 1 - int(velocity_table[direction][2])
        parts.append(
            padded[
                direction,
                shift_x : shift_x + size_x,
                shift_y : shift_y + size_y,
                shift_z : shift_z + size_z,
            ]
        )
    read = jnp.stack(parts)
    total_y = size_y * lax.axis_size("gy")
    total_z = size_z * lax.axis_size("gz")
    global_y = lax.axis_index("gy") * size_y + jnp.arange(size_y, dtype=jnp.int32)
    global_z = lax.axis_index("gz") * size_z + jnp.arange(size_z, dtype=jnp.int32)
    on_side = ((global_y == 0) | (global_y == total_y - 1))[:, None] | (
        (global_z == 0) | (global_z == total_z - 1)
    )[None, :]
    far_field = jnp.array(equilibrium(1.0, list(far_velocity)), dtype=jnp.float32)
    populations_next = jnp.where(on_side[None, None], far_field[:, None, None, None], read)
    return (populations_next, marker_force.reshape(1, 1, 1, owned, 3, mark))


def full(shape):
    return jax.ShapeDtypeStruct(shape, jnp.float32)


def kernel_params():
    return pltpu.CompilerParams(vmem_limit_bytes=vmem_bytes)


def low_half(shape):
    return lax.broadcasted_iota(jnp.int32, shape, 1) < shape[1] // 2


def fetch(pairs, sems):
    copies = [
        pltpu.make_async_copy(source, target, sems.at[i])
        for i, (source, target) in enumerate(pairs)
    ]
    for copy in copies:
        copy.start()
    return copies


def shard_rows(slots, owned):
    return 8 + owned + 3 * slots


def sample_kernel(
    place_ref, pop_any, cells_any, weights_any, areas_any, owner_any, block_any, trains_any,
    out_ref, pop_ref, cells_ref, weights_ref, areas_ref, owner_ref, block_ref, trains_ref,
    table, parts_ref, lines_ref, spread_ref, sems,
):
    rows, lanes = (pop_ref.shape[1], pop_ref.shape[2])
    mark = cells_ref.shape[1]
    owned = areas_ref.shape[0]
    slots = owner_ref.shape[1]
    kernel = cells_ref.shape[0] // slots
    copies = fetch(
        (
            (pop_any, pop_ref),
            (cells_any, cells_ref),
            (weights_any, weights_ref),
            (areas_any, areas_ref),
            (owner_any, owner_ref),
            (block_any, block_ref),
            (trains_any, trains_ref),
        ),
        sems,
    )

    copies[0].wait()
    density, momentum = moments([pop_ref[q] for q in range(19)])
    speed = [momentum[c] / density for c in range(3)]
    largest = jnp.maximum(jnp.maximum(jnp.abs(speed[0]), jnp.abs(speed[1])), jnp.abs(speed[2]))
    largest = jnp.max(largest, axis=(0, 1), keepdims=True) + 1e-20
    scale = largest * (1.0 / 32767.0)
    fixed = [(speed[c] * (1.0 / scale) + 32768.5).astype(jnp.int32) for c in range(3)]
    words = jnp.concatenate(
        [
            (fixed[0] << 16) | fixed[1],
            (fixed[2][: rows // 2] << 16) | fixed[2][rows // 2 :],
        ],
        axis=0,
    )
    for r in range(table.shape[0]):
        table[r] = jnp.broadcast_to(words[r : r + 1], (group, lanes))
    for c in range(3):
        value = speed[c] * (224.0 / largest)
        for part in range(4):
            piece = value.astype(fine)
            parts_ref[c * rows : (c + 1) * rows, part * lanes : (part + 1) * lanes] = piece
            value = value - piece.astype(jnp.float32)
    for copy in copies[1:]:
        copy.wait()
    out_ref[8 : 8 + owned, :] = areas_ref[...]
    out_ref[0:8, :] = jnp.zeros((8, mark), jnp.float32)
    ids = (owner_ref[...] * owned + block_ref[...]).astype(jnp.float32)
    out_ref[0:1, :] = jnp.concatenate([ids] * (mark // slots), axis=1)
    out_ref[1:2, 0:owned] = trains_ref[...].astype(jnp.float32)
    mine = lax.broadcasted_iota(jnp.int32, (1, mark), 1) % owned + place_ref[2] * owned
    out_ref[2:3, :] = mine.astype(jnp.float32)

    bf = jnp.bfloat16
    iota = lax.broadcasted_iota(jnp.int32, (16, mark), 0).astype(jnp.float32)
    steps = [(iota + 16.0 * j).astype(bf) for j in range(lanes // 16)]
    line_at = [iota[0:8] + 8.0 * j for j in range(rows // 8)]
    one, zero = (jnp.ones((16, mark), bf), jnp.zeros((16, mark), bf))

    def by_matrix(first):
        for which, k in enumerate(range(kernel - matrix_points, kernel)):
            at = pl.ds(first * kernel + k, group, stride=kernel)
            cells = cells_ref[at, :]
            lines_ref[which, 0] = (cells & (lanes - 1)).astype(jnp.float32)
            lines_ref[which, 1] = (cells >> (lanes.bit_length() - 1)).astype(jnp.float32)
            lines_ref[which, 2] = weights_ref[at, :]
        for i in range(group):
            sums = [jnp.zeros((8, mark), jnp.float32) for c in range(3)]
            for which in range(matrix_points):
                lane, row, weight = (
                    lines_ref[which, entry, pl.ds(i, 8, stride=0), :] for entry in range(3)
                )
                lane = jnp.concatenate([lane, lane], axis=0).astype(bf)
                match = [jnp.where(step == lane, one, zero) for step in steps]
                match = jnp.concatenate(match, axis=0).astype(fine)
                got = jnp.dot(
                    parts_ref[...],
                    jnp.concatenate([match] * 4, axis=0),
                    preferred_element_type=jnp.float32,
                )
                for j in range(rows // 8):
                    share = jnp.where(line_at[j] == row, weight, 0.0)
                    for c in range(3):
                        here = c * rows + 8 * j
                        sums[c] = sums[c] + share * got[here : here + 8]
            for c in range(3):
                spread_ref[c, 8 * i : 8 * i + 8, :] = sums[c]
        result = []
        for c in range(3):
            total = spread_ref[c, pl.ds(0, group, stride=8), :]
            for j in range(1, 8):
                total = total + spread_ref[c, pl.ds(j, group, stride=8), :]
            result.append(total)
        return result

    def body(step, carry):
        first = pl.multiple_of(step * group, group)
        total = [jnp.zeros((group, mark), jnp.float32) for c in range(3)]
        other = by_matrix(first)
        for k in range(kernel - matrix_points):
            at = pl.ds(first * kernel + k, group, stride=kernel)
            cells = cells_ref[at, :]
            lane = cells & (lanes - 1)
            row = cells >> (lanes.bit_length() - 1)
            bits = [(row >> bit) & 1 == 1 for bit in range(rows.bit_length() - 1)]

            def choose(low, level):
                if level < 0:
                    return jnp.take_along_axis(table[low], lane, axis=1, mode="promise_in_bounds")
                lower = choose(low, level - 1)
                return jnp.where(bits[level], choose(low + (1 << level), level - 1), lower)

            pair = choose(0, len(bits) - 1)
            third = choose(rows, len(bits) - 2)
            picked = [
                lax.shift_right_logical(pair, 16),
                pair & 65535,
                jnp.where(bits[-1], third & 65535, lax.shift_right_logical(third, 16)),
            ]
            weight = weights_ref[at, :]
            for c in range(3):
                total[c] = total[c] + weight * (picked[c].astype(jnp.float32) - 32768.0)
        for c in range(3):
            here = pl.ds(pl.multiple_of(8 + owned + c * slots + first, group), group)
            out_ref[here, :] = total[c] * scale + other[c] * (largest * (1.0 / 224.0))
        return carry

    lax.fori_loop(0, slots // group, body, 0)


def sample(place, populations, cells, weights, areas, owner, block, trains):
    smem = pl.BlockSpec(memory_space=pltpu.SMEM)
    hbm = pl.BlockSpec(memory_space=pltpu.HBM)
    vmem = pl.BlockSpec(memory_space=pltpu.VMEM)
    kept = (populations, cells, weights)
    count = shard_rows(owner.shape[1], areas.shape[0])
    return pl.pallas_call(
        sample_kernel,
        out_shape=[full((count, cells.shape[1]))]
        + [jax.ShapeDtypeStruct(entries.shape, entries.dtype) for entries in kept],
        in_specs=[smem] + [hbm] * 7,
        out_specs=[vmem] * 4,
        scratch_shapes=[
            pltpu.VMEM(entries.shape, entries.dtype) for entries in (areas, owner, block, trains)
        ]
        + [
            pltpu.VMEM((populations.shape[1] * 3 // 2, group, populations.shape[2]), jnp.int32),
            pltpu.VMEM((3 * populations.shape[1], 4 * populations.shape[2]), fine),
            pltpu.VMEM((matrix_points, 3, group, cells.shape[1]), jnp.float32),
            pltpu.VMEM((3, 8 * group, cells.shape[1]), jnp.float32),
            pltpu.SemaphoreType.DMA((7,)),
        ],
        compiler_params=kernel_params(),
        name="sample",
    )(place, populations, cells, weights, areas, owner, block, trains)


def three_parts(values):
    parts = []
    for _ in range(3):
        parts.append(values.astype(jnp.bfloat16))
        values = values - parts[-1].astype(jnp.float32)
    return parts


def one_hot(mask):
    return jnp.where(mask, 1.0, 0.0).astype(jnp.bfloat16)


def wanted_labels(own_ref, slots, owned):
    mark = own_ref.shape[1]
    own = own_ref[0:8, :]
    ids, trains, mine = (jnp.broadcast_to(own[i : i + 1], (mark, mark)).T for i in range(3))
    return (ids[0:slots], mine[0:owned], trains[0:owned])


def add_shards(totals, shards, ids, mine):
    slots, owned = (ids.shape[0], mine.shape[0])
    wanted = jnp.concatenate([ids, mine], axis=0)
    for shard in shards:
        match = one_hot(wanted == shard[0:1, :])
        match = jnp.concatenate([match, match[:, 0:slots]], axis=1)
        starts = [8 + owned + c * slots for c in range(3)]
        values = jnp.concatenate([shard[at : at + slots, :] for at in starts], axis=1)
        sums = jnp.dot(
            match, jnp.concatenate(three_parts(values), axis=0), preferred_element_type=jnp.float32
        )
        held = ids == shard[2:3, :]
        parts = three_parts(shard[8 : 8 + owned, :])
        parts.append(jnp.zeros_like(parts[0]))
        area = jnp.dot(
            one_hot(held), jnp.concatenate(parts, axis=0), preferred_element_type=jnp.float32
        )
        got = (sums, area, jnp.where(held, shard[1:2, :], 0.0))
        totals = got if totals is None else [total + new for total, new in zip(totals, got)]
    return totals


def settle_kernel(slots, owned, speeds_ref, *refs):
    *shards, sums_ref, area_ref, trains_ref, rows_ref, labels_ref = refs
    mark = rows_ref.shape[1]
    for train in range(speeds_ref.shape[0]):
        for c in range(3):
            at = 3 * train + c
            rows_ref[at : at + 1, :] = jnp.full((1, mark), speeds_ref[train, c], jnp.float32)
    ids, mine, own_trains = wanted_labels(shards[0], slots, owned)
    labels_ref[...] = jnp.concatenate([ids, mine, own_trains], axis=0)
    sums_ref[...], area_ref[...], trains_ref[...] = add_shards(None, shards, ids, mine)


def settle_early(slots, owned, speeds, shards):
    mark = shards[0].shape[1]
    smem = pl.BlockSpec(memory_space=pltpu.SMEM)
    vmem = pl.BlockSpec(memory_space=pltpu.VMEM)
    return pl.pallas_call(
        functools.partial(settle_kernel, slots, owned),
        out_shape=(
            full((slots + owned, 3 * mark)),
            full((slots, mark)),
            full((slots, mark)),
            full((3 * speeds.shape[0], mark)),
            full((slots + 2 * owned, mark)),
        ),
        in_specs=[smem] + [vmem] * len(shards),
        compiler_params=kernel_params(),
        cost_estimate=pl.CostEstimate(
            flops=10**9, bytes_accessed=len(shards) * shards[0].size * 4, transcendentals=0
        ),
        name="settle",
    )(speeds, *shards)


def block_forces(rows_ref, totals, own_ref, own_trains):
    mark = own_ref.shape[1]
    sums, area, trains = totals
    slots, owned = (area.shape[0], own_trains.shape[0])
    trains = jnp.broadcast_to(jnp.sum(trains, axis=1, keepdims=True), area.shape)
    own_area = own_ref[8 : 8 + owned, :]
    forces, own_forces = ([], [])
    for c in range(3):
        target, own_target = (jnp.zeros_like(area), jnp.zeros_like(own_area))
        for train in range(rows_ref.shape[0] // 3):
            at = 3 * train + c
            speed = rows_ref[at : at + 1, :]
            target = jnp.where(trains == float(train), speed, target)
            own_target = jnp.where(own_trains == float(train), speed, own_target)
        got = sums[:, c * mark : (c + 1) * mark]
        forces.append(stiffness * area * (target - got[0:slots]))
        own_forces.append(stiffness * own_area * (own_target - got[slots:]))
    return (forces, own_forces)


def spread_kernel(
    slots, owned, place_ref, own_ref, last_ref, sums_ref, area_ref, trains_ref, speeds_ref,
    labels_ref,
    cells_ref, weights_ref, pop_ref, solid_ref,
    relaxed_ref, far_ref, near_ref, side_ref, marker_any, marker_ref, force_ref, lines_ref, acc,
    sem,
):
    rows, lanes = (pop_ref.shape[1], pop_ref.shape[2])
    size_y = 8
    mark = cells_ref.shape[1]
    kernel = cells_ref.shape[0] // slots
    bf = jnp.bfloat16
    ids = labels_ref[0:slots]
    mine, own_trains = (labels_ref[at : at + owned] for at in (slots, slots + owned))
    totals = add_shards((sums_ref[...], area_ref[...], trains_ref[...]), [last_ref], ids, mine)
    forces, own_forces = block_forces(speeds_ref, totals, own_ref, own_trains)
    largest = jnp.maximum(jnp.maximum(jnp.abs(forces[0]), jnp.abs(forces[1])), jnp.abs(forces[2]))
    largest = jnp.maximum(jnp.max(largest, axis=(0, 1), keepdims=True), 1e-20)
    scale = (224.0 * 16.0) / largest
    for c in range(3):
        force_ref[c] = forces[c] * scale
        marker_ref[c] = own_forces[c]
    marker_copy = pltpu.make_async_copy(marker_ref, marker_any, sem)
    marker_copy.start()

    acc[...] = jnp.zeros_like(acc)
    iota = lax.broadcasted_iota(jnp.int32, (16, mark), 0).astype(jnp.float32)
    steps = [(iota + 16.0 * j).astype(bf) for j in range(max(rows, lanes) // 16)]
    one, zero = (jnp.ones((16, mark), bf), jnp.zeros((16, mark), bf))

    def body(step, carry):
        first = pl.multiple_of(step * group, group)
        force = [force_ref[c, pl.ds(first, group), :] for c in range(3)]
        for k in range(kernel):
            at = pl.ds(first * kernel + k, group, stride=kernel)
            cells = cells_ref[at, :]
            weight = weights_ref[at, :]
            lane = (cells & (lanes - 1)).astype(jnp.float32)
            row = (cells >> (lanes.bit_length() - 1)).astype(jnp.float32)
            parts = []
            for c in range(3):
                value = weight * force[c]
                for _ in range(3):
                    parts.append(value.astype(fine).astype(jnp.float32))
                    value = (value - parts[-1]) * 16.0
            for which, entries in enumerate([lane, row] + parts):
                lines_ref[k, which] = entries

            def wide(which, i):
                entries = lines_ref[k, which, pl.ds(i, 8, stride=0), :]
                return jnp.concatenate([entries, entries], axis=0).astype(bf)

            left, right = ([], [])
            for i in range(group):
                lane_i, row_i = (wide(0, i), wide(1, i))
                match = [jnp.where(steps[j] == lane_i, one, zero) for j in range(lanes // 16)]
                right.append(jnp.concatenate(match, axis=0).astype(fine))
                masks = [steps[j] == row_i for j in range(rows // 16)]
                pieces = []
                for which in range(len(parts)):
                    part_i = wide(2 + which, i)
                    piece = [jnp.where(mask, part_i, zero) for mask in masks]
                    pieces.append(jnp.concatenate(piece, axis=0).astype(fine))
                left.append(jnp.concatenate(pieces, axis=0))
            acc[...] += lax.dot_general(
                jnp.concatenate(left, axis=1),
                jnp.concatenate(right, axis=1),
                (((1,), (1,)), ((), ())),
                preferred_element_type=jnp.float32,
            )
        return carry

    lax.fori_loop(0, slots // group, body, 0)
    cell_force = []
    for c in range(3):
        total = acc[3 * c * rows : (3 * c + 1) * rows, :]
        total = total + acc[(3 * c + 1) * rows : (3 * c + 2) * rows, :] * (1.0 / 16.0)
        total = total + acc[(3 * c + 2) * rows : (3 * c + 3) * rows, :] * (1.0 / 256.0)
        cell_force.append(total * (1.0 / scale))
    relaxed = collide([pop_ref[q] for q in range(19)], cell_force, solid_ref[...])
    for q in range(19):
        relaxed_ref[q] = relaxed[q]
    even = place_ref[3] == 0
    for i in range(5):
        ahead = relaxed[going(0, 1)[i]][rows - size_y :]
        behind = relaxed[going(0, -1)[i]][:size_y]
        far_ref[i] = jnp.where(even, behind, ahead)
        near_ref[i] = jnp.where(even, ahead, behind)
        for x in range(rows // size_y):
            up = relaxed[going(1, 1)[i]][size_y * x + size_y - 1 : size_y * x + size_y, :]
            down = relaxed[going(1, -1)[i]][size_y * x : size_y * x + 1, :]
            at = rows // size_y * i + x
            side_ref[at : at + 1, :] = jnp.where(place_ref[0] == 0, up, down)
    marker_copy.wait()


def spread(owned, place, own, last, early, cells, weights, populations, solid):
    mark = cells.shape[1]
    slots = early[1].shape[0]
    line_count, lanes = solid.shape
    smem = pl.BlockSpec(memory_space=pltpu.SMEM)
    vmem = pl.BlockSpec(memory_space=pltpu.VMEM)
    return pl.pallas_call(
        functools.partial(spread_kernel, slots, owned),
        out_shape=(
            full(populations.shape),
            full((5, 8, lanes)),
            full((5, 8, lanes)),
            full((24, lanes)),
            full((3, owned, mark)),
        ),
        in_specs=[smem] + [vmem] * 11,
        out_specs=[vmem] * 4 + [pl.BlockSpec(memory_space=pltpu.HBM)],
        scratch_shapes=[
            pltpu.VMEM((3, owned, mark), jnp.float32),
            pltpu.VMEM((3, slots, mark), jnp.float32),
            pltpu.VMEM((cells.shape[0] // slots, 11, group, mark), jnp.float32),
            pltpu.VMEM((9 * line_count, lanes), jnp.float32),
            pltpu.SemaphoreType.DMA,
        ],
        compiler_params=kernel_params(),
        name="spread",
    )(place, own, last, *early, cells, weights, populations, solid)


def downwind(place_ref, relaxed_ref, far_ref, near_ref):
    size_y = far_ref.shape[1]
    size_x = relaxed_ref.shape[1] // size_y
    even = place_ref[3] == 0

    def cells(q, x):
        step = int(velocity_table[q][0])
        source = x - step
        if 0 <= source < size_x:
            return relaxed_ref[q, source * size_y : (source + 1) * size_y, :]
        i = going(0, step).index(q)
        if step == 1:
            return jnp.where(even, far_ref[i], near_ref[i])
        return jnp.where(even, near_ref[i], far_ref[i])

    return cells


def sideways(cells, side_ref, edge):
    def result(q, x, y_at):
        step_x, step_y = (int(step) for step in velocity_table[q][:2])
        size_y = y_at.shape[0]
        size_x = side_ref.shape[0] // 6
        if step_y == 0:
            return cells(q, x)
        source = x - step_x
        at = size_x * going(1, step_y).index(q) + source
        halo = side_ref[at : at + 1, :] if 0 <= source < size_x else edge(q)
        turned = pltpu.roll(cells(q, x), step_y % size_y, 0)
        return jnp.where(y_at == (0 if step_y == 1 else size_y - 1), halo, turned)

    return result


def corner_index(q):
    step_y = int(velocity_table[q][1])
    return [p for p in going(1, step_y) if int(velocity_table[p][0]) != 0].index(q)


def pack_kernel(
    place_ref, relaxed_ref, far_ref, near_ref, side_ref, corner_ref, first_ref, second_ref
):
    size_y, lanes = far_ref.shape[1:]
    size_x = relaxed_ref.shape[1] // size_y
    cells = downwind(place_ref, relaxed_ref, far_ref, near_ref)
    corner_ref[...] = jnp.zeros(corner_ref.shape, jnp.float32)
    for ahead in going(1, 1):
        step_x = int(velocity_table[ahead][0])
        if step_x == 0:
            continue
        behind = opposite_table[ahead]
        up = cells(ahead, 0 if step_x == 1 else size_x - 1)[size_y - 1 : size_y, :]
        down = cells(behind, size_x - 1 if step_x == 1 else 0)[0:1, :]
        at = corner_index(ahead)
        from_behind = corner_index(behind)
        lower = place_ref[0] == 0

        @pl.when(lower)
        def _(at=at, up=up):
            corner_ref[at : at + 1, :] = up

        @pl.when(jnp.logical_not(lower))
        def _(at=from_behind, down=down):
            corner_ref[at : at + 1, :] = down

    y_at = lax.broadcasted_iota(jnp.int32, (size_y, lanes), 0)
    lane_at = lax.broadcasted_iota(jnp.int32, (size_y, lanes), 1)
    level = sideways(cells, side_ref, None)
    packs = []
    for step in (1, -1):
        packed = jnp.zeros((size_y, lanes), jnp.float32)
        for i, q in enumerate(going(2, step)):
            edge = lanes - 1 if step == 1 else 0
            for x in range(size_x):
                at = 8 * x + i
                moved = pltpu.roll(level(q, x, y_at), (at - edge) % lanes, 1)
                packed = jnp.where(lane_at == at, moved, packed)
        packs.append(packed)
    even = place_ref[1] % 2 == 0
    first_ref[...] = jnp.where(even, packs[0], packs[1])
    second_ref[...] = jnp.where(even, packs[1], packs[0])


def pack(place, relaxed, far, near, side):
    smem = pl.BlockSpec(memory_space=pltpu.SMEM)
    vmem = pl.BlockSpec(memory_space=pltpu.VMEM)
    edge = full(far.shape[1:])
    return pl.pallas_call(
        pack_kernel,
        out_shape=(edge, edge, edge),
        in_specs=[smem] + [vmem] * 4,
        compiler_params=kernel_params(),
        name="pack",
    )(place, relaxed, far, near, side)


def stream_kernel(
    count_z, place_ref, relaxed_ref, far_ref, near_ref, side_ref, second_ref, corner_ref,
    first_ref, out_any, out_ref, sems,
):
    size_x, size_y, lanes = out_ref.shape[1:]
    shape = (size_y, lanes)
    y_at = lax.broadcasted_iota(jnp.int32, shape, 0)
    z_at = lax.broadcasted_iota(jnp.int32, shape, 1)
    y_index, z_index = (place_ref[0], place_ref[1])
    streamed = sideways(
        downwind(place_ref, relaxed_ref, far_ref, near_ref),
        side_ref,
        lambda q: corner_ref[corner_index(q) : corner_index(q) + 1, :],
    )
    even = z_index % 2 == 0
    columns = {
        -1: jnp.where(even, first_ref[...], second_ref[...]),
        1: jnp.where(even, second_ref[...], first_ref[...]),
    }
    on_side = y_at == jnp.where(y_index == 0, 0, size_y - 1)
    on_side = on_side | ((z_at == 0) & (z_index == 0))
    on_side = on_side | ((z_at == lanes - 1) & (z_index == count_z - 1))
    copies = []
    for q in range(19):
        step_z = int(velocity_table[q][2])
        z_edge = 0 if step_z == 1 else lanes - 1
        for x in range(size_x):
            cells = streamed(q, x, y_at)
            if step_z != 0:
                at = 8 * x + going(2, step_z).index(q)
                cells = jnp.where(
                    z_at == z_edge,
                    pltpu.roll(columns[step_z], (z_edge - at) % lanes, 1),
                    pltpu.roll(cells, step_z % lanes, 1),
                )
            out_ref[q, x] = jnp.where(on_side, far_field[q], cells)
        copies.append(pltpu.make_async_copy(out_ref.at[q], out_any.at[q], sems.at[q]))
        copies[-1].start()
    for copy in copies:
        copy.wait()


def stream(count_z, place, relaxed, *halos):
    rows, lanes = relaxed.shape[1:]
    size_y = halos[0].shape[1]
    smem = pl.BlockSpec(memory_space=pltpu.SMEM)
    vmem = pl.BlockSpec(memory_space=pltpu.VMEM)
    shape = (19, rows // size_y, size_y, lanes)
    return pl.pallas_call(
        functools.partial(stream_kernel, count_z),
        out_shape=full(shape),
        in_specs=[smem] + [vmem] * (1 + len(halos)),
        out_specs=pl.BlockSpec(memory_space=pltpu.HBM),
        scratch_shapes=[pltpu.VMEM(shape, jnp.float32), pltpu.SemaphoreType.DMA((19,))],
        compiler_params=kernel_params(),
        name="stream",
    )(place, relaxed, *halos)


def per_device(
    populations,
    solid_cells,
    slot_cells,
    slot_weights,
    slot_owner,
    slot_block,
    train_of_block,
    marker_area,
    train_velocity,
):
    size_x, size_y, size_z = (populations.shape[1], populations.shape[2], populations.shape[3])
    lines = size_x * size_y
    slots, kernel, mark = (slot_cells.shape[3], slot_cells.shape[4], slot_cells.shape[5])
    owned = train_of_block.shape[3]
    count_x, count_y, count_z = (lax.axis_size(axis) for axis in ("gx", "gy", "gz"))
    x_index, y_index, z_index = (lax.axis_index(axis) for axis in ("gx", "gy", "gz"))
    place = jnp.stack([y_index, z_index, x_index * count_y + y_index, x_index % 2])
    place = place.astype(jnp.int32)
    inputs = [
        pltpu.with_memory_space_constraint(entries, pltpu.HBM)
        for entries in (
            populations.reshape(19, lines, size_z),
            slot_cells.reshape(slots * kernel, mark),
            slot_weights.reshape(slots * kernel, mark),
            marker_area.reshape(owned, mark),
            slot_owner.reshape(1, slots),
            slot_block.reshape(1, slots),
            train_of_block.reshape(1, owned),
        )
    ]
    own, pops, cells, weights = sample(place, *inputs)
    swap = [(0, 1), (1, 0)]

    def across_x(entries, distance):
        return lax.ppermute(entries, "gx", [(i, i ^ distance) for i in range(count_x)])

    def across_y(entries):
        return lax.ppermute(entries, "gy", swap)

    third, first = (across_x(own, distance) for distance in (3, 1))
    beside = across_y(own)
    third_beside = across_y(third)
    second = across_x(lax.optimization_barrier((third, beside))[0], 1)
    first_beside = across_y(first)
    last = across_x(third_beside, 1)
    whole = [own, first, third, second, beside, first_beside, third_beside]
    early = settle_early(slots, owned, train_velocity, whole)
    solid = solid_cells.reshape(lines, size_z)
    relaxed, far, near, side, marker_force = spread(
        owned, place, own, last, early, cells, weights, pops, solid
    )
    evens = range(0, count_x, 2)
    far = lax.ppermute(
        far,
        "gx",
        [(i, (i - 1) % count_x) for i in evens] + [((i - 1) % count_x, i) for i in evens],
    )
    near = lax.ppermute(near, "gx", [(i, i + 1) for i in evens] + [(i + 1, i) for i in evens])
    side = across_y(side)
    corner, up_first, down_first = pack(place, relaxed, far, near, side)
    inner = [(i, i + 1) for i in range(0, count_z - 1, 2)]
    outer = [(i, i + 1) for i in range(1, count_z - 1, 2)]
    down_first = lax.ppermute(down_first, "gz", outer + [(j, i) for i, j in outer])
    corner = across_y(corner)
    up_first = lax.ppermute(up_first, "gz", inner + [(j, i) for i, j in inner])
    populations_next = stream(
        count_z, place, relaxed, far, near, side, down_first, corner, up_first
    )
    marker_force = marker_force.transpose(1, 0, 2).reshape(1, 1, 1, owned, 3, mark)
    return (populations_next, marker_force)


def solution(mesh):
    placed = (
        P(None, "gx", "gy", "gz"),
        P("gx", "gy", "gz"),
        P("gx", "gy", "gz", None, None, None),
        P("gx", "gy", "gz", None, None, None),
        P("gx", "gy", "gz", None, None),
        P("gx", "gy", "gz", None),
        P("gx", "gy", "gz", None),
        P("gx", "gy", "gz", None, None),
        P(),
    )
    small = mesh.shape["gy"] == 2 and mesh.shape["gx"] == 4 and mesh.shape["gz"] % 2 == 0
    return jax.shard_map(
        per_device if small else per_device_general,
        mesh=mesh,
        in_specs=placed,
        out_specs=(P(None, "gx", "gy", "gz"), P("gx", "gy", "gz", None, None, None)),
        check_vma=False,
    )
```

```python
import functools
import jax
import jax.numpy as jnp
import numpy as np
from jax import lax
from jax.experimental import pallas as pl
from jax.experimental.pallas import tpu as pltpu
from jax.sharding import PartitionSpec as P

velocity_table = np.array(
    [
        [0, 0, 0],
        [1, 0, 0],
        [-1, 0, 0],
        [0, 1, 0],
        [0, -1, 0],
        [0, 0, 1],
        [0, 0, -1],
        [1, 1, 0],
        [-1, -1, 0],
        [1, -1, 0],
        [-1, 1, 0],
        [1, 0, 1],
        [-1, 0, -1],
        [1, 0, -1],
        [-1, 0, 1],
        [0, 1, 1],
        [0, -1, -1],
        [0, 1, -1],
        [0, -1, 1],
    ]
)
weight_table = [1.0 / 3.0] + [1.0 / 18.0] * 6 + [1.0 / 36.0] * 12
opposite_table = [0, 2, 1, 4, 3, 6, 5, 8, 7, 10, 9, 12, 11, 14, 13, 16, 15, 18, 17]
stress_pairs = [(0, 0), (1, 1), (2, 2), (0, 1), (0, 2), (1, 2)]
tau_base = 0.55
smag_term = 18.0 * 1.4142135623730951 * 0.17 * 0.17
regular_eps = 0.0001
stiffness = 2.0
far_velocity = (0.02, 0.06, 0.0)
vmem_bytes = 16 << 20
group = 8
fine = jnp.float8_e4m3fn
matrix_points = 2


def going(axis, step):
    return [q for q in range(19) if int(velocity_table[q][axis]) == step]


def project(direction, vector):
    projection = 0.0 * vector[0]
    for component in range(3):
        lattice_step = int(velocity_table[direction][component])
        if lattice_step != 0:
            projection = projection + lattice_step * vector[component]
    return projection


def moments(populations):
    density = populations[0]
    momentum = [jnp.zeros_like(density) for component in range(3)]
    for direction in range(1, 19):
        density = density + populations[direction]
        for component in range(3):
            lattice_step = int(velocity_table[direction][component])
            if lattice_step == 1:
                momentum[component] = momentum[component] + populations[direction]
            elif lattice_step == -1:
                momentum[component] = momentum[component] - populations[direction]
    return (density, momentum)


def equilibrium(density, velocity):
    speed_sq = velocity[0] * velocity[0] + velocity[1] * velocity[1] + velocity[2] * velocity[2]
    result = []
    for direction in range(19):
        projected = project(direction, velocity)
        result.append(
            weight_table[direction]
            * density
            * (1.0 + 3.0 * projected + 4.5 * projected * projected - 1.5 * speed_sq)
        )
    return result


far_field = [float(np.float32(value)) for value in equilibrium(1.0, list(far_velocity))]


def collide(populations, cell_force, solid_cells):
    density, momentum = moments(populations)
    velocity = [
        (momentum[component] + 0.5 * cell_force[component]) / density for component in range(3)
    ]
    balance = equilibrium(density, velocity)
    stress = [jnp.zeros_like(density) for pair_pos in range(6)]
    for direction in range(19):
        non_eq = populations[direction] - balance[direction]
        for pair_pos in range(6):
            row_axis, col_axis = stress_pairs[pair_pos]
            factor = int(velocity_table[direction][row_axis] * velocity_table[direction][col_axis])
            if factor != 0:
                stress[pair_pos] = stress[pair_pos] + factor * non_eq
    shear_sq = stress[0] * stress[0] + stress[1] * stress[1] + stress[2] * stress[2]
    shear_sq = shear_sq + 2.0 * (
        stress[3] * stress[3] + stress[4] * stress[4] + stress[5] * stress[5]
    )
    magnitude = jnp.sqrt(shear_sq + regular_eps)
    relax_time = 0.5 * (tau_base + jnp.sqrt(tau_base * tau_base + smag_term * magnitude / density))
    relax_rate = 1.0 / relax_time
    guo_factor = 1.0 - 0.5 * relax_rate
    speed_force = (
        velocity[0] * cell_force[0] + velocity[1] * cell_force[1] + velocity[2] * cell_force[2]
    )
    result = []
    for direction in range(19):
        along_force = project(direction, cell_force)
        along_speed = project(direction, velocity)
        source = (
            guo_factor
            * weight_table[direction]
            * (3.0 * (along_force - speed_force) + 9.0 * along_speed * along_force)
        )
        relaxed = (
            populations[direction]
            - (populations[direction] - balance[direction]) * relax_rate
            + source
        )
        result.append(jnp.where(solid_cells == 1, populations[opposite_table[direction]], relaxed))
    return result


def with_halo(cells, sides, width):
    for axis, dim in sides:
        count = lax.axis_size(axis)
        head = lax.slice_in_dim(cells, 0, width, axis=dim)
        tail = lax.slice_in_dim(cells, cells.shape[dim] - width, cells.shape[dim], axis=dim)
        cells = jnp.concatenate(
            [
                lax.ppermute(tail, axis, [(i, (i + 1) % count) for i in range(count)]),
                cells,
                lax.ppermute(head, axis, [((i + 1) % count, i) for i in range(count)]),
            ],
            axis=dim,
        )
    return cells


def settle(received, labels, owned, train_of_block, marker_area, train_velocity, mark):
    rows_in = received.reshape(-1, 3 * mark)
    label_rows = labels.reshape(-1)
    owner_match = (label_rows[None, :] == jnp.arange(owned, dtype=jnp.int32)[:, None]).astype(
        jnp.float32
    )
    marker_velocity = jnp.dot(owner_match, rows_in, precision=lax.Precision.HIGHEST).reshape(
        owned, 3, mark
    )
    trains = train_velocity.shape[0]
    train_rows = train_of_block.reshape(owned)
    train_match = (train_rows[:, None] == jnp.arange(trains, dtype=jnp.int32)[None, :]).astype(
        jnp.float32
    )
    target = jnp.dot(train_match, train_velocity, precision=lax.Precision.HIGHEST)
    areas = marker_area.reshape(owned, mark)
    marker_force = stiffness * areas[:, None, :] * (target[:, :, None] - marker_velocity)
    back_rows = jnp.dot(
        owner_match.T, marker_force.reshape(owned, 3 * mark), precision=lax.Precision.HIGHEST
    )
    return (marker_force, back_rows)


def per_device_general(
    populations,
    solid_cells,
    slot_cells,
    slot_weights,
    slot_owner,
    slot_block,
    train_of_block,
    marker_area,
    train_velocity,
):
    size_x, size_y, size_z = (populations.shape[1], populations.shape[2], populations.shape[3])
    cell_count = size_x * size_y * size_z
    slots, kernel, mark = (slot_cells.shape[3], slot_cells.shape[4], slot_cells.shape[5])
    owned = train_of_block.shape[3]
    peers_x = lax.axis_size("gx")
    peers_y = lax.axis_size("gy")
    peers = peers_x * peers_y
    capacity = max(2, 2 * slots // peers)
    density, momentum = moments(populations)
    rest_velocity = jnp.stack([momentum[component] / density for component in range(3)]).reshape(
        3, cell_count
    )
    cells = slot_cells.reshape(slots, kernel, mark)
    weights = slot_weights.reshape(slots, kernel, mark)
    partial_value = jnp.sum(rest_velocity[:, cells] * weights[None], axis=2)
    slot_rows = partial_value.transpose(1, 0, 2).reshape(slots, 3 * mark)
    slot_dest = slot_owner.reshape(slots)
    blocks = slot_block.reshape(slots)
    order = jnp.arange(slots, dtype=jnp.int32)
    earlier = (slot_dest[None, :] == slot_dest[:, None]) & (order[None, :] < order[:, None])
    slot_rank = jnp.sum(earlier.astype(jnp.int32), axis=1)
    target_row = slot_dest * capacity + slot_rank
    buffer_rows = jnp.arange(peers * capacity, dtype=jnp.int32)
    matches = buffer_rows[:, None] == target_row[None, :]
    placement = matches.astype(jnp.float32)
    outgoing = jnp.dot(placement, slot_rows, precision=lax.Precision.HIGHEST)
    labels = jnp.sum(jnp.where(matches, blocks[None, :] + 1, 0), axis=1) - 1
    received, got_labels = (
        lax.all_to_all(
            outgoing.reshape(peers, capacity, 3 * mark),
            ("gx", "gy"),
            split_axis=0,
            concat_axis=0,
            tiled=True,
        ),
        lax.all_to_all(
            labels.reshape(peers, capacity), ("gx", "gy"), split_axis=0, concat_axis=0, tiled=True
        ),
    )
    marker_force, back_rows = settle(
        received, got_labels, owned, train_of_block, marker_area, train_velocity, mark
    )
    returned = lax.all_to_all(
        back_rows.reshape(peers, capacity, 3 * mark),
        ("gx", "gy"),
        split_axis=0,
        concat_axis=0,
        tiled=True,
    )
    slot_force = jnp.dot(
        placement.T, returned.reshape(peers * capacity, 3 * mark), precision=lax.Precision.HIGHEST
    )
    slot_force = slot_force.reshape(slots, 3, mark).transpose(1, 0, 2)
    contrib = weights[None] * slot_force[:, :, None, :]
    cell_force = (
        jnp.zeros((3, cell_count), jnp.float32).at[:, cells.reshape(-1)].add(contrib.reshape(3, -1))
    )
    cell_force = cell_force.reshape(3, size_x, size_y, size_z)
    relaxed = collide(populations, cell_force, solid_cells)
    padded = with_halo(jnp.stack(relaxed), (("gx", 1), ("gy", 2), ("gz", 3)), 1)
    parts = []
    for direction in range(19):
        shift_x = 1 - int(velocity_table[direction][0])
        shift_y = 1 - int(velocity_table[direction][1])
        shift_z = 1 - int(velocity_table[direction][2])
        parts.append(
            padded[
                direction,
                shift_x : shift_x + size_x,
                shift_y : shift_y + size_y,
                shift_z : shift_z + size_z,
            ]
        )
    read = jnp.stack(parts)
    total_y = size_y * lax.axis_size("gy")
    total_z = size_z * lax.axis_size("gz")
    global_y = lax.axis_index("gy") * size_y + jnp.arange(size_y, dtype=jnp.int32)
    global_z = lax.axis_index("gz") * size_z + jnp.arange(size_z, dtype=jnp.int32)
    on_side = ((global_y == 0) | (global_y == total_y - 1))[:, None] | (
        (global_z == 0) | (global_z == total_z - 1)
    )[None, :]
    far_field = jnp.array(equilibrium(1.0, list(far_velocity)), dtype=jnp.float32)
    populations_next = jnp.where(on_side[None, None], far_field[:, None, None, None], read)
    return (populations_next, marker_force.reshape(1, 1, 1, owned, 3, mark))


def full(shape):
    return jax.ShapeDtypeStruct(shape, jnp.float32)


def kernel_params():
    return pltpu.CompilerParams(vmem_limit_bytes=vmem_bytes)


def low_half(shape):
    return lax.broadcasted_iota(jnp.int32, shape, 1) < shape[1] // 2


def fetch(pairs, sems):
    copies = [
        pltpu.make_async_copy(source, target, sems.at[i])
        for i, (source, target) in enumerate(pairs)
    ]
    for copy in copies:
        copy.start()
    return copies


def shard_rows(slots, owned):
    return 8 + owned + 3 * slots


def sample_kernel(
    place_ref, pop_any, cells_any, weights_any, areas_any, owner_any, block_any, trains_any,
    out_ref, pop_ref, cells_ref, weights_ref, areas_ref, owner_ref, block_ref, trains_ref,
    table, parts_ref, lines_ref, spread_ref, sems,
):
    rows, lanes = (pop_ref.shape[1], pop_ref.shape[2])
    mark = cells_ref.shape[1]
    owned = areas_ref.shape[0]
    slots = owner_ref.shape[1]
    kernel = cells_ref.shape[0] // slots
    copies = fetch(
        (
            (pop_any, pop_ref),
            (cells_any, cells_ref),
            (weights_any, weights_ref),
            (areas_any, areas_ref),
            (owner_any, owner_ref),
            (block_any, block_ref),
            (trains_any, trains_ref),
        ),
        sems,
    )

    copies[0].wait()
    density, momentum = moments([pop_ref[q] for q in range(19)])
    speed = [momentum[c] / density for c in range(3)]
    largest = jnp.maximum(jnp.maximum(jnp.abs(speed[0]), jnp.abs(speed[1])), jnp.abs(speed[2]))
    largest = jnp.max(largest, axis=(0, 1), keepdims=True) + 1e-20
    scale = largest * (1.0 / 32767.0)
    fixed = [(speed[c] * (1.0 / scale) + 32768.5).astype(jnp.int32) for c in range(3)]
    words = jnp.concatenate(
        [
            (fixed[0] << 16) | fixed[1],
            (fixed[2][: rows // 2] << 16) | fixed[2][rows // 2 :],
        ],
        axis=0,
    )
    for r in range(table.shape[0]):
        table[r] = jnp.broadcast_to(words[r : r + 1], (group, lanes))
    for c in range(3):
        value = speed[c] * (224.0 / largest)
        for part in range(4):
            piece = value.astype(fine)
            parts_ref[c * rows : (c + 1) * rows, part * lanes : (part + 1) * lanes] = piece
            value = value - piece.astype(jnp.float32)
    for copy in copies[1:]:
        copy.wait()
    out_ref[8 : 8 + owned, :] = areas_ref[...]
    out_ref[0:8, :] = jnp.zeros((8, mark), jnp.float32)
    ids = (owner_ref[...] * owned + block_ref[...]).astype(jnp.float32)
    out_ref[0:1, :] = jnp.concatenate([ids] * (mark // slots), axis=1)
    out_ref[1:2, 0:owned] = trains_ref[...].astype(jnp.float32)
    mine = lax.broadcasted_iota(jnp.int32, (1, mark), 1) % owned + place_ref[2] * owned
    out_ref[2:3, :] = mine.astype(jnp.float32)

    bf = jnp.bfloat16
    iota = lax.broadcasted_iota(jnp.int32, (16, mark), 0).astype(jnp.float32)
    steps = [(iota + 16.0 * j).astype(bf) for j in range(lanes // 16)]
    line_at = [iota[0:8] + 8.0 * j for j in range(rows // 8)]
    one, zero = (jnp.ones((16, mark), bf), jnp.zeros((16, mark), bf))

    def by_matrix(first):
        for which, k in enumerate(range(kernel - matrix_points, kernel)):
            at = pl.ds(first * kernel + k, group, stride=kernel)
            cells = cells_ref[at, :]
            lines_ref[which, 0] = (cells & (lanes - 1)).astype(jnp.float32)
            lines_ref[which, 1] = (cells >> (lanes.bit_length() - 1)).astype(jnp.float32)
            lines_ref[which, 2] = weights_ref[at, :]
        for i in range(group):
            sums = [jnp.zeros((8, mark), jnp.float32) for c in range(3)]
            for which in range(matrix_points):
                lane, row, weight = (
                    lines_ref[which, entry, pl.ds(i, 8, stride=0), :] for entry in range(3)
                )
                lane = jnp.concatenate([lane, lane], axis=0).astype(bf)
                match = [jnp.where(step == lane, one, zero) for step in steps]
                match = jnp.concatenate(match, axis=0).astype(fine)
                got = jnp.dot(
                    parts_ref[...],
                    jnp.concatenate([match] * 4, axis=0),
                    preferred_element_type=jnp.float32,
                )
                for j in range(rows // 8):
                    share = jnp.where(line_at[j] == row, weight, 0.0)
                    for c in range(3):
                        here = c * rows + 8 * j
                        sums[c] = sums[c] + share * got[here : here + 8]
            for c in range(3):
                spread_ref[c, 8 * i : 8 * i + 8, :] = sums[c]
        result = []
        for c in range(3):
            total = spread_ref[c, pl.ds(0, group, stride=8), :]
            for j in range(1, 8):
                total = total + spread_ref[c, pl.ds(j, group, stride=8), :]
            result.append(total)
        return result

    def body(step, carry):
        first = pl.multiple_of(step * group, group)
        total = [jnp.zeros((group, mark), jnp.float32) for c in range(3)]
        other = by_matrix(first)
        for k in range(kernel - matrix_points):
            at = pl.ds(first * kernel + k, group, stride=kernel)
            cells = cells_ref[at, :]
            lane = cells & (lanes - 1)
            row = cells >> (lanes.bit_length() - 1)
            bits = [(row >> bit) & 1 == 1 for bit in range(rows.bit_length() - 1)]

            def choose(low, level):
                if level < 0:
                    return jnp.take_along_axis(table[low], lane, axis=1, mode="promise_in_bounds")
                lower = choose(low, level - 1)
                return jnp.where(bits[level], choose(low + (1 << level), level - 1), lower)

            pair = choose(0, len(bits) - 1)
            third = choose(rows, len(bits) - 2)
            picked = [
                lax.shift_right_logical(pair, 16),
                pair & 65535,
                jnp.where(bits[-1], third & 65535, lax.shift_right_logical(third, 16)),
            ]
            weight = weights_ref[at, :]
            for c in range(3):
                total[c] = total[c] + weight * (picked[c].astype(jnp.float32) - 32768.0)
        for c in range(3):
            here = pl.ds(pl.multiple_of(8 + owned + c * slots + first, group), group)
            out_ref[here, :] = total[c] * scale + other[c] * (largest * (1.0 / 224.0))
        return carry

    lax.fori_loop(0, slots // group, body, 0)


def sample(place, populations, cells, weights, areas, owner, block, trains):
    smem = pl.BlockSpec(memory_space=pltpu.SMEM)
    hbm = pl.BlockSpec(memory_space=pltpu.HBM)
    vmem = pl.BlockSpec(memory_space=pltpu.VMEM)
    kept = (populations, cells, weights)
    count = shard_rows(owner.shape[1], areas.shape[0])
    return pl.pallas_call(
        sample_kernel,
        out_shape=[full((count, cells.shape[1]))]
        + [jax.ShapeDtypeStruct(entries.shape, entries.dtype) for entries in kept],
        in_specs=[smem] + [hbm] * 7,
        out_specs=[vmem] * 4,
        scratch_shapes=[
            pltpu.VMEM(entries.shape, entries.dtype) for entries in (areas, owner, block, trains)
        ]
        + [
            pltpu.VMEM((populations.shape[1] * 3 // 2, group, populations.shape[2]), jnp.int32),
            pltpu.VMEM((3 * populations.shape[1], 4 * populations.shape[2]), fine),
            pltpu.VMEM((matrix_points, 3, group, cells.shape[1]), jnp.float32),
            pltpu.VMEM((3, 8 * group, cells.shape[1]), jnp.float32),
            pltpu.SemaphoreType.DMA((7,)),
        ],
        compiler_params=kernel_params(),
        name="sample",
    )(place, populations, cells, weights, areas, owner, block, trains)


def three_parts(values):
    parts = []
    for _ in range(3):
        parts.append(values.astype(jnp.bfloat16))
        values = values - parts[-1].astype(jnp.float32)
    return parts


def one_hot(mask):
    return jnp.where(mask, 1.0, 0.0).astype(jnp.bfloat16)


def wanted_labels(own_ref, slots, owned):
    mark = own_ref.shape[1]
    own = own_ref[0:8, :]
    ids, trains, mine = (jnp.broadcast_to(own[i : i + 1], (mark, mark)).T for i in range(3))
    return (ids[0:slots], mine[0:owned], trains[0:owned])


def add_shards(totals, shards, ids, mine):
    slots, owned = (ids.shape[0], mine.shape[0])
    wanted = jnp.concatenate([ids, mine], axis=0)
    for shard in shards:
        match = one_hot(wanted == shard[0:1, :])
        match = jnp.concatenate([match, match[:, 0:slots]], axis=1)
        starts = [8 + owned + c * slots for c in range(3)]
        values = jnp.concatenate([shard[at : at + slots, :] for at in starts], axis=1)
        sums = jnp.dot(
            match, jnp.concatenate(three_parts(values), axis=0), preferred_element_type=jnp.float32
        )
        held = ids == shard[2:3, :]
        parts = three_parts(shard[8 : 8 + owned, :])
        parts.append(jnp.zeros_like(parts[0]))
        area = jnp.dot(
            one_hot(held), jnp.concatenate(parts, axis=0), preferred_element_type=jnp.float32
        )
        got = (sums, area, jnp.where(held, shard[1:2, :], 0.0))
        totals = got if totals is None else [total + new for total, new in zip(totals, got)]
    return totals


def settle_kernel(slots, owned, speeds_ref, *refs):
    *shards, sums_ref, area_ref, trains_ref, rows_ref, labels_ref = refs
    mark = rows_ref.shape[1]
    for train in range(speeds_ref.shape[0]):
        for c in range(3):
            at = 3 * train + c
            rows_ref[at : at + 1, :] = jnp.full((1, mark), speeds_ref[train, c], jnp.float32)
    ids, mine, own_trains = wanted_labels(shards[0], slots, owned)
    labels_ref[...] = jnp.concatenate([ids, mine, own_trains], axis=0)
    sums_ref[...], area_ref[...], trains_ref[...] = add_shards(None, shards, ids, mine)


def settle_early(slots, owned, speeds, shards):
    mark = shards[0].shape[1]
    smem = pl.BlockSpec(memory_space=pltpu.SMEM)
    vmem = pl.BlockSpec(memory_space=pltpu.VMEM)
    return pl.pallas_call(
        functools.partial(settle_kernel, slots, owned),
        out_shape=(
            full((slots + owned, 3 * mark)),
            full((slots, mark)),
            full((slots, mark)),
            full((3 * speeds.shape[0], mark)),
            full((slots + 2 * owned, mark)),
        ),
        in_specs=[smem] + [vmem] * len(shards),
        compiler_params=kernel_params(),
        cost_estimate=pl.CostEstimate(
            flops=10**9, bytes_accessed=len(shards) * shards[0].size * 4, transcendentals=0
        ),
        name="settle",
    )(speeds, *shards)


def block_forces(rows_ref, totals, own_ref, own_trains):
    mark = own_ref.shape[1]
    sums, area, trains = totals
    slots, owned = (area.shape[0], own_trains.shape[0])
    trains = jnp.broadcast_to(jnp.sum(trains, axis=1, keepdims=True), area.shape)
    own_area = own_ref[8 : 8 + owned, :]
    forces, own_forces = ([], [])
    for c in range(3):
        target, own_target = (jnp.zeros_like(area), jnp.zeros_like(own_area))
        for train in range(rows_ref.shape[0] // 3):
            at = 3 * train + c
            speed = rows_ref[at : at + 1, :]
            target = jnp.where(trains == float(train), speed, target)
            own_target = jnp.where(own_trains == float(train), speed, own_target)
        got = sums[:, c * mark : (c + 1) * mark]
        forces.append(stiffness * area * (target - got[0:slots]))
        own_forces.append(stiffness * own_area * (own_target - got[slots:]))
    return (forces, own_forces)


def spread_kernel(
    slots, owned, place_ref, own_ref, last_ref, sums_ref, area_ref, trains_ref, speeds_ref,
    labels_ref,
    cells_ref, weights_ref, pop_ref, solid_ref,
    relaxed_ref, far_ref, near_ref, side_ref, marker_any, marker_ref, force_ref, lines_ref, acc,
    sem,
):
    rows, lanes = (pop_ref.shape[1], pop_ref.shape[2])
    size_y = 8
    mark = cells_ref.shape[1]
    kernel = cells_ref.shape[0] // slots
    bf = jnp.bfloat16
    ids = labels_ref[0:slots]
    mine, own_trains = (labels_ref[at : at + owned] for at in (slots, slots + owned))
    totals = add_shards((sums_ref[...], area_ref[...], trains_ref[...]), [last_ref], ids, mine)
    forces, own_forces = block_forces(speeds_ref, totals, own_ref, own_trains)
    largest = jnp.maximum(jnp.maximum(jnp.abs(forces[0]), jnp.abs(forces[1])), jnp.abs(forces[2]))
    largest = jnp.maximum(jnp.max(largest, axis=(0, 1), keepdims=True), 1e-20)
    scale = (224.0 * 16.0) / largest
    for c in range(3):
        force_ref[c] = forces[c] * scale
        marker_ref[c] = own_forces[c]
    marker_copy = pltpu.make_async_copy(marker_ref, marker_any, sem)
    marker_copy.start()

    acc[...] = jnp.zeros_like(acc)
    iota = lax.broadcasted_iota(jnp.int32, (16, mark), 0).astype(jnp.float32)
    steps = [(iota + 16.0 * j).astype(bf) for j in range(max(rows, lanes) // 16)]
    one, zero = (jnp.ones((16, mark), bf), jnp.zeros((16, mark), bf))

    def body(step, carry):
        first = pl.multiple_of(step * group, group)
        force = [force_ref[c, pl.ds(first, group), :] for c in range(3)]
        for k in range(kernel):
            at = pl.ds(first * kernel + k, group, stride=kernel)
            cells = cells_ref[at, :]
            weight = weights_ref[at, :]
            lane = (cells & (lanes - 1)).astype(jnp.float32)
            row = (cells >> (lanes.bit_length() - 1)).astype(jnp.float32)
            parts = []
            for c in range(3):
                value = weight * force[c]
                for _ in range(3):
                    parts.append(value.astype(fine).astype(jnp.float32))
                    value = (value - parts[-1]) * 16.0
            for which, entries in enumerate([lane, row] + parts):
                lines_ref[k, which] = entries

            def wide(which, i):
                entries = lines_ref[k, which, pl.ds(i, 8, stride=0), :]
                return jnp.concatenate([entries, entries], axis=0).astype(bf)

            left, right = ([], [])
            for i in range(group):
                lane_i, row_i = (wide(0, i), wide(1, i))
                match = [jnp.where(steps[j] == lane_i, one, zero) for j in range(lanes // 16)]
                right.append(jnp.concatenate(match, axis=0).astype(fine))
                masks = [steps[j] == row_i for j in range(rows // 16)]
                pieces = []
                for which in range(len(parts)):
                    part_i = wide(2 + which, i)
                    piece = [jnp.where(mask, part_i, zero) for mask in masks]
                    pieces.append(jnp.concatenate(piece, axis=0).astype(fine))
                left.append(jnp.concatenate(pieces, axis=0))
            acc[...] += lax.dot_general(
                jnp.concatenate(left, axis=1),
                jnp.concatenate(right, axis=1),
                (((1,), (1,)), ((), ())),
                preferred_element_type=jnp.float32,
            )
        return carry

    lax.fori_loop(0, slots // group, body, 0)
    cell_force = []
    for c in range(3):
        total = acc[3 * c * rows : (3 * c + 1) * rows, :]
        total = total + acc[(3 * c + 1) * rows : (3 * c + 2) * rows, :] * (1.0 / 16.0)
        total = total + acc[(3 * c + 2) * rows : (3 * c + 3) * rows, :] * (1.0 / 256.0)
        cell_force.append(total * (1.0 / scale))
    relaxed = collide([pop_ref[q] for q in range(19)], cell_force, solid_ref[...])
    for q in range(19):
        relaxed_ref[q] = relaxed[q]
    even = place_ref[3] == 0
    for i in range(5):
        ahead = relaxed[going(0, 1)[i]][rows - size_y :]
        behind = relaxed[going(0, -1)[i]][:size_y]
        far_ref[i] = jnp.where(even, behind, ahead)
        near_ref[i] = jnp.where(even, ahead, behind)
        for x in range(rows // size_y):
            up = relaxed[going(1, 1)[i]][size_y * x + size_y - 1 : size_y * x + size_y, :]
            down = relaxed[going(1, -1)[i]][size_y * x : size_y * x + 1, :]
            at = rows // size_y * i + x
            side_ref[at : at + 1, :] = jnp.where(place_ref[0] == 0, up, down)
    marker_copy.wait()


def spread(owned, place, own, last, early, cells, weights, populations, solid):
    mark = cells.shape[1]
    slots = early[1].shape[0]
    line_count, lanes = solid.shape
    smem = pl.BlockSpec(memory_space=pltpu.SMEM)
    vmem = pl.BlockSpec(memory_space=pltpu.VMEM)
    return pl.pallas_call(
        functools.partial(spread_kernel, slots, owned),
        out_shape=(
            full(populations.shape),
            full((5, 8, lanes)),
            full((5, 8, lanes)),
            full((24, lanes)),
            full((3, owned, mark)),
        ),
        in_specs=[smem] + [vmem] * 11,
        out_specs=[vmem] * 4 + [pl.BlockSpec(memory_space=pltpu.HBM)],
        scratch_shapes=[
            pltpu.VMEM((3, owned, mark), jnp.float32),
            pltpu.VMEM((3, slots, mark), jnp.float32),
            pltpu.VMEM((cells.shape[0] // slots, 11, group, mark), jnp.float32),
            pltpu.VMEM((9 * line_count, lanes), jnp.float32),
            pltpu.SemaphoreType.DMA,
        ],
        compiler_params=kernel_params(),
        name="spread",
    )(place, own, last, *early, cells, weights, populations, solid)


def downwind(place_ref, relaxed_ref, far_ref, near_ref):
    size_y = far_ref.shape[1]
    size_x = relaxed_ref.shape[1] // size_y
    even = place_ref[3] == 0

    def cells(q, x):
        step = int(velocity_table[q][0])
        source = x - step
        if 0 <= source < size_x:
            return relaxed_ref[q, source * size_y : (source + 1) * size_y, :]
        i = going(0, step).index(q)
        if step == 1:
            return jnp.where(even, far_ref[i], near_ref[i])
        return jnp.where(even, near_ref[i], far_ref[i])

    return cells


def sideways(cells, side_ref, edge):
    def result(q, x, y_at):
        step_x, step_y = (int(step) for step in velocity_table[q][:2])
        size_y = y_at.shape[0]
        size_x = side_ref.shape[0] // 6
        if step_y == 0:
            return cells(q, x)
        source = x - step_x
        at = size_x * going(1, step_y).index(q) + source
        halo = side_ref[at : at + 1, :] if 0 <= source < size_x else edge(q)
        turned = pltpu.roll(cells(q, x), step_y % size_y, 0)
        return jnp.where(y_at == (0 if step_y == 1 else size_y - 1), halo, turned)

    return result


def corner_index(q):
    step_y = int(velocity_table[q][1])
    return [p for p in going(1, step_y) if int(velocity_table[p][0]) != 0].index(q)


def pack_kernel(
    place_ref, relaxed_ref, far_ref, near_ref, side_ref, corner_ref, first_ref, second_ref
):
    size_y, lanes = far_ref.shape[1:]
    size_x = relaxed_ref.shape[1] // size_y
    cells = downwind(place_ref, relaxed_ref, far_ref, near_ref)
    corner_ref[...] = jnp.zeros(corner_ref.shape, jnp.float32)
    for ahead in going(1, 1):
        step_x = int(velocity_table[ahead][0])
        if step_x == 0:
            continue
        behind = opposite_table[ahead]
        up = cells(ahead, 0 if step_x == 1 else size_x - 1)[size_y - 1 : size_y, :]
        down = cells(behind, size_x - 1 if step_x == 1 else 0)[0:1, :]
        at = corner_index(ahead)
        from_behind = corner_index(behind)
        lower = place_ref[0] == 0

        @pl.when(lower)
        def _(at=at, up=up):
            corner_ref[at : at + 1, :] = up

        @pl.when(jnp.logical_not(lower))
        def _(at=from_behind, down=down):
            corner_ref[at : at + 1, :] = down

    y_at = lax.broadcasted_iota(jnp.int32, (size_y, lanes), 0)
    lane_at = lax.broadcasted_iota(jnp.int32, (size_y, lanes), 1)
    level = sideways(cells, side_ref, None)
    packs = []
    for step in (1, -1):
        packed = jnp.zeros((size_y, lanes), jnp.float32)
        for i, q in enumerate(going(2, step)):
            edge = lanes - 1 if step == 1 else 0
            for x in range(size_x):
                at = 8 * x + i
                moved = pltpu.roll(level(q, x, y_at), (at - edge) % lanes, 1)
                packed = jnp.where(lane_at == at, moved, packed)
        packs.append(packed)
    even = place_ref[1] % 2 == 0
    first_ref[...] = jnp.where(even, packs[0], packs[1])
    second_ref[...] = jnp.where(even, packs[1], packs[0])


def pack(place, relaxed, far, near, side):
    smem = pl.BlockSpec(memory_space=pltpu.SMEM)
    vmem = pl.BlockSpec(memory_space=pltpu.VMEM)
    edge = full(far.shape[1:])
    return pl.pallas_call(
        pack_kernel,
        out_shape=(edge, edge, edge),
        in_specs=[smem] + [vmem] * 4,
        compiler_params=kernel_params(),
        name="pack",
    )(place, relaxed, far, near, side)


def stream_kernel(
    count_z, place_ref, relaxed_ref, far_ref, near_ref, side_ref, second_ref, corner_ref,
    first_ref, out_any, out_ref, sems,
):
    size_x, size_y, lanes = out_ref.shape[1:]
    shape = (size_y, lanes)
    y_at = lax.broadcasted_iota(jnp.int32, shape, 0)
    z_at = lax.broadcasted_iota(jnp.int32, shape, 1)
    y_index, z_index = (place_ref[0], place_ref[1])
    streamed = sideways(
        downwind(place_ref, relaxed_ref, far_ref, near_ref),
        side_ref,
        lambda q: corner_ref[corner_index(q) : corner_index(q) + 1, :],
    )
    even = z_index % 2 == 0
    columns = {
        -1: jnp.where(even, first_ref[...], second_ref[...]),
        1: jnp.where(even, second_ref[...], first_ref[...]),
    }
    on_side = y_at == jnp.where(y_index == 0, 0, size_y - 1)
    on_side = on_side | ((z_at == 0) & (z_index == 0))
    on_side = on_side | ((z_at == lanes - 1) & (z_index == count_z - 1))
    copies = []
    for q in range(19):
        step_z = int(velocity_table[q][2])
        z_edge = 0 if step_z == 1 else lanes - 1
        for x in range(size_x):
            cells = streamed(q, x, y_at)
            if step_z != 0:
                at = 8 * x + going(2, step_z).index(q)
                cells = jnp.where(
                    z_at == z_edge,
                    pltpu.roll(columns[step_z], (z_edge - at) % lanes, 1),
                    pltpu.roll(cells, step_z % lanes, 1),
                )
            out_ref[q, x] = jnp.where(on_side, far_field[q], cells)
        copies.append(pltpu.make_async_copy(out_ref.at[q], out_any.at[q], sems.at[q]))
        copies[-1].start()
    for copy in copies:
        copy.wait()


def stream(count_z, place, relaxed, *halos):
    rows, lanes = relaxed.shape[1:]
    size_y = halos[0].shape[1]
    smem = pl.BlockSpec(memory_space=pltpu.SMEM)
    vmem = pl.BlockSpec(memory_space=pltpu.VMEM)
    shape = (19, rows // size_y, size_y, lanes)
    return pl.pallas_call(
        functools.partial(stream_kernel, count_z),
        out_shape=full(shape),
        in_specs=[smem] + [vmem] * (1 + len(halos)),
        out_specs=pl.BlockSpec(memory_space=pltpu.HBM),
        scratch_shapes=[pltpu.VMEM(shape, jnp.float32), pltpu.SemaphoreType.DMA((19,))],
        compiler_params=kernel_params(),
        name="stream",
    )(place, relaxed, *halos)


def per_device(
    populations,
    solid_cells,
    slot_cells,
    slot_weights,
    slot_owner,
    slot_block,
    train_of_block,
    marker_area,
    train_velocity,
):
    size_x, size_y, size_z = (populations.shape[1], populations.shape[2], populations.shape[3])
    lines = size_x * size_y
    slots, kernel, mark = (slot_cells.shape[3], slot_cells.shape[4], slot_cells.shape[5])
    owned = train_of_block.shape[3]
    count_x, count_y, count_z = (lax.axis_size(axis) for axis in ("gx", "gy", "gz"))
    x_index, y_index, z_index = (lax.axis_index(axis) for axis in ("gx", "gy", "gz"))
    place = jnp.stack([y_index, z_index, x_index * count_y + y_index, x_index % 2])
    place = place.astype(jnp.int32)
    inputs = [
        pltpu.with_memory_space_constraint(entries, pltpu.HBM)
        for entries in (
            populations.reshape(19, lines, size_z),
            slot_cells.reshape(slots * kernel, mark),
            slot_weights.reshape(slots * kernel, mark),
            marker_area.reshape(owned, mark),
            slot_owner.reshape(1, slots),
            slot_block.reshape(1, slots),
            train_of_block.reshape(1, owned),
        )
    ]
    own, pops, cells, weights = sample(place, *inputs)
    swap = [(0, 1), (1, 0)]

    def across_x(entries, distance):
        return lax.ppermute(entries, "gx", [(i, i ^ distance) for i in range(count_x)])

    def across_y(entries):
        return lax.ppermute(entries, "gy", swap)

    third, first = (across_x(own, distance) for distance in (3, 1))
    beside = across_y(own)
    third_beside = across_y(third)
    second = across_x(lax.optimization_barrier((third, beside))[0], 1)
    first_beside = across_y(lax.optimization_barrier((first, second))[0])
    last = across_x(third_beside, 1)
    whole = [own, first, third, second, beside, first_beside, third_beside]
    early = settle_early(slots, owned, train_velocity, whole)
    solid = solid_cells.reshape(lines, size_z)
    relaxed, far, near, side, marker_force = spread(
        owned, place, own, last, early, cells, weights, pops, solid
    )
    evens = range(0, count_x, 2)
    far = lax.ppermute(
        far,
        "gx",
        [(i, (i - 1) % count_x) for i in evens] + [((i - 1) % count_x, i) for i in evens],
    )
    near = lax.ppermute(near, "gx", [(i, i + 1) for i in evens] + [(i + 1, i) for i in evens])
    side = across_y(side)
    corner, up_first, down_first = pack(place, relaxed, far, near, side)
    inner = [(i, i + 1) for i in range(0, count_z - 1, 2)]
    outer = [(i, i + 1) for i in range(1, count_z - 1, 2)]
    down_first = lax.ppermute(down_first, "gz", outer + [(j, i) for i, j in outer])
    corner = across_y(corner)
    up_first = lax.ppermute(up_first, "gz", inner + [(j, i) for i, j in inner])
    populations_next = stream(
        count_z, place, relaxed, far, near, side, down_first, corner, up_first
    )
    marker_force = marker_force.transpose(1, 0, 2).reshape(1, 1, 1, owned, 3, mark)
    return (populations_next, marker_force)


def solution(mesh):
    placed = (
        P(None, "gx", "gy", "gz"),
        P("gx", "gy", "gz"),
        P("gx", "gy", "gz", None, None, None),
        P("gx", "gy", "gz", None, None, None),
        P("gx", "gy", "gz", None, None),
        P("gx", "gy", "gz", None),
        P("gx", "gy", "gz", None),
        P("gx", "gy", "gz", None, None),
        P(),
    )
    small = mesh.shape["gy"] == 2 and mesh.shape["gx"] == 4 and mesh.shape["gz"] % 2 == 0
    return jax.shard_map(
        per_device if small else per_device_general,
        mesh=mesh,
        in_specs=placed,
        out_specs=(P(None, "gx", "gy", "gz"), P("gx", "gy", "gz", None, None, None)),
        check_vma=False,
    )
```
